32 devices in a mesh: dp: 16 (over z, y, x), fsdp: 2 (over core).
Axes of the slice: x: 2, y: 2, z: 4, core: 2. Of those that a mesh axis runs over, the one named last changes fastest.
Arguments:
- teacher_feat: bfloat16 [1024, 256], P(('dp', 'fsdp')), may hold values from -1 to 1
- student_feat: bfloat16 [1024, 256], P(('dp', 'fsdp')), may hold values from -1 to 1
- crop_weight: bfloat16 [1024], P(('dp', 'fsdp')), may hold values from -96 to 96
- teacher_v: bfloat16 [256, 32768], P(None, 'fsdp'), may hold values from -2 to 2
- student_v: bfloat16 [256, 32768], P(None, 'fsdp'), may hold values from -2 to 2
Outputs:
- grad_v: float32 [256, 32768], P('dp', 'fsdp')
- grad_feat: float32 [1024, 256], P(('dp', 'fsdp'))
The draws below stay inside these ranges and needn't reach their ends.
All inputs are finite; a program needn't handle non-finite values.
Results may differ from the reference program's by a relative error of at most 0.0073.
Values may be sent and summed in bfloat16 or wider, within the bound.
No kernel may reach another device: no remote copies, remote signals or barrier semaphores. Data moves between devices by JAX's collectives and lax.ppermute only.
A program may use at most 128 MiB of HBM per device.

```python
import jax
import jax.numpy as jnp
from jax import lax

BOT = 256
K = 32768
ITERS = 3
CROPS = 1024


groups = 8


def directions(key):
    return jnp.clip(jax.random.normal(jax.random.fold_in(key, 100), (groups, BOT), jnp.float32), -4.0, 4.0)


def crop_groups(key):
    levels = jax.random.randint(jax.random.fold_in(key, 101), (CROPS,), 1, 256)
    counted = jnp.zeros((CROPS,), jnp.int32)
    for exponent in range(1, groups):
        counted = counted + (levels >= 2 ** exponent).astype(jnp.int32)
    return counted


def prototype_groups(key):
    return jax.random.randint(jax.random.fold_in(key, 102), (K,), 0, groups)


def crop_shared(key):
    return jnp.take(directions(key), crop_groups(key), axis=0)


def prototype_shared(key):
    return jnp.transpose(jnp.take(directions(key), prototype_groups(key), axis=0))


def draw_teacher_feat(key, part):
    shared = crop_shared(key)
    key = jax.random.fold_in(key, 3)
    jitter = jnp.clip(jax.random.normal(key, (CROPS, BOT), jnp.float32), -4.0, 4.0)
    values = 0.5 * shared + jitter
    return (0.0625 * values).astype(jnp.bfloat16)


def draw_student_feat(key, part):
    shared = crop_shared(key)
    key = jax.random.fold_in(key, 4)
    jitter = jnp.clip(jax.random.normal(key, (CROPS, BOT), jnp.float32), -4.0, 4.0)
    values = 0.6 * shared + jitter
    return (0.0625 * values).astype(jnp.bfloat16)


def draw_teacher_v(key, part):
    shared = prototype_shared(key)
    key = jax.random.fold_in(key, 5)
    jitter = jnp.clip(jax.random.normal(key, (BOT, K), jnp.float32), -4.0, 4.0)
    values = 0.5 * shared + jitter
    return (values * BOT ** (-0.5)).astype(jnp.bfloat16)


def draw_student_v(key, part):
    shared = prototype_shared(key)
    key = jax.random.fold_in(key, 6)
    position = jnp.arange(K).astype(jnp.float32)[None, :] / K
    jitter = jnp.clip(jax.random.normal(key, (BOT, K), jnp.float32), -4.0, 4.0)
    values = 2.0 * position * shared + jitter
    return jnp.clip(values * BOT ** (-0.5), -2.0, 2.0).astype(jnp.bfloat16)


def block_scale(stream_key, shape, pieces, low, largest):
    loudness = 1.0
    for dim, blocks in pieces:
        steps = jax.random.uniform(jax.random.fold_in(jax.random.fold_in(stream_key, 6), dim), (blocks,), jnp.float32, low / len(pieces), largest / len(pieces))
        loudness = loudness * jnp.repeat(jnp.exp(steps), shape[dim] // blocks).reshape((-1,) + (1,) * (len(shape) - 1 - dim))
    return loudness


def bell_draw(stream_key, dims, width, limit, cuts=(), dtype=jnp.bfloat16):
    loudness = block_scale(stream_key, dims, cuts, -0.22, 0.18) if cuts else 1.0
    result = jax.random.normal(stream_key, dims, jnp.float32) * width * loudness
    return jnp.minimum(jnp.maximum(result, -limit), limit).astype(dtype)


def setup_inputs(seed: int = 0) -> dict:
    key_of = jax.random.split(jax.random.key(seed), 6)
    teacher_feat = draw_teacher_feat(jax.random.fold_in(key_of[5], 71), 0)
    student_feat = draw_student_feat(jax.random.fold_in(key_of[5], 71), 0)
    crop_weight = bell_draw(key_of[2], (CROPS,), 16.0, 96.0, ((0, 32),))
    teacher_v = draw_teacher_v(jax.random.fold_in(key_of[5], 71), 0)
    student_v = draw_student_v(jax.random.fold_in(key_of[5], 71), 0)
    return {"teacher_feat": teacher_feat, "student_feat": student_feat, "crop_weight": crop_weight, "teacher_v": teacher_v, "student_v": student_v}


teacher_temp = 0.04
student_temp = 0.1
epsilon = 1e-06
block_rows = 512

def unit_rows(values):
    floats = values.astype(jnp.float32)
    length = jnp.sqrt(lax.optimization_barrier(jnp.sum(floats * floats, axis=1, keepdims=True)) + epsilon)
    return (floats / length, length)

def unit_columns(values):
    floats = values.astype(jnp.float32)
    length = jnp.sqrt(lax.optimization_barrier(jnp.sum(floats * floats, axis=0, keepdims=True)) + epsilon)
    return (floats / length, length)

def reference(teacher_feat, student_feat, crop_weight, teacher_v, student_v):
    teacher_hat, _ = unit_rows(teacher_feat)
    student_hat, student_len = unit_rows(student_feat)
    teacher_w, _ = unit_columns(teacher_v)
    student_w, student_wlen = unit_columns(student_v)
    teacher_wunit = teacher_w.astype(jnp.bfloat16)
    student_wunit = student_w.astype(jnp.bfloat16)
    blocks = max(CROPS // block_rows, 1)
    rows_each = CROPS // blocks
    teacher_blocks = teacher_hat.astype(jnp.bfloat16).reshape(blocks, rows_each, BOT)
    student_blocks = student_hat.astype(jnp.bfloat16).reshape(blocks, rows_each, BOT)
    weight_blocks = crop_weight.astype(jnp.float32).reshape(blocks, rows_each)

    def teacher_mass(rows_teacher):
        return jnp.exp(jnp.dot(rows_teacher, teacher_wunit, preferred_element_type=jnp.float32) / teacher_temp)
    row_scale = jnp.ones((blocks, rows_each), jnp.float32)
    col_scale = jnp.ones((K,), jnp.float32)
    for sweep_index in range(ITERS):

        def add_columns(running, inputs):
            rows_teacher, scale_rows = inputs
            mass = teacher_mass(rows_teacher) * scale_rows[:, None] * col_scale[None, :]
            return (running + lax.optimization_barrier(jnp.sum(mass, axis=0)), None)
        proto_mass, _ = lax.scan(add_columns, jnp.zeros((K,), jnp.float32), (teacher_blocks, row_scale))
        col_scale = col_scale / (proto_mass * K)

        def sum_rows(inputs):
            rows_teacher, scale_rows = inputs
            mass = teacher_mass(rows_teacher) * scale_rows[:, None] * col_scale[None, :]
            return lax.optimization_barrier(jnp.sum(mass, axis=1))
        crop_mass = lax.map(sum_rows, (teacher_blocks, row_scale))
        row_scale = row_scale / (crop_mass * CROPS)

    def backward(running, inputs):
        rows_teacher, rows_student, scale_rows, weight_rows = inputs
        target = teacher_mass(rows_teacher) * scale_rows[:, None] * col_scale[None, :] * CROPS
        student_mass = jnp.exp(jnp.dot(rows_student, student_wunit, preferred_element_type=jnp.float32) / student_temp)
        student_prob = student_mass / lax.optimization_barrier(jnp.sum(student_mass, axis=1, keepdims=True))
        gradient = ((student_prob - target) * weight_rows[:, None] / student_temp).astype(jnp.bfloat16)
        running = running + lax.dot_general(rows_student, gradient, (((0,), (0,)), ((), ())), preferred_element_type=jnp.float32)
        feature_part = lax.dot_general(gradient, student_wunit, (((1,), (1,)), ((), ())), preferred_element_type=jnp.float32)
        return (running, feature_part)
    weight_grad, feature_grad = lax.scan(backward, jnp.zeros((BOT, K), jnp.float32), (teacher_blocks, student_blocks, row_scale, weight_blocks))
    feature_grad = feature_grad.reshape(CROPS, BOT)
    grad_feat = (feature_grad - student_hat * lax.optimization_barrier(jnp.sum(student_hat * feature_grad, axis=1, keepdims=True))) / student_len
    grad_v = (weight_grad - student_w * lax.optimization_barrier(jnp.sum(student_w * weight_grad, axis=0, keepdims=True))) / student_wlen
    return (grad_v, grad_feat)
```

```python
import jax
import jax.numpy as jnp
from jax import lax
from jax.sharding import PartitionSpec as P

ITERS = 3

teacher_temp = 0.04
student_temp = 0.1
epsilon = 1e-06

EVERY = ("dp", "fsdp")


def unit_rows(values):
    floats = values.astype(jnp.float32)
    length = jnp.sqrt(jnp.sum(floats * floats, axis=1, keepdims=True) + epsilon)
    return (floats / length, length)


def unit_columns(values):
    floats = values.astype(jnp.float32)
    length = jnp.sqrt(jnp.sum(floats * floats, axis=0, keepdims=True) + epsilon)
    return (floats / length, length)


def body(teacher_feat, student_feat, crop_weight, teacher_v, student_v):
    devices = lax.axis_size("dp") * lax.axis_size("fsdp")
    own_rows, width = teacher_feat.shape
    crops = own_rows * devices
    block = teacher_v.shape[1] // lax.axis_size("dp")
    prototypes = block * devices
    first = lax.axis_index("dp") * block

    teacher_hat, _ = unit_rows(teacher_feat)
    student_hat, student_len = unit_rows(student_feat)
    units = jnp.concatenate(
        [teacher_hat.astype(jnp.bfloat16), student_hat.astype(jnp.bfloat16)], axis=1
    )
    units = lax.all_gather(units, EVERY, axis=0, tiled=True)
    teacher_unit, student_unit = units[:, :width], units[:, width:]
    weights = lax.all_gather(crop_weight, EVERY, axis=0, tiled=True).astype(jnp.float32)

    teacher_w, _ = unit_columns(lax.dynamic_slice_in_dim(teacher_v, first, block, 1))
    student_w, student_wlen = unit_columns(lax.dynamic_slice_in_dim(student_v, first, block, 1))
    student_wunit = student_w.astype(jnp.bfloat16)

    mass = jnp.exp(
        jnp.dot(teacher_unit, teacher_w.astype(jnp.bfloat16), preferred_element_type=jnp.float32)
        / teacher_temp
    )
    student_mass = jnp.exp(
        jnp.dot(student_unit, student_wunit, preferred_element_type=jnp.float32) / student_temp
    )
    student_part = jnp.sum(student_mass, axis=1)

    crop_scale = None
    for sweep in range(ITERS):
        scaled = mass if sweep == 0 else mass * crop_scale[:, None]
        proto_scale = 1.0 / (prototypes * jnp.sum(scaled, axis=0))
        crop_part = jnp.sum(mass * proto_scale[None, :], axis=1)
        if sweep == 0:
            sums = lax.psum(jnp.stack([crop_part, student_part]), EVERY)
            crop_mass, student_total = sums[0], sums[1]
        else:
            crop_mass = lax.psum(crop_part, EVERY)
        crop_scale = 1.0 / (crops * crop_mass)

    target = crops * (mass * crop_scale[:, None] * proto_scale[None, :])
    student_prob = student_mass / student_total[:, None]
    gradient = ((student_prob - target) * weights[:, None] / student_temp).astype(jnp.bfloat16)
    feature_part = lax.dot_general(
        gradient, student_wunit, (((1,), (1,)), ((), ())), preferred_element_type=jnp.float32
    )
    weight_grad = lax.dot_general(
        student_unit, gradient, (((0,), (0,)), ((), ())), preferred_element_type=jnp.float32
    )
    weight_dot = jnp.sum(student_w * weight_grad, axis=0, keepdims=True)
    grad_block = (weight_grad - student_w * weight_dot) / student_wlen

    feature_all = lax.all_to_all(
        feature_part.astype(jnp.bfloat16).reshape(devices, own_rows, width), EVERY, 0, 0
    )
    feature_grad = jnp.sum(feature_all.astype(jnp.float32), axis=0)
    grad_feat = (
        feature_grad - student_hat * jnp.sum(student_hat * feature_grad, axis=1, keepdims=True)
    ) / student_len
    grad_v = lax.all_to_all(grad_block.astype(jnp.bfloat16), "dp", 0, 1, tiled=True)
    return (grad_v.astype(jnp.float32), grad_feat)


def solution(mesh):
    placed = (
        P(EVERY, None),
        P(EVERY, None),
        P(EVERY),
        P(None, "fsdp"),
        P(None, "fsdp"),
    )
    return jax.shard_map(
        body,
        mesh=mesh,
        in_specs=placed,
        out_specs=(P("dp", "fsdp"), P(EVERY, None)),
        check_vma=False,
    )
```

```python
import jax
import jax.numpy as jnp
from jax import lax
from jax.sharding import PartitionSpec as P

ITERS = 3

teacher_temp = 0.04
student_temp = 0.1
epsilon = 1e-06

EVERY = ("dp", "fsdp")


def unit_rows(values):
    floats = values.astype(jnp.float32)
    length = jnp.sqrt(jnp.sum(floats * floats, axis=1, keepdims=True) + epsilon)
    return (floats / length, length)


def unit_columns(values):
    floats = values.astype(jnp.float32)
    length = jnp.sqrt(jnp.sum(floats * floats, axis=0, keepdims=True) + epsilon)
    return (floats / length, length)


COPY_BYTES = 1 << 22


def share(values, axes):
    count = lax.axis_size(axes)
    if count * values.size * values.dtype.itemsize > COPY_BYTES:
        return lax.all_gather(values, axes)
    return lax.all_to_all(jnp.broadcast_to(values, (count, *values.shape)), axes, 0, 0)


def add_up(values):
    if lax.axis_size(EVERY) * values.size * values.dtype.itemsize > COPY_BYTES:
        return lax.psum(values, EVERY)
    return jnp.sum(share(values, EVERY), axis=0)


def body(teacher_feat, student_feat, crop_weight, teacher_v, student_v):
    fsdp = lax.axis_size("fsdp")
    devices = lax.axis_size("dp") * fsdp
    own_rows, width = teacher_feat.shape
    crops = own_rows * devices
    block = teacher_v.shape[1] // lax.axis_size("dp")
    prototypes = block * devices
    first = lax.axis_index("dp") * block

    teacher_hat, _ = unit_rows(teacher_feat)
    student_hat, student_len = unit_rows(student_feat)
    units = jnp.concatenate(
        [teacher_hat.astype(jnp.bfloat16), student_hat.astype(jnp.bfloat16)], axis=1
    )
    units = share(share(units, "dp"), "fsdp").reshape(crops, 2 * width)
    teacher_unit, student_unit = units[:, :width], units[:, width:]

    teacher_w, _ = unit_columns(lax.dynamic_slice_in_dim(teacher_v, first, block, 1))
    student_w, student_wlen = unit_columns(lax.dynamic_slice_in_dim(student_v, first, block, 1))
    student_wunit = student_w.astype(jnp.bfloat16)

    mass = jnp.exp(
        jnp.dot(teacher_unit, teacher_w.astype(jnp.bfloat16), preferred_element_type=jnp.float32)
        / teacher_temp
    )
    student_mass = jnp.exp(
        jnp.dot(student_unit, student_wunit, preferred_element_type=jnp.float32) / student_temp
    )
    student_part = jnp.sum(student_mass, axis=1)

    crop_scale = None
    for sweep in range(ITERS):
        scaled = mass if sweep == 0 else mass * crop_scale[:, None]
        proto_scale = 1.0 / (prototypes * jnp.sum(scaled, axis=0))
        crop_part = jnp.sum(mass * proto_scale[None, :], axis=1)
        if sweep == 0:
            placed = jnp.zeros((fsdp, crops // (fsdp * own_rows), own_rows), jnp.float32)
            own = crop_weight.astype(jnp.float32)[None, None]
            spot = (lax.axis_index("fsdp"), lax.axis_index("dp"), 0)
            placed = lax.dynamic_update_slice(placed, own, spot).reshape(crops)
            sums = add_up(jnp.stack([crop_part, student_part, placed]))
            crop_mass, student_total, weights = sums[0], sums[1], sums[2]
        else:
            crop_mass = add_up(crop_part)
        crop_scale = 1.0 / (crops * crop_mass)

    target = crops * (mass * crop_scale[:, None] * proto_scale[None, :])
    student_prob = student_mass / student_total[:, None]
    gradient = ((student_prob - target) * weights[:, None] / student_temp).astype(jnp.bfloat16)
    feature_part = lax.dot_general(
        gradient, student_wunit, (((1,), (1,)), ((), ())), preferred_element_type=jnp.float32
    )
    weight_grad = lax.dot_general(
        student_unit, gradient, (((0,), (0,)), ((), ())), preferred_element_type=jnp.float32
    )
    weight_dot = jnp.sum(student_w * weight_grad, axis=0, keepdims=True)
    grad_block = (weight_grad - student_w * weight_dot) / student_wlen

    feature_sent = feature_part.astype(jnp.bfloat16).reshape(fsdp, -1, own_rows, width)
    feature_sent = jnp.swapaxes(feature_sent, 0, 1).reshape(devices, own_rows, width)
    feature_all = lax.all_to_all(feature_sent, EVERY, 0, 0)
    feature_grad = jnp.sum(feature_all.astype(jnp.float32), axis=0)
    grad_feat = (
        feature_grad - student_hat * jnp.sum(student_hat * feature_grad, axis=1, keepdims=True)
    ) / student_len
    grad_v = lax.all_to_all(grad_block.astype(jnp.bfloat16), "dp", 0, 1, tiled=True)
    return (grad_v.astype(jnp.float32), grad_feat)


def solution(mesh):
    placed = (
        P(EVERY, None),
        P(EVERY, None),
        P(EVERY),
        P(None, "fsdp"),
        P(None, "fsdp"),
    )
    return jax.shard_map(
        body,
        mesh=mesh,
        in_specs=placed,
        out_specs=(P("dp", "fsdp"), P(EVERY, None)),
        check_vma=False,
    )
```

```python
import functools
import math

import jax
import jax.numpy as jnp
from jax import lax
from jax.experimental import pallas as pl
from jax.experimental.pallas import tpu as pltpu
from jax.sharding import Mesh
from jax.sharding import PartitionSpec as P

ITERS = 3

teacher_temp = 0.04
student_temp = 0.1
epsilon = 1e-06

GROUPS = 4
TILE = 256
SWEEP_TILE = 64
VMEM_BYTES = 24 << 20
KEPT_BYTES = 34 << 20

EVERY = ("dp", "fsdp")
GROUP = ("block", "fsdp")


def unit_rows(values):
    floats = values.astype(jnp.float32)
    length = jnp.sqrt(jnp.sum(floats * floats, axis=1, keepdims=True) + epsilon)
    return (floats / length, length)


def unit_columns(values):
    floats = values.astype(jnp.float32)
    length = jnp.sqrt(jnp.sum(floats * floats, axis=0, keepdims=True) + epsilon)
    return (floats / length, length)


COPY_BYTES = 1 << 22


def share(values, axes):
    count = lax.axis_size(axes)
    if count * values.size * values.dtype.itemsize > COPY_BYTES:
        return lax.all_gather(values, axes)
    return lax.all_to_all(jnp.broadcast_to(values, (count, *values.shape)), axes, 0, 0)


def add_up(values):
    if lax.axis_size(EVERY) * values.size * values.dtype.itemsize > COPY_BYTES:
        return lax.psum(values, EVERY)
    return jnp.sum(share(values, EVERY), axis=0)


def plain_body(teacher_feat, student_feat, crop_weight, teacher_v, student_v):
    fsdp = lax.axis_size("fsdp")
    devices = lax.axis_size("dp") * fsdp
    own_rows, width = teacher_feat.shape
    crops = own_rows * devices
    block = teacher_v.shape[1] // lax.axis_size("dp")
    prototypes = block * devices
    first = lax.axis_index("dp") * block

    teacher_hat, _ = unit_rows(teacher_feat)
    student_hat, student_len = unit_rows(student_feat)
    units = jnp.concatenate(
        [teacher_hat.astype(jnp.bfloat16), student_hat.astype(jnp.bfloat16)], axis=1
    )
    units = share(share(units, "dp"), "fsdp").reshape(crops, 2 * width)
    teacher_unit, student_unit = units[:, :width], units[:, width:]

    teacher_w, _ = unit_columns(lax.dynamic_slice_in_dim(teacher_v, first, block, 1))
    student_w, student_wlen = unit_columns(lax.dynamic_slice_in_dim(student_v, first, block, 1))
    student_wunit = student_w.astype(jnp.bfloat16)

    mass = jnp.exp(
        jnp.dot(teacher_unit, teacher_w.astype(jnp.bfloat16), preferred_element_type=jnp.float32)
        / teacher_temp
    )
    student_mass = jnp.exp(
        jnp.dot(student_unit, student_wunit, preferred_element_type=jnp.float32) / student_temp
    )
    student_part = jnp.sum(student_mass, axis=1)

    crop_scale = None
    for sweep in range(ITERS):
        scaled = mass if sweep == 0 else mass * crop_scale[:, None]
        proto_scale = 1.0 / (prototypes * jnp.sum(scaled, axis=0))
        crop_part = jnp.sum(mass * proto_scale[None, :], axis=1)
        if sweep == 0:
            placed = jnp.zeros((fsdp, crops // (fsdp * own_rows), own_rows), jnp.float32)
            own = crop_weight.astype(jnp.float32)[None, None]
            spot = (lax.axis_index("fsdp"), lax.axis_index("dp"), 0)
            placed = lax.dynamic_update_slice(placed, own, spot).reshape(crops)
            sums = add_up(jnp.stack([crop_part, student_part, placed]))
            crop_mass, student_total, weights = sums[0], sums[1], sums[2]
        else:
            crop_mass = add_up(crop_part)
        crop_scale = 1.0 / (crops * crop_mass)

    target = crops * (mass * crop_scale[:, None] * proto_scale[None, :])
    student_prob = student_mass / student_total[:, None]
    gradient = ((student_prob - target) * weights[:, None] / student_temp).astype(jnp.bfloat16)
    feature_part = lax.dot_general(
        gradient, student_wunit, (((1,), (1,)), ((), ())), preferred_element_type=jnp.float32
    )
    weight_grad = lax.dot_general(
        student_unit, gradient, (((0,), (0,)), ((), ())), preferred_element_type=jnp.float32
    )
    weight_dot = jnp.sum(student_w * weight_grad, axis=0, keepdims=True)
    grad_block = (weight_grad - student_w * weight_dot) / student_wlen

    feature_sent = feature_part.astype(jnp.bfloat16).reshape(fsdp, -1, own_rows, width)
    feature_sent = jnp.swapaxes(feature_sent, 0, 1).reshape(devices, own_rows, width)
    feature_all = lax.all_to_all(feature_sent, EVERY, 0, 0)
    feature_grad = jnp.sum(feature_all.astype(jnp.float32), axis=0)
    grad_feat = (
        feature_grad - student_hat * jnp.sum(student_hat * feature_grad, axis=1, keepdims=True)
    ) / student_len
    grad_v = lax.all_to_all(grad_block.astype(jnp.bfloat16), "dp", 0, 1, tiled=True)
    return (grad_v.astype(jnp.float32), grad_feat)


def call(kernel, out_shape, flops=0, moved=0, exps=0, **more):
    return pl.pallas_call(
        kernel,
        out_shape=out_shape,
        compiler_params=pltpu.CompilerParams(vmem_limit_bytes=VMEM_BYTES),
        cost_estimate=pl.CostEstimate(flops=flops, bytes_accessed=moved, transcendentals=exps),
        **more,
    )


def units_kernel(teacher_ref, student_ref, weight_ref, sent_ref):
    rows, width = teacher_ref.shape
    teacher, _ = unit_rows(teacher_ref[...])
    student, _ = unit_rows(student_ref[...])
    for group in range(sent_ref.shape[0]):
        sent_ref[group, :rows, :width] = teacher.astype(jnp.bfloat16)
        sent_ref[group, :rows, width:] = student.astype(jnp.bfloat16)
        sent_ref[group, rows:, :] = weight_ref[...]


def directions_kernel(block_ref, teacher_ref, student_ref, teacher_out, student_out, copy_out, inverse_out):
    teacher, _ = unit_columns(teacher_ref[...])
    teacher_out[...] = jnp.transpose(teacher).astype(jnp.bfloat16)
    student, length = unit_columns(student_ref[...])
    student_out[...] = jnp.transpose(student).astype(jnp.bfloat16)
    copy_out[...] = student_ref[...]
    inverse_out[...] = 1.0 / length


def in_crop_order(got_ref, units_ref):
    devices, per_device, _ = got_ref.shape
    rows = per_device // (units_ref.shape[0] // (devices * per_device) * GROUPS)
    for device in range(devices):
        for group in range(GROUPS):
            start = (group * devices + device) * rows
            units_ref[start : start + rows, :] = got_ref[device, group * rows : (group + 1) * rows, :]


def exponentials(directions, units, temperature):
    logits = lax.dot_general(
        directions, units, (((1,), (1,)), ((), ())), preferred_element_type=jnp.float32
    )
    return jnp.exp2(logits * (math.log2(math.e) / temperature))


def fold(values):
    rows, lanes = values.shape
    return jnp.sum(values.reshape(rows // 8, 8, lanes), axis=0)


def teacher_kernel(prototypes, directions_ref, got_ref, weight_ref, mass_ref, sent_ref, units_ref, total_ref):
    in_crop_order(got_ref, units_ref)
    total_ref[...] = jnp.zeros_like(total_ref)

    @pl.loop(0, directions_ref.shape[0] // TILE)
    def _(step):
        here = pl.ds(pl.multiple_of(step * TILE, TILE), TILE)
        mass = exponentials(directions_ref[here, :], units_ref[...], teacher_temp)
        mass_ref[here, :] = mass
        scale = 1.0 / (prototypes * jnp.sum(mass, axis=1, keepdims=True))
        total_ref[...] += fold(mass * scale)

    total = jnp.sum(total_ref[...], axis=0, keepdims=True)
    for device in range(sent_ref.shape[0]):
        sent_ref[device, 0:1, :] = total
        sent_ref[device, 1:2, :] = weight_ref[...]


def student_kernel(directions_ref, got_ref, mass_ref, part_ref, turned_ref, units_ref, total_ref):
    in_crop_order(got_ref, units_ref)
    turned_ref[...] = jnp.transpose(units_ref[...].astype(jnp.float32)).astype(jnp.bfloat16)
    total_ref[...] = jnp.zeros_like(total_ref)

    @pl.loop(0, directions_ref.shape[0] // TILE)
    def _(step):
        here = pl.ds(pl.multiple_of(step * TILE, TILE), TILE)
        mass = exponentials(directions_ref[here, :], units_ref[...], student_temp)
        mass_ref[here, :] = mass
        total_ref[...] += fold(mass)

    part_ref[...] = jnp.sum(total_ref[...], axis=0, keepdims=True)


def received(got_ref, row):
    total = got_ref[0, row : row + 1, :]
    for device in range(1, got_ref.shape[0]):
        total = total + got_ref[device, row : row + 1, :]
    return total


def sweep_kernel(prototypes, crops, extra, mass_ref, got_ref, *refs):
    part_ref = refs[0] if extra else None
    sent_ref, scale_ref, total_ref = refs[-3:]
    crop_scale = 1.0 / (crops * received(got_ref, 0))
    total_ref[...] = jnp.zeros_like(total_ref)

    @pl.loop(0, mass_ref.shape[0] // SWEEP_TILE)
    def _(step):
        here = pl.ds(pl.multiple_of(step * SWEEP_TILE, SWEEP_TILE), SWEEP_TILE)
        mass = mass_ref[here, :]
        scale = 1.0 / (prototypes * jnp.sum(mass * crop_scale, axis=1, keepdims=True))
        scale_ref[here, :] = scale
        total_ref[...] += fold(mass * scale)

    total = jnp.sum(total_ref[...], axis=0, keepdims=True)
    for device in range(sent_ref.shape[0]):
        sent_ref[device, 0:1, :] = total
        if extra:
            sent_ref[device, 1:2, :] = part_ref[...]


def gradient_kernel(
    group_ref, teacher_ref, student_ref, scale_ref, got_ref, first_ref, turned_ref, copy_ref, inverse_ref,
    sent_ref, feature_ref, gradient_ref, weight_ref, unit_ref, sum_ref,
):
    group = group_ref[0]
    crops = student_ref.shape[1]
    width = turned_ref.shape[0]
    peers, rows_each, _ = sent_ref.shape
    kept = peers * rows_each
    own_crops = crops // GROUPS
    weights = received(first_ref, 1) / student_temp
    teacher_scale = weights / received(got_ref, 0)
    student_scale = weights / received(got_ref, 1)
    sum_ref[...] = jnp.zeros_like(sum_ref)
    own_rows = pl.ds(pl.multiple_of(group * kept, kept), kept)
    own_lanes = pl.ds(pl.multiple_of(group * own_crops, own_crops), own_crops)

    @pl.loop(0, student_ref.shape[0] // TILE)
    def _(step):
        here = pl.ds(pl.multiple_of(step * TILE, TILE), TILE)
        gradient = student_ref[here, :] * student_scale - teacher_ref[here, :] * scale_ref[here, :] * teacher_scale
        gradient_ref[...] = gradient.astype(jnp.bfloat16)
        weight_grad = lax.dot_general(
            turned_ref[...], gradient_ref[...], (((1,), (1,)), ((), ())), preferred_element_type=jnp.float32
        )
        inverse = inverse_ref[:, here]
        unit = copy_ref[:, here].astype(jnp.float32) * inverse
        dot = jnp.sum(unit * weight_grad, axis=0, keepdims=True)
        weight_ref[...] = weight_grad
        unit_ref[...] = unit
        own = (weight_ref[own_rows, :] - unit_ref[own_rows, :] * dot) * inverse
        sent_ref[:, :, here] = own.astype(jnp.bfloat16).reshape(peers, rows_each, TILE)
        sum_ref[...] += jnp.dot(
            unit.astype(jnp.bfloat16), gradient_ref[:, own_lanes], preferred_element_type=jnp.float32
        )

    features = jnp.transpose(sum_ref[...]).astype(jnp.bfloat16)
    feature_ref[...] = features.reshape(feature_ref.shape)


def feature_kernel(got_ref, student_ref, out_ref):
    total = got_ref[0].astype(jnp.float32)
    for device in range(1, got_ref.shape[0]):
        total = total + got_ref[device].astype(jnp.float32)
    hat, length = unit_rows(student_ref[...])
    out_ref[...] = (total - hat * jnp.sum(hat * total, axis=1, keepdims=True)) / length


def widen_kernel(got_ref, out_ref):
    out_ref[...] = got_ref[0].astype(jnp.float32)


def group_body(teacher_feat, student_feat, crop_weight, teacher_v, student_v):
    f32, bf16 = jnp.float32, jnp.bfloat16
    shape = jax.ShapeDtypeStruct
    blocks, fsdp = lax.axis_size("block"), lax.axis_size("fsdp")
    members = blocks * fsdp
    rows, width = teacher_feat.shape
    crops = rows * members * GROUPS
    kept = teacher_v.shape[1]
    prototypes = kept * fsdp
    count = kept // blocks
    block = lax.axis_index("block")
    elements = count * crops

    spare = jnp.pad(crop_weight[None, :], ((0, 15), (0, 2 * width - rows)))
    sent = call(units_kernel, shape((GROUPS, rows + 16, 2 * width), bf16))(teacher_feat, student_feat, spare)
    got = lax.all_to_all(sent, "group", 0, 0)
    spread = lambda values: jnp.broadcast_to(values, (members, *values.shape))
    teacher_got = lax.all_to_all(
        spread(got[:, :rows, :width].reshape(GROUPS * rows, width)), GROUP, 0, 0
    )
    student_got = lax.all_to_all(
        spread(got[:, :rows, width:].reshape(GROUPS * rows, width)), GROUP, 0, 0
    )
    member = block * fsdp + lax.axis_index("fsdp")
    weights = lax.dynamic_update_slice(
        jnp.zeros((GROUPS, members, rows), f32), got[:, rows, None, :rows].astype(f32), (0, member, 0)
    ).reshape(1, crops)

    tiles = count // TILE
    column = pl.BlockSpec((width, TILE), lambda step, at: (0, at[0] * tiles + step))
    turned = pl.BlockSpec((TILE, width), lambda step, at: (step, 0))
    straight = pl.BlockSpec((width, TILE), lambda step, at: (0, step))
    line = pl.BlockSpec((1, TILE), lambda step, at: (0, step))
    teacher_w, student_w, student_copy, inverse = call(
        directions_kernel,
        (
            shape((count, width), bf16),
            shape((count, width), bf16),
            shape((width, count), bf16),
            shape((1, count), f32),
        ),
        flops=12 * count * width,
        moved=10 * count * width,
        grid_spec=pltpu.PrefetchScalarGridSpec(
            num_scalar_prefetch=1,
            grid=(tiles,),
            in_specs=[column, column],
            out_specs=[turned, turned, straight, line],
        ),
    )(block[None], teacher_v, student_v)

    units = pltpu.VMEM((crops, width), bf16)
    total = pltpu.VMEM((8, crops), f32)
    mass, sent = call(
        functools.partial(teacher_kernel, prototypes),
        (pltpu.VMEM((count, crops), f32), shape((members, 2, crops), f32)),
        flops=2 * elements * width,
        exps=elements,
        scratch_shapes=[units, total],
    )(teacher_w, teacher_got, weights)
    first = lax.all_to_all(sent, GROUP, 0, 0)

    student_mass, student_part, student_turned = call(
        student_kernel,
        (pltpu.VMEM((count, crops), f32), shape((1, crops), f32), shape((width, crops), bf16)),
        flops=2 * elements * width,
        exps=elements,
        scratch_shapes=[units, total],
    )(student_w, student_got)

    got = first
    for sweep in range(1, ITERS):
        extra = sweep == ITERS - 1
        sent, scale = call(
            functools.partial(sweep_kernel, prototypes, crops, extra),
            (shape((members, 1 + extra, crops), f32), shape((count, 1), f32)),
            flops=4 * elements,
            scratch_shapes=[total],
        )(mass, got, *([student_part] if extra else []))
        got = lax.all_to_all(sent, GROUP, 0, 0)

    out_rows = width // (GROUPS * blocks)
    own_crops = crops // GROUPS
    vmem = pl.BlockSpec(memory_space=pltpu.VMEM)
    sent, feature_sent = call(
        gradient_kernel,
        (shape((blocks, out_rows, count), bf16), shape((members, rows, width), bf16)),
        flops=4 * elements * width,
        in_specs=[pl.BlockSpec(memory_space=pltpu.SMEM)] + [vmem] * 8,
        scratch_shapes=[
            pltpu.VMEM((TILE, crops), bf16),
            pltpu.VMEM((width, TILE), f32),
            pltpu.VMEM((width, TILE), f32),
            pltpu.VMEM((width, own_crops), f32),
        ],
    )(
        lax.axis_index("group")[None], mass, student_mass, scale, got, first, student_turned, student_copy, inverse
    )
    grad_got = lax.all_to_all(sent, "block", 0, 0)
    feature_got = lax.all_to_all(feature_sent, GROUP, 0, 0)
    grad_feat = call(feature_kernel, shape((rows, width), f32))(feature_got, student_feat)
    grad_v = call(
        widen_kernel,
        shape((out_rows, kept), f32),
        grid=(blocks,),
        in_specs=[pl.BlockSpec((1, out_rows, count), lambda step: (step, 0, 0))],
        out_specs=pl.BlockSpec((out_rows, count), lambda step: (0, step)),
    )(grad_got)
    return (grad_v, grad_feat)


def solution(mesh):
    dp, fsdp = mesh.shape["dp"], mesh.shape["fsdp"]

    def run(teacher_feat, student_feat, crop_weight, teacher_v, student_v):
        crops = teacher_feat.shape[0]
        count = teacher_v.shape[1] * GROUPS // (dp * fsdp)
        fits = dp % GROUPS == 0 and count % TILE == 0 and 8 * count * crops <= KEPT_BYTES and crops <= 2048
        if fits:
            shape = (GROUPS, dp // GROUPS, fsdp)
            grid, body, rows = Mesh(mesh.devices.reshape(shape), ("group", "block", "fsdp")), group_body, ("group", "block")
        else:
            grid, body, rows = mesh, plain_body, ("dp",)
        every = P((*rows, "fsdp"))
        return jax.shard_map(
            body,
            mesh=grid,
            in_specs=(every, every, every, P(None, "fsdp"), P(None, "fsdp")),
            out_specs=(P(rows, "fsdp"), every),
            check_vma=False,
        )(teacher_feat, student_feat, crop_weight, teacher_v, student_v)

    return run
```

```python
import functools
import math

import jax
import jax.numpy as jnp
from jax import lax
from jax.experimental import pallas as pl
from jax.experimental.pallas import tpu as pltpu
from jax.sharding import PartitionSpec as P

ITERS = 3

teacher_temp = 0.04
student_temp = 0.1
epsilon = 1e-06

TILE = 256
LANES = 128
VMEM_BYTES = 24 << 20
KEPT_BYTES = 16 << 20

EVERY = ("dp", "fsdp")


def unit_rows(values):
    floats = values.astype(jnp.float32)
    length = jnp.sqrt(jnp.sum(floats * floats, axis=1, keepdims=True) + epsilon)
    return (floats / length, length)


def unit_columns(values):
    floats = values.astype(jnp.float32)
    length = jnp.sqrt(jnp.sum(floats * floats, axis=0, keepdims=True) + epsilon)
    return (floats / length, length)


COPY_BYTES = 1 << 22


def share(values, axes):
    count = lax.axis_size(axes)
    if count * values.size * values.dtype.itemsize > COPY_BYTES:
        return lax.all_gather(values, axes)
    return lax.all_to_all(jnp.broadcast_to(values, (count, *values.shape)), axes, 0, 0)


def add_up(values):
    if lax.axis_size(EVERY) * values.size * values.dtype.itemsize > COPY_BYTES:
        return lax.psum(values, EVERY)
    return jnp.sum(share(values, EVERY), axis=0)


def plain_body(teacher_feat, student_feat, crop_weight, teacher_v, student_v):
    fsdp = lax.axis_size("fsdp")
    devices = lax.axis_size("dp") * fsdp
    own_rows, width = teacher_feat.shape
    crops = own_rows * devices
    block = teacher_v.shape[1] // lax.axis_size("dp")
    prototypes = block * devices
    first = lax.axis_index("dp") * block

    teacher_hat, _ = unit_rows(teacher_feat)
    student_hat, student_len = unit_rows(student_feat)
    units = jnp.concatenate(
        [teacher_hat.astype(jnp.bfloat16), student_hat.astype(jnp.bfloat16)], axis=1
    )
    units = share(share(units, "dp"), "fsdp").reshape(crops, 2 * width)
    teacher_unit, student_unit = units[:, :width], units[:, width:]

    teacher_w, _ = unit_columns(lax.dynamic_slice_in_dim(teacher_v, first, block, 1))
    student_w, student_wlen = unit_columns(lax.dynamic_slice_in_dim(student_v, first, block, 1))
    student_wunit = student_w.astype(jnp.bfloat16)

    mass = jnp.exp(
        jnp.dot(teacher_unit, teacher_w.astype(jnp.bfloat16), preferred_element_type=jnp.float32)
        / teacher_temp
    )
    student_mass = jnp.exp(
        jnp.dot(student_unit, student_wunit, preferred_element_type=jnp.float32) / student_temp
    )
    student_part = jnp.sum(student_mass, axis=1)

    crop_scale = None
    for sweep in range(ITERS):
        scaled = mass if sweep == 0 else mass * crop_scale[:, None]
        proto_scale = 1.0 / (prototypes * jnp.sum(scaled, axis=0))
        crop_part = jnp.sum(mass * proto_scale[None, :], axis=1)
        if sweep == 0:
            placed = jnp.zeros((fsdp, crops // (fsdp * own_rows), own_rows), jnp.float32)
            own = crop_weight.astype(jnp.float32)[None, None]
            spot = (lax.axis_index("fsdp"), lax.axis_index("dp"), 0)
            placed = lax.dynamic_update_slice(placed, own, spot).reshape(crops)
            sums = add_up(jnp.stack([crop_part, student_part, placed]))
            crop_mass, student_total, weights = sums[0], sums[1], sums[2]
        else:
            crop_mass = add_up(crop_part)
        crop_scale = 1.0 / (crops * crop_mass)

    target = crops * (mass * crop_scale[:, None] * proto_scale[None, :])
    student_prob = student_mass / student_total[:, None]
    gradient = ((student_prob - target) * weights[:, None] / student_temp).astype(jnp.bfloat16)
    feature_part = lax.dot_general(
        gradient, student_wunit, (((1,), (1,)), ((), ())), preferred_element_type=jnp.float32
    )
    weight_grad = lax.dot_general(
        student_unit, gradient, (((0,), (0,)), ((), ())), preferred_element_type=jnp.float32
    )
    weight_dot = jnp.sum(student_w * weight_grad, axis=0, keepdims=True)
    grad_block = (weight_grad - student_w * weight_dot) / student_wlen

    feature_sent = feature_part.astype(jnp.bfloat16).reshape(fsdp, -1, own_rows, width)
    feature_sent = jnp.swapaxes(feature_sent, 0, 1).reshape(devices, own_rows, width)
    feature_all = lax.all_to_all(feature_sent, EVERY, 0, 0)
    feature_grad = jnp.sum(feature_all.astype(jnp.float32), axis=0)
    grad_feat = (
        feature_grad - student_hat * jnp.sum(student_hat * feature_grad, axis=1, keepdims=True)
    ) / student_len
    grad_v = lax.all_to_all(grad_block.astype(jnp.bfloat16), "dp", 0, 1, tiled=True)
    return (grad_v.astype(jnp.float32), grad_feat)


def call(kernel, out_shape, flops=0, moved=0, exps=0, **more):
    return pl.pallas_call(
        kernel,
        out_shape=out_shape,
        compiler_params=pltpu.CompilerParams(vmem_limit_bytes=VMEM_BYTES),
        cost_estimate=pl.CostEstimate(flops=flops, bytes_accessed=moved, transcendentals=exps),
        **more,
    )


def units_kernel(teacher_ref, student_ref, teacher_out, student_out):
    teacher, _ = unit_rows(teacher_ref[...])
    student, _ = unit_rows(student_ref[...])
    for chip in range(teacher_out.shape[0]):
        teacher_out[chip] = teacher.astype(jnp.bfloat16)
        student_out[chip] = student.astype(jnp.bfloat16)


def directions_kernel(block_ref, teacher_ref, student_ref, teacher_out, student_out, copy_out, inverse_out):
    teacher, _ = unit_columns(teacher_ref[...])
    teacher_out[...] = jnp.transpose(teacher).astype(jnp.bfloat16)
    student, length = unit_columns(student_ref[...])
    student_out[...] = jnp.transpose(student).astype(jnp.bfloat16)
    copy_out[...] = student_ref[...]
    inverse_out[...] = 1.0 / length


def in_crop_order(core, own_ref, other_ref, units_ref):
    chips, rows, _ = own_ref.shape
    for chip in range(chips):
        units_ref[pl.ds(pl.multiple_of((2 * chip + core) * rows, rows), rows), :] = own_ref[chip]
        units_ref[pl.ds(pl.multiple_of((2 * chip + 1 - core) * rows, rows), rows), :] = other_ref[chip]


def exponentials(directions, units, temperature):
    logits = lax.dot_general(
        directions, units, (((1,), (1,)), ((), ())), preferred_element_type=jnp.float32
    )
    return jnp.exp2(logits * (math.log2(math.e) / temperature))


def fold(values):
    rows, lanes = values.shape
    return jnp.sum(values.reshape(rows // 8, 8, lanes), axis=0)


def as_rows(line):
    return jnp.concatenate([line[:, at : at + LANES] for at in range(0, line.shape[1], LANES)], axis=0)


def as_line(rows):
    return jnp.concatenate([rows[at : at + 1, :] for at in range(rows.shape[0])], axis=1)


def send(sent_ref, total, *more):
    values = jnp.concatenate([as_rows(total), *more], axis=0).astype(jnp.bfloat16)
    for device in range(sent_ref.shape[0]):
        sent_ref[device] = values


def received(got_ref):
    total = got_ref[0].astype(jnp.float32)
    for device in range(1, got_ref.shape[0]):
        total = total + got_ref[device].astype(jnp.float32)
    return total


def teacher_kernel(prototypes, core_ref, directions_ref, own_ref, other_ref, weight_ref, mass_ref, sent_ref, units_ref, total_ref):
    in_crop_order(core_ref[0], own_ref, other_ref, units_ref)
    total_ref[...] = jnp.zeros_like(total_ref)

    @pl.loop(0, directions_ref.shape[0] // TILE)
    def _(step):
        here = pl.ds(pl.multiple_of(step * TILE, TILE), TILE)
        mass = exponentials(directions_ref[here, :], units_ref[...], teacher_temp)
        mass_ref[here, :] = mass
        scale = 1.0 / (prototypes * jnp.sum(mass, axis=1, keepdims=True))
        total_ref[...] += fold(mass * scale)

    send(sent_ref, jnp.sum(total_ref[...], axis=0, keepdims=True), weight_ref[...])


def student_kernel(core_ref, directions_ref, own_ref, other_ref, mass_ref, part_ref, turned_ref, units_ref, total_ref):
    in_crop_order(core_ref[0], own_ref, other_ref, units_ref)
    turned_ref[...] = jnp.transpose(units_ref[...].astype(jnp.float32)).astype(jnp.bfloat16)
    total_ref[...] = jnp.zeros_like(total_ref)

    @pl.loop(0, directions_ref.shape[0] // TILE)
    def _(step):
        here = pl.ds(pl.multiple_of(step * TILE, TILE), TILE)
        mass = exponentials(directions_ref[here, :], units_ref[...], student_temp)
        mass_ref[here, :] = mass
        total_ref[...] += fold(mass)

    part_ref[...] = as_rows(jnp.sum(total_ref[...], axis=0, keepdims=True))


def sweep_kernel(prototypes, crops, extra, mass_ref, got_ref, *refs):
    sent_ref, scale_ref, total_ref = refs[-3:]
    crop_scale = as_line(1.0 / (crops * received(got_ref)[: crops // LANES]))
    total_ref[...] = jnp.zeros_like(total_ref)

    @pl.loop(0, mass_ref.shape[0] // TILE)
    def _(step):
        here = pl.ds(pl.multiple_of(step * TILE, TILE), TILE)
        mass = mass_ref[here, :]
        scale = 1.0 / (prototypes * jnp.sum(mass * crop_scale, axis=1, keepdims=True))
        scale_ref[here, :] = scale
        total_ref[...] += fold(mass * scale)

    more = [refs[0][...]] if extra else []
    send(sent_ref, jnp.sum(total_ref[...], axis=0, keepdims=True), *more)


def gradient_kernel(
    core_ref, teacher_ref, student_ref, scale_ref, got_ref, crop_ref, turned_ref, copy_ref, inverse_ref,
    sent_ref, keep_ref, give_ref, gradient_ref, sum_ref,
):
    core = core_ref[0]
    chips, rows_each, _ = sent_ref.shape
    lines = student_ref.shape[1] // LANES
    totals = received(got_ref)
    weights = crop_ref[...] / student_temp
    teacher_scale = as_line(weights / totals[:lines])
    student_scale = as_line(weights / totals[lines:])
    sum_ref[...] = jnp.zeros_like(sum_ref)

    @pl.loop(0, student_ref.shape[0] // TILE)
    def _(step):
        here = pl.ds(pl.multiple_of(step * TILE, TILE), TILE)
        gradient = student_ref[here, :] * student_scale - teacher_ref[here, :] * scale_ref[here, :] * teacher_scale
        gradient_ref[...] = gradient.astype(jnp.bfloat16)
        weight_grad = lax.dot_general(
            turned_ref[...], gradient_ref[...], (((1,), (1,)), ((), ())), preferred_element_type=jnp.float32
        )
        inverse = inverse_ref[:, here]
        unit = copy_ref[:, here].astype(jnp.float32) * inverse
        dot = jnp.sum(unit * weight_grad, axis=0, keepdims=True)
        grad = (weight_grad - unit * dot) * inverse
        sent_ref[:, :, here] = grad.astype(jnp.bfloat16).reshape(chips, rows_each, TILE)
        sum_ref[...] += jnp.dot(
            unit.astype(jnp.bfloat16), gradient_ref[...], preferred_element_type=jnp.float32
        )

    for chip in range(chips):
        rows = keep_ref.shape[1]
        both = jnp.transpose(sum_ref[:, 2 * chip * rows : (2 * chip + 2) * rows])
        first, second = both[:rows], both[rows:]
        keep_ref[chip] = jnp.where(core == 0, first, second)
        give_ref[chip] = jnp.where(core == 0, second, first).astype(jnp.bfloat16)


def pair_kernel(keep_ref, other_ref, out_ref):
    out_ref[...] = (keep_ref[...] + other_ref[...].astype(jnp.float32)).astype(jnp.bfloat16)


def feature_kernel(got_ref, student_ref, out_ref):
    total = received(got_ref)
    hat, length = unit_rows(student_ref[...])
    out_ref[...] = (total - hat * jnp.sum(hat * total, axis=1, keepdims=True)) / length


def widen_kernel(got_ref, out_ref):
    out_ref[...] = got_ref[0].astype(jnp.float32)


def kernel_body(teacher_feat, student_feat, crop_weight, teacher_v, student_v):
    f32, bf16 = jnp.float32, jnp.bfloat16
    shape = jax.ShapeDtypeStruct
    chips, fsdp = lax.axis_size("dp"), lax.axis_size("fsdp")
    devices = chips * fsdp
    rows, width = teacher_feat.shape
    crops = rows * devices
    lines = crops // LANES
    kept = teacher_v.shape[1]
    prototypes = kept * fsdp
    count = kept // chips
    block = lax.axis_index("dp")
    core = lax.axis_index("fsdp")[None]
    elements = count * crops
    smem, vmem = pl.BlockSpec(memory_space=pltpu.SMEM), pl.BlockSpec(memory_space=pltpu.VMEM)

    def swap(values):
        return lax.ppermute(values, "fsdp", [(0, 1), (1, 0)])

    teacher_sent, student_sent = call(
        units_kernel, (shape((chips, rows, width), bf16), shape((chips, rows, width), bf16))
    )(teacher_feat, student_feat)
    teacher_own = lax.all_to_all(teacher_sent, "dp", 0, 0)
    teacher_other = swap(teacher_own)
    student_own = lax.all_to_all(student_sent, "dp", 0, 0)
    student_other = swap(student_own)
    weights = jnp.pad(crop_weight[None, :].astype(f32), ((0, 7), (0, LANES - rows)))

    tiles = count // TILE
    column = pl.BlockSpec((width, TILE), lambda step, at: (0, at[0] * tiles + step))
    turned = pl.BlockSpec((TILE, width), lambda step, at: (step, 0))
    straight = pl.BlockSpec((width, TILE), lambda step, at: (0, step))
    line = pl.BlockSpec((1, TILE), lambda step, at: (0, step))
    teacher_w, student_w, student_copy, inverse = call(
        directions_kernel,
        (
            shape((count, width), bf16),
            shape((count, width), bf16),
            shape((width, count), bf16),
            shape((1, count), f32),
        ),
        flops=12 * count * width,
        moved=10 * count * width,
        grid_spec=pltpu.PrefetchScalarGridSpec(
            num_scalar_prefetch=1,
            grid=(tiles,),
            in_specs=[column, column],
            out_specs=[turned, turned, straight, line],
        ),
    )(
        block[None],
        pltpu.with_memory_space_constraint(teacher_v, pltpu.HBM),
        pltpu.with_memory_space_constraint(student_v, pltpu.HBM),
    )

    units = pltpu.VMEM((crops, width), bf16)
    total = pltpu.VMEM((8, crops), f32)
    mass, sent = call(
        functools.partial(teacher_kernel, prototypes),
        (pltpu.VMEM((count, crops), f32), shape((devices, lines + 8, LANES), bf16)),
        flops=2 * elements * width,
        exps=elements,
        in_specs=[smem] + [vmem] * 4,
        scratch_shapes=[units, total],
    )(core, teacher_w, teacher_own, teacher_other, weights)
    got = lax.all_to_all(sent, EVERY, 0, 0)
    crop_rows = got[:, lines, :rows].astype(f32).reshape(lines, LANES)

    student_mass, student_part, student_turned = call(
        student_kernel,
        (pltpu.VMEM((count, crops), f32), shape((lines, LANES), f32), shape((width, crops), bf16)),
        flops=2 * elements * width,
        exps=elements,
        in_specs=[smem] + [vmem] * 3,
        scratch_shapes=[units, total],
    )(core, student_w, student_own, student_other)

    for sweep in range(1, ITERS):
        extra = sweep == ITERS - 1
        sent, scale = call(
            functools.partial(sweep_kernel, prototypes, crops, extra),
            (shape((devices, lines * (1 + extra), LANES), bf16), shape((count, 1), f32)),
            flops=4 * elements,
            scratch_shapes=[total],
        )(mass, got, *([student_part] if extra else []))
        got = lax.all_to_all(sent, EVERY, 0, 0)

    out_rows = width // chips
    sent, keep, give = call(
        gradient_kernel,
        (
            shape((chips, out_rows, count), bf16),
            shape((chips, rows, width), f32),
            shape((chips, rows, width), bf16),
        ),
        flops=4 * elements * width,
        in_specs=[smem] + [vmem] * 8,
        scratch_shapes=[pltpu.VMEM((TILE, crops), bf16), pltpu.VMEM((width, crops), f32)],
    )(core, mass, student_mass, scale, got, crop_rows, student_turned, student_copy, inverse)
    grad_got = lax.all_to_all(sent, "dp", 0, 0)
    paired = call(pair_kernel, shape((chips, rows, width), bf16))(keep, swap(give))
    feature_got = lax.all_to_all(paired, "dp", 0, 0)
    grad_feat = call(feature_kernel, shape((rows, width), f32))(feature_got, student_feat)
    grad_v = call(
        widen_kernel,
        shape((out_rows, kept), f32),
        grid=(chips,),
        in_specs=[pl.BlockSpec((1, out_rows, count), lambda step: (step, 0, 0))],
        out_specs=pl.BlockSpec((out_rows, count), lambda step: (0, step)),
    )(grad_got)
    return (grad_v, grad_feat)


def solution(mesh):
    dp, fsdp = mesh.shape["dp"], mesh.shape["fsdp"]

    def run(teacher_feat, student_feat, crop_weight, teacher_v, student_v):
        crops = teacher_feat.shape[0]
        count = teacher_v.shape[1] // (dp * fsdp)
        fits = fsdp == 2 and count % TILE == 0 and crops % 1024 == 0 and 8 * count * crops <= KEPT_BYTES
        every = P(EVERY)
        return jax.shard_map(
            kernel_body if fits else plain_body,
            mesh=mesh,
            in_specs=(every, every, every, P(None, "fsdp"), P(None, "fsdp")),
            out_specs=(P("dp", "fsdp"), every),
            check_vma=False,
        )(teacher_feat, student_feat, crop_weight, teacher_v, student_v)

    return run
```

```python
import functools
import math

import jax
import jax.numpy as jnp
from jax import lax
from jax.experimental import pallas as pl
from jax.experimental.pallas import tpu as pltpu
from jax.sharding import PartitionSpec as P

ITERS = 3

teacher_temp = 0.04
student_temp = 0.1
epsilon = 1e-06

TILE = 256
LANES = 128
PLANE = 4
VMEM_BYTES = 24 << 20
KEPT_BYTES = 16 << 20

EVERY = ("dp", "fsdp")


def unit_rows(values):
    floats = values.astype(jnp.float32)
    length = jnp.sqrt(jnp.sum(floats * floats, axis=1, keepdims=True) + epsilon)
    return (floats / length, length)


def unit_columns(values):
    floats = values.astype(jnp.float32)
    length = jnp.sqrt(jnp.sum(floats * floats, axis=0, keepdims=True) + epsilon)
    return (floats / length, length)


COPY_BYTES = 1 << 22


def share(values, axes):
    count = lax.axis_size(axes)
    if count * values.size * values.dtype.itemsize > COPY_BYTES:
        return lax.all_gather(values, axes)
    return lax.all_to_all(jnp.broadcast_to(values, (count, *values.shape)), axes, 0, 0)


def add_up(values):
    if lax.axis_size(EVERY) * values.size * values.dtype.itemsize > COPY_BYTES:
        return lax.psum(values, EVERY)
    return jnp.sum(share(values, EVERY), axis=0)


def plain_body(teacher_feat, student_feat, crop_weight, teacher_v, student_v):
    fsdp = lax.axis_size("fsdp")
    devices = lax.axis_size("dp") * fsdp
    own_rows, width = teacher_feat.shape
    crops = own_rows * devices
    block = teacher_v.shape[1] // lax.axis_size("dp")
    prototypes = block * devices
    first = lax.axis_index("dp") * block

    teacher_hat, _ = unit_rows(teacher_feat)
    student_hat, student_len = unit_rows(student_feat)
    units = jnp.concatenate(
        [teacher_hat.astype(jnp.bfloat16), student_hat.astype(jnp.bfloat16)], axis=1
    )
    units = share(share(units, "dp"), "fsdp").reshape(crops, 2 * width)
    teacher_unit, student_unit = units[:, :width], units[:, width:]

    teacher_w, _ = unit_columns(lax.dynamic_slice_in_dim(teacher_v, first, block, 1))
    student_w, student_wlen = unit_columns(lax.dynamic_slice_in_dim(student_v, first, block, 1))
    student_wunit = student_w.astype(jnp.bfloat16)

    mass = jnp.exp(
        jnp.dot(teacher_unit, teacher_w.astype(jnp.bfloat16), preferred_element_type=jnp.float32)
        / teacher_temp
    )
    student_mass = jnp.exp(
        jnp.dot(student_unit, student_wunit, preferred_element_type=jnp.float32) / student_temp
    )
    student_part = jnp.sum(student_mass, axis=1)

    crop_scale = None
    for sweep in range(ITERS):
        scaled = mass if sweep == 0 else mass * crop_scale[:, None]
        proto_scale = 1.0 / (prototypes * jnp.sum(scaled, axis=0))
        crop_part = jnp.sum(mass * proto_scale[None, :], axis=1)
        if sweep == 0:
            placed = jnp.zeros((fsdp, crops // (fsdp * own_rows), own_rows), jnp.float32)
            own = crop_weight.astype(jnp.float32)[None, None]
            spot = (lax.axis_index("fsdp"), lax.axis_index("dp"), 0)
            placed = lax.dynamic_update_slice(placed, own, spot).reshape(crops)
            sums = add_up(jnp.stack([crop_part, student_part, placed]))
            crop_mass, student_total, weights = sums[0], sums[1], sums[2]
        else:
            crop_mass = add_up(crop_part)
        crop_scale = 1.0 / (crops * crop_mass)

    target = crops * (mass * crop_scale[:, None] * proto_scale[None, :])
    student_prob = student_mass / student_total[:, None]
    gradient = ((student_prob - target) * weights[:, None] / student_temp).astype(jnp.bfloat16)
    feature_part = lax.dot_general(
        gradient, student_wunit, (((1,), (1,)), ((), ())), preferred_element_type=jnp.float32
    )
    weight_grad = lax.dot_general(
        student_unit, gradient, (((0,), (0,)), ((), ())), preferred_element_type=jnp.float32
    )
    weight_dot = jnp.sum(student_w * weight_grad, axis=0, keepdims=True)
    grad_block = (weight_grad - student_w * weight_dot) / student_wlen

    feature_sent = feature_part.astype(jnp.bfloat16).reshape(fsdp, -1, own_rows, width)
    feature_sent = jnp.swapaxes(feature_sent, 0, 1).reshape(devices, own_rows, width)
    feature_all = lax.all_to_all(feature_sent, EVERY, 0, 0)
    feature_grad = jnp.sum(feature_all.astype(jnp.float32), axis=0)
    grad_feat = (
        feature_grad - student_hat * jnp.sum(student_hat * feature_grad, axis=1, keepdims=True)
    ) / student_len
    grad_v = lax.all_to_all(grad_block.astype(jnp.bfloat16), "dp", 0, 1, tiled=True)
    return (grad_v.astype(jnp.float32), grad_feat)


def call(kernel, out_shape, flops=0, moved=0, exps=0, **more):
    return pl.pallas_call(
        kernel,
        out_shape=out_shape,
        compiler_params=pltpu.CompilerParams(vmem_limit_bytes=VMEM_BYTES),
        cost_estimate=pl.CostEstimate(flops=flops, bytes_accessed=moved, transcendentals=exps),
        **more,
    )


def units_kernel(teacher_ref, student_ref, teacher_out, student_out):
    teacher_out[...] = unit_rows(teacher_ref[...])[0].astype(jnp.bfloat16)
    student_out[...] = unit_rows(student_ref[...])[0].astype(jnp.bfloat16)


def directions_kernel(block_ref, teacher_ref, student_ref, teacher_out, student_out, copy_out, inverse_out):
    teacher, _ = unit_columns(teacher_ref[...])
    teacher_out[...] = jnp.transpose(teacher).astype(jnp.bfloat16)
    student, length = unit_columns(student_ref[...])
    student_out[...] = jnp.transpose(student).astype(jnp.bfloat16)
    copy_out[...] = student_ref[...]
    inverse_out[...] = 1.0 / length


def in_crop_order(chip, core, layers, got_refs, units_ref):
    layer, place = chip // PLANE, chip % PLANE
    for index, got_ref in enumerate(got_refs):
        other, move = divmod(index, PLANE)
        rows = got_ref.shape[0] // layers
        for back in range(layers):
            device = 2 * (((layer + layers - back) % layers) * PLANE + (place ^ move)) + (core ^ other)
            here = pl.ds(pl.multiple_of(device * rows, rows), rows)
            units_ref[here, :] = got_ref[back * rows : (back + 1) * rows, :]


def exponentials(directions, units, temperature):
    logits = lax.dot_general(
        directions, units, (((1,), (1,)), ((), ())), preferred_element_type=jnp.float32
    )
    return jnp.exp2(logits * (math.log2(math.e) / temperature))


def fold(values):
    rows, lanes = values.shape
    return jnp.sum(values.reshape(rows // 8, 8, lanes), axis=0)


def as_rows(line):
    return jnp.concatenate([line[:, at : at + LANES] for at in range(0, line.shape[1], LANES)], axis=0)


def as_line(rows):
    return jnp.concatenate([rows[at : at + 1, :] for at in range(rows.shape[0])], axis=1)


def added(refs):
    total = refs[0][...].astype(jnp.float32)
    for ref in refs[1:]:
        total = total + ref[...].astype(jnp.float32)
    return total


def teacher_kernel(prototypes, layers, place_ref, directions_ref, *refs):
    *got_refs, weight_ref, mass_ref, sent_ref, units_ref, total_ref = refs
    in_crop_order(place_ref[0], place_ref[1], layers, got_refs, units_ref)
    total_ref[...] = jnp.zeros_like(total_ref)

    @pl.loop(0, directions_ref.shape[0] // TILE)
    def _(step):
        here = pl.ds(pl.multiple_of(step * TILE, TILE), TILE)
        mass = exponentials(directions_ref[here, :], units_ref[...], teacher_temp)
        mass_ref[here, :] = mass
        scale = 1.0 / (prototypes * jnp.sum(mass, axis=1, keepdims=True))
        total_ref[...] += fold(mass * scale)

    lines = weight_ref.shape[0]
    sent_ref[:lines, :] = as_rows(jnp.sum(total_ref[...], axis=0, keepdims=True))
    sent_ref[lines:, :] = weight_ref[...]


def student_kernel(layers, place_ref, directions_ref, *refs):
    *got_refs, mass_ref, part_ref, turned_ref, units_ref, total_ref = refs
    in_crop_order(place_ref[0], place_ref[1], layers, got_refs, units_ref)
    turned_ref[...] = jnp.transpose(units_ref[...].astype(jnp.float32)).astype(jnp.bfloat16)
    total_ref[...] = jnp.zeros_like(total_ref)

    @pl.loop(0, directions_ref.shape[0] // TILE)
    def _(step):
        here = pl.ds(pl.multiple_of(step * TILE, TILE), TILE)
        mass = exponentials(directions_ref[here, :], units_ref[...], student_temp)
        mass_ref[here, :] = mass
        total_ref[...] += fold(mass)

    part_ref[...] = as_rows(jnp.sum(total_ref[...], axis=0, keepdims=True))


def sweep_kernel(prototypes, crops, layers, mass_ref, *refs):
    part_refs = refs[layers:-3]
    sent_ref, scale_ref, total_ref = refs[-3:]
    lines = crops // LANES
    crop_scale = as_line(1.0 / (crops * added(refs[:layers])[:lines]))
    total_ref[...] = jnp.zeros_like(total_ref)

    @pl.loop(0, mass_ref.shape[0] // TILE)
    def _(step):
        here = pl.ds(pl.multiple_of(step * TILE, TILE), TILE)
        mass = mass_ref[here, :]
        scale = 1.0 / (prototypes * jnp.sum(mass * crop_scale, axis=1, keepdims=True))
        scale_ref[here, :] = scale
        total_ref[...] += fold(mass * scale)

    sent_ref[:lines, :] = as_rows(jnp.sum(total_ref[...], axis=0, keepdims=True))
    for part_ref in part_refs:
        sent_ref[lines:, :] = part_ref[...]


def gradient_kernel(layers, chips, place_ref, teacher_ref, student_ref, scale_ref, turned_ref, copy_ref, inverse_ref, *refs):
    total_refs, crop_refs, refs = refs[:layers], refs[layers : 2 * layers], refs[2 * layers :]
    sent_refs, (keep_ref, give_ref, gradient_ref, grad_ref, sum_ref) = refs[:chips], refs[chips:]
    chip, core = place_ref[0], place_ref[1]
    rows_each = sent_refs[0].shape[0]
    lines = student_ref.shape[1] // LANES
    totals = added(total_refs)
    weights = added(crop_refs)[lines:] / student_temp
    teacher_scale = as_line(weights / totals[:lines])
    student_scale = as_line(weights / totals[lines:])
    sum_ref[...] = jnp.zeros_like(sum_ref)

    @pl.loop(0, student_ref.shape[0] // TILE)
    def _(step):
        here = pl.ds(pl.multiple_of(step * TILE, TILE), TILE)
        gradient = student_ref[here, :] * student_scale - teacher_ref[here, :] * scale_ref[here, :] * teacher_scale
        gradient_ref[...] = gradient.astype(jnp.bfloat16)
        weight_grad = lax.dot_general(
            turned_ref[...], gradient_ref[...], (((1,), (1,)), ((), ())), preferred_element_type=jnp.float32
        )
        inverse = inverse_ref[:, here]
        unit = copy_ref[:, here].astype(jnp.float32) * inverse
        dot = jnp.sum(unit * weight_grad, axis=0, keepdims=True)
        grad_ref[...] = (weight_grad - unit * dot) * inverse
        for move in range(chips):
            rows = pl.ds(pl.multiple_of((chip ^ move) * rows_each, rows_each), rows_each)
            sent_refs[move][:, here] = grad_ref[rows, :].astype(jnp.bfloat16)
        sum_ref[...] += jnp.dot(
            unit.astype(jnp.bfloat16), gradient_ref[...], preferred_element_type=jnp.float32
        )

    rows = keep_ref.shape[2]
    for source in range(chips):
        layer, place = divmod(source, PLANE)
        both = jnp.transpose(sum_ref[:, 2 * source * rows : (2 * source + 2) * rows])
        first, second = both[:rows], both[rows:]
        move = (chip % PLANE) ^ place
        keep_ref[move, layer] = jnp.where(core == 0, first, second)
        give_ref[move, layer] = jnp.where(core == 0, second, first).astype(jnp.bfloat16)


def pair_kernel(keep_ref, other_ref, own_out, *out_refs):
    own_out[...] = keep_ref[0] + other_ref[0].astype(jnp.float32)
    for move, out_ref in enumerate(out_refs, 1):
        out_ref[...] = (keep_ref[move] + other_ref[move].astype(jnp.float32)).astype(jnp.bfloat16)


def plane_kernel(place_ref, *refs):
    got_refs, (own_out, *out_refs) = refs[:PLANE], refs[PLANE:]
    layers = got_refs[0].shape[0]
    layer = place_ref[0] // PLANE
    for back in range(layers):
        at = (layer + layers - back) % layers
        total = got_refs[0][at]
        for got_ref in got_refs[1:]:
            total = total + got_ref[at].astype(jnp.float32)
        if back == 0:
            own_out[...] = total
        else:
            out_refs[back - 1][...] = total.astype(jnp.bfloat16)


def feature_kernel(student_ref, *refs):
    total = added(refs[:-1])
    hat, length = unit_rows(student_ref[...])
    refs[-1][...] = (total - hat * jnp.sum(hat * total, axis=1, keepdims=True)) / length


def widen_kernel(place_ref, *refs):
    *got_refs, out_ref = refs
    columns = got_refs[0].shape[1]
    for move, got_ref in enumerate(got_refs):
        here = pl.ds(pl.multiple_of((place_ref[0] ^ move) * columns, columns), columns)
        out_ref[:, here] = got_ref[...].astype(jnp.float32)


def kernel_body(teacher_feat, student_feat, crop_weight, teacher_v, student_v):
    f32, bf16 = jnp.float32, jnp.bfloat16
    shape = jax.ShapeDtypeStruct
    chips, fsdp = lax.axis_size("dp"), lax.axis_size("fsdp")
    devices = chips * fsdp
    rows, width = teacher_feat.shape
    crops = rows * devices
    lines = crops // LANES
    kept = teacher_v.shape[1]
    prototypes = kept * fsdp
    count = kept // chips
    layers = chips // PLANE
    chip, core = lax.axis_index("dp"), lax.axis_index("fsdp")
    place = jnp.stack([chip, core])
    elements = count * crops
    smem, vmem = pl.BlockSpec(memory_space=pltpu.SMEM), pl.BlockSpec(memory_space=pltpu.VMEM)

    def swap(values):
        return lax.ppermute(values, "fsdp", [(0, 1), (1, 0)])

    def across(values, move):
        return lax.ppermute(values, "dp", [(at, at ^ move) for at in range(chips)])

    def along(values, back):
        return lax.ppermute(values, "dp", [(at, (at + back * PLANE) % chips) for at in range(chips)])

    def gather(values):
        column = jnp.concatenate([values] + [along(values, back) for back in range(1, layers)])
        own = [column] + [across(column, move) for move in range(1, PLANE)]
        return own + [swap(piece) for piece in own]

    def add_up(values):
        perms = [
            [(at, at ^ move) for at in range(devices)] for move in range(1, 2 * PLANE)
        ]
        total = values
        for got in [lax.ppermute(values, EVERY, perm) for perm in perms]:
            total = total + got
        return [total] + [along(total, back) for back in range(1, layers)]

    teacher_unit, student_unit = call(
        units_kernel, (shape((rows, width), bf16), shape((rows, width), bf16))
    )(teacher_feat, student_feat)
    teacher_got = gather(teacher_unit)
    student_unit, teacher_got = lax.optimization_barrier((student_unit, teacher_got))
    student_got = gather(student_unit)
    weights = lax.dynamic_update_slice(
        jnp.zeros((crops,), f32), crop_weight.astype(f32), ((2 * chip + core) * rows,)
    ).reshape(lines, LANES)

    tiles = count // TILE
    column = pl.BlockSpec((width, TILE), lambda step, at: (0, at[0] * tiles + step))
    turned = pl.BlockSpec((TILE, width), lambda step, at: (step, 0))
    straight = pl.BlockSpec((width, TILE), lambda step, at: (0, step))
    line = pl.BlockSpec((1, TILE), lambda step, at: (0, step))
    teacher_w, student_w, student_copy, inverse = call(
        directions_kernel,
        (
            shape((count, width), bf16),
            shape((count, width), bf16),
            shape((width, count), bf16),
            shape((1, count), f32),
        ),
        flops=12 * count * width,
        moved=10 * count * width,
        grid_spec=pltpu.PrefetchScalarGridSpec(
            num_scalar_prefetch=1,
            grid=(tiles,),
            in_specs=[column, column],
            out_specs=[turned, turned, straight, line],
        ),
    )(
        chip[None],
        pltpu.with_memory_space_constraint(teacher_v, pltpu.HBM),
        pltpu.with_memory_space_constraint(student_v, pltpu.HBM),
    )

    units = pltpu.VMEM((crops, width), bf16)
    total = pltpu.VMEM((8, crops), f32)
    mass, sent = call(
        functools.partial(teacher_kernel, prototypes, layers),
        (shape((count, crops), f32), shape((2 * lines, LANES), f32)),
        flops=2 * elements * width,
        exps=elements,
        in_specs=[smem] + [vmem] * (2 + len(teacher_got)),
        scratch_shapes=[units, total],
    )(place, teacher_w, *teacher_got, weights)
    first = got = add_up(sent)

    student_mass, student_part, student_turned = call(
        functools.partial(student_kernel, layers),
        (shape((count, crops), f32), shape((lines, LANES), f32), shape((width, crops), bf16)),
        flops=2 * elements * width,
        exps=elements,
        in_specs=[smem] + [vmem] * (1 + len(student_got)),
        scratch_shapes=[units, total],
    )(place, student_w, *student_got)

    for sweep in range(1, ITERS):
        extra = sweep == ITERS - 1
        sent, scale = call(
            functools.partial(sweep_kernel, prototypes, crops, layers),
            (shape((lines * (1 + extra), LANES), f32), shape((count, 1), f32)),
            flops=4 * elements,
            scratch_shapes=[total],
        )(mass, *got, *([student_part] if extra else []))
        got = add_up(sent)

    out_rows = width // chips
    *sent, keep, give = call(
        functools.partial(gradient_kernel, layers, chips),
        [shape((out_rows, count), bf16)] * chips
        + [shape((PLANE, layers, rows, width), f32), shape((PLANE, layers, rows, width), bf16)],
        flops=4 * elements * width,
        in_specs=[smem] + [vmem] * (6 + 2 * layers),
        scratch_shapes=[
            pltpu.VMEM((TILE, crops), bf16),
            pltpu.VMEM((width, TILE), f32),
            pltpu.VMEM((width, crops), f32),
        ],
    )(place, mass, student_mass, scale, student_turned, student_copy, inverse, *got, *first)
    other = swap(give)
    grads = [sent[0]] + [across(sent[move], move) for move in range(1, chips)]
    own, *pairs = call(
        pair_kernel,
        [shape((layers, rows, width), f32)] + [shape((layers, rows, width), bf16)] * (PLANE - 1),
    )(keep, other)
    pairs = [own] + [across(pair, move) for move, pair in enumerate(pairs, 1)]
    own, *planes = call(
        plane_kernel,
        [shape((rows, width), f32)] + [shape((rows, width), bf16)] * (layers - 1),
        in_specs=[smem] + [vmem] * PLANE,
    )(place, *pairs)
    planes = [own] + [along(part, layers - back) for back, part in enumerate(planes, 1)]
    grad_feat = call(feature_kernel, shape((rows, width), f32))(student_feat, *planes)
    grad_v = call(
        widen_kernel,
        shape((out_rows, kept), f32),
        in_specs=[smem] + [vmem] * chips,
    )(place, *grads)
    return (grad_v, grad_feat)


def solution(mesh):
    dp, fsdp = mesh.shape["dp"], mesh.shape["fsdp"]

    def run(teacher_feat, student_feat, crop_weight, teacher_v, student_v):
        crops = teacher_feat.shape[0]
        count = teacher_v.shape[1] // (dp * fsdp)
        fits = fsdp == 2 and dp in (8, 16) and count % TILE == 0 and crops % 1024 == 0 and 8 * count * crops <= KEPT_BYTES
        every = P(EVERY)
        return jax.shard_map(
            kernel_body if fits else plain_body,
            mesh=mesh,
            in_specs=(every, every, every, P(None, "fsdp"), P(None, "fsdp")),
            out_specs=(P("dp", "fsdp"), every),
            check_vma=False,
        )(teacher_feat, student_feat, crop_weight, teacher_v, student_v)

    return run
```

```python
import functools
import math

import jax
import jax.numpy as jnp
from jax import lax
from jax.experimental import pallas as pl
from jax.experimental.pallas import tpu as pltpu
from jax.sharding import Mesh
from jax.sharding import PartitionSpec as P

ITERS = 3

teacher_temp = 0.04
student_temp = 0.1
epsilon = 1e-06

GROUPS = 2
TILE = 256
LANES = 128
VMEM_BYTES = 24 << 20
KEPT_BYTES = 18 << 20

EVERY = ("dp", "fsdp")
CHIPS = ("group", "block")


def unit_rows(values):
    floats = values.astype(jnp.float32)
    length = jnp.sqrt(jnp.sum(floats * floats, axis=1, keepdims=True) + epsilon)
    return (floats / length, length)


def unit_columns(values):
    floats = values.astype(jnp.float32)
    length = jnp.sqrt(jnp.sum(floats * floats, axis=0, keepdims=True) + epsilon)
    return (floats / length, length)


COPY_BYTES = 1 << 22


def share(values, axes):
    count = lax.axis_size(axes)
    if count * values.size * values.dtype.itemsize > COPY_BYTES:
        return lax.all_gather(values, axes)
    return lax.all_to_all(jnp.broadcast_to(values, (count, *values.shape)), axes, 0, 0)


def add_up(values):
    if lax.axis_size(EVERY) * values.size * values.dtype.itemsize > COPY_BYTES:
        return lax.psum(values, EVERY)
    return jnp.sum(share(values, EVERY), axis=0)


def plain_body(teacher_feat, student_feat, crop_weight, teacher_v, student_v):
    fsdp = lax.axis_size("fsdp")
    devices = lax.axis_size("dp") * fsdp
    own_rows, width = teacher_feat.shape
    crops = own_rows * devices
    block = teacher_v.shape[1] // lax.axis_size("dp")
    prototypes = block * devices
    first = lax.axis_index("dp") * block

    teacher_hat, _ = unit_rows(teacher_feat)
    student_hat, student_len = unit_rows(student_feat)
    units = jnp.concatenate(
        [teacher_hat.astype(jnp.bfloat16), student_hat.astype(jnp.bfloat16)], axis=1
    )
    units = share(share(units, "dp"), "fsdp").reshape(crops, 2 * width)
    teacher_unit, student_unit = units[:, :width], units[:, width:]

    teacher_w, _ = unit_columns(lax.dynamic_slice_in_dim(teacher_v, first, block, 1))
    student_w, student_wlen = unit_columns(lax.dynamic_slice_in_dim(student_v, first, block, 1))
    student_wunit = student_w.astype(jnp.bfloat16)

    mass = jnp.exp(
        jnp.dot(teacher_unit, teacher_w.astype(jnp.bfloat16), preferred_element_type=jnp.float32)
        / teacher_temp
    )
    student_mass = jnp.exp(
        jnp.dot(student_unit, student_wunit, preferred_element_type=jnp.float32) / student_temp
    )
    student_part = jnp.sum(student_mass, axis=1)

    crop_scale = None
    for sweep in range(ITERS):
        scaled = mass if sweep == 0 else mass * crop_scale[:, None]
        proto_scale = 1.0 / (prototypes * jnp.sum(scaled, axis=0))
        crop_part = jnp.sum(mass * proto_scale[None, :], axis=1)
        if sweep == 0:
            placed = jnp.zeros((fsdp, crops // (fsdp * own_rows), own_rows), jnp.float32)
            own = crop_weight.astype(jnp.float32)[None, None]
            spot = (lax.axis_index("fsdp"), lax.axis_index("dp"), 0)
            placed = lax.dynamic_update_slice(placed, own, spot).reshape(crops)
            sums = add_up(jnp.stack([crop_part, student_part, placed]))
            crop_mass, student_total, weights = sums[0], sums[1], sums[2]
        else:
            crop_mass = add_up(crop_part)
        crop_scale = 1.0 / (crops * crop_mass)

    target = crops * (mass * crop_scale[:, None] * proto_scale[None, :])
    student_prob = student_mass / student_total[:, None]
    gradient = ((student_prob - target) * weights[:, None] / student_temp).astype(jnp.bfloat16)
    feature_part = lax.dot_general(
        gradient, student_wunit, (((1,), (1,)), ((), ())), preferred_element_type=jnp.float32
    )
    weight_grad = lax.dot_general(
        student_unit, gradient, (((0,), (0,)), ((), ())), preferred_element_type=jnp.float32
    )
    weight_dot = jnp.sum(student_w * weight_grad, axis=0, keepdims=True)
    grad_block = (weight_grad - student_w * weight_dot) / student_wlen

    feature_sent = feature_part.astype(jnp.bfloat16).reshape(fsdp, -1, own_rows, width)
    feature_sent = jnp.swapaxes(feature_sent, 0, 1).reshape(devices, own_rows, width)
    feature_all = lax.all_to_all(feature_sent, EVERY, 0, 0)
    feature_grad = jnp.sum(feature_all.astype(jnp.float32), axis=0)
    grad_feat = (
        feature_grad - student_hat * jnp.sum(student_hat * feature_grad, axis=1, keepdims=True)
    ) / student_len
    grad_v = lax.all_to_all(grad_block.astype(jnp.bfloat16), "dp", 0, 1, tiled=True)
    return (grad_v.astype(jnp.float32), grad_feat)


def call(kernel, out_shape, flops=0, moved=0, exps=0, **more):
    return pl.pallas_call(
        kernel,
        out_shape=out_shape,
        compiler_params=pltpu.CompilerParams(vmem_limit_bytes=VMEM_BYTES),
        cost_estimate=pl.CostEstimate(flops=flops, bytes_accessed=moved, transcendentals=exps),
        **more,
    )


def units_kernel(teacher_ref, student_ref, weight_ref, teacher_out, student_out):
    rows = teacher_ref.shape[0]
    teacher = unit_rows(teacher_ref[...])[0].astype(jnp.bfloat16)
    student = unit_rows(student_ref[...])[0].astype(jnp.bfloat16)
    for chip in range(teacher_out.shape[0]):
        teacher_out[chip] = teacher
        student_out[chip, :rows, :] = student
        student_out[chip, rows:, :] = weight_ref[...]


def directions_kernel(block_ref, teacher_ref, student_ref, teacher_out, student_out, copy_out, inverse_out):
    teacher, _ = unit_columns(teacher_ref[...])
    teacher_out[...] = jnp.transpose(teacher).astype(jnp.bfloat16)
    student, length = unit_columns(student_ref[...])
    student_out[...] = jnp.transpose(student).astype(jnp.bfloat16)
    copy_out[...] = student_ref[...]
    inverse_out[...] = 1.0 / length


def in_crop_order(core, rows, own_ref, other_ref, units_ref):
    for chip in range(own_ref.shape[0]):
        units_ref[pl.ds(pl.multiple_of((2 * chip + core) * rows, rows), rows), :] = own_ref[chip, :rows, :]
        units_ref[pl.ds(pl.multiple_of((2 * chip + 1 - core) * rows, rows), rows), :] = other_ref[chip, :rows, :]


def exponentials(directions, units, temperature):
    logits = lax.dot_general(
        directions, units, (((1,), (1,)), ((), ())), preferred_element_type=jnp.float32
    )
    return jnp.exp2(logits * (math.log2(math.e) / temperature))


def fold(values):
    rows, lanes = values.shape
    return jnp.sum(values.reshape(rows // 8, 8, lanes), axis=0)


def as_rows(line):
    return jnp.concatenate([line[:, at : at + LANES] for at in range(0, line.shape[1], LANES)], axis=0)


def as_line(rows):
    return jnp.concatenate([rows[at : at + 1, :] for at in range(rows.shape[0])], axis=1)


def teacher_kernel(prototypes, rows, core_ref, directions_ref, own_ref, other_ref, mass_ref, sent_ref, units_ref):
    in_crop_order(core_ref[0], rows, own_ref, other_ref, units_ref)
    total = 0.0
    for start in range(0, directions_ref.shape[0], TILE):
        mass = exponentials(directions_ref[start : start + TILE, :], units_ref[...], teacher_temp)
        mass_ref[start : start + TILE, :] = mass
        scale = 1.0 / (prototypes * jnp.sum(mass, axis=1, keepdims=True))
        total = total + fold(mass * scale)
    sent_ref[...] = as_rows(jnp.sum(total, axis=0, keepdims=True))


def student_kernel(rows, core_ref, directions_ref, own_ref, other_ref, mass_ref, part_ref, turned_ref, units_ref):
    in_crop_order(core_ref[0], rows, own_ref, other_ref, units_ref)
    turned_ref[...] = jnp.transpose(units_ref[...].astype(jnp.float32)).astype(jnp.bfloat16)
    total = 0.0
    for start in range(0, directions_ref.shape[0], TILE):
        mass = exponentials(directions_ref[start : start + TILE, :], units_ref[...], student_temp)
        mass_ref[start : start + TILE, :] = mass
        total = total + fold(mass)
    part_ref[...] = as_rows(jnp.sum(total, axis=0, keepdims=True))


def sweep_kernel(prototypes, crops, mass_ref, got_ref, *refs):
    part_refs, (sent_ref, scale_ref) = refs[:-2], refs[-2:]
    lines = crops // LANES
    crop_scale = as_line(1.0 / (crops * got_ref[...]))
    total = 0.0
    for start in range(0, mass_ref.shape[0], TILE):
        mass = mass_ref[start : start + TILE, :]
        scale = 1.0 / (prototypes * jnp.sum(mass * crop_scale, axis=1, keepdims=True))
        scale_ref[start : start + TILE, :] = scale
        total = total + fold(mass * scale)
    sent_ref[:lines, :] = as_rows(jnp.sum(total, axis=0, keepdims=True))
    for part_ref in part_refs:
        sent_ref[lines:, :] = part_ref[...]


def gradient_kernel(
    group_ref, teacher_ref, student_ref, scale_ref, got_ref, crop_ref, turned_ref, copy_ref, inverse_ref,
    sent_ref, gradient_ref, grad_ref,
):
    group = group_ref[0]
    chips, rows_each, _ = sent_ref.shape
    count, crops = student_ref.shape
    width = turned_ref.shape[0]
    lines = crops // LANES
    own_crops = crops // GROUPS
    weights = crop_ref[...] / student_temp
    teacher_scale = as_line(weights / got_ref[:lines, :])
    student_scale = as_line(weights / got_ref[lines:, :])
    own_rows = pl.ds(pl.multiple_of(group * (width // GROUPS), width // GROUPS), width // GROUPS)
    own_lanes = pl.ds(pl.multiple_of(group * own_crops, own_crops), own_crops)
    features = 0.0
    for start in range(0, count, TILE):
        here, slot = slice(start, start + TILE), (start // TILE) % 2
        gradient = student_ref[here, :] * student_scale - teacher_ref[here, :] * scale_ref[here, :] * teacher_scale
        gradient_ref[slot] = gradient.astype(jnp.bfloat16)
        weight_grad = lax.dot_general(
            turned_ref[...], gradient_ref[slot], (((1,), (1,)), ((), ())), preferred_element_type=jnp.float32
        )
        inverse = inverse_ref[:, here]
        unit = copy_ref[:, here].astype(jnp.float32) * inverse
        dot = jnp.sum(unit * weight_grad, axis=0, keepdims=True)
        grad_ref[slot] = (weight_grad - unit * dot) * inverse
        own = grad_ref[slot, own_rows, :].astype(jnp.bfloat16)
        sent_ref[:, :, here] = own.reshape(chips, rows_each, TILE)
        features = features + jnp.dot(
            unit.astype(jnp.bfloat16), gradient_ref[slot, :, own_lanes], preferred_element_type=jnp.float32
        )

    features = jnp.transpose(features).astype(jnp.bfloat16)
    per_chip = own_crops // chips
    for chip in range(chips):
        for piece in range(per_chip // rows_each):
            start = chip * per_chip + piece * rows_each
            at = count + piece * width
            sent_ref[chip, :, at : at + width] = features[start : start + rows_each, :]


def collect_kernel(core_ref, got_ref, keep_ref, give_ref):
    chips, rows_each, _ = got_ref.shape
    rows, width = keep_ref.shape
    total = got_ref[0].astype(jnp.float32)
    for chip in range(1, chips):
        total = total + got_ref[chip].astype(jnp.float32)
    pieces = rows // rows_each
    for piece in range(pieces):
        first = total[:, piece * width : (piece + 1) * width]
        second = total[:, (pieces + piece) * width : (pieces + piece + 1) * width]
        here = slice(piece * rows_each, (piece + 1) * rows_each)
        keep_ref[here, :] = jnp.where(core_ref[0] == 0, first, second)
        give_ref[here, :] = jnp.where(core_ref[0] == 0, second, first)


def feature_kernel(keep_ref, other_ref, student_ref, out_ref):
    total = keep_ref[...] + other_ref[...]
    hat, length = unit_rows(student_ref[...])
    out_ref[...] = (total - hat * jnp.sum(hat * total, axis=1, keepdims=True)) / length


def widen_kernel(got_ref, out_ref):
    chips, _, columns = got_ref.shape
    for chip in range(chips):
        out_ref[:, chip * columns : (chip + 1) * columns] = got_ref[chip].astype(jnp.float32)


def kernel_body(teacher_feat, student_feat, crop_weight, teacher_v, student_v):
    f32, bf16 = jnp.float32, jnp.bfloat16
    shape = jax.ShapeDtypeStruct
    blocks, fsdp = lax.axis_size("block"), lax.axis_size("fsdp")
    chips = blocks * GROUPS
    devices = chips * fsdp
    rows, width = teacher_feat.shape
    crops = rows * devices
    lines = crops // LANES
    kept = teacher_v.shape[1]
    prototypes = kept * fsdp
    count = kept // blocks
    group, block = lax.axis_index("group")[None], lax.axis_index("block")[None]
    core = lax.axis_index("fsdp")[None]
    elements = count * crops
    smem, vmem = pl.BlockSpec(memory_space=pltpu.SMEM), pl.BlockSpec(memory_space=pltpu.VMEM)

    def swap(values):
        return lax.ppermute(values, "fsdp", [(0, 1), (1, 0)])

    def add_up(values):
        values = values + swap(values)
        bit = 1
        while bit < blocks:
            values = values + lax.ppermute(values, "block", [(at, at ^ bit) for at in range(blocks)])
            bit *= 2
        return values

    spare = jnp.pad(crop_weight[None, :], ((0, 15), (0, width - rows)))
    teacher_sent, student_sent = call(
        units_kernel, (shape((chips, rows, width), bf16), shape((chips, rows + 16, width), bf16))
    )(teacher_feat, student_feat, spare)
    student_own = lax.all_to_all(student_sent, CHIPS, 0, 0)
    teacher_own = lax.all_to_all(teacher_sent, CHIPS, 0, 0)
    student_other = swap(student_own)
    teacher_other = swap(teacher_own)
    mine, others = student_own[:, rows, :rows], student_other[:, rows, :rows]
    weights = jnp.where(core == 0, jnp.stack([mine, others], 1), jnp.stack([others, mine], 1))
    weights = weights.astype(f32).reshape(lines, LANES)

    span = 2 * TILE
    spans = count // span
    column = pl.BlockSpec((width, span), lambda step, at: (0, at[0] * spans + step))
    turned = pl.BlockSpec((span, width), lambda step, at: (step, 0))
    straight = pl.BlockSpec((width, span), lambda step, at: (0, step))
    line = pl.BlockSpec((1, span), lambda step, at: (0, step))
    teacher_w, student_w, student_copy, inverse = call(
        directions_kernel,
        (
            shape((count, width), bf16),
            shape((count, width), bf16),
            shape((width, count), bf16),
            shape((1, count), f32),
        ),
        flops=12 * count * width,
        moved=10 * count * width,
        grid_spec=pltpu.PrefetchScalarGridSpec(
            num_scalar_prefetch=1,
            grid=(spans,),
            in_specs=[column, column],
            out_specs=[turned, turned, straight, line],
        ),
    )(
        block,
        pltpu.with_memory_space_constraint(teacher_v, pltpu.HBM),
        pltpu.with_memory_space_constraint(student_v, pltpu.HBM),
    )

    units = pltpu.VMEM((crops, width), bf16)
    student_mass, student_part, student_turned = call(
        functools.partial(student_kernel, rows),
        (shape((count, crops), f32), shape((lines, LANES), f32), shape((width, crops), bf16)),
        flops=2 * elements * width,
        exps=elements,
        in_specs=[smem] + [vmem] * 3,
        scratch_shapes=[units],
    )(core, student_w, student_own, student_other)
    mass, sent = call(
        functools.partial(teacher_kernel, prototypes, rows),
        (shape((count, crops), f32), shape((lines, LANES), f32)),
        flops=2 * elements * width,
        exps=elements,
        in_specs=[smem] + [vmem] * 3,
        scratch_shapes=[units],
    )(core, teacher_w, teacher_own, teacher_other)

    for sweep in range(1, ITERS):
        extra = sweep == ITERS - 1
        sent, scale = call(
            functools.partial(sweep_kernel, prototypes, crops),
            (shape((lines * (1 + extra), LANES), f32), shape((count, 1), f32)),
            flops=4 * elements,
        )(mass, add_up(sent), *([student_part] if extra else []))

    out_rows = width // chips
    per_chip = rows * fsdp * width // out_rows
    sent = call(
        gradient_kernel,
        shape((blocks, out_rows, count + per_chip), bf16),
        flops=4 * elements * width,
        in_specs=[smem] + [vmem] * 8,
        scratch_shapes=[pltpu.VMEM((2, TILE, crops), bf16), pltpu.VMEM((2, width, TILE), f32)],
    )(group, mass, student_mass, scale, add_up(sent), weights, student_turned, student_copy, inverse)
    got = lax.all_to_all(sent, "block", 0, 0)
    keep, give = call(
        collect_kernel,
        [shape((rows, width), f32)] * 2,
        grid=(1,),
        in_specs=[smem, pl.BlockSpec((blocks, out_rows, per_chip), lambda step: (0, 0, count // per_chip))],
    )(core, got)
    grad_feat = call(feature_kernel, shape((rows, width), f32))(keep, swap(give), student_feat)
    grad_v = call(
        widen_kernel,
        shape((out_rows, kept), f32),
        grid=(1,),
        in_specs=[pl.BlockSpec((blocks, out_rows, count), lambda step: (0, 0, 0))],
        out_specs=pl.BlockSpec((out_rows, kept), lambda step: (0, 0)),
    )(got)
    return (grad_v, grad_feat)


def solution(mesh):
    dp, fsdp = mesh.shape["dp"], mesh.shape["fsdp"]
    blocks = dp // GROUPS

    def run(teacher_feat, student_feat, crop_weight, teacher_v, student_v):
        crops = teacher_feat.shape[0]
        count = teacher_v.shape[1] // (blocks * fsdp)
        fits = fsdp == 2 and dp == 16 and count % (2 * TILE) == 0 and crops == 1024
        if fits and 8 * count * crops <= KEPT_BYTES:
            grid = Mesh(mesh.devices.reshape(GROUPS, blocks, fsdp), (*CHIPS, "fsdp"))
            body, chips = kernel_body, CHIPS
        else:
            grid, body, chips = mesh, plain_body, ("dp",)
        every = P((*chips, "fsdp"))
        return jax.shard_map(
            body,
            mesh=grid,
            in_specs=(every, every, every, P(None, "fsdp"), P(None, "fsdp")),
            out_specs=(P(chips, "fsdp"), every),
            check_vma=False,
        )(teacher_feat, student_feat, crop_weight, teacher_v, student_v)

    return run
```

```python
import functools
import math

import jax
import jax.numpy as jnp
from jax import lax
from jax.experimental import pallas as pl
from jax.experimental.pallas import tpu as pltpu
from jax.sharding import Mesh
from jax.sharding import PartitionSpec as P

ITERS = 3

teacher_temp = 0.04
student_temp = 0.1
epsilon = 1e-06

GROUPS = 2
TILE = 256
LANES = 128
VMEM_BYTES = 12 << 20
KEPT_BYTES = 18 << 20

EVERY = ("dp", "fsdp")
CHIPS = ("group", "block")
GROUP = ("block", "fsdp")


def unit_rows(values):
    floats = values.astype(jnp.float32)
    length = jnp.sqrt(jnp.sum(floats * floats, axis=1, keepdims=True) + epsilon)
    return (floats / length, length)


def unit_columns(values):
    floats = values.astype(jnp.float32)
    length = jnp.sqrt(jnp.sum(floats * floats, axis=0, keepdims=True) + epsilon)
    return (floats / length, length)


COPY_BYTES = 1 << 22


def share(values, axes):
    count = lax.axis_size(axes)
    if count * values.size * values.dtype.itemsize > COPY_BYTES:
        return lax.all_gather(values, axes)
    return lax.all_to_all(jnp.broadcast_to(values, (count, *values.shape)), axes, 0, 0)


def add_up(values):
    if lax.axis_size(EVERY) * values.size * values.dtype.itemsize > COPY_BYTES:
        return lax.psum(values, EVERY)
    return jnp.sum(share(values, EVERY), axis=0)


def plain_body(teacher_feat, student_feat, crop_weight, teacher_v, student_v):
    fsdp = lax.axis_size("fsdp")
    devices = lax.axis_size("dp") * fsdp
    own_rows, width = teacher_feat.shape
    crops = own_rows * devices
    block = teacher_v.shape[1] // lax.axis_size("dp")
    prototypes = block * devices
    first = lax.axis_index("dp") * block

    teacher_hat, _ = unit_rows(teacher_feat)
    student_hat, student_len = unit_rows(student_feat)
    units = jnp.concatenate(
        [teacher_hat.astype(jnp.bfloat16), student_hat.astype(jnp.bfloat16)], axis=1
    )
    units = share(share(units, "dp"), "fsdp").reshape(crops, 2 * width)
    teacher_unit, student_unit = units[:, :width], units[:, width:]

    teacher_w, _ = unit_columns(lax.dynamic_slice_in_dim(teacher_v, first, block, 1))
    student_w, student_wlen = unit_columns(lax.dynamic_slice_in_dim(student_v, first, block, 1))
    student_wunit = student_w.astype(jnp.bfloat16)

    mass = jnp.exp(
        jnp.dot(teacher_unit, teacher_w.astype(jnp.bfloat16), preferred_element_type=jnp.float32)
        / teacher_temp
    )
    student_mass = jnp.exp(
        jnp.dot(student_unit, student_wunit, preferred_element_type=jnp.float32) / student_temp
    )
    student_part = jnp.sum(student_mass, axis=1)

    crop_scale = None
    for sweep in range(ITERS):
        scaled = mass if sweep == 0 else mass * crop_scale[:, None]
        proto_scale = 1.0 / (prototypes * jnp.sum(scaled, axis=0))
        crop_part = jnp.sum(mass * proto_scale[None, :], axis=1)
        if sweep == 0:
            placed = jnp.zeros((fsdp, crops // (fsdp * own_rows), own_rows), jnp.float32)
            own = crop_weight.astype(jnp.float32)[None, None]
            spot = (lax.axis_index("fsdp"), lax.axis_index("dp"), 0)
            placed = lax.dynamic_update_slice(placed, own, spot).reshape(crops)
            sums = add_up(jnp.stack([crop_part, student_part, placed]))
            crop_mass, student_total, weights = sums[0], sums[1], sums[2]
        else:
            crop_mass = add_up(crop_part)
        crop_scale = 1.0 / (crops * crop_mass)

    target = crops * (mass * crop_scale[:, None] * proto_scale[None, :])
    student_prob = student_mass / student_total[:, None]
    gradient = ((student_prob - target) * weights[:, None] / student_temp).astype(jnp.bfloat16)
    feature_part = lax.dot_general(
        gradient, student_wunit, (((1,), (1,)), ((), ())), preferred_element_type=jnp.float32
    )
    weight_grad = lax.dot_general(
        student_unit, gradient, (((0,), (0,)), ((), ())), preferred_element_type=jnp.float32
    )
    weight_dot = jnp.sum(student_w * weight_grad, axis=0, keepdims=True)
    grad_block = (weight_grad - student_w * weight_dot) / student_wlen

    feature_sent = feature_part.astype(jnp.bfloat16).reshape(fsdp, -1, own_rows, width)
    feature_sent = jnp.swapaxes(feature_sent, 0, 1).reshape(devices, own_rows, width)
    feature_all = lax.all_to_all(feature_sent, EVERY, 0, 0)
    feature_grad = jnp.sum(feature_all.astype(jnp.float32), axis=0)
    grad_feat = (
        feature_grad - student_hat * jnp.sum(student_hat * feature_grad, axis=1, keepdims=True)
    ) / student_len
    grad_v = lax.all_to_all(grad_block.astype(jnp.bfloat16), "dp", 0, 1, tiled=True)
    return (grad_v.astype(jnp.float32), grad_feat)


def call(kernel, out_shape, flops=0, moved=0, exps=0, **more):
    return pl.pallas_call(
        kernel,
        out_shape=out_shape,
        compiler_params=pltpu.CompilerParams(vmem_limit_bytes=VMEM_BYTES),
        cost_estimate=pl.CostEstimate(flops=flops, bytes_accessed=moved, transcendentals=exps),
        **more,
    )


def units_kernel(teacher_ref, student_ref, weight_ref, teacher_out, student_out):
    rows = teacher_ref.shape[0]
    teacher = unit_rows(teacher_ref[...])[0].astype(jnp.bfloat16)
    student = unit_rows(student_ref[...])[0].astype(jnp.bfloat16)
    for chip in range(teacher_out.shape[0]):
        teacher_out[chip] = teacher
    student_out[:rows, :] = student
    student_out[rows:, :] = weight_ref[...]


def directions_kernel(block_ref, teacher_ref, student_ref, teacher_out, student_out, copy_out, inverse_out):
    teacher, _ = unit_columns(teacher_ref[...])
    teacher_out[...] = jnp.transpose(teacher).astype(jnp.bfloat16)
    student, length = unit_columns(student_ref[...])
    student_out[...] = jnp.transpose(student).astype(jnp.bfloat16)
    copy_out[...] = student_ref[...]
    inverse_out[...] = 1.0 / length


def in_crop_order(core, rows, own_ref, other_ref, units_ref):
    for chip in range(own_ref.shape[0]):
        units_ref[pl.ds(pl.multiple_of((2 * chip + core) * rows, rows), rows), :] = own_ref[chip, :rows, :]
        units_ref[pl.ds(pl.multiple_of((2 * chip + 1 - core) * rows, rows), rows), :] = other_ref[chip, :rows, :]


def exponentials(directions, units, temperature):
    logits = lax.dot_general(
        directions, units, (((1,), (1,)), ((), ())), preferred_element_type=jnp.float32
    )
    return jnp.exp2(logits * (math.log2(math.e) / temperature))


def fold(values):
    rows, lanes = values.shape
    return jnp.sum(values.reshape(rows // 8, 8, lanes), axis=0)


def as_rows(line):
    return jnp.concatenate([line[:, at : at + LANES] for at in range(0, line.shape[1], LANES)], axis=0)


def as_line(rows):
    return jnp.concatenate([rows[at : at + 1, :] for at in range(rows.shape[0])], axis=1)


def send(sent_ref, total, *more):
    values = jnp.concatenate([as_rows(jnp.sum(total, axis=0, keepdims=True)), *more], axis=0)
    for device in range(sent_ref.shape[0]):
        sent_ref[device] = values


def received(got_ref):
    total = got_ref[0]
    for device in range(1, got_ref.shape[0]):
        total = total + got_ref[device]
    return total


def teacher_kernel(prototypes, rows, core_ref, directions_ref, own_ref, other_ref, mass_ref, sent_ref, units_ref):
    in_crop_order(core_ref[0], rows, own_ref, other_ref, units_ref)
    total = 0.0
    for start in range(0, directions_ref.shape[0], TILE):
        mass = exponentials(directions_ref[start : start + TILE, :], units_ref[...], teacher_temp)
        mass_ref[start : start + TILE, :] = mass
        scale = 1.0 / (prototypes * jnp.sum(mass, axis=1, keepdims=True))
        total = total + fold(mass * scale)
    send(sent_ref, total)


def student_kernel(rows, core_ref, directions_ref, own_ref, other_ref, mass_ref, part_ref, turned_ref, units_ref):
    in_crop_order(core_ref[0], rows, own_ref, other_ref, units_ref)
    turned_ref[...] = jnp.transpose(units_ref[...].astype(jnp.float32)).astype(jnp.bfloat16)
    total = 0.0
    for start in range(0, directions_ref.shape[0], TILE):
        mass = exponentials(directions_ref[start : start + TILE, :], units_ref[...], student_temp)
        mass_ref[start : start + TILE, :] = mass
        total = total + fold(mass)
    part_ref[...] = as_rows(jnp.sum(total, axis=0, keepdims=True))


def sweep_kernel(prototypes, crops, mass_ref, got_ref, *refs):
    part_refs, (sent_ref, scale_ref) = refs[:-2], refs[-2:]
    crop_scale = as_line(1.0 / (crops * received(got_ref)))
    total = 0.0
    for start in range(0, mass_ref.shape[0], TILE):
        mass = mass_ref[start : start + TILE, :]
        scale = 1.0 / (prototypes * jnp.sum(mass * crop_scale, axis=1, keepdims=True))
        scale_ref[start : start + TILE, :] = scale
        total = total + fold(mass * scale)
    send(sent_ref, total, *(part_ref[...] for part_ref in part_refs))


def gradient_kernel(
    group_ref, teacher_ref, student_ref, scale_ref, got_ref, crop_ref, turned_ref, copy_ref, inverse_ref,
    sent_ref, gradient_ref, grad_ref,
):
    group = group_ref[0]
    chips, rows_each, _ = sent_ref.shape
    count, crops = student_ref.shape
    width = turned_ref.shape[0]
    lines = crops // LANES
    own_crops = crops // GROUPS
    weights = crop_ref[...] / student_temp
    totals = received(got_ref)
    teacher_scale = as_line(weights / totals[:lines])
    student_scale = as_line(weights / totals[lines:])
    own_rows = pl.ds(pl.multiple_of(group * (width // GROUPS), width // GROUPS), width // GROUPS)
    own_lanes = pl.ds(pl.multiple_of(group * own_crops, own_crops), own_crops)
    features = 0.0
    for start in range(0, count, TILE):
        here, slot = slice(start, start + TILE), (start // TILE) % 2
        gradient = student_ref[here, :] * student_scale - teacher_ref[here, :] * scale_ref[here, :] * teacher_scale
        gradient_ref[slot] = gradient.astype(jnp.bfloat16)
        weight_grad = lax.dot_general(
            turned_ref[...], gradient_ref[slot], (((1,), (1,)), ((), ())), preferred_element_type=jnp.float32
        )
        inverse = inverse_ref[:, here]
        unit = copy_ref[:, here].astype(jnp.float32) * inverse
        dot = jnp.sum(unit * weight_grad, axis=0, keepdims=True)
        grad_ref[slot] = (weight_grad - unit * dot) * inverse
        own = grad_ref[slot, own_rows, :].astype(jnp.bfloat16)
        sent_ref[:, :, here] = own.reshape(chips, rows_each, TILE)
        features = features + jnp.dot(
            unit.astype(jnp.bfloat16), gradient_ref[slot, :, own_lanes], preferred_element_type=jnp.float32
        )

    features = jnp.transpose(features).astype(jnp.bfloat16)
    per_chip = own_crops // chips
    for chip in range(chips):
        for piece in range(per_chip // rows_each):
            start = chip * per_chip + piece * rows_each
            at = count + piece * width
            sent_ref[chip, :, at : at + width] = features[start : start + rows_each, :]


def collect_kernel(core_ref, got_ref, keep_ref, give_ref):
    chips, rows_each, _ = got_ref.shape
    rows, width = keep_ref.shape
    total = got_ref[0].astype(jnp.float32)
    for chip in range(1, chips):
        total = total + got_ref[chip].astype(jnp.float32)
    pieces = rows // rows_each
    for piece in range(pieces):
        first = total[:, piece * width : (piece + 1) * width]
        second = total[:, (pieces + piece) * width : (pieces + piece + 1) * width]
        here = slice(piece * rows_each, (piece + 1) * rows_each)
        keep_ref[here, :] = jnp.where(core_ref[0] == 0, first, second)
        give_ref[here, :] = jnp.where(core_ref[0] == 0, second, first)


def feature_kernel(keep_ref, other_ref, student_ref, out_ref):
    total = keep_ref[...] + other_ref[...]
    hat, length = unit_rows(student_ref[...])
    out_ref[...] = (total - hat * jnp.sum(hat * total, axis=1, keepdims=True)) / length


def widen_kernel(got_ref, out_ref):
    chips, _, columns = got_ref.shape
    for chip in range(chips):
        out_ref[:, chip * columns : (chip + 1) * columns] = got_ref[chip].astype(jnp.float32)


def kernel_body(teacher_feat, student_feat, crop_weight, teacher_v, student_v):
    f32, bf16 = jnp.float32, jnp.bfloat16
    shape = jax.ShapeDtypeStruct
    blocks, fsdp = lax.axis_size("block"), lax.axis_size("fsdp")
    chips = blocks * GROUPS
    members, devices = blocks * fsdp, chips * fsdp
    rows, width = teacher_feat.shape
    crops = rows * devices
    lines = crops // LANES
    kept = teacher_v.shape[1]
    prototypes = kept * fsdp
    count = kept // blocks
    group, block = lax.axis_index("group")[None], lax.axis_index("block")[None]
    core = lax.axis_index("fsdp")[None]
    elements = count * crops
    smem, vmem = pl.BlockSpec(memory_space=pltpu.SMEM), pl.BlockSpec(memory_space=pltpu.VMEM)

    def swap(values):
        return lax.ppermute(values, "fsdp", [(0, 1), (1, 0)])

    def share(values):
        return lax.all_to_all(values, GROUP, 0, 0)

    spare = jnp.pad(crop_weight[None, :], ((0, 15), (0, width - rows)))
    teacher_sent, student_sent = call(
        units_kernel, (shape((chips, rows, width), bf16), shape((rows + 16, width), bf16))
    )(teacher_feat, student_feat, spare)
    teacher_own = lax.all_to_all(teacher_sent, CHIPS, 0, 0)
    student_own = lax.all_gather(student_sent, CHIPS)
    span = 2 * TILE
    spans = count // span
    column = pl.BlockSpec((width, span), lambda step, at: (0, at[0] * spans + step))
    turned = pl.BlockSpec((span, width), lambda step, at: (step, 0))
    straight = pl.BlockSpec((width, span), lambda step, at: (0, step))
    line = pl.BlockSpec((1, span), lambda step, at: (0, step))
    teacher_w, student_w, student_copy, inverse = call(
        directions_kernel,
        (
            shape((count, width), bf16),
            shape((count, width), bf16),
            shape((width, count), bf16),
            shape((1, count), f32),
        ),
        flops=12 * count * width,
        moved=10 * count * width,
        grid_spec=pltpu.PrefetchScalarGridSpec(
            num_scalar_prefetch=1,
            grid=(spans,),
            in_specs=[column, column],
            out_specs=[turned, turned, straight, line],
        ),
    )(
        block,
        pltpu.with_memory_space_constraint(teacher_v, pltpu.HBM),
        pltpu.with_memory_space_constraint(student_v, pltpu.HBM),
    )

    teacher_own, teacher_w = lax.optimization_barrier((teacher_own, teacher_w))
    teacher_other = swap(teacher_own)

    units = pltpu.VMEM((crops, width), bf16)
    mass, sent = call(
        functools.partial(teacher_kernel, prototypes, rows),
        (shape((count, crops), f32), shape((members, lines, LANES), f32)),
        flops=2 * elements * width,
        exps=elements,
        in_specs=[smem] + [vmem] * 3,
        scratch_shapes=[units],
    )(core, teacher_w, teacher_own, teacher_other)

    got = share(sent)
    student_own, _ = lax.optimization_barrier((student_own, got))
    student_other = swap(student_own)
    mine, others = student_own[:, rows, :rows], student_other[:, rows, :rows]
    weights = jnp.where(core == 0, jnp.stack([mine, others], 1), jnp.stack([others, mine], 1))
    weights = weights.astype(f32).reshape(lines, LANES)

    student_mass, student_part, student_turned = call(
        functools.partial(student_kernel, rows),
        (shape((count, crops), f32), shape((lines, LANES), f32), shape((width, crops), bf16)),
        flops=2 * elements * width,
        exps=elements,
        in_specs=[smem] + [vmem] * 3,
        scratch_shapes=[units],
    )(core, student_w, student_own, student_other)
    for sweep in range(1, ITERS):
        extra = sweep == ITERS - 1
        sent, scale = call(
            functools.partial(sweep_kernel, prototypes, crops),
            (shape((members, lines * (1 + extra), LANES), f32), shape((count, 1), f32)),
            flops=4 * elements,
        )(mass, got, *([student_part] if extra else []))
        got = share(sent)

    out_rows = width // chips
    per_chip = rows * fsdp * width // out_rows
    sent = call(
        gradient_kernel,
        shape((blocks, out_rows, count + per_chip), bf16),
        flops=4 * elements * width,
        in_specs=[smem] + [vmem] * 8,
        scratch_shapes=[pltpu.VMEM((2, TILE, crops), bf16), pltpu.VMEM((2, width, TILE), f32)],
    )(group, mass, student_mass, scale, got, weights, student_turned, student_copy, inverse)
    got = lax.all_to_all(sent, "block", 0, 0)
    keep, give = call(
        collect_kernel,
        [shape((rows, width), f32)] * 2,
        grid=(1,),
        in_specs=[smem, pl.BlockSpec((blocks, out_rows, per_chip), lambda step: (0, 0, count // per_chip))],
    )(core, got)
    grad_feat = call(feature_kernel, shape((rows, width), f32))(keep, swap(give), student_feat)
    grad_v = call(
        widen_kernel,
        shape((out_rows, kept), f32),
        grid=(1,),
        in_specs=[pl.BlockSpec((blocks, out_rows, count), lambda step: (0, 0, 0))],
        out_specs=pl.BlockSpec((out_rows, kept), lambda step: (0, 0)),
    )(got)
    return (grad_v, grad_feat)


def solution(mesh):
    dp, fsdp = mesh.shape["dp"], mesh.shape["fsdp"]
    blocks = dp // GROUPS

    def run(teacher_feat, student_feat, crop_weight, teacher_v, student_v):
        crops = teacher_feat.shape[0]
        count = teacher_v.shape[1] // (blocks * fsdp)
        fits = fsdp == 2 and dp == 16 and count % (2 * TILE) == 0 and crops == 1024
        if fits and 8 * count * crops <= KEPT_BYTES:
            grid = Mesh(mesh.devices.reshape(GROUPS, blocks, fsdp), (*CHIPS, "fsdp"))
            body, chips = kernel_body, CHIPS
        else:
            grid, body, chips = mesh, plain_body, ("dp",)
        every = P((*chips, "fsdp"))
        return jax.shard_map(
            body,
            mesh=grid,
            in_specs=(every, every, every, P(None, "fsdp"), P(None, "fsdp")),
            out_specs=(P(chips, "fsdp"), every),
            check_vma=False,
        )(teacher_feat, student_feat, crop_weight, teacher_v, student_v)

    return run
```

```python
import functools
import math

import jax
import jax.numpy as jnp
from jax import lax
from jax.experimental import pallas as pl
from jax.experimental.pallas import tpu as pltpu
from jax.sharding import Mesh
from jax.sharding import PartitionSpec as P

ITERS = 3

teacher_temp = 0.04
student_temp = 0.1
epsilon = 1e-06

GROUPS = 2
TILE = 256
LANES = 128
VMEM_BYTES = 12 << 20
KEPT_BYTES = 18 << 20

EVERY = ("dp", "fsdp")
CHIPS = ("group", "block")
GROUP = ("block", "fsdp")


def unit_rows(values):
    floats = values.astype(jnp.float32)
    length = jnp.sqrt(jnp.sum(floats * floats, axis=1, keepdims=True) + epsilon)
    return (floats / length, length)


def unit_columns(values):
    floats = values.astype(jnp.float32)
    length = jnp.sqrt(jnp.sum(floats * floats, axis=0, keepdims=True) + epsilon)
    return (floats / length, length)


COPY_BYTES = 1 << 22


def share(values, axes):
    count = lax.axis_size(axes)
    if count * values.size * values.dtype.itemsize > COPY_BYTES:
        return lax.all_gather(values, axes)
    return lax.all_to_all(jnp.broadcast_to(values, (count, *values.shape)), axes, 0, 0)


def add_up(values):
    if lax.axis_size(EVERY) * values.size * values.dtype.itemsize > COPY_BYTES:
        return lax.psum(values, EVERY)
    return jnp.sum(share(values, EVERY), axis=0)


def plain_body(teacher_feat, student_feat, crop_weight, teacher_v, student_v):
    fsdp = lax.axis_size("fsdp")
    devices = lax.axis_size("dp") * fsdp
    own_rows, width = teacher_feat.shape
    crops = own_rows * devices
    block = teacher_v.shape[1] // lax.axis_size("dp")
    prototypes = block * devices
    first = lax.axis_index("dp") * block

    teacher_hat, _ = unit_rows(teacher_feat)
    student_hat, student_len = unit_rows(student_feat)
    units = jnp.concatenate(
        [teacher_hat.astype(jnp.bfloat16), student_hat.astype(jnp.bfloat16)], axis=1
    )
    units = share(share(units, "dp"), "fsdp").reshape(crops, 2 * width)
    teacher_unit, student_unit = units[:, :width], units[:, width:]

    teacher_w, _ = unit_columns(lax.dynamic_slice_in_dim(teacher_v, first, block, 1))
    student_w, student_wlen = unit_columns(lax.dynamic_slice_in_dim(student_v, first, block, 1))
    student_wunit = student_w.astype(jnp.bfloat16)

    mass = jnp.exp(
        jnp.dot(teacher_unit, teacher_w.astype(jnp.bfloat16), preferred_element_type=jnp.float32)
        / teacher_temp
    )
    student_mass = jnp.exp(
        jnp.dot(student_unit, student_wunit, preferred_element_type=jnp.float32) / student_temp
    )
    student_part = jnp.sum(student_mass, axis=1)

    crop_scale = None
    for sweep in range(ITERS):
        scaled = mass if sweep == 0 else mass * crop_scale[:, None]
        proto_scale = 1.0 / (prototypes * jnp.sum(scaled, axis=0))
        crop_part = jnp.sum(mass * proto_scale[None, :], axis=1)
        if sweep == 0:
            placed = jnp.zeros((fsdp, crops // (fsdp * own_rows), own_rows), jnp.float32)
            own = crop_weight.astype(jnp.float32)[None, None]
            spot = (lax.axis_index("fsdp"), lax.axis_index("dp"), 0)
            placed = lax.dynamic_update_slice(placed, own, spot).reshape(crops)
            sums = add_up(jnp.stack([crop_part, student_part, placed]))
            crop_mass, student_total, weights = sums[0], sums[1], sums[2]
        else:
            crop_mass = add_up(crop_part)
        crop_scale = 1.0 / (crops * crop_mass)

    target = crops * (mass * crop_scale[:, None] * proto_scale[None, :])
    student_prob = student_mass / student_total[:, None]
    gradient = ((student_prob - target) * weights[:, None] / student_temp).astype(jnp.bfloat16)
    feature_part = lax.dot_general(
        gradient, student_wunit, (((1,), (1,)), ((), ())), preferred_element_type=jnp.float32
    )
    weight_grad = lax.dot_general(
        student_unit, gradient, (((0,), (0,)), ((), ())), preferred_element_type=jnp.float32
    )
    weight_dot = jnp.sum(student_w * weight_grad, axis=0, keepdims=True)
    grad_block = (weight_grad - student_w * weight_dot) / student_wlen

    feature_sent = feature_part.astype(jnp.bfloat16).reshape(fsdp, -1, own_rows, width)
    feature_sent = jnp.swapaxes(feature_sent, 0, 1).reshape(devices, own_rows, width)
    feature_all = lax.all_to_all(feature_sent, EVERY, 0, 0)
    feature_grad = jnp.sum(feature_all.astype(jnp.float32), axis=0)
    grad_feat = (
        feature_grad - student_hat * jnp.sum(student_hat * feature_grad, axis=1, keepdims=True)
    ) / student_len
    grad_v = lax.all_to_all(grad_block.astype(jnp.bfloat16), "dp", 0, 1, tiled=True)
    return (grad_v.astype(jnp.float32), grad_feat)


def call(kernel, out_shape, flops=0, moved=0, exps=0, **more):
    return pl.pallas_call(
        kernel,
        out_shape=out_shape,
        compiler_params=pltpu.CompilerParams(vmem_limit_bytes=VMEM_BYTES),
        cost_estimate=pl.CostEstimate(flops=flops, bytes_accessed=moved, transcendentals=exps),
        **more,
    )


def units_kernel(teacher_ref, student_ref, sent_ref, teacher_vmem, student_vmem, sems):
    copies = [
        pltpu.make_async_copy(teacher_ref, teacher_vmem, sems.at[0]),
        pltpu.make_async_copy(student_ref, student_vmem, sems.at[1]),
    ]
    for copy in copies:
        copy.start()
    for copy in copies:
        copy.wait()
    width = teacher_vmem.shape[1]
    teacher = unit_rows(teacher_vmem[...])[0].astype(jnp.bfloat16)
    student = unit_rows(student_vmem[...])[0].astype(jnp.bfloat16)
    for chip in range(sent_ref.shape[0]):
        sent_ref[chip, :, :width] = teacher
        sent_ref[chip, :, width:] = student


def directions_kernel(block_ref, teacher_ref, student_ref, teacher_out, student_out, inverse_out):
    teacher, _ = unit_columns(teacher_ref[...])
    teacher_out[...] = jnp.transpose(teacher).astype(jnp.bfloat16)
    student, length = unit_columns(student_ref[...])
    student_out[...] = jnp.transpose(student).astype(jnp.bfloat16)
    inverse_out[...] = 1.0 / length


def in_crop_order(core, own_ref, other_ref, teacher_ref, student_ref):
    chips, rows, _ = own_ref.shape
    width = teacher_ref.shape[1]
    for chip in range(chips):
        for got_ref, side in ((own_ref, core), (other_ref, 1 - core)):
            here = pl.ds(pl.multiple_of((2 * chip + side) * rows, rows), rows)
            teacher_ref[here, :] = got_ref[chip, :, :width]
            student_ref[here, :] = got_ref[chip, :, width:]


def exponentials(directions, units, temperature):
    logits = lax.dot_general(
        directions, units, (((1,), (1,)), ((), ())), preferred_element_type=jnp.float32
    )
    return jnp.exp2(logits * (math.log2(math.e) / temperature))


def fold(values):
    rows, lanes = values.shape
    return jnp.sum(values.reshape(rows // 8, 8, lanes), axis=0)


def as_rows(line):
    return jnp.concatenate([line[:, at : at + LANES] for at in range(0, line.shape[1], LANES)], axis=0)


def as_line(rows):
    return jnp.concatenate([rows[at : at + 1, :] for at in range(rows.shape[0])], axis=1)


def send(sent_ref, total, *more):
    values = jnp.concatenate([as_rows(jnp.sum(total, axis=0, keepdims=True)), *more], axis=0)
    for device in range(sent_ref.shape[0]):
        sent_ref[device] = values


def received(got_ref):
    total = got_ref[0]
    for device in range(1, got_ref.shape[0]):
        total = total + got_ref[device]
    return total


def masses_kernel(
    prototypes, core_ref, teacher_w_ref, student_w_ref, own_ref, other_ref, weight_ref,
    teacher_ref, student_ref, sent_ref, part_ref, turned_ref, teacher_units, student_units,
):
    in_crop_order(core_ref[0], own_ref, other_ref, teacher_units, student_units)
    total = part = 0.0
    for start in range(0, teacher_ref.shape[0], TILE):
        here = slice(start, start + TILE)
        mass = exponentials(teacher_w_ref[here, :], teacher_units[...], teacher_temp)
        teacher_ref[here, :] = mass
        scale = 1.0 / (prototypes * jnp.sum(mass, axis=1, keepdims=True))
        total = total + fold(mass * scale)
        mass = exponentials(student_w_ref[here, :], student_units[...], student_temp)
        student_ref[here, :] = mass
        part = part + fold(mass)
    send(sent_ref, total, weight_ref[...])
    part_ref[...] = as_rows(jnp.sum(part, axis=0, keepdims=True))
    turned_ref[...] = jnp.transpose(student_units[...].astype(jnp.float32)).astype(jnp.bfloat16)


def sweep_kernel(prototypes, crops, last, mass_ref, got_ref, *refs):
    crop_scale = as_line(1.0 / (crops * received(got_ref)[: crops // LANES]))
    total = 0.0
    for start in range(0, mass_ref.shape[0], TILE):
        mass = mass_ref[start : start + TILE, :]
        scale = 1.0 / (prototypes * jnp.sum(mass * crop_scale, axis=1, keepdims=True))
        total = total + fold(mass * scale)
        if last:
            refs[1][start : start + TILE, :] = scale
    if last:
        send(refs[0], total)
    else:
        send(refs[1], total, refs[0][...])


def gradient_kernel(
    place_ref, teacher_ref, student_ref, scale_ref, first_ref, second_ref, third_ref, turned_ref, inverse_ref, directions_ref,
    sent_ref, gradient_ref, grad_ref, copy_ref, sem,
):
    group, block = place_ref[0], place_ref[1]
    chips, rows_each, _ = sent_ref.shape
    count, crops = student_ref.shape
    width = turned_ref.shape[0]
    columns = pl.ds(pl.multiple_of(block * count, count), count)
    copy = pltpu.make_async_copy(directions_ref.at[:, columns], copy_ref, sem)
    copy.start()
    lines = crops // LANES
    own_crops = crops // GROUPS
    weights = received(first_ref)[lines:] / student_temp
    teacher_scale = as_line(weights / received(third_ref))
    student_scale = as_line(weights / received(second_ref)[lines:])
    own_rows = pl.ds(pl.multiple_of(group * (width // GROUPS), width // GROUPS), width // GROUPS)
    own_lanes = pl.ds(pl.multiple_of(group * own_crops, own_crops), own_crops)
    features = 0.0
    for start in range(0, count, TILE):
        here, slot = slice(start, start + TILE), (start // TILE) % 2
        gradient = student_ref[here, :] * student_scale - teacher_ref[here, :] * scale_ref[here, :] * teacher_scale
        gradient_ref[slot] = gradient.astype(jnp.bfloat16)
        if start == 0:
            copy.wait()
        weight_grad = lax.dot_general(
            turned_ref[...], gradient_ref[slot], (((1,), (1,)), ((), ())), preferred_element_type=jnp.float32
        )
        inverse = inverse_ref[:, here]
        unit = copy_ref[:, here].astype(jnp.float32) * inverse
        dot = jnp.sum(unit * weight_grad, axis=0, keepdims=True)
        grad_ref[slot] = (weight_grad - unit * dot) * inverse
        own = grad_ref[slot, own_rows, :].astype(jnp.bfloat16)
        sent_ref[:, :, here] = own.reshape(chips, rows_each, TILE)
        features = features + jnp.dot(
            unit.astype(jnp.bfloat16), gradient_ref[slot, :, own_lanes], preferred_element_type=jnp.float32
        )

    features = jnp.transpose(features).astype(jnp.bfloat16)
    per_chip = own_crops // chips
    for chip in range(chips):
        for piece in range(per_chip // rows_each):
            start = chip * per_chip + piece * rows_each
            at = count + piece * width
            sent_ref[chip, :, at : at + width] = features[start : start + rows_each, :]


def collect_kernel(core_ref, got_ref, keep_ref, give_ref):
    chips, rows_each, _ = got_ref.shape
    rows, width = keep_ref.shape
    total = got_ref[0].astype(jnp.float32)
    for chip in range(1, chips):
        total = total + got_ref[chip].astype(jnp.float32)
    pieces = rows // rows_each
    for piece in range(pieces):
        first = total[:, piece * width : (piece + 1) * width]
        second = total[:, (pieces + piece) * width : (pieces + piece + 1) * width]
        here = slice(piece * rows_each, (piece + 1) * rows_each)
        keep_ref[here, :] = jnp.where(core_ref[0] == 0, first, second)
        give_ref[here, :] = jnp.where(core_ref[0] == 0, second, first)


def feature_kernel(keep_ref, other_ref, student_ref, out_ref):
    total = keep_ref[...] + other_ref[...]
    hat, length = unit_rows(student_ref[...])
    out_ref[...] = (total - hat * jnp.sum(hat * total, axis=1, keepdims=True)) / length


def widen_kernel(got_ref, out_ref):
    chips, _, columns = got_ref.shape
    for chip in range(chips):
        out_ref[:, chip * columns : (chip + 1) * columns] = got_ref[chip].astype(jnp.float32)


def kernel_body(teacher_feat, student_feat, crop_weight, teacher_v, student_v):
    f32, bf16 = jnp.float32, jnp.bfloat16
    shape = jax.ShapeDtypeStruct
    blocks, fsdp = lax.axis_size("block"), lax.axis_size("fsdp")
    chips = blocks * GROUPS
    members, devices = blocks * fsdp, chips * fsdp
    rows, width = teacher_feat.shape
    crops = rows * devices
    lines = crops // LANES
    kept = teacher_v.shape[1]
    prototypes = kept * fsdp
    count = kept // blocks
    group, block = lax.axis_index("group")[None], lax.axis_index("block")[None]
    core = lax.axis_index("fsdp")[None]
    elements = count * crops
    smem, vmem = pl.BlockSpec(memory_space=pltpu.SMEM), pl.BlockSpec(memory_space=pltpu.VMEM)

    def swap(values):
        return lax.ppermute(values, "fsdp", [(0, 1), (1, 0)])

    def share(values):
        return lax.all_to_all(values, GROUP, 0, 0)

    dma = pltpu.SemaphoreType.DMA
    hbm = functools.partial(pltpu.with_memory_space_constraint, memory_space=pltpu.HBM)
    sent = call(
        units_kernel,
        shape((chips, rows, 2 * width), bf16),
        in_specs=[pl.BlockSpec(memory_space=pl.ANY)] * 2,
        scratch_shapes=[pltpu.VMEM((rows, width), bf16), pltpu.VMEM((rows, width), bf16), dma((2,))],
    )(hbm(teacher_feat), hbm(student_feat))
    own = lax.all_to_all(sent, CHIPS, 0, 0)

    device = ((group[0] * blocks + block[0]) * fsdp + core[0]) * rows
    weights = lax.dynamic_update_slice(jnp.zeros((crops,), f32), crop_weight.astype(f32), (device,)).reshape(lines, LANES)
    placed = weights
    for move in range(1, GROUPS):
        placed = placed + lax.ppermute(weights, "group", [(at, (at + move) % GROUPS) for at in range(GROUPS)])

    span = 2 * TILE
    spans = count // span
    column = pl.BlockSpec((width, span), lambda step, at: (0, at[0] * spans + step))
    turned = pl.BlockSpec((span, width), lambda step, at: (step, 0))
    line = pl.BlockSpec((1, span), lambda step, at: (0, step))
    teacher_w, student_w, inverse = call(
        directions_kernel,
        (
            shape((count, width), bf16),
            shape((count, width), bf16),
            shape((1, count), f32),
        ),
        flops=12 * count * width,
        moved=8 * count * width,
        grid_spec=pltpu.PrefetchScalarGridSpec(
            num_scalar_prefetch=1,
            grid=(spans,),
            in_specs=[column, column],
            out_specs=[turned, turned, line],
        ),
    )(
        block,
        hbm(teacher_v),
        hbm(student_v),
    )

    own, teacher_w = lax.optimization_barrier((own, teacher_w))
    other = swap(own)
    units = pltpu.VMEM((crops, width), bf16)
    mass, student_mass, sent, student_part, student_turned = call(
        functools.partial(masses_kernel, prototypes),
        (
            shape((count, crops), f32),
            shape((count, crops), f32),
            shape((members, 2 * lines, LANES), f32),
            shape((lines, LANES), f32),
            shape((width, crops), bf16),
        ),
        flops=4 * elements * width,
        exps=2 * elements,
        in_specs=[smem] + [vmem] * 5,
        scratch_shapes=[units, units],
    )(core, teacher_w, student_w, own, other, placed)
    first = share(sent)
    sent = call(
        functools.partial(sweep_kernel, prototypes, crops, False),
        shape((members, 2 * lines, LANES), f32),
        flops=4 * elements,
    )(mass, first, student_part)
    second = share(sent)
    sent, scale = call(
        functools.partial(sweep_kernel, prototypes, crops, True),
        (shape((members, lines, LANES), f32), shape((count, 1), f32)),
        flops=4 * elements,
    )(mass, second)
    third = share(sent)

    out_rows = width // chips
    per_chip = rows * fsdp * width // out_rows
    sent = call(
        gradient_kernel,
        shape((blocks, out_rows, count + per_chip), bf16),
        flops=4 * elements * width,
        in_specs=[smem] + [vmem] * 8 + [pl.BlockSpec(memory_space=pl.ANY)],
        scratch_shapes=[
            pltpu.VMEM((2, TILE, crops), bf16),
            pltpu.VMEM((2, width, TILE), f32),
            pltpu.VMEM((width, count), bf16),
            dma,
        ],
    )(
        jnp.concatenate([group, block]), mass, student_mass, scale, first, second, third, student_turned, inverse, hbm(student_v)
    )
    got = lax.all_to_all(sent, "block", 0, 0)
    keep, give = call(
        collect_kernel,
        [shape((rows, width), f32)] * 2,
        grid=(1,),
        in_specs=[smem, pl.BlockSpec((blocks, out_rows, per_chip), lambda step: (0, 0, count // per_chip))],
    )(core, got)
    grad_feat = call(feature_kernel, shape((rows, width), f32))(keep, swap(give), student_feat)
    grad_v = call(
        widen_kernel,
        shape((out_rows, kept), f32),
        grid=(1,),
        in_specs=[pl.BlockSpec((blocks, out_rows, count), lambda step: (0, 0, 0))],
        out_specs=pl.BlockSpec((out_rows, kept), lambda step: (0, 0)),
    )(got)
    return (grad_v, grad_feat)


def solution(mesh):
    dp, fsdp = mesh.shape["dp"], mesh.shape["fsdp"]
    blocks = dp // GROUPS

    def run(teacher_feat, student_feat, crop_weight, teacher_v, student_v):
        crops = teacher_feat.shape[0]
        count = teacher_v.shape[1] // (blocks * fsdp)
        fits = fsdp == 2 and dp == 16 and count % (2 * TILE) == 0 and crops == 1024
        if fits and 8 * count * crops <= KEPT_BYTES:
            grid = Mesh(mesh.devices.reshape(GROUPS, blocks, fsdp), (*CHIPS, "fsdp"))
            body, chips = kernel_body, CHIPS
        else:
            grid, body, chips = mesh, plain_body, ("dp",)
        every = P((*chips, "fsdp"))
        return jax.shard_map(
            body,
            mesh=grid,
            in_specs=(every, every, every, P(None, "fsdp"), P(None, "fsdp")),
            out_specs=(P(chips, "fsdp"), every),
            check_vma=False,
        )(teacher_feat, student_feat, crop_weight, teacher_v, student_v)

    return run
```

```python
import functools
import math

import jax
import jax.numpy as jnp
from jax import lax
from jax.experimental import pallas as pl
from jax.experimental.pallas import tpu as pltpu
from jax.sharding import Mesh
from jax.sharding import PartitionSpec as P

ITERS = 3

teacher_temp = 0.04
student_temp = 0.1
epsilon = 1e-06

GROUPS = 2
TILE = 256
FETCH = 2
LANES = 128
VMEM_BYTES = 12 << 20
KEPT_BYTES = 18 << 20

EVERY = ("dp", "fsdp")
CHIPS = ("group", "block")
GROUP = ("block", "fsdp")


def unit_rows(values):
    floats = values.astype(jnp.float32)
    length = jnp.sqrt(jnp.sum(floats * floats, axis=1, keepdims=True) + epsilon)
    return (floats / length, length)


def unit_columns(values):
    floats = values.astype(jnp.float32)
    length = jnp.sqrt(jnp.sum(floats * floats, axis=0, keepdims=True) + epsilon)
    return (floats / length, length)


COPY_BYTES = 1 << 22


def share(values, axes):
    count = lax.axis_size(axes)
    if count * values.size * values.dtype.itemsize > COPY_BYTES:
        return lax.all_gather(values, axes)
    return lax.all_to_all(jnp.broadcast_to(values, (count, *values.shape)), axes, 0, 0)


def add_up(values):
    if lax.axis_size(EVERY) * values.size * values.dtype.itemsize > COPY_BYTES:
        return lax.psum(values, EVERY)
    return jnp.sum(share(values, EVERY), axis=0)


def plain_body(teacher_feat, student_feat, crop_weight, teacher_v, student_v):
    fsdp = lax.axis_size("fsdp")
    devices = lax.axis_size("dp") * fsdp
    own_rows, width = teacher_feat.shape
    crops = own_rows * devices
    block = teacher_v.shape[1] // lax.axis_size("dp")
    prototypes = block * devices
    first = lax.axis_index("dp") * block

    teacher_hat, _ = unit_rows(teacher_feat)
    student_hat, student_len = unit_rows(student_feat)
    units = jnp.concatenate(
        [teacher_hat.astype(jnp.bfloat16), student_hat.astype(jnp.bfloat16)], axis=1
    )
    units = share(share(units, "dp"), "fsdp").reshape(crops, 2 * width)
    teacher_unit, student_unit = units[:, :width], units[:, width:]

    teacher_w, _ = unit_columns(lax.dynamic_slice_in_dim(teacher_v, first, block, 1))
    student_w, student_wlen = unit_columns(lax.dynamic_slice_in_dim(student_v, first, block, 1))
    student_wunit = student_w.astype(jnp.bfloat16)

    mass = jnp.exp(
        jnp.dot(teacher_unit, teacher_w.astype(jnp.bfloat16), preferred_element_type=jnp.float32)
        / teacher_temp
    )
    student_mass = jnp.exp(
        jnp.dot(student_unit, student_wunit, preferred_element_type=jnp.float32) / student_temp
    )
    student_part = jnp.sum(student_mass, axis=1)

    crop_scale = None
    for sweep in range(ITERS):
        scaled = mass if sweep == 0 else mass * crop_scale[:, None]
        proto_scale = 1.0 / (prototypes * jnp.sum(scaled, axis=0))
        crop_part = jnp.sum(mass * proto_scale[None, :], axis=1)
        if sweep == 0:
            placed = jnp.zeros((fsdp, crops // (fsdp * own_rows), own_rows), jnp.float32)
            own = crop_weight.astype(jnp.float32)[None, None]
            spot = (lax.axis_index("fsdp"), lax.axis_index("dp"), 0)
            placed = lax.dynamic_update_slice(placed, own, spot).reshape(crops)
            sums = add_up(jnp.stack([crop_part, student_part, placed]))
            crop_mass, student_total, weights = sums[0], sums[1], sums[2]
        else:
            crop_mass = add_up(crop_part)
        crop_scale = 1.0 / (crops * crop_mass)

    target = crops * (mass * crop_scale[:, None] * proto_scale[None, :])
    student_prob = student_mass / student_total[:, None]
    gradient = ((student_prob - target) * weights[:, None] / student_temp).astype(jnp.bfloat16)
    feature_part = lax.dot_general(
        gradient, student_wunit, (((1,), (1,)), ((), ())), preferred_element_type=jnp.float32
    )
    weight_grad = lax.dot_general(
        student_unit, gradient, (((0,), (0,)), ((), ())), preferred_element_type=jnp.float32
    )
    weight_dot = jnp.sum(student_w * weight_grad, axis=0, keepdims=True)
    grad_block = (weight_grad - student_w * weight_dot) / student_wlen

    feature_sent = feature_part.astype(jnp.bfloat16).reshape(fsdp, -1, own_rows, width)
    feature_sent = jnp.swapaxes(feature_sent, 0, 1).reshape(devices, own_rows, width)
    feature_all = lax.all_to_all(feature_sent, EVERY, 0, 0)
    feature_grad = jnp.sum(feature_all.astype(jnp.float32), axis=0)
    grad_feat = (
        feature_grad - student_hat * jnp.sum(student_hat * feature_grad, axis=1, keepdims=True)
    ) / student_len
    grad_v = lax.all_to_all(grad_block.astype(jnp.bfloat16), "dp", 0, 1, tiled=True)
    return (grad_v.astype(jnp.float32), grad_feat)


def call(kernel, out_shape, flops=0, moved=0, exps=0, **more):
    return pl.pallas_call(
        kernel,
        out_shape=out_shape,
        compiler_params=pltpu.CompilerParams(vmem_limit_bytes=VMEM_BYTES),
        cost_estimate=pl.CostEstimate(flops=flops, bytes_accessed=moved, transcendentals=exps),
        **more,
    )


def units_kernel(teacher_ref, student_ref, sent_ref, teacher_vmem, student_vmem, sems):
    copies = [
        pltpu.make_async_copy(teacher_ref, teacher_vmem, sems.at[0]),
        pltpu.make_async_copy(student_ref, student_vmem, sems.at[1]),
    ]
    for copy in copies:
        copy.start()
    for copy in copies:
        copy.wait()
    width = teacher_vmem.shape[1]
    teacher = unit_rows(teacher_vmem[...])[0].astype(jnp.bfloat16)
    student = unit_rows(student_vmem[...])[0].astype(jnp.bfloat16)
    for chip in range(sent_ref.shape[0]):
        sent_ref[chip, :, :width] = teacher
        sent_ref[chip, :, width:] = student


def directions_kernel(block_ref, teacher_ref, student_ref, teacher_out, student_out, inverse_out):
    teacher, _ = unit_columns(teacher_ref[...])
    teacher_out[...] = jnp.transpose(teacher).astype(jnp.bfloat16)
    student, length = unit_columns(student_ref[...])
    student_out[...] = jnp.transpose(student).astype(jnp.bfloat16)
    inverse_out[...] = 1.0 / length


def in_crop_order(core, own_ref, other_ref, teacher_ref, student_ref):
    chips, rows, _ = own_ref.shape
    width = teacher_ref.shape[1]
    for chip in range(chips):
        for got_ref, side in ((own_ref, core), (other_ref, 1 - core)):
            here = pl.ds(pl.multiple_of((2 * chip + side) * rows, rows), rows)
            teacher_ref[here, :] = got_ref[chip, :, :width]
            student_ref[here, :] = got_ref[chip, :, width:]


def exponentials(directions, units, temperature):
    logits = lax.dot_general(
        directions, units, (((1,), (1,)), ((), ())), preferred_element_type=jnp.float32
    )
    return jnp.exp2(logits * (math.log2(math.e) / temperature))


def fold(values):
    rows, lanes = values.shape
    return jnp.sum(values.reshape(rows // 8, 8, lanes), axis=0)


def as_rows(line):
    return jnp.concatenate([line[:, at : at + LANES] for at in range(0, line.shape[1], LANES)], axis=0)


def as_line(rows):
    return jnp.concatenate([rows[at : at + 1, :] for at in range(rows.shape[0])], axis=1)


def send(sent_ref, total, *more):
    values = jnp.concatenate([as_rows(jnp.sum(total, axis=0, keepdims=True)), *more], axis=0)
    for device in range(sent_ref.shape[0]):
        sent_ref[device] = values


def received(got_ref):
    total = got_ref[0]
    for device in range(1, got_ref.shape[0]):
        total = total + got_ref[device]
    return total


def masses_kernel(
    prototypes, place_ref, teacher_hbm, student_hbm, own_ref, other_ref, weight_ref,
    teacher_ref, student_ref, sent_ref, part_ref, turned_ref, teacher_units, student_units, teacher_w_ref, student_w_ref, sems,
):
    span = FETCH * TILE
    copies = []
    for piece in range(teacher_ref.shape[0] // span):
        rows = pl.ds(piece * span, span)
        copies.append((
            pltpu.make_async_copy(teacher_hbm.at[rows], teacher_w_ref.at[rows], sems.at[0, piece]),
            pltpu.make_async_copy(student_hbm.at[rows], student_w_ref.at[rows], sems.at[1, piece]),
        ))
        copies[-1][0].start()
        copies[-1][1].start()
    in_crop_order(place_ref[2], own_ref, other_ref, teacher_units, student_units)
    total = part = 0.0
    for start in range(0, teacher_ref.shape[0], TILE):
        here = slice(start, start + TILE)
        if start % span == 0:
            copies[start // span][0].wait()
            copies[start // span][1].wait()
        mass = exponentials(teacher_w_ref[here, :], teacher_units[...], teacher_temp)
        teacher_ref[here, :] = mass
        scale = 1.0 / (prototypes * jnp.sum(mass, axis=1, keepdims=True))
        total = total + fold(mass * scale)
        mass = exponentials(student_w_ref[here, :], student_units[...], student_temp)
        student_ref[here, :] = mass
        part = part + fold(mass)
    send(sent_ref, total, weight_ref[...])
    part_ref[...] = as_rows(jnp.sum(part, axis=0, keepdims=True))
    turned_ref[...] = jnp.transpose(student_units[...].astype(jnp.float32)).astype(jnp.bfloat16)


def sweep_kernel(prototypes, crops, last, mass_ref, got_ref, *refs):
    crop_scale = as_line(1.0 / (crops * received(got_ref)[: crops // LANES]))
    total = 0.0
    for start in range(0, mass_ref.shape[0], TILE):
        mass = mass_ref[start : start + TILE, :]
        scale = 1.0 / (prototypes * jnp.sum(mass * crop_scale, axis=1, keepdims=True))
        total = total + fold(mass * scale)
        if last:
            refs[1][start : start + TILE, :] = scale
    if last:
        send(refs[0], total)
    else:
        send(refs[1], total, refs[0][...])


def gradient_kernel(
    place_ref, teacher_ref, student_ref, scale_ref, first_ref, second_ref, third_ref, turned_ref, inverse_ref, directions_ref,
    sent_ref, gradient_ref, grad_ref, copy_ref, sems,
):
    group, block = place_ref[0], place_ref[1]
    chips, rows_each, _ = sent_ref.shape
    count, crops = student_ref.shape
    width = turned_ref.shape[0]
    span = FETCH * TILE
    copies = []
    for piece in range(count // span):
        columns = pl.ds(pl.multiple_of(block * count + piece * span, span), span)
        copies.append(pltpu.make_async_copy(directions_ref.at[:, columns], copy_ref.at[piece], sems.at[piece]))
        copies[-1].start()
    lines = crops // LANES
    own_crops = crops // GROUPS
    weights = received(first_ref)[lines:] / student_temp
    teacher_scale = as_line(weights / received(third_ref))
    student_scale = as_line(weights / received(second_ref)[lines:])
    own_rows = pl.ds(pl.multiple_of(group * (width // GROUPS), width // GROUPS), width // GROUPS)
    own_lanes = pl.ds(pl.multiple_of(group * own_crops, own_crops), own_crops)
    features = 0.0
    for start in range(0, count, TILE):
        here, slot = slice(start, start + TILE), (start // TILE) % 2
        gradient = student_ref[here, :] * student_scale - teacher_ref[here, :] * scale_ref[here, :] * teacher_scale
        gradient_ref[slot] = gradient.astype(jnp.bfloat16)
        if start % span == 0:
            copies[start // span].wait()
        weight_grad = lax.dot_general(
            turned_ref[...], gradient_ref[slot], (((1,), (1,)), ((), ())), preferred_element_type=jnp.float32
        )
        inverse = inverse_ref[:, here]
        piece = slice(start % span, start % span + TILE)
        unit = copy_ref[start // span, :, piece].astype(jnp.float32) * inverse
        dot = jnp.sum(unit * weight_grad, axis=0, keepdims=True)
        grad_ref[slot] = (weight_grad - unit * dot) * inverse
        own = grad_ref[slot, own_rows, :].astype(jnp.bfloat16)
        sent_ref[:, :, here] = own.reshape(chips, rows_each, TILE)
        features = features + jnp.dot(
            unit.astype(jnp.bfloat16), gradient_ref[slot, :, own_lanes], preferred_element_type=jnp.float32
        )

    features = jnp.transpose(features).astype(jnp.bfloat16)
    per_chip = own_crops // chips
    for chip in range(chips):
        for piece in range(per_chip // rows_each):
            start = chip * per_chip + piece * rows_each
            at = count + piece * width
            sent_ref[chip, :, at : at + width] = features[start : start + rows_each, :]


def collect_kernel(place_ref, got_ref, keep_ref, give_ref):
    chips, rows_each, _ = got_ref.shape
    rows, width = keep_ref.shape
    total = got_ref[0].astype(jnp.float32)
    for chip in range(1, chips):
        total = total + got_ref[chip].astype(jnp.float32)
    pieces = rows // rows_each
    for piece in range(pieces):
        first = total[:, piece * width : (piece + 1) * width]
        second = total[:, (pieces + piece) * width : (pieces + piece + 1) * width]
        here = slice(piece * rows_each, (piece + 1) * rows_each)
        keep_ref[here, :] = jnp.where(place_ref[2] == 0, first, second)
        give_ref[here, :] = jnp.where(place_ref[2] == 0, second, first)


def feature_kernel(keep_ref, other_ref, student_ref, out_ref):
    total = keep_ref[...] + other_ref[...]
    hat, length = unit_rows(student_ref[...])
    out_ref[...] = (total - hat * jnp.sum(hat * total, axis=1, keepdims=True)) / length


def widen_kernel(got_ref, out_ref):
    chips, _, columns = got_ref.shape
    for chip in range(chips):
        out_ref[:, chip * columns : (chip + 1) * columns] = got_ref[chip].astype(jnp.float32)


def kernel_body(teacher_feat, student_feat, crop_weight, teacher_v, student_v):
    f32, bf16 = jnp.float32, jnp.bfloat16
    shape = jax.ShapeDtypeStruct
    blocks, fsdp = lax.axis_size("block"), lax.axis_size("fsdp")
    chips = blocks * GROUPS
    members, devices = blocks * fsdp, chips * fsdp
    rows, width = teacher_feat.shape
    crops = rows * devices
    lines = crops // LANES
    kept = teacher_v.shape[1]
    prototypes = kept * fsdp
    count = kept // blocks
    group, block = lax.axis_index("group")[None], lax.axis_index("block")[None]
    core = lax.axis_index("fsdp")[None]
    place = jnp.concatenate([group, block, core])
    elements = count * crops
    smem, vmem = pl.BlockSpec(memory_space=pltpu.SMEM), pl.BlockSpec(memory_space=pltpu.VMEM)

    def swap(values):
        return lax.ppermute(values, "fsdp", [(0, 1), (1, 0)])

    def share(values):
        return lax.all_to_all(values, GROUP, 0, 0)

    dma = pltpu.SemaphoreType.DMA
    hbm = functools.partial(pltpu.with_memory_space_constraint, memory_space=pltpu.HBM)
    sent = call(
        units_kernel,
        shape((chips, rows, 2 * width), bf16),
        in_specs=[pl.BlockSpec(memory_space=pl.ANY)] * 2,
        scratch_shapes=[pltpu.VMEM((rows, width), bf16), pltpu.VMEM((rows, width), bf16), dma((2,))],
    )(hbm(teacher_feat), hbm(student_feat))
    own = lax.all_to_all(sent, CHIPS, 0, 0)

    device = ((group[0] * blocks + block[0]) * fsdp + core[0]) * rows
    weights = lax.dynamic_update_slice(jnp.zeros((crops,), f32), crop_weight.astype(f32), (device,)).reshape(lines, LANES)
    placed = weights
    for move in range(1, GROUPS):
        placed = placed + lax.ppermute(weights, "group", [(at, (at + move) % GROUPS) for at in range(GROUPS)])

    span = 2 * TILE
    spans = count // span
    column = pl.BlockSpec((width, span), lambda step, at: (0, at[0] * spans + step))
    turned = pl.BlockSpec((span, width), lambda step, at: (step, 0))
    line = pl.BlockSpec((1, span), lambda step, at: (0, step))
    teacher_w, student_w, inverse = call(
        directions_kernel,
        (
            pltpu.HBM((count, width), bf16),
            pltpu.HBM((count, width), bf16),
            shape((1, count), f32),
        ),
        flops=12 * count * width,
        moved=8 * count * width,
        grid_spec=pltpu.PrefetchScalarGridSpec(
            num_scalar_prefetch=1,
            grid=(spans,),
            in_specs=[column, column],
            out_specs=[turned, turned, line],
        ),
    )(
        block,
        hbm(teacher_v),
        hbm(student_v),
    )

    own, teacher_w, placed = lax.optimization_barrier((own, teacher_w, placed))
    other = swap(own)
    units = pltpu.VMEM((crops, width), bf16)
    mass, student_mass, sent, student_part, student_turned = call(
        functools.partial(masses_kernel, prototypes),
        (
            shape((count, crops), f32),
            shape((count, crops), f32),
            shape((members, 2 * lines, LANES), f32),
            shape((lines, LANES), f32),
            shape((width, crops), bf16),
        ),
        flops=4 * elements * width,
        exps=2 * elements,
        in_specs=[smem] + [pl.BlockSpec(memory_space=pl.ANY)] * 2 + [vmem] * 3,
        scratch_shapes=[units, units] + [pltpu.VMEM((count, width), bf16)] * 2 + [dma((2, count // (FETCH * TILE)))],
    )(place, hbm(teacher_w), hbm(student_w), own, other, placed)
    first = share(sent)
    sent = call(
        functools.partial(sweep_kernel, prototypes, crops, False),
        shape((members, 2 * lines, LANES), f32),
        flops=4 * elements,
    )(mass, first, student_part)
    second = share(sent)
    sent, scale = call(
        functools.partial(sweep_kernel, prototypes, crops, True),
        (shape((members, lines, LANES), f32), shape((count, 1), f32)),
        flops=4 * elements,
    )(mass, second)
    third = share(sent)

    out_rows = width // chips
    per_chip = rows * fsdp * width // out_rows
    sent = call(
        gradient_kernel,
        shape((blocks, out_rows, count + per_chip), bf16),
        flops=4 * elements * width,
        in_specs=[smem] + [vmem] * 8 + [pl.BlockSpec(memory_space=pl.ANY)],
        scratch_shapes=[
            pltpu.VMEM((2, TILE, crops), bf16),
            pltpu.VMEM((2, width, TILE), f32),
            pltpu.VMEM((count // (FETCH * TILE), width, FETCH * TILE), bf16),
            dma((count // (FETCH * TILE),)),
        ],
    )(
        place, mass, student_mass, scale, first, second, third, student_turned, inverse, hbm(student_v)
    )
    got = lax.all_to_all(sent, "block", 0, 0)
    keep, give = call(
        collect_kernel,
        [shape((rows, width), f32)] * 2,
        grid=(1,),
        in_specs=[smem, pl.BlockSpec((blocks, out_rows, per_chip), lambda step: (0, 0, count // per_chip))],
    )(place, got)
    grad_feat = call(feature_kernel, shape((rows, width), f32))(keep, swap(give), student_feat)
    grad_v = call(
        widen_kernel,
        shape((out_rows, kept), f32),
        grid=(1,),
        in_specs=[pl.BlockSpec((blocks, out_rows, count), lambda step: (0, 0, 0))],
        out_specs=pl.BlockSpec((out_rows, kept), lambda step: (0, 0)),
    )(got)
    return (grad_v, grad_feat)


def solution(mesh):
    dp, fsdp = mesh.shape["dp"], mesh.shape["fsdp"]
    blocks = dp // GROUPS

    def run(teacher_feat, student_feat, crop_weight, teacher_v, student_v):
        crops = teacher_feat.shape[0]
        count = teacher_v.shape[1] // (blocks * fsdp)
        fits = fsdp == 2 and dp == 16 and count % (2 * TILE) == 0 and crops == 1024
        if fits and 8 * count * crops <= KEPT_BYTES:
            grid = Mesh(mesh.devices.reshape(GROUPS, blocks, fsdp), (*CHIPS, "fsdp"))
            body, chips = kernel_body, CHIPS
        else:
            grid, body, chips = mesh, plain_body, ("dp",)
        every = P((*chips, "fsdp"))
        return jax.shard_map(
            body,
            mesh=grid,
            in_specs=(every, every, every, P(None, "fsdp"), P(None, "fsdp")),
            out_specs=(P(chips, "fsdp"), every),
            check_vma=False,
        )(teacher_feat, student_feat, crop_weight, teacher_v, student_v)

    return run
```

```python
import functools
import math

import jax
import jax.numpy as jnp
from jax import lax
from jax.experimental import pallas as pl
from jax.experimental.pallas import tpu as pltpu
from jax.sharding import Mesh
from jax.sharding import PartitionSpec as P

ITERS = 3

teacher_temp = 0.04
student_temp = 0.1
epsilon = 1e-06

GROUPS = 2
TILE = 256
FETCH = 2
LANES = 128
VMEM_BYTES = 12 << 20
KEPT_BYTES = 18 << 20

EVERY = ("dp", "fsdp")
CHIPS = ("group", "block")
GROUP = ("block", "fsdp")


def unit_rows(values):
    floats = values.astype(jnp.float32)
    length = jnp.sqrt(jnp.sum(floats * floats, axis=1, keepdims=True) + epsilon)
    return (floats / length, length)


def unit_columns(values):
    floats = values.astype(jnp.float32)
    length = jnp.sqrt(jnp.sum(floats * floats, axis=0, keepdims=True) + epsilon)
    return (floats / length, length)


COPY_BYTES = 1 << 22


def share(values, axes):
    count = lax.axis_size(axes)
    if count * values.size * values.dtype.itemsize > COPY_BYTES:
        return lax.all_gather(values, axes)
    return lax.all_to_all(jnp.broadcast_to(values, (count, *values.shape)), axes, 0, 0)


def add_up(values):
    if lax.axis_size(EVERY) * values.size * values.dtype.itemsize > COPY_BYTES:
        return lax.psum(values, EVERY)
    return jnp.sum(share(values, EVERY), axis=0)


def plain_body(teacher_feat, student_feat, crop_weight, teacher_v, student_v):
    fsdp = lax.axis_size("fsdp")
    devices = lax.axis_size("dp") * fsdp
    own_rows, width = teacher_feat.shape
    crops = own_rows * devices
    block = teacher_v.shape[1] // lax.axis_size("dp")
    prototypes = block * devices
    first = lax.axis_index("dp") * block

    teacher_hat, _ = unit_rows(teacher_feat)
    student_hat, student_len = unit_rows(student_feat)
    units = jnp.concatenate(
        [teacher_hat.astype(jnp.bfloat16), student_hat.astype(jnp.bfloat16)], axis=1
    )
    units = share(share(units, "dp"), "fsdp").reshape(crops, 2 * width)
    teacher_unit, student_unit = units[:, :width], units[:, width:]

    teacher_w, _ = unit_columns(lax.dynamic_slice_in_dim(teacher_v, first, block, 1))
    student_w, student_wlen = unit_columns(lax.dynamic_slice_in_dim(student_v, first, block, 1))
    student_wunit = student_w.astype(jnp.bfloat16)

    mass = jnp.exp(
        jnp.dot(teacher_unit, teacher_w.astype(jnp.bfloat16), preferred_element_type=jnp.float32)
        / teacher_temp
    )
    student_mass = jnp.exp(
        jnp.dot(student_unit, student_wunit, preferred_element_type=jnp.float32) / student_temp
    )
    student_part = jnp.sum(student_mass, axis=1)

    crop_scale = None
    for sweep in range(ITERS):
        scaled = mass if sweep == 0 else mass * crop_scale[:, None]
        proto_scale = 1.0 / (prototypes * jnp.sum(scaled, axis=0))
        crop_part = jnp.sum(mass * proto_scale[None, :], axis=1)
        if sweep == 0:
            placed = jnp.zeros((fsdp, crops // (fsdp * own_rows), own_rows), jnp.float32)
            own = crop_weight.astype(jnp.float32)[None, None]
            spot = (lax.axis_index("fsdp"), lax.axis_index("dp"), 0)
            placed = lax.dynamic_update_slice(placed, own, spot).reshape(crops)
            sums = add_up(jnp.stack([crop_part, student_part, placed]))
            crop_mass, student_total, weights = sums[0], sums[1], sums[2]
        else:
            crop_mass = add_up(crop_part)
        crop_scale = 1.0 / (crops * crop_mass)

    target = crops * (mass * crop_scale[:, None] * proto_scale[None, :])
    student_prob = student_mass / student_total[:, None]
    gradient = ((student_prob - target) * weights[:, None] / student_temp).astype(jnp.bfloat16)
    feature_part = lax.dot_general(
        gradient, student_wunit, (((1,), (1,)), ((), ())), preferred_element_type=jnp.float32
    )
    weight_grad = lax.dot_general(
        student_unit, gradient, (((0,), (0,)), ((), ())), preferred_element_type=jnp.float32
    )
    weight_dot = jnp.sum(student_w * weight_grad, axis=0, keepdims=True)
    grad_block = (weight_grad - student_w * weight_dot) / student_wlen

    feature_sent = feature_part.astype(jnp.bfloat16).reshape(fsdp, -1, own_rows, width)
    feature_sent = jnp.swapaxes(feature_sent, 0, 1).reshape(devices, own_rows, width)
    feature_all = lax.all_to_all(feature_sent, EVERY, 0, 0)
    feature_grad = jnp.sum(feature_all.astype(jnp.float32), axis=0)
    grad_feat = (
        feature_grad - student_hat * jnp.sum(student_hat * feature_grad, axis=1, keepdims=True)
    ) / student_len
    grad_v = lax.all_to_all(grad_block.astype(jnp.bfloat16), "dp", 0, 1, tiled=True)
    return (grad_v.astype(jnp.float32), grad_feat)


def call(kernel, out_shape, flops=0, moved=0, exps=0, **more):
    return pl.pallas_call(
        kernel,
        out_shape=out_shape,
        compiler_params=pltpu.CompilerParams(vmem_limit_bytes=VMEM_BYTES),
        cost_estimate=pl.CostEstimate(flops=flops, bytes_accessed=moved, transcendentals=exps),
        **more,
    )


def units_kernel(teacher_ref, student_ref, sent_ref, teacher_vmem, student_vmem, sems):
    copies = [
        pltpu.make_async_copy(teacher_ref, teacher_vmem, sems.at[0]),
        pltpu.make_async_copy(student_ref, student_vmem, sems.at[1]),
    ]
    for copy in copies:
        copy.start()
    for copy in copies:
        copy.wait()
    width = teacher_vmem.shape[1]
    teacher = unit_rows(teacher_vmem[...])[0].astype(jnp.bfloat16)
    student = unit_rows(student_vmem[...])[0].astype(jnp.bfloat16)
    for chip in range(sent_ref.shape[0]):
        sent_ref[chip, :, :width] = teacher
        sent_ref[chip, :, width:] = student


def directions_kernel(block_ref, teacher_ref, student_ref, teacher_out, student_out, inverse_out):
    teacher, _ = unit_columns(teacher_ref[...])
    teacher_out[...] = jnp.transpose(teacher).astype(jnp.bfloat16)
    student, length = unit_columns(student_ref[...])
    student_out[...] = jnp.transpose(student).astype(jnp.bfloat16)
    inverse_out[...] = 1.0 / length


def exponentials(directions, units, temperature):
    logits = lax.dot_general(
        directions, units, (((1,), (1,)), ((), ())), preferred_element_type=jnp.float32
    )
    return jnp.exp2(logits * (math.log2(math.e) / temperature))


def fold(values):
    rows, lanes = values.shape
    return jnp.sum(values.reshape(rows // 8, 8, lanes), axis=0)


def as_rows(line):
    return jnp.concatenate([line[:, at : at + LANES] for at in range(0, line.shape[1], LANES)], axis=0)


def as_line(rows):
    return jnp.concatenate([rows[at : at + 1, :] for at in range(rows.shape[0])], axis=1)


def by_core(core, own, other):
    return jnp.concatenate([jnp.where(core == 0, own, other), jnp.where(core == 0, other, own)], axis=0)


def halves(core, rows):
    half = rows.shape[0] // 2
    first, second = rows[:half], rows[half:]
    return as_line(jnp.where(core == 0, first, second)), as_line(jnp.where(core == 0, second, first))


def send(sent_ref, core, own, other, *more):
    own, other = (as_rows(jnp.sum(total, axis=0, keepdims=True)) for total in (own, other))
    values = jnp.concatenate([by_core(core, own, other), *more], axis=0)
    for device in range(sent_ref.shape[0]):
        sent_ref[device] = values


def received(got_ref):
    total = got_ref[0]
    for device in range(1, got_ref.shape[0]):
        total = total + got_ref[device]
    return total


def units_of(got_ref, width, side):
    chips, rows, _ = got_ref.shape
    return got_ref[:, :, side * width : (side + 1) * width].reshape(chips * rows, width)


def turn(units):
    return jnp.transpose(units.astype(jnp.float32)).astype(jnp.bfloat16)


def own_kernel(
    teacher_hbm, student_hbm, got_ref, teacher_ref, student_ref, teacher_w_ref, student_w_ref, part_ref, turned_ref, sems
):
    count, width = teacher_w_ref.shape
    span = FETCH * TILE
    copies = []
    for piece in range(count // span):
        rows = pl.ds(piece * span, span)
        copies.append((
            pltpu.make_async_copy(teacher_hbm.at[rows], teacher_w_ref.at[rows], sems.at[0, piece]),
            pltpu.make_async_copy(student_hbm.at[rows], student_w_ref.at[rows], sems.at[1, piece]),
        ))
        copies[-1][0].start()
        copies[-1][1].start()
    teacher, student = units_of(got_ref, width, 0), units_of(got_ref, width, 1)
    turned_ref[...] = turn(student)
    part = 0.0
    for start in range(0, count, TILE):
        here = slice(start, start + TILE)
        if start % span == 0:
            copies[start // span][0].wait()
            copies[start // span][1].wait()
        teacher_ref[here, :] = exponentials(teacher_w_ref[here, :], teacher, teacher_temp)
        mass = exponentials(student_w_ref[here, :], student, student_temp)
        student_ref[here, :] = mass
        part = part + fold(mass)
    part_ref[...] = part


def other_kernel(
    prototypes, place_ref, teacher_w_ref, student_w_ref, got_ref, own_ref, own_part_ref, weight_ref,
    teacher_ref, student_ref, sent_ref, part_ref, turned_ref,
):
    count, width = teacher_w_ref.shape
    core = place_ref[2]
    teacher, student = units_of(got_ref, width, 0), units_of(got_ref, width, 1)
    turned_ref[...] = turn(student)
    own_total = total = part = 0.0
    for start in range(0, count, TILE):
        here = slice(start, start + TILE)
        mass = exponentials(teacher_w_ref[here, :], teacher, teacher_temp)
        teacher_ref[here, :] = mass
        own = own_ref[here, :]
        proto = jnp.sum(own, axis=1, keepdims=True) + jnp.sum(mass, axis=1, keepdims=True)
        scale = 1.0 / (prototypes * proto)
        own_total = own_total + fold(own * scale)
        total = total + fold(mass * scale)
        mass = exponentials(student_w_ref[here, :], student, student_temp)
        student_ref[here, :] = mass
        part = part + fold(mass)
    send(sent_ref, core, own_total, total, weight_ref[...])
    own_part = as_rows(jnp.sum(own_part_ref[...], axis=0, keepdims=True))
    part_ref[...] = by_core(core, own_part, as_rows(jnp.sum(part, axis=0, keepdims=True)))


def sweep(prototypes, crops, place_ref, own_ref, other_ref, got_ref):
    own_crop, other_crop = halves(place_ref[2], 1.0 / (crops * received(got_ref)[: crops // LANES]))
    own_total = other_total = 0.0
    scales = []
    for start in range(0, own_ref.shape[0], TILE):
        own, other = own_ref[start : start + TILE, :], other_ref[start : start + TILE, :]
        proto = jnp.sum(own * own_crop, axis=1, keepdims=True) + jnp.sum(other * other_crop, axis=1, keepdims=True)
        scales.append(1.0 / (prototypes * proto))
        own_total = own_total + fold(own * scales[-1])
        other_total = other_total + fold(other * scales[-1])
    return own_total, other_total, scales


def sweep_kernel(prototypes, crops, place_ref, own_ref, other_ref, got_ref, part_ref, sent_ref):
    own, other, _ = sweep(prototypes, crops, place_ref, own_ref, other_ref, got_ref)
    send(sent_ref, place_ref[2], own, other, part_ref[...])


def last_sweep_kernel(
    prototypes, crops, place_ref, own_ref, other_ref, got_ref, directions_ref, sent_ref, scale_ref, copy_ref, sems
):
    pieces, _, span = copy_ref.shape
    copies = []
    for piece in range(pieces):
        columns = pl.ds(pl.multiple_of((place_ref[1] * pieces + piece) * span, span), span)
        copies.append(pltpu.make_async_copy(directions_ref.at[:, columns], copy_ref.at[piece], sems.at[piece]))
        copies[-1].start()
    own, other, scales = sweep(prototypes, crops, place_ref, own_ref, other_ref, got_ref)
    for index, scale in enumerate(scales):
        scale_ref[index * TILE : (index + 1) * TILE, :] = scale
    send(sent_ref, place_ref[2], own, other)
    for copy in copies:
        copy.wait()


def gradient_kernel(
    place_ref, own_mass_ref, other_mass_ref, own_student_ref, other_student_ref, scale_ref, first_ref, second_ref, third_ref,
    own_turned_ref, other_turned_ref, inverse_ref, copy_ref, sent_ref, gradient_ref, grad_ref, unit_ref,
):
    group, core = place_ref[0], place_ref[2]
    chips, rows_each, _ = sent_ref.shape
    count, half = own_mass_ref.shape
    width = own_turned_ref.shape[0]
    span = copy_ref.shape[2]
    lines = 2 * half // LANES
    weights = received(first_ref)[lines:] / student_temp
    teacher_scales = halves(core, weights / received(third_ref))
    student_scales = halves(core, weights / received(second_ref)[lines:])
    masses, students = (own_mass_ref, other_mass_ref), (own_student_ref, other_student_ref)
    own_rows = pl.ds(pl.multiple_of(group * (width // GROUPS), width // GROUPS), width // GROUPS)
    kept = half // GROUPS
    for start in range(0, count, TILE):
        here, slot = slice(start, start + TILE), start // TILE
        piece = slice(start % span, start % span + TILE)
        inverse = inverse_ref[:, here]
        unit = copy_ref[start // span, :, piece].astype(jnp.float32) * inverse
        for side in range(2):
            teacher = masses[side][here, :] * scale_ref[here, :] * teacher_scales[side]
            gradient = students[side][here, :] * student_scales[side] - teacher
            gradient_ref[slot, side] = gradient.astype(jnp.bfloat16)
        weight_grad = 0.0
        for side, turned_ref in enumerate((own_turned_ref, other_turned_ref)):
            weight_grad = weight_grad + lax.dot_general(
                turned_ref[...], gradient_ref[slot, side], (((1,), (1,)), ((), ())), preferred_element_type=jnp.float32
            )
        dot = jnp.sum(unit * weight_grad, axis=0, keepdims=True)
        grad_ref[slot] = (weight_grad - unit * dot) * inverse
        own = grad_ref[slot, own_rows, :].astype(jnp.bfloat16)
        sent_ref[:, :, here] = own.reshape(chips, rows_each, TILE)
        unit_ref[:, here] = unit.astype(jnp.bfloat16)

    per_core = kept // chips
    pieces = per_core // rows_each
    for side in range(2):
        lanes = pl.ds(pl.multiple_of(group * kept, kept), kept)
        gradient = gradient_ref[:, side, :, lanes].reshape(count, kept)
        feature = jnp.dot(unit_ref[...], gradient, preferred_element_type=jnp.float32)
        feature = jnp.transpose(feature).astype(jnp.bfloat16)
        for chip in range(chips):
            for piece in range(pieces):
                start = chip * per_core + piece * rows_each
                at = count + (side * pieces + piece) * width
                sent_ref[chip, :, at : at + width] = feature[start : start + rows_each, :]


def collect_kernel(got_ref, keep_ref, give_ref):
    rows_each = got_ref.shape[1]
    rows, width = keep_ref.shape
    total = got_ref[0].astype(jnp.float32)
    for chip in range(1, got_ref.shape[0]):
        total = total + got_ref[chip].astype(jnp.float32)
    pieces = rows // rows_each
    for piece in range(2 * pieces):
        out_ref, at = (keep_ref, piece) if piece < pieces else (give_ref, piece - pieces)
        out_ref[at * rows_each : (at + 1) * rows_each, :] = total[:, piece * width : (piece + 1) * width]


def feature_kernel(keep_ref, other_ref, student_ref, out_ref):
    total = keep_ref[...] + other_ref[...]
    hat, length = unit_rows(student_ref[...])
    out_ref[...] = (total - hat * jnp.sum(hat * total, axis=1, keepdims=True)) / length


def widen_kernel(got_ref, out_ref):
    chips, _, columns = got_ref.shape
    for chip in range(chips):
        out_ref[:, chip * columns : (chip + 1) * columns] = got_ref[chip].astype(jnp.float32)


def kernel_body(teacher_feat, student_feat, crop_weight, teacher_v, student_v):
    f32, bf16 = jnp.float32, jnp.bfloat16
    shape = jax.ShapeDtypeStruct
    blocks, fsdp = lax.axis_size("block"), lax.axis_size("fsdp")
    chips = blocks * GROUPS
    members, devices = blocks * fsdp, chips * fsdp
    rows, width = teacher_feat.shape
    crops = rows * devices
    lines = crops // LANES
    kept = teacher_v.shape[1]
    prototypes = kept * fsdp
    count = kept // blocks
    group, block = lax.axis_index("group")[None], lax.axis_index("block")[None]
    core = lax.axis_index("fsdp")[None]
    place = jnp.concatenate([group, block, core])
    elements = count * crops
    smem, vmem = pl.BlockSpec(memory_space=pltpu.SMEM), pl.BlockSpec(memory_space=pltpu.VMEM)

    def swap(values):
        return lax.ppermute(values, "fsdp", [(0, 1), (1, 0)])

    def share(values):
        return lax.all_to_all(values, GROUP, 0, 0)

    dma = pltpu.SemaphoreType.DMA
    hbm = functools.partial(pltpu.with_memory_space_constraint, memory_space=pltpu.HBM)
    sent = call(
        units_kernel,
        shape((chips, rows, 2 * width), bf16),
        in_specs=[pl.BlockSpec(memory_space=pl.ANY)] * 2,
        scratch_shapes=[pltpu.VMEM((rows, width), bf16), pltpu.VMEM((rows, width), bf16), dma((2,))],
    )(hbm(teacher_feat), hbm(student_feat))
    own = lax.all_to_all(sent, CHIPS, 0, 0)

    device = (core[0] * chips + group[0] * blocks + block[0]) * rows
    weights = lax.dynamic_update_slice(jnp.zeros((crops,), f32), crop_weight.astype(f32), (device,)).reshape(lines, LANES)
    placed = weights
    for move in range(1, GROUPS):
        placed = placed + lax.ppermute(weights, "group", [(at, (at + move) % GROUPS) for at in range(GROUPS)])

    span = 2 * TILE
    spans = count // span
    column = pl.BlockSpec((width, span), lambda step, at: (0, at[0] * spans + step))
    turned = pl.BlockSpec((span, width), lambda step, at: (step, 0))
    line = pl.BlockSpec((1, span), lambda step, at: (0, step))
    teacher_w, student_w, inverse = call(
        directions_kernel,
        (
            pltpu.HBM((count, width), bf16),
            pltpu.HBM((count, width), bf16),
            shape((1, count), f32),
        ),
        flops=12 * count * width,
        moved=8 * count * width,
        grid_spec=pltpu.PrefetchScalarGridSpec(
            num_scalar_prefetch=1,
            grid=(spans,),
            in_specs=[column, column],
            out_specs=[turned, turned, line],
        ),
    )(
        block,
        hbm(teacher_v),
        hbm(student_v),
    )

    own, teacher_w, placed = lax.optimization_barrier((own, teacher_w, placed))
    other = swap(own)
    half = crops // 2
    anyspace = pl.BlockSpec(memory_space=pl.ANY)
    pieces = count // (FETCH * TILE)
    halved = dict(flops=2 * elements * width, exps=elements)
    own_mass, own_student, teacher_w, student_w, own_part, own_turned = call(
        own_kernel,
        (
            shape((count, half), f32),
            shape((count, half), f32),
            shape((count, width), bf16),
            shape((count, width), bf16),
            shape((8, half), f32),
            shape((width, half), bf16),
        ),
        in_specs=[anyspace] * 2 + [vmem],
        scratch_shapes=[dma((2, pieces))],
        **halved,
    )(hbm(teacher_w), hbm(student_w), own)
    other_mass, other_student, sent, student_part, other_turned = call(
        functools.partial(other_kernel, prototypes),
        (
            shape((count, half), f32),
            shape((count, half), f32),
            shape((members, 2 * lines, LANES), f32),
            shape((lines, LANES), f32),
            shape((width, half), bf16),
        ),
        in_specs=[smem] + [vmem] * 6,
        **halved,
    )(place, teacher_w, student_w, other, own_mass, own_part, placed)
    first = share(sent)
    sent = call(
        functools.partial(sweep_kernel, prototypes, crops),
        shape((members, 2 * lines, LANES), f32),
        flops=4 * elements,
        in_specs=[smem] + [vmem] * 4,
    )(place, own_mass, other_mass, first, student_part)
    second = share(sent)
    sent, scale, student_copy = call(
        functools.partial(last_sweep_kernel, prototypes, crops),
        (
            shape((members, lines, LANES), f32),
            shape((count, 1), f32),
            shape((pieces, width, count // pieces), bf16),
        ),
        flops=4 * elements,
        in_specs=[smem] + [vmem] * 3 + [anyspace],
        scratch_shapes=[dma((pieces,))],
    )(place, own_mass, other_mass, second, hbm(student_v))
    third = share(sent)

    out_rows = width // chips
    per_chip = rows * fsdp * width // out_rows
    sent = call(
        gradient_kernel,
        shape((blocks, out_rows, count + per_chip), bf16),
        flops=4 * elements * width,
        in_specs=[smem] + [vmem] * 12,
        scratch_shapes=[
            pltpu.VMEM((count // TILE, 2, TILE, half), bf16),
            pltpu.VMEM((count // TILE, width, TILE), f32),
            pltpu.VMEM((width, count), bf16),
        ],
    )(
        place, own_mass, other_mass, own_student, other_student, scale, first, second, third,
        own_turned, other_turned, inverse, student_copy,
    )
    got = lax.all_to_all(sent, "block", 0, 0)
    keep, give = call(
        collect_kernel,
        [shape((rows, width), f32)] * 2,
        grid=(1,),
        in_specs=[pl.BlockSpec((blocks, out_rows, per_chip), lambda step: (0, 0, count // per_chip))],
    )(got)
    grad_feat = call(feature_kernel, shape((rows, width), f32))(keep, swap(give), student_feat)
    grad_v = call(
        widen_kernel,
        shape((out_rows, kept), f32),
        grid=(1,),
        in_specs=[pl.BlockSpec((blocks, out_rows, count), lambda step: (0, 0, 0))],
        out_specs=pl.BlockSpec((out_rows, kept), lambda step: (0, 0)),
    )(got)
    return (grad_v, grad_feat)


def solution(mesh):
    dp, fsdp = mesh.shape["dp"], mesh.shape["fsdp"]
    blocks = dp // GROUPS

    def run(teacher_feat, student_feat, crop_weight, teacher_v, student_v):
        crops = teacher_feat.shape[0]
        count = teacher_v.shape[1] // (blocks * fsdp)
        fits = fsdp == 2 and dp == 16 and count % (2 * TILE) == 0 and crops == 1024
        if fits and 8 * count * crops <= KEPT_BYTES:
            grid = Mesh(mesh.devices.reshape(GROUPS, blocks, fsdp), (*CHIPS, "fsdp"))
            body, chips = kernel_body, CHIPS
        else:
            grid, body, chips = mesh, plain_body, ("dp",)
        every = P((*chips, "fsdp"))
        return jax.shard_map(
            body,
            mesh=grid,
            in_specs=(every, every, every, P(None, "fsdp"), P(None, "fsdp")),
            out_specs=(P(chips, "fsdp"), every),
            check_vma=False,
        )(teacher_feat, student_feat, crop_weight, teacher_v, student_v)

    return run
```

```python
import functools
import math

import jax
import jax.numpy as jnp
from jax import lax
from jax.experimental import pallas as pl
from jax.experimental.pallas import tpu as pltpu
from jax.sharding import Mesh
from jax.sharding import PartitionSpec as P

ITERS = 3

teacher_temp = 0.04
student_temp = 0.1
epsilon = 1e-06

GROUPS = 2
TILE = 256
HALF_TILE = 512
FETCH = 2
LANES = 128
VMEM_BYTES = 12 << 20
KEPT_BYTES = 18 << 20

EVERY = ("dp", "fsdp")
CHIPS = ("group", "block")
GROUP = ("block", "fsdp")


def unit_rows(values):
    floats = values.astype(jnp.float32)
    length = jnp.sqrt(jnp.sum(floats * floats, axis=1, keepdims=True) + epsilon)
    return (floats / length, length)


def unit_columns(values):
    floats = values.astype(jnp.float32)
    length = jnp.sqrt(jnp.sum(floats * floats, axis=0, keepdims=True) + epsilon)
    return (floats / length, length)


COPY_BYTES = 1 << 22


def share(values, axes):
    count = lax.axis_size(axes)
    if count * values.size * values.dtype.itemsize > COPY_BYTES:
        return lax.all_gather(values, axes)
    return lax.all_to_all(jnp.broadcast_to(values, (count, *values.shape)), axes, 0, 0)


def add_up(values):
    if lax.axis_size(EVERY) * values.size * values.dtype.itemsize > COPY_BYTES:
        return lax.psum(values, EVERY)
    return jnp.sum(share(values, EVERY), axis=0)


def plain_body(teacher_feat, student_feat, crop_weight, teacher_v, student_v):
    fsdp = lax.axis_size("fsdp")
    devices = lax.axis_size("dp") * fsdp
    own_rows, width = teacher_feat.shape
    crops = own_rows * devices
    block = teacher_v.shape[1] // lax.axis_size("dp")
    prototypes = block * devices
    first = lax.axis_index("dp") * block

    teacher_hat, _ = unit_rows(teacher_feat)
    student_hat, student_len = unit_rows(student_feat)
    units = jnp.concatenate(
        [teacher_hat.astype(jnp.bfloat16), student_hat.astype(jnp.bfloat16)], axis=1
    )
    units = share(share(units, "dp"), "fsdp").reshape(crops, 2 * width)
    teacher_unit, student_unit = units[:, :width], units[:, width:]

    teacher_w, _ = unit_columns(lax.dynamic_slice_in_dim(teacher_v, first, block, 1))
    student_w, student_wlen = unit_columns(lax.dynamic_slice_in_dim(student_v, first, block, 1))
    student_wunit = student_w.astype(jnp.bfloat16)

    mass = jnp.exp(
        jnp.dot(teacher_unit, teacher_w.astype(jnp.bfloat16), preferred_element_type=jnp.float32)
        / teacher_temp
    )
    student_mass = jnp.exp(
        jnp.dot(student_unit, student_wunit, preferred_element_type=jnp.float32) / student_temp
    )
    student_part = jnp.sum(student_mass, axis=1)

    crop_scale = None
    for sweep in range(ITERS):
        scaled = mass if sweep == 0 else mass * crop_scale[:, None]
        proto_scale = 1.0 / (prototypes * jnp.sum(scaled, axis=0))
        crop_part = jnp.sum(mass * proto_scale[None, :], axis=1)
        if sweep == 0:
            placed = jnp.zeros((fsdp, crops // (fsdp * own_rows), own_rows), jnp.float32)
            own = crop_weight.astype(jnp.float32)[None, None]
            spot = (lax.axis_index("fsdp"), lax.axis_index("dp"), 0)
            placed = lax.dynamic_update_slice(placed, own, spot).reshape(crops)
            sums = add_up(jnp.stack([crop_part, student_part, placed]))
            crop_mass, student_total, weights = sums[0], sums[1], sums[2]
        else:
            crop_mass = add_up(crop_part)
        crop_scale = 1.0 / (crops * crop_mass)

    target = crops * (mass * crop_scale[:, None] * proto_scale[None, :])
    student_prob = student_mass / student_total[:, None]
    gradient = ((student_prob - target) * weights[:, None] / student_temp).astype(jnp.bfloat16)
    feature_part = lax.dot_general(
        gradient, student_wunit, (((1,), (1,)), ((), ())), preferred_element_type=jnp.float32
    )
    weight_grad = lax.dot_general(
        student_unit, gradient, (((0,), (0,)), ((), ())), preferred_element_type=jnp.float32
    )
    weight_dot = jnp.sum(student_w * weight_grad, axis=0, keepdims=True)
    grad_block = (weight_grad - student_w * weight_dot) / student_wlen

    feature_sent = feature_part.astype(jnp.bfloat16).reshape(fsdp, -1, own_rows, width)
    feature_sent = jnp.swapaxes(feature_sent, 0, 1).reshape(devices, own_rows, width)
    feature_all = lax.all_to_all(feature_sent, EVERY, 0, 0)
    feature_grad = jnp.sum(feature_all.astype(jnp.float32), axis=0)
    grad_feat = (
        feature_grad - student_hat * jnp.sum(student_hat * feature_grad, axis=1, keepdims=True)
    ) / student_len
    grad_v = lax.all_to_all(grad_block.astype(jnp.bfloat16), "dp", 0, 1, tiled=True)
    return (grad_v.astype(jnp.float32), grad_feat)


def call(kernel, out_shape, flops=0, moved=0, exps=0, **more):
    return pl.pallas_call(
        kernel,
        out_shape=out_shape,
        compiler_params=pltpu.CompilerParams(vmem_limit_bytes=VMEM_BYTES),
        cost_estimate=pl.CostEstimate(flops=flops, bytes_accessed=moved, transcendentals=exps),
        **more,
    )


def units_kernel(teacher_ref, student_ref, sent_ref, teacher_vmem, student_vmem, sems):
    copies = [
        pltpu.make_async_copy(teacher_ref, teacher_vmem, sems.at[0]),
        pltpu.make_async_copy(student_ref, student_vmem, sems.at[1]),
    ]
    for copy in copies:
        copy.start()
    for copy in copies:
        copy.wait()
    width = teacher_vmem.shape[1]
    teacher = unit_rows(teacher_vmem[...])[0].astype(jnp.bfloat16)
    student = unit_rows(student_vmem[...])[0].astype(jnp.bfloat16)
    for chip in range(sent_ref.shape[0]):
        sent_ref[chip, :, :width] = teacher
        sent_ref[chip, :, width:] = student


def directions_kernel(block_ref, teacher_ref, student_ref, teacher_out, student_out, inverse_out):
    teacher, _ = unit_columns(teacher_ref[...])
    teacher_out[...] = jnp.transpose(teacher).astype(jnp.bfloat16)
    student, length = unit_columns(student_ref[...])
    student_out[...] = jnp.transpose(student).astype(jnp.bfloat16)
    inverse_out[...] = 1.0 / length


def exponentials(directions, units, temperature):
    logits = lax.dot_general(
        directions, units, (((1,), (1,)), ((), ())), preferred_element_type=jnp.float32
    )
    return jnp.exp2(logits * (math.log2(math.e) / temperature))


def fold(values):
    rows, lanes = values.shape
    return jnp.sum(values.reshape(rows // 8, 8, lanes), axis=0)


def as_rows(line):
    return jnp.concatenate([line[:, at : at + LANES] for at in range(0, line.shape[1], LANES)], axis=0)


def as_line(rows):
    return jnp.concatenate([rows[at : at + 1, :] for at in range(rows.shape[0])], axis=1)


def by_core(core, own, other):
    return jnp.concatenate([jnp.where(core == 0, own, other), jnp.where(core == 0, other, own)], axis=0)


def halves(core, rows):
    half = rows.shape[0] // 2
    first, second = rows[:half], rows[half:]
    return as_line(jnp.where(core == 0, first, second)), as_line(jnp.where(core == 0, second, first))


def send(sent_ref, core, own, other, *more):
    own, other = (as_rows(jnp.sum(total, axis=0, keepdims=True)) for total in (own, other))
    values = jnp.concatenate([by_core(core, own, other), *more], axis=0).astype(jnp.bfloat16)
    for device in range(sent_ref.shape[0]):
        sent_ref[device] = values


def received(got_ref):
    total = got_ref[0].astype(jnp.float32)
    for device in range(1, got_ref.shape[0]):
        total = total + got_ref[device].astype(jnp.float32)
    return total


def units_of(got_ref, width, side):
    chips, rows, _ = got_ref.shape
    return got_ref[:, :, side * width : (side + 1) * width].reshape(chips * rows, width)


def turn(units):
    return jnp.transpose(units.astype(jnp.float32)).astype(jnp.bfloat16)


def own_kernel(
    teacher_hbm, student_hbm, got_ref, teacher_ref, student_ref, teacher_w_ref, student_w_ref, part_ref, turned_ref, sems
):
    count, width = teacher_w_ref.shape
    span = FETCH * TILE
    copies = []
    for piece in range(count // span):
        rows = pl.ds(piece * span, span)
        copies.append((
            pltpu.make_async_copy(teacher_hbm.at[rows], teacher_w_ref.at[rows], sems.at[0, piece]),
            pltpu.make_async_copy(student_hbm.at[rows], student_w_ref.at[rows], sems.at[1, piece]),
        ))
        copies[-1][0].start()
        copies[-1][1].start()
    teacher, student = units_of(got_ref, width, 0), units_of(got_ref, width, 1)
    turned_ref[...] = turn(student)
    part = 0.0
    for start in range(0, count, HALF_TILE):
        here = slice(start, start + HALF_TILE)
        if start % span == 0:
            copies[start // span][0].wait()
            copies[start // span][1].wait()
        teacher_ref[here, :] = exponentials(teacher_w_ref[here, :], teacher, teacher_temp)
        mass = exponentials(student_w_ref[here, :], student, student_temp)
        student_ref[here, :] = mass
        part = part + fold(mass)
    part_ref[...] = part


def other_kernel(
    prototypes, place_ref, teacher_w_ref, student_w_ref, got_ref, own_ref, own_part_ref, weight_ref,
    teacher_ref, student_ref, sent_ref, part_ref, turned_ref,
):
    count, width = teacher_w_ref.shape
    core = place_ref[2]
    teacher, student = units_of(got_ref, width, 0), units_of(got_ref, width, 1)
    turned_ref[...] = turn(student)
    own_total = total = part = 0.0
    for start in range(0, count, HALF_TILE):
        here = slice(start, start + HALF_TILE)
        mass = exponentials(teacher_w_ref[here, :], teacher, teacher_temp)
        teacher_ref[here, :] = mass
        own = own_ref[here, :]
        proto = jnp.sum(own + mass, axis=1, keepdims=True)
        scale = 1.0 / (prototypes * proto)
        own_total = own_total + fold(own * scale)
        total = total + fold(mass * scale)
        mass = exponentials(student_w_ref[here, :], student, student_temp)
        student_ref[here, :] = mass
        part = part + fold(mass)
    send(sent_ref, core, own_total, total, weight_ref[...])
    own_part = as_rows(jnp.sum(own_part_ref[...], axis=0, keepdims=True))
    part_ref[...] = by_core(core, own_part, as_rows(jnp.sum(part, axis=0, keepdims=True)))


def sweep(prototypes, crops, place_ref, own_ref, other_ref, got_ref):
    own_crop, other_crop = halves(place_ref[2], 1.0 / (crops * received(got_ref)[: crops // LANES]))
    own_total = other_total = 0.0
    scales = []
    for start in range(0, own_ref.shape[0], TILE):
        own, other = own_ref[start : start + TILE, :], other_ref[start : start + TILE, :]
        proto = jnp.sum(own * own_crop + other * other_crop, axis=1, keepdims=True)
        scales.append(1.0 / (prototypes * proto))
        own_total = own_total + fold(own * scales[-1])
        other_total = other_total + fold(other * scales[-1])
    return own_total, other_total, scales


def sweep_kernel(prototypes, crops, place_ref, own_ref, other_ref, got_ref, part_ref, sent_ref):
    own, other, _ = sweep(prototypes, crops, place_ref, own_ref, other_ref, got_ref)
    send(sent_ref, place_ref[2], own, other, part_ref[...])


def last_sweep_kernel(
    prototypes, crops, place_ref, own_ref, other_ref, got_ref, directions_ref, sent_ref, scale_ref, copy_ref, sems
):
    pieces, _, span = copy_ref.shape
    copies = []
    for piece in range(pieces):
        columns = pl.ds(pl.multiple_of((place_ref[1] * pieces + piece) * span, span), span)
        copies.append(pltpu.make_async_copy(directions_ref.at[:, columns], copy_ref.at[piece], sems.at[piece]))
        copies[-1].start()
    own, other, scales = sweep(prototypes, crops, place_ref, own_ref, other_ref, got_ref)
    for index, scale in enumerate(scales):
        scale_ref[index * TILE : (index + 1) * TILE, :] = scale
    send(sent_ref, place_ref[2], own, other)
    for copy in copies:
        copy.wait()


def gradient_kernel(
    place_ref, own_mass_ref, other_mass_ref, own_student_ref, other_student_ref, scale_ref, first_ref, second_ref, third_ref,
    own_turned_ref, other_turned_ref, inverse_ref, copy_ref, sent_ref, gradient_ref, grad_ref, unit_ref,
):
    group, core = place_ref[0], place_ref[2]
    chips, rows_each, _ = sent_ref.shape
    count, half = own_mass_ref.shape
    width = own_turned_ref.shape[0]
    span = copy_ref.shape[2]
    lines = 2 * half // LANES
    weights = received(first_ref)[lines:] / student_temp
    teacher_scales = halves(core, weights / received(third_ref))
    student_scales = halves(core, weights / received(second_ref)[lines:])
    masses, students = (own_mass_ref, other_mass_ref), (own_student_ref, other_student_ref)
    own_rows = pl.ds(pl.multiple_of(group * (width // GROUPS), width // GROUPS), width // GROUPS)
    kept = half // GROUPS
    for start in range(0, count, TILE):
        here, slot = slice(start, start + TILE), start // TILE
        piece = slice(start % span, start % span + TILE)
        inverse = inverse_ref[:, here]
        unit = copy_ref[start // span, :, piece].astype(jnp.float32) * inverse
        for side in range(2):
            teacher = masses[side][here, :] * scale_ref[here, :] * teacher_scales[side]
            gradient = students[side][here, :] * student_scales[side] - teacher
            gradient_ref[slot, side] = gradient.astype(jnp.bfloat16)
        weight_grad = 0.0
        for side, turned_ref in enumerate((own_turned_ref, other_turned_ref)):
            weight_grad = weight_grad + lax.dot_general(
                turned_ref[...], gradient_ref[slot, side], (((1,), (1,)), ((), ())), preferred_element_type=jnp.float32
            )
        dot = jnp.sum(unit * weight_grad, axis=0, keepdims=True)
        grad_ref[slot] = (weight_grad - unit * dot) * inverse
        own = grad_ref[slot, own_rows, :].astype(jnp.bfloat16)
        sent_ref[:, :, here] = own.reshape(chips, rows_each, TILE)
        unit_ref[:, here] = unit.astype(jnp.bfloat16)

    per_core = kept // chips
    pieces = per_core // rows_each
    for side in range(2):
        lanes = pl.ds(pl.multiple_of(group * kept, kept), kept)
        gradient = gradient_ref[:, side, :, lanes].reshape(count, kept)
        feature = jnp.dot(unit_ref[...], gradient, preferred_element_type=jnp.float32)
        feature = jnp.transpose(feature).astype(jnp.bfloat16)
        for chip in range(chips):
            for piece in range(pieces):
                start = chip * per_core + piece * rows_each
                at = count + (side * pieces + piece) * width
                sent_ref[chip, :, at : at + width] = feature[start : start + rows_each, :]


def collect_kernel(got_ref, keep_ref, give_ref):
    rows_each = got_ref.shape[1]
    rows, width = keep_ref.shape
    total = got_ref[0].astype(jnp.float32)
    for chip in range(1, got_ref.shape[0]):
        total = total + got_ref[chip].astype(jnp.float32)
    pieces = rows // rows_each
    for piece in range(2 * pieces):
        out_ref, at = (keep_ref, piece) if piece < pieces else (give_ref, piece - pieces)
        out_ref[at * rows_each : (at + 1) * rows_each, :] = total[:, piece * width : (piece + 1) * width]


def feature_kernel(keep_ref, other_ref, student_ref, out_ref):
    total = keep_ref[...] + other_ref[...]
    hat, length = unit_rows(student_ref[...])
    out_ref[...] = (total - hat * jnp.sum(hat * total, axis=1, keepdims=True)) / length


def widen_kernel(got_ref, out_ref):
    chips, _, columns = got_ref.shape
    for chip in range(chips):
        out_ref[:, chip * columns : (chip + 1) * columns] = got_ref[chip].astype(jnp.float32)


def kernel_body(teacher_feat, student_feat, crop_weight, teacher_v, student_v):
    f32, bf16 = jnp.float32, jnp.bfloat16
    shape = jax.ShapeDtypeStruct
    blocks, fsdp = lax.axis_size("block"), lax.axis_size("fsdp")
    chips = blocks * GROUPS
    members, devices = blocks * fsdp, chips * fsdp
    rows, width = teacher_feat.shape
    crops = rows * devices
    lines = crops // LANES
    kept = teacher_v.shape[1]
    prototypes = kept * fsdp
    count = kept // blocks
    group, block = lax.axis_index("group")[None], lax.axis_index("block")[None]
    core = lax.axis_index("fsdp")[None]
    place = jnp.concatenate([group, block, core])
    elements = count * crops
    smem, vmem = pl.BlockSpec(memory_space=pltpu.SMEM), pl.BlockSpec(memory_space=pltpu.VMEM)

    def swap(values):
        return lax.ppermute(values, "fsdp", [(0, 1), (1, 0)])

    def share(values):
        return lax.all_to_all(values, GROUP, 0, 0)

    dma = pltpu.SemaphoreType.DMA
    hbm = functools.partial(pltpu.with_memory_space_constraint, memory_space=pltpu.HBM)
    sent = call(
        units_kernel,
        shape((chips, rows, 2 * width), bf16),
        in_specs=[pl.BlockSpec(memory_space=pl.ANY)] * 2,
        scratch_shapes=[pltpu.VMEM((rows, width), bf16), pltpu.VMEM((rows, width), bf16), dma((2,))],
    )(hbm(teacher_feat), hbm(student_feat))
    own = lax.all_to_all(sent, CHIPS, 0, 0)

    device = (core[0] * chips + group[0] * blocks + block[0]) * rows
    weights = lax.dynamic_update_slice(jnp.zeros((crops,), f32), crop_weight.astype(f32), (device,)).reshape(lines, LANES)
    placed = weights
    for move in range(1, GROUPS):
        placed = placed + lax.ppermute(weights, "group", [(at, (at + move) % GROUPS) for at in range(GROUPS)])

    span = 2 * TILE
    spans = count // span
    column = pl.BlockSpec((width, span), lambda step, at: (0, at[0] * spans + step))
    turned = pl.BlockSpec((span, width), lambda step, at: (step, 0))
    line = pl.BlockSpec((1, span), lambda step, at: (0, step))
    teacher_w, student_w, inverse = call(
        directions_kernel,
        (
            pltpu.HBM((count, width), bf16),
            pltpu.HBM((count, width), bf16),
            shape((1, count), f32),
        ),
        flops=12 * count * width,
        moved=8 * count * width,
        grid_spec=pltpu.PrefetchScalarGridSpec(
            num_scalar_prefetch=1,
            grid=(spans,),
            in_specs=[column, column],
            out_specs=[turned, turned, line],
        ),
    )(
        block,
        hbm(teacher_v),
        hbm(student_v),
    )

    own, teacher_w, placed = lax.optimization_barrier((own, teacher_w, placed))
    other = swap(own)
    half = crops // 2
    anyspace = pl.BlockSpec(memory_space=pl.ANY)
    pieces = count // (FETCH * TILE)
    halved = dict(flops=2 * elements * width, exps=elements)
    own_mass, own_student, teacher_w, student_w, own_part, own_turned = call(
        own_kernel,
        (
            shape((count, half), f32),
            shape((count, half), f32),
            shape((count, width), bf16),
            shape((count, width), bf16),
            shape((8, half), f32),
            shape((width, half), bf16),
        ),
        in_specs=[anyspace] * 2 + [vmem],
        scratch_shapes=[dma((2, pieces))],
        **halved,
    )(hbm(teacher_w), hbm(student_w), own)
    other_mass, other_student, sent, student_part, other_turned = call(
        functools.partial(other_kernel, prototypes),
        (
            shape((count, half), f32),
            shape((count, half), f32),
            shape((members, 2 * lines, LANES), bf16),
            shape((lines, LANES), f32),
            shape((width, half), bf16),
        ),
        in_specs=[smem] + [vmem] * 6,
        **halved,
    )(place, teacher_w, student_w, other, own_mass, own_part, placed)
    first = share(sent)
    sent = call(
        functools.partial(sweep_kernel, prototypes, crops),
        shape((members, 2 * lines, LANES), bf16),
        flops=4 * elements,
        in_specs=[smem] + [vmem] * 4,
    )(place, own_mass, other_mass, first, student_part)
    second = share(sent)
    sent, scale, student_copy = call(
        functools.partial(last_sweep_kernel, prototypes, crops),
        (
            shape((members, lines, LANES), bf16),
            shape((count, 1), f32),
            shape((pieces, width, count // pieces), bf16),
        ),
        flops=4 * elements,
        in_specs=[smem] + [vmem] * 3 + [anyspace],
        scratch_shapes=[dma((pieces,))],
    )(place, own_mass, other_mass, second, hbm(student_v))
    third = share(sent)

    out_rows = width // chips
    per_chip = rows * fsdp * width // out_rows
    sent = call(
        gradient_kernel,
        shape((blocks, out_rows, count + per_chip), bf16),
        flops=4 * elements * width,
        in_specs=[smem] + [vmem] * 12,
        scratch_shapes=[
            pltpu.VMEM((count // TILE, 2, TILE, half), bf16),
            pltpu.VMEM((count // TILE, width, TILE), f32),
            pltpu.VMEM((width, count), bf16),
        ],
    )(
        place, own_mass, other_mass, own_student, other_student, scale, first, second, third,
        own_turned, other_turned, inverse, student_copy,
    )
    got = lax.all_to_all(sent, "block", 0, 0)
    keep, give = call(
        collect_kernel,
        [shape((rows, width), f32)] * 2,
        grid=(1,),
        in_specs=[pl.BlockSpec((blocks, out_rows, per_chip), lambda step: (0, 0, count // per_chip))],
    )(got)
    grad_feat = call(feature_kernel, shape((rows, width), f32))(keep, swap(give), student_feat)
    grad_v = call(
        widen_kernel,
        shape((out_rows, kept), f32),
        grid=(1,),
        in_specs=[pl.BlockSpec((blocks, out_rows, count), lambda step: (0, 0, 0))],
        out_specs=pl.BlockSpec((out_rows, kept), lambda step: (0, 0)),
    )(got)
    return (grad_v, grad_feat)


def solution(mesh):
    dp, fsdp = mesh.shape["dp"], mesh.shape["fsdp"]
    blocks = dp // GROUPS

    def run(teacher_feat, student_feat, crop_weight, teacher_v, student_v):
        crops = teacher_feat.shape[0]
        count = teacher_v.shape[1] // (blocks * fsdp)
        fits = fsdp == 2 and dp == 16 and count % (2 * TILE) == 0 and crops == 1024
        if fits and 8 * count * crops <= KEPT_BYTES:
            grid = Mesh(mesh.devices.reshape(GROUPS, blocks, fsdp), (*CHIPS, "fsdp"))
            body, chips = kernel_body, CHIPS
        else:
            grid, body, chips = mesh, plain_body, ("dp",)
        every = P((*chips, "fsdp"))
        return jax.shard_map(
            body,
            mesh=grid,
            in_specs=(every, every, every, P(None, "fsdp"), P(None, "fsdp")),
            out_specs=(P(chips, "fsdp"), every),
            check_vma=False,
        )(teacher_feat, student_feat, crop_weight, teacher_v, student_v)

    return run
```

```python
import functools
import math

import jax
import jax.numpy as jnp
from jax import lax
from jax.experimental import pallas as pl
from jax.experimental.pallas import tpu as pltpu
from jax.sharding import Mesh
from jax.sharding import PartitionSpec as P

ITERS = 3

teacher_temp = 0.04
student_temp = 0.1
epsilon = 1e-06

GROUPS = 2
TILE = 256
HALF_TILE = 512
FETCH = 2
LANES = 128
VMEM_BYTES = 12 << 20
KEPT_BYTES = 18 << 20

EVERY = ("dp", "fsdp")
CHIPS = ("group", "block")
GROUP = ("block", "fsdp")


def unit_rows(values):
    floats = values.astype(jnp.float32)
    length = jnp.sqrt(jnp.sum(floats * floats, axis=1, keepdims=True) + epsilon)
    return (floats / length, length)


def unit_columns(values):
    floats = values.astype(jnp.float32)
    length = jnp.sqrt(jnp.sum(floats * floats, axis=0, keepdims=True) + epsilon)
    return (floats / length, length)


COPY_BYTES = 1 << 22


def share(values, axes):
    count = lax.axis_size(axes)
    if count * values.size * values.dtype.itemsize > COPY_BYTES:
        return lax.all_gather(values, axes)
    return lax.all_to_all(jnp.broadcast_to(values, (count, *values.shape)), axes, 0, 0)


def add_up(values):
    if lax.axis_size(EVERY) * values.size * values.dtype.itemsize > COPY_BYTES:
        return lax.psum(values, EVERY)
    return jnp.sum(share(values, EVERY), axis=0)


def plain_body(teacher_feat, student_feat, crop_weight, teacher_v, student_v):
    fsdp = lax.axis_size("fsdp")
    devices = lax.axis_size("dp") * fsdp
    own_rows, width = teacher_feat.shape
    crops = own_rows * devices
    block = teacher_v.shape[1] // lax.axis_size("dp")
    prototypes = block * devices
    first = lax.axis_index("dp") * block

    teacher_hat, _ = unit_rows(teacher_feat)
    student_hat, student_len = unit_rows(student_feat)
    units = jnp.concatenate(
        [teacher_hat.astype(jnp.bfloat16), student_hat.astype(jnp.bfloat16)], axis=1
    )
    units = share(share(units, "dp"), "fsdp").reshape(crops, 2 * width)
    teacher_unit, student_unit = units[:, :width], units[:, width:]

    teacher_w, _ = unit_columns(lax.dynamic_slice_in_dim(teacher_v, first, block, 1))
    student_w, student_wlen = unit_columns(lax.dynamic_slice_in_dim(student_v, first, block, 1))
    student_wunit = student_w.astype(jnp.bfloat16)

    mass = jnp.exp(
        jnp.dot(teacher_unit, teacher_w.astype(jnp.bfloat16), preferred_element_type=jnp.float32)
        / teacher_temp
    )
    student_mass = jnp.exp(
        jnp.dot(student_unit, student_wunit, preferred_element_type=jnp.float32) / student_temp
    )
    student_part = jnp.sum(student_mass, axis=1)

    crop_scale = None
    for sweep in range(ITERS):
        scaled = mass if sweep == 0 else mass * crop_scale[:, None]
        proto_scale = 1.0 / (prototypes * jnp.sum(scaled, axis=0))
        crop_part = jnp.sum(mass * proto_scale[None, :], axis=1)
        if sweep == 0:
            placed = jnp.zeros((fsdp, crops // (fsdp * own_rows), own_rows), jnp.float32)
            own = crop_weight.astype(jnp.float32)[None, None]
            spot = (lax.axis_index("fsdp"), lax.axis_index("dp"), 0)
            placed = lax.dynamic_update_slice(placed, own, spot).reshape(crops)
            sums = add_up(jnp.stack([crop_part, student_part, placed]))
            crop_mass, student_total, weights = sums[0], sums[1], sums[2]
        else:
            crop_mass = add_up(crop_part)
        crop_scale = 1.0 / (crops * crop_mass)

    target = crops * (mass * crop_scale[:, None] * proto_scale[None, :])
    student_prob = student_mass / student_total[:, None]
    gradient = ((student_prob - target) * weights[:, None] / student_temp).astype(jnp.bfloat16)
    feature_part = lax.dot_general(
        gradient, student_wunit, (((1,), (1,)), ((), ())), preferred_element_type=jnp.float32
    )
    weight_grad = lax.dot_general(
        student_unit, gradient, (((0,), (0,)), ((), ())), preferred_element_type=jnp.float32
    )
    weight_dot = jnp.sum(student_w * weight_grad, axis=0, keepdims=True)
    grad_block = (weight_grad - student_w * weight_dot) / student_wlen

    feature_sent = feature_part.astype(jnp.bfloat16).reshape(fsdp, -1, own_rows, width)
    feature_sent = jnp.swapaxes(feature_sent, 0, 1).reshape(devices, own_rows, width)
    feature_all = lax.all_to_all(feature_sent, EVERY, 0, 0)
    feature_grad = jnp.sum(feature_all.astype(jnp.float32), axis=0)
    grad_feat = (
        feature_grad - student_hat * jnp.sum(student_hat * feature_grad, axis=1, keepdims=True)
    ) / student_len
    grad_v = lax.all_to_all(grad_block.astype(jnp.bfloat16), "dp", 0, 1, tiled=True)
    return (grad_v.astype(jnp.float32), grad_feat)


def call(kernel, out_shape, flops=0, moved=0, exps=0, **more):
    return pl.pallas_call(
        kernel,
        out_shape=out_shape,
        compiler_params=pltpu.CompilerParams(vmem_limit_bytes=VMEM_BYTES),
        cost_estimate=pl.CostEstimate(flops=flops, bytes_accessed=moved, transcendentals=exps),
        **more,
    )


def units_kernel(teacher_ref, student_ref, sent_ref, teacher_vmem, student_vmem, sems):
    copies = [
        pltpu.make_async_copy(teacher_ref, teacher_vmem, sems.at[0]),
        pltpu.make_async_copy(student_ref, student_vmem, sems.at[1]),
    ]
    for copy in copies:
        copy.start()
    for copy in copies:
        copy.wait()
    width = teacher_vmem.shape[1]
    teacher = unit_rows(teacher_vmem[...])[0].astype(jnp.bfloat16)
    student = unit_rows(student_vmem[...])[0].astype(jnp.bfloat16)
    for chip in range(sent_ref.shape[0]):
        sent_ref[chip, :, :width] = teacher
        sent_ref[chip, :, width:] = student


def directions_kernel(block_ref, teacher_ref, student_ref, teacher_out, student_out, inverse_out):
    teacher, _ = unit_columns(teacher_ref[...])
    teacher_out[...] = jnp.transpose(teacher).astype(jnp.bfloat16)
    student, length = unit_columns(student_ref[...])
    student_out[...] = jnp.transpose(student).astype(jnp.bfloat16)
    inverse_out[...] = 1.0 / length


def exponentials(directions, units, temperature):
    logits = lax.dot_general(
        directions, units, (((1,), (1,)), ((), ())), preferred_element_type=jnp.float32
    )
    return jnp.exp2(logits * (math.log2(math.e) / temperature))


def fold(values):
    rows, lanes = values.shape
    return jnp.sum(values.reshape(rows // 8, 8, lanes), axis=0)


def as_rows(line):
    return jnp.concatenate([line[:, at : at + LANES] for at in range(0, line.shape[1], LANES)], axis=0)


def as_line(rows):
    return jnp.concatenate([rows[at : at + 1, :] for at in range(rows.shape[0])], axis=1)


def in_core_order(core, own, other, body):
    @pl.when(core == 0)
    def _():
        body(own, other)

    @pl.when(core == 1)
    def _():
        body(other, own)


def sums(first, second):
    lines = [as_rows(jnp.sum(total, axis=0, keepdims=True)) for total in (first, second)]
    return jnp.concatenate(lines, axis=0)


def send(sent_ref, *rows):
    values = jnp.concatenate(rows, axis=0).astype(jnp.bfloat16)
    for device in range(sent_ref.shape[0]):
        sent_ref[device] = values


def halves(rows):
    line = as_line(rows)
    half = line.shape[1] // 2
    return line[:, :half], line[:, half:]


def received(got_ref):
    total = got_ref[0].astype(jnp.float32)
    for device in range(1, got_ref.shape[0]):
        total = total + got_ref[device].astype(jnp.float32)
    return total


def units_of(got_ref, width, side):
    chips, rows, _ = got_ref.shape
    return got_ref[:, :, side * width : (side + 1) * width].reshape(chips * rows, width)


def turn(units):
    return jnp.transpose(units.astype(jnp.float32)).astype(jnp.bfloat16)


def own_kernel(
    teacher_hbm, student_hbm, got_ref, teacher_ref, student_ref, teacher_w_ref, student_w_ref, part_ref, turned_ref, sems
):
    count, width = teacher_w_ref.shape
    span = FETCH * TILE
    copies = []
    for piece in range(count // span):
        rows = pl.ds(piece * span, span)
        copies.append((
            pltpu.make_async_copy(teacher_hbm.at[rows], teacher_w_ref.at[rows], sems.at[0, piece]),
            pltpu.make_async_copy(student_hbm.at[rows], student_w_ref.at[rows], sems.at[1, piece]),
        ))
        copies[-1][0].start()
        copies[-1][1].start()
    teacher, student = units_of(got_ref, width, 0), units_of(got_ref, width, 1)
    turned_ref[...] = turn(student)
    part = 0.0
    for start in range(0, count, HALF_TILE):
        here = slice(start, start + HALF_TILE)
        if start % span == 0:
            copies[start // span][0].wait()
            copies[start // span][1].wait()
        teacher_ref[here, :] = exponentials(teacher_w_ref[here, :], teacher, teacher_temp)
        mass = exponentials(student_w_ref[here, :], student, student_temp)
        student_ref[here, :] = mass
        part = part + fold(mass)
    part_ref[...] = part


def other_kernel(
    prototypes, place_ref, teacher_w_ref, student_w_ref, got_ref, own_ref, own_part_ref, weight_ref,
    teacher_ref, student_ref, sent_ref, part_ref, turned_ref,
):
    count, width = teacher_w_ref.shape
    core = place_ref[2]
    teacher, student = units_of(got_ref, width, 0), units_of(got_ref, width, 1)
    turned_ref[...] = turn(student)
    own_total = total = part = 0.0
    for start in range(0, count, HALF_TILE):
        here = slice(start, start + HALF_TILE)
        mass = exponentials(teacher_w_ref[here, :], teacher, teacher_temp)
        teacher_ref[here, :] = mass
        own = own_ref[here, :]
        proto = jnp.sum(own + mass, axis=1, keepdims=True)
        scale = 1.0 / (prototypes * proto)
        own_total = own_total + fold(own * scale)
        total = total + fold(mass * scale)
        mass = exponentials(student_w_ref[here, :], student, student_temp)
        student_ref[here, :] = mass
        part = part + fold(mass)

    def finish(first, second):
        send(sent_ref, sums(first[0], second[0]), weight_ref[...])
        part_ref[...] = sums(first[1], second[1])

    in_core_order(core, (own_total, own_part_ref[...]), (total, part), finish)


def sweep(prototypes, crops, first_ref, second_ref, got_ref):
    first_crop, second_crop = halves(1.0 / (crops * received(got_ref)[: crops // LANES]))
    first_total = second_total = 0.0
    scales = []
    for start in range(0, first_ref.shape[0], TILE):
        first, second = first_ref[start : start + TILE, :], second_ref[start : start + TILE, :]
        proto = jnp.sum(first * first_crop + second * second_crop, axis=1, keepdims=True)
        scales.append(1.0 / (prototypes * proto))
        first_total = first_total + fold(first * scales[-1])
        second_total = second_total + fold(second * scales[-1])
    return sums(first_total, second_total), scales


def sweep_kernel(prototypes, crops, place_ref, own_ref, other_ref, got_ref, part_ref, sent_ref):
    def body(first_ref, second_ref):
        send(sent_ref, sweep(prototypes, crops, first_ref, second_ref, got_ref)[0], part_ref[...])

    in_core_order(place_ref[2], own_ref, other_ref, body)


def last_sweep_kernel(
    prototypes, crops, place_ref, own_ref, other_ref, got_ref, directions_ref, sent_ref, scale_ref, copy_ref, sems
):
    pieces, _, span = copy_ref.shape
    copies = []
    for piece in range(pieces):
        columns = pl.ds(pl.multiple_of((place_ref[1] * pieces + piece) * span, span), span)
        copies.append(pltpu.make_async_copy(directions_ref.at[:, columns], copy_ref.at[piece], sems.at[piece]))
        copies[-1].start()

    def body(first_ref, second_ref):
        total, scales = sweep(prototypes, crops, first_ref, second_ref, got_ref)
        for index, scale in enumerate(scales):
            scale_ref[index * TILE : (index + 1) * TILE, :] = scale
        send(sent_ref, total)

    in_core_order(place_ref[2], own_ref, other_ref, body)
    for copy in copies:
        copy.wait()


def units_tile(copy_ref, inverse_ref, start):
    span = copy_ref.shape[2]
    at = start % span
    return copy_ref[start // span, :, at : at + TILE].astype(jnp.float32) * inverse_ref[:, start : start + TILE]


def gradient_kernel(
    place_ref, own_mass_ref, other_mass_ref, own_student_ref, other_student_ref, scale_ref, first_ref, second_ref, third_ref,
    inverse_ref, copy_ref, gradient_ref, keep_ref, give_ref, unit_ref,
):
    group, core = place_ref[0], place_ref[2]
    count, half = own_mass_ref.shape
    lines = 2 * half // LANES
    weights = received(first_ref)[lines:] / student_temp
    teacher_scales = halves(weights / received(third_ref))
    student_scales = halves(weights / received(second_ref)[lines:])

    def body(first_refs, second_refs):
        for start in range(0, count, TILE):
            here = slice(start, start + TILE)
            for (side, mass_ref, student_ref), teacher_scale, student_scale in zip(
                (first_refs, second_refs), teacher_scales, student_scales
            ):
                teacher = mass_ref[here, :] * scale_ref[here, :] * teacher_scale
                gradient = student_ref[here, :] * student_scale - teacher
                gradient_ref[side, start : start + TILE, :] = gradient.astype(jnp.bfloat16)

    in_core_order(core, (0, own_mass_ref, own_student_ref), (1, other_mass_ref, other_student_ref), body)
    for start in range(0, count, TILE):
        unit_ref[:, start : start + TILE] = units_tile(copy_ref, inverse_ref, start).astype(jnp.bfloat16)
    kept = half // GROUPS
    lanes = pl.ds(pl.multiple_of(group * kept, kept), kept)
    for side, out_ref in enumerate((keep_ref, give_ref)):
        feature = jnp.dot(unit_ref[...], gradient_ref[side, :, lanes], preferred_element_type=jnp.float32)
        out_ref[...] = jnp.transpose(feature).astype(out_ref.dtype)


def weight_kernel(place_ref, gradient_ref, own_turned_ref, other_turned_ref, inverse_ref, copy_ref, sent_ref, grad_ref):
    chips, rows_each, _ = sent_ref.shape
    count = gradient_ref.shape[1]
    width = own_turned_ref.shape[0]
    own_rows = pl.ds(pl.multiple_of(place_ref[0] * (width // GROUPS), width // GROUPS), width // GROUPS)
    for start in range(0, count, TILE):
        here, slot = slice(start, start + TILE), start // TILE
        weight_grad = 0.0
        for side, turned_ref in enumerate((own_turned_ref, other_turned_ref)):
            weight_grad = weight_grad + lax.dot_general(
                turned_ref[...], gradient_ref[side, here, :], (((1,), (1,)), ((), ())), preferred_element_type=jnp.float32
            )
        unit = units_tile(copy_ref, inverse_ref, start)
        dot = jnp.sum(unit * weight_grad, axis=0, keepdims=True)
        grad_ref[slot] = (weight_grad - unit * dot) * inverse_ref[:, here]
        own = grad_ref[slot, own_rows, :].astype(jnp.bfloat16)
        sent_ref[:, :, here] = own.reshape(chips, rows_each, TILE)


def pack_kernel(keep_ref, other_ref, _, sent_ref, packed_ref, sem):
    chips, rows_each, lanes = packed_ref.shape
    width = keep_ref.shape[1]
    total = (keep_ref[...] + other_ref[...].astype(jnp.float32)).astype(jnp.bfloat16)
    total = total.reshape(chips, -1, width)
    for piece in range(lanes // width):
        packed_ref[:, :, piece * width : (piece + 1) * width] = total[:, piece * rows_each : (piece + 1) * rows_each, :]
    copy = pltpu.make_async_copy(packed_ref, sent_ref.at[:, :, pl.ds(sent_ref.shape[2] - lanes, lanes)], sem)
    copy.start()
    copy.wait()


def outputs_kernel(got_ref, student_ref, weight_out, feature_out):
    chips, rows_each, columns = got_ref.shape
    rows, width = student_ref.shape
    pieces = rows // rows_each
    count = columns - pieces * width
    total = got_ref[0, :, count:].astype(jnp.float32)
    for chip in range(1, chips):
        total = total + got_ref[chip, :, count:].astype(jnp.float32)
    total = jnp.concatenate([total[:, piece * width : (piece + 1) * width] for piece in range(pieces)], axis=0)
    hat, length = unit_rows(student_ref[...])
    feature_out[...] = (total - hat * jnp.sum(hat * total, axis=1, keepdims=True)) / length
    for chip in range(chips):
        weight_out[:, chip * count : (chip + 1) * count] = got_ref[chip, :, :count].astype(jnp.float32)


def kernel_body(teacher_feat, student_feat, crop_weight, teacher_v, student_v):
    f32, bf16 = jnp.float32, jnp.bfloat16
    shape = jax.ShapeDtypeStruct
    blocks, fsdp = lax.axis_size("block"), lax.axis_size("fsdp")
    chips = blocks * GROUPS
    members, devices = blocks * fsdp, chips * fsdp
    rows, width = teacher_feat.shape
    crops = rows * devices
    lines = crops // LANES
    kept = teacher_v.shape[1]
    prototypes = kept * fsdp
    count = kept // blocks
    group, block = lax.axis_index("group")[None], lax.axis_index("block")[None]
    core = lax.axis_index("fsdp")[None]
    place = jnp.concatenate([group, block, core])
    elements = count * crops
    smem, vmem = pl.BlockSpec(memory_space=pltpu.SMEM), pl.BlockSpec(memory_space=pltpu.VMEM)

    def swap(values):
        return lax.ppermute(values, "fsdp", [(0, 1), (1, 0)])

    def share(values):
        return lax.all_to_all(values, GROUP, 0, 0)

    dma = pltpu.SemaphoreType.DMA
    hbm = functools.partial(pltpu.with_memory_space_constraint, memory_space=pltpu.HBM)
    sent = call(
        units_kernel,
        shape((chips, rows, 2 * width), bf16),
        in_specs=[pl.BlockSpec(memory_space=pl.ANY)] * 2,
        scratch_shapes=[pltpu.VMEM((rows, width), bf16), pltpu.VMEM((rows, width), bf16), dma((2,))],
    )(hbm(teacher_feat), hbm(student_feat))
    own = lax.all_to_all(sent, CHIPS, 0, 0)

    device = (core[0] * chips + group[0] * blocks + block[0]) * rows
    weights = lax.dynamic_update_slice(jnp.zeros((crops,), f32), crop_weight.astype(f32), (device,)).reshape(lines, LANES)
    placed = weights
    for move in range(1, GROUPS):
        placed = placed + lax.ppermute(weights, "group", [(at, (at + move) % GROUPS) for at in range(GROUPS)])

    span = 2 * TILE
    spans = count // span
    column = pl.BlockSpec((width, span), lambda step, at: (0, at[0] * spans + step))
    turned = pl.BlockSpec((span, width), lambda step, at: (step, 0))
    line = pl.BlockSpec((1, span), lambda step, at: (0, step))
    teacher_w, student_w, inverse = call(
        directions_kernel,
        (
            pltpu.HBM((count, width), bf16),
            pltpu.HBM((count, width), bf16),
            shape((1, count), f32),
        ),
        flops=12 * count * width,
        moved=8 * count * width,
        grid_spec=pltpu.PrefetchScalarGridSpec(
            num_scalar_prefetch=1,
            grid=(spans,),
            in_specs=[column, column],
            out_specs=[turned, turned, line],
        ),
    )(
        block,
        hbm(teacher_v),
        hbm(student_v),
    )

    own, teacher_w, placed = lax.optimization_barrier((own, teacher_w, placed))
    other = swap(own)
    half = crops // 2
    anyspace = pl.BlockSpec(memory_space=pl.ANY)
    pieces = count // (FETCH * TILE)
    halved = dict(flops=2 * elements * width, exps=elements)
    own_mass, own_student, teacher_w, student_w, own_part, own_turned = call(
        own_kernel,
        (
            shape((count, half), f32),
            shape((count, half), f32),
            shape((count, width), bf16),
            shape((count, width), bf16),
            shape((8, half), f32),
            shape((width, half), bf16),
        ),
        in_specs=[anyspace] * 2 + [vmem],
        scratch_shapes=[dma((2, pieces))],
        **halved,
    )(hbm(teacher_w), hbm(student_w), own)
    other_mass, other_student, sent, student_part, other_turned = call(
        functools.partial(other_kernel, prototypes),
        (
            shape((count, half), f32),
            shape((count, half), f32),
            shape((members, 2 * lines, LANES), bf16),
            shape((lines, LANES), f32),
            shape((width, half), bf16),
        ),
        in_specs=[smem] + [vmem] * 6,
        **halved,
    )(place, teacher_w, student_w, other, own_mass, own_part, placed)
    first = share(sent)
    sent = call(
        functools.partial(sweep_kernel, prototypes, crops),
        shape((members, 2 * lines, LANES), bf16),
        flops=4 * elements,
        in_specs=[smem] + [vmem] * 4,
    )(place, own_mass, other_mass, first, student_part)
    second = share(sent)
    sent, scale, student_copy = call(
        functools.partial(last_sweep_kernel, prototypes, crops),
        (
            shape((members, lines, LANES), bf16),
            shape((count, 1), f32),
            shape((pieces, width, count // pieces), bf16),
        ),
        flops=4 * elements,
        in_specs=[smem] + [vmem] * 3 + [anyspace],
        scratch_shapes=[dma((pieces,))],
    )(place, own_mass, other_mass, second, hbm(student_v))
    third = share(sent)

    gradient, keep, give = call(
        gradient_kernel,
        (shape((2, count, half), bf16), shape((half // GROUPS, width), f32), shape((half // GROUPS, width), bf16)),
        flops=2 * elements * width // GROUPS,
        in_specs=[smem] + [vmem] * 10,
        scratch_shapes=[pltpu.VMEM((width, count), bf16)],
    )(place, own_mass, other_mass, own_student, other_student, scale, first, second, third, inverse, student_copy)
    other = swap(give)
    out_rows = width // chips
    per_chip = rows * width // out_rows
    sent = call(
        weight_kernel,
        shape((blocks, out_rows, count + per_chip), bf16),
        flops=2 * elements * width,
        in_specs=[smem] + [vmem] * 5,
        scratch_shapes=[pltpu.VMEM((count // TILE, width, TILE), f32)],
    )(place, gradient, own_turned, other_turned, inverse, student_copy)
    sent = call(
        pack_kernel,
        shape((blocks, out_rows, count + per_chip), bf16),
        in_specs=[vmem] * 2 + [anyspace],
        out_specs=anyspace,
        input_output_aliases={2: 0},
        scratch_shapes=[pltpu.VMEM((blocks, out_rows, per_chip), bf16), dma],
    )(keep, other, sent)
    got = lax.all_to_all(sent, "block", 0, 0)
    return call(
        outputs_kernel, (shape((out_rows, kept), f32), shape((rows, width), f32))
    )(got, student_feat)


def solution(mesh):
    dp, fsdp = mesh.shape["dp"], mesh.shape["fsdp"]
    blocks = dp // GROUPS

    def run(teacher_feat, student_feat, crop_weight, teacher_v, student_v):
        crops = teacher_feat.shape[0]
        count = teacher_v.shape[1] // (blocks * fsdp)
        fits = fsdp == 2 and dp == 16 and count % (2 * TILE) == 0 and crops == 1024
        if fits and 8 * count * crops <= KEPT_BYTES:
            grid = Mesh(mesh.devices.reshape(GROUPS, blocks, fsdp), (*CHIPS, "fsdp"))
            body, chips = kernel_body, CHIPS
        else:
            grid, body, chips = mesh, plain_body, ("dp",)
        every = P((*chips, "fsdp"))
        return jax.shard_map(
            body,
            mesh=grid,
            in_specs=(every, every, every, P(None, "fsdp"), P(None, "fsdp")),
            out_specs=(P(chips, "fsdp"), every),
            check_vma=False,
        )(teacher_feat, student_feat, crop_weight, teacher_v, student_v)

    return run
```

```python
import functools
import math

import jax
import jax.numpy as jnp
from jax import lax
from jax.experimental import pallas as pl
from jax.experimental.pallas import tpu as pltpu
from jax.sharding import Mesh
from jax.sharding import PartitionSpec as P

ITERS = 3

teacher_temp = 0.04
student_temp = 0.1
epsilon = 1e-06

GROUPS = 2
TILE = 256
HALF_TILE = 512
FETCH = 2
LANES = 128
VMEM_BYTES = 12 << 20
KEPT_BYTES = 18 << 20

EVERY = ("dp", "fsdp")
CHIPS = ("group", "block")
GROUP = ("block", "fsdp")


def unit_rows(values):
    floats = values.astype(jnp.float32)
    length = jnp.sqrt(jnp.sum(floats * floats, axis=1, keepdims=True) + epsilon)
    return (floats / length, length)


def unit_columns(values):
    floats = values.astype(jnp.float32)
    length = jnp.sqrt(jnp.sum(floats * floats, axis=0, keepdims=True) + epsilon)
    return (floats / length, length)


COPY_BYTES = 1 << 22


def share(values, axes):
    count = lax.axis_size(axes)
    if count * values.size * values.dtype.itemsize > COPY_BYTES:
        return lax.all_gather(values, axes)
    return lax.all_to_all(jnp.broadcast_to(values, (count, *values.shape)), axes, 0, 0)


def add_up(values):
    if lax.axis_size(EVERY) * values.size * values.dtype.itemsize > COPY_BYTES:
        return lax.psum(values, EVERY)
    return jnp.sum(share(values, EVERY), axis=0)


def plain_body(teacher_feat, student_feat, crop_weight, teacher_v, student_v):
    fsdp = lax.axis_size("fsdp")
    devices = lax.axis_size("dp") * fsdp
    own_rows, width = teacher_feat.shape
    crops = own_rows * devices
    block = teacher_v.shape[1] // lax.axis_size("dp")
    prototypes = block * devices
    first = lax.axis_index("dp") * block

    teacher_hat, _ = unit_rows(teacher_feat)
    student_hat, student_len = unit_rows(student_feat)
    units = jnp.concatenate(
        [teacher_hat.astype(jnp.bfloat16), student_hat.astype(jnp.bfloat16)], axis=1
    )
    units = share(share(units, "dp"), "fsdp").reshape(crops, 2 * width)
    teacher_unit, student_unit = units[:, :width], units[:, width:]

    teacher_w, _ = unit_columns(lax.dynamic_slice_in_dim(teacher_v, first, block, 1))
    student_w, student_wlen = unit_columns(lax.dynamic_slice_in_dim(student_v, first, block, 1))
    student_wunit = student_w.astype(jnp.bfloat16)

    mass = jnp.exp(
        jnp.dot(teacher_unit, teacher_w.astype(jnp.bfloat16), preferred_element_type=jnp.float32)
        / teacher_temp
    )
    student_mass = jnp.exp(
        jnp.dot(student_unit, student_wunit, preferred_element_type=jnp.float32) / student_temp
    )
    student_part = jnp.sum(student_mass, axis=1)

    crop_scale = None
    for sweep in range(ITERS):
        scaled = mass if sweep == 0 else mass * crop_scale[:, None]
        proto_scale = 1.0 / (prototypes * jnp.sum(scaled, axis=0))
        crop_part = jnp.sum(mass * proto_scale[None, :], axis=1)
        if sweep == 0:
            placed = jnp.zeros((fsdp, crops // (fsdp * own_rows), own_rows), jnp.float32)
            own = crop_weight.astype(jnp.float32)[None, None]
            spot = (lax.axis_index("fsdp"), lax.axis_index("dp"), 0)
            placed = lax.dynamic_update_slice(placed, own, spot).reshape(crops)
            sums = add_up(jnp.stack([crop_part, student_part, placed]))
            crop_mass, student_total, weights = sums[0], sums[1], sums[2]
        else:
            crop_mass = add_up(crop_part)
        crop_scale = 1.0 / (crops * crop_mass)

    target = crops * (mass * crop_scale[:, None] * proto_scale[None, :])
    student_prob = student_mass / student_total[:, None]
    gradient = ((student_prob - target) * weights[:, None] / student_temp).astype(jnp.bfloat16)
    feature_part = lax.dot_general(
        gradient, student_wunit, (((1,), (1,)), ((), ())), preferred_element_type=jnp.float32
    )
    weight_grad = lax.dot_general(
        student_unit, gradient, (((0,), (0,)), ((), ())), preferred_element_type=jnp.float32
    )
    weight_dot = jnp.sum(student_w * weight_grad, axis=0, keepdims=True)
    grad_block = (weight_grad - student_w * weight_dot) / student_wlen

    feature_sent = feature_part.astype(jnp.bfloat16).reshape(fsdp, -1, own_rows, width)
    feature_sent = jnp.swapaxes(feature_sent, 0, 1).reshape(devices, own_rows, width)
    feature_all = lax.all_to_all(feature_sent, EVERY, 0, 0)
    feature_grad = jnp.sum(feature_all.astype(jnp.float32), axis=0)
    grad_feat = (
        feature_grad - student_hat * jnp.sum(student_hat * feature_grad, axis=1, keepdims=True)
    ) / student_len
    grad_v = lax.all_to_all(grad_block.astype(jnp.bfloat16), "dp", 0, 1, tiled=True)
    return (grad_v.astype(jnp.float32), grad_feat)


def call(kernel, out_shape, flops=0, moved=0, exps=0, **more):
    return pl.pallas_call(
        kernel,
        out_shape=out_shape,
        compiler_params=pltpu.CompilerParams(vmem_limit_bytes=VMEM_BYTES),
        cost_estimate=pl.CostEstimate(flops=flops, bytes_accessed=moved, transcendentals=exps),
        **more,
    )


def units_kernel(teacher_ref, student_ref, sent_ref, teacher_vmem, student_vmem, sems):
    copies = [
        pltpu.make_async_copy(teacher_ref, teacher_vmem, sems.at[0]),
        pltpu.make_async_copy(student_ref, student_vmem, sems.at[1]),
    ]
    for copy in copies:
        copy.start()
    for copy in copies:
        copy.wait()
    width = teacher_vmem.shape[1]
    teacher = unit_rows(teacher_vmem[...])[0].astype(jnp.bfloat16)
    student = unit_rows(student_vmem[...])[0].astype(jnp.bfloat16)
    for chip in range(sent_ref.shape[0]):
        sent_ref[chip, :, :width] = teacher
        sent_ref[chip, :, width:] = student


def directions_kernel(block_ref, teacher_ref, student_ref, teacher_out, student_out, inverse_out):
    teacher, _ = unit_columns(teacher_ref[...])
    teacher_out[...] = jnp.transpose(teacher).astype(jnp.bfloat16)
    student, length = unit_columns(student_ref[...])
    student_out[...] = jnp.transpose(student).astype(jnp.bfloat16)
    inverse_out[...] = 1.0 / length


def exponentials(directions, units, temperature):
    logits = lax.dot_general(
        directions, units, (((1,), (1,)), ((), ())), preferred_element_type=jnp.float32
    )
    return jnp.exp2(logits * (math.log2(math.e) / temperature))


def fold(values):
    rows, lanes = values.shape
    return jnp.sum(values.reshape(rows // 8, 8, lanes), axis=0)


def as_rows(line):
    return jnp.concatenate([line[:, at : at + LANES] for at in range(0, line.shape[1], LANES)], axis=0)


def as_line(rows):
    return jnp.concatenate([rows[at : at + 1, :] for at in range(rows.shape[0])], axis=1)


def in_core_order(core, own, other, body):
    @pl.when(core == 0)
    def _():
        body(own, other)

    @pl.when(core == 1)
    def _():
        body(other, own)


def lane_blocks(values):
    return [values[:, at : at + LANES] for at in range(0, values.shape[1], LANES)]


def spread(prototypes, proto):
    return 1.0 / (prototypes * jnp.broadcast_to(proto, (proto.shape[0], LANES)))


def add_scaled(totals, values, scale):
    return [total + fold(block * scale) for total, block in zip(totals, lane_blocks(values))]


def sums(first, second):
    return jnp.concatenate([jnp.sum(total, axis=0, keepdims=True) for total in (*first, *second)], axis=0)


def send(sent_ref, *rows):
    values = jnp.concatenate(rows, axis=0).astype(jnp.bfloat16)
    for device in range(sent_ref.shape[0]):
        sent_ref[device] = values


def halves(rows):
    line = as_line(rows)
    half = line.shape[1] // 2
    return line[:, :half], line[:, half:]


def received(got_ref):
    total = got_ref[0].astype(jnp.float32)
    for device in range(1, got_ref.shape[0]):
        total = total + got_ref[device].astype(jnp.float32)
    return total


def units_of(got_ref, width, side):
    chips, rows, _ = got_ref.shape
    return got_ref[:, :, side * width : (side + 1) * width].reshape(chips * rows, width)


def turn(units):
    return jnp.transpose(units.astype(jnp.float32)).astype(jnp.bfloat16)


def own_kernel(
    teacher_hbm, student_hbm, got_ref, teacher_ref, student_ref, teacher_w_ref, student_w_ref, part_ref, turned_ref, sems
):
    count, width = teacher_w_ref.shape
    span = FETCH * TILE
    copies = []
    for piece in range(count // span):
        rows = pl.ds(piece * span, span)
        copies.append((
            pltpu.make_async_copy(teacher_hbm.at[rows], teacher_w_ref.at[rows], sems.at[0, piece]),
            pltpu.make_async_copy(student_hbm.at[rows], student_w_ref.at[rows], sems.at[1, piece]),
        ))
        copies[-1][0].start()
        copies[-1][1].start()
    teacher, student = units_of(got_ref, width, 0), units_of(got_ref, width, 1)
    turned_ref[...] = turn(student)
    part = 0.0
    for start in range(0, count, HALF_TILE):
        here = slice(start, start + HALF_TILE)
        if start % span == 0:
            copies[start // span][0].wait()
            copies[start // span][1].wait()
        teacher_ref[here, :] = exponentials(teacher_w_ref[here, :], teacher, teacher_temp)
        mass = exponentials(student_w_ref[here, :], student, student_temp)
        student_ref[here, :] = mass
        part = part + fold(mass)
    part_ref[...] = part


def other_kernel(
    prototypes, place_ref, teacher_w_ref, student_w_ref, got_ref, own_ref, own_part_ref, weight_ref,
    teacher_ref, student_ref, sent_ref, part_ref, turned_ref,
):
    count, width = teacher_w_ref.shape
    core = place_ref[2]
    teacher, student = units_of(got_ref, width, 0), units_of(got_ref, width, 1)
    turned_ref[...] = turn(student)
    blocks = got_ref.shape[0] * got_ref.shape[1] // LANES
    own_total = total = [0.0] * blocks
    part = 0.0
    for start in range(0, count, HALF_TILE):
        here = slice(start, start + HALF_TILE)
        mass = exponentials(teacher_w_ref[here, :], teacher, teacher_temp)
        teacher_ref[here, :] = mass
        own = own_ref[here, :]
        scale = spread(prototypes, jnp.sum(own + mass, axis=1, keepdims=True))
        own_total = add_scaled(own_total, own, scale)
        total = add_scaled(total, mass, scale)
        mass = exponentials(student_w_ref[here, :], student, student_temp)
        student_ref[here, :] = mass
        part = part + fold(mass)

    def finish(first, second):
        send(sent_ref, sums(first[0], second[0]), weight_ref[...])
        part_ref[...] = sums(first[1], second[1])

    in_core_order(core, (own_total, lane_blocks(own_part_ref[...])), (total, lane_blocks(part)), finish)


def sweep(prototypes, crops, first_ref, second_ref, got_ref):
    first_crop, second_crop = halves(1.0 / (crops * received(got_ref)[: crops // LANES]))
    first_total = second_total = [0.0] * (first_ref.shape[1] // LANES)
    scales = []
    for start in range(0, first_ref.shape[0], TILE):
        first, second = first_ref[start : start + TILE, :], second_ref[start : start + TILE, :]
        proto = jnp.sum(first * first_crop + second * second_crop, axis=1, keepdims=True)
        scales.append(spread(prototypes, proto))
        first_total = add_scaled(first_total, first, scales[-1])
        second_total = add_scaled(second_total, second, scales[-1])
    return sums(first_total, second_total), scales


def sweep_kernel(prototypes, crops, place_ref, own_ref, other_ref, got_ref, part_ref, sent_ref):
    def body(first_ref, second_ref):
        send(sent_ref, sweep(prototypes, crops, first_ref, second_ref, got_ref)[0], part_ref[...])

    in_core_order(place_ref[2], own_ref, other_ref, body)


def last_sweep_kernel(
    prototypes, crops, place_ref, own_ref, other_ref, got_ref, directions_ref, sent_ref, scale_ref, copy_ref, sems
):
    pieces, _, span = copy_ref.shape
    copies = []
    for piece in range(pieces):
        columns = pl.ds(pl.multiple_of((place_ref[1] * pieces + piece) * span, span), span)
        copies.append(pltpu.make_async_copy(directions_ref.at[:, columns], copy_ref.at[piece], sems.at[piece]))
        copies[-1].start()

    def body(first_ref, second_ref):
        total, scales = sweep(prototypes, crops, first_ref, second_ref, got_ref)
        for index, scale in enumerate(scales):
            scale_ref[index * TILE : (index + 1) * TILE, :] = scale
        send(sent_ref, total)

    in_core_order(place_ref[2], own_ref, other_ref, body)
    for copy in copies:
        copy.wait()


def units_tile(copy_ref, inverse_ref, start):
    span = copy_ref.shape[2]
    at = start % span
    return copy_ref[start // span, :, at : at + TILE].astype(jnp.float32) * inverse_ref[:, start : start + TILE]


def gradient_kernel(
    place_ref, own_mass_ref, other_mass_ref, own_student_ref, other_student_ref, scale_ref, first_ref, second_ref, third_ref,
    inverse_ref, copy_ref, gradient_ref, keep_ref, give_ref, unit_ref,
):
    group, core = place_ref[0], place_ref[2]
    count, half = own_mass_ref.shape
    lines = 2 * half // LANES
    weights = received(first_ref)[lines:] / student_temp
    teacher_scales = halves(weights / received(third_ref))
    student_scales = halves(weights / received(second_ref)[lines:])

    def body(first_refs, second_refs):
        for start in range(0, count, TILE):
            here = slice(start, start + TILE)
            for (side, mass_ref, student_ref), teacher_scale, student_scale in zip(
                (first_refs, second_refs), teacher_scales, student_scales
            ):
                for at in range(0, half, LANES):
                    lanes = slice(at, at + LANES)
                    teacher = mass_ref[here, lanes] * scale_ref[here, :] * teacher_scale[:, lanes]
                    gradient = student_ref[here, lanes] * student_scale[:, lanes] - teacher
                    gradient_ref[side, here, lanes] = gradient.astype(jnp.bfloat16)

    in_core_order(core, (0, own_mass_ref, own_student_ref), (1, other_mass_ref, other_student_ref), body)
    for start in range(0, count, TILE):
        unit_ref[:, start : start + TILE] = units_tile(copy_ref, inverse_ref, start).astype(jnp.bfloat16)
    kept = half // GROUPS
    lanes = pl.ds(pl.multiple_of(group * kept, kept), kept)
    for side, out_ref in enumerate((keep_ref, give_ref)):
        feature = jnp.dot(unit_ref[...], gradient_ref[side, :, lanes], preferred_element_type=jnp.float32)
        out_ref[...] = jnp.transpose(feature).astype(out_ref.dtype)


def weight_kernel(place_ref, gradient_ref, own_turned_ref, other_turned_ref, inverse_ref, copy_ref, sent_ref, grad_ref):
    chips, rows_each, _ = sent_ref.shape
    count = gradient_ref.shape[1]
    width = own_turned_ref.shape[0]
    own_rows = pl.ds(pl.multiple_of(place_ref[0] * (width // GROUPS), width // GROUPS), width // GROUPS)
    for start in range(0, count, TILE):
        here, slot = slice(start, start + TILE), start // TILE
        weight_grad = 0.0
        for side, turned_ref in enumerate((own_turned_ref, other_turned_ref)):
            weight_grad = weight_grad + lax.dot_general(
                turned_ref[...], gradient_ref[side, here, :], (((1,), (1,)), ((), ())), preferred_element_type=jnp.float32
            )
        unit = units_tile(copy_ref, inverse_ref, start)
        dot = jnp.sum(unit * weight_grad, axis=0, keepdims=True)
        grad_ref[slot] = (weight_grad - unit * dot) * inverse_ref[:, here]
        own = grad_ref[slot, own_rows, :].astype(jnp.bfloat16)
        sent_ref[:, :, here] = own.reshape(chips, rows_each, TILE)


def pack_kernel(keep_ref, other_ref, _, sent_ref, packed_ref, sem):
    chips, rows_each, lanes = packed_ref.shape
    width = keep_ref.shape[1]
    total = (keep_ref[...] + other_ref[...].astype(jnp.float32)).astype(jnp.bfloat16)
    total = total.reshape(chips, -1, width)
    for piece in range(lanes // width):
        packed_ref[:, :, piece * width : (piece + 1) * width] = total[:, piece * rows_each : (piece + 1) * rows_each, :]
    copy = pltpu.make_async_copy(packed_ref, sent_ref.at[:, :, pl.ds(sent_ref.shape[2] - lanes, lanes)], sem)
    copy.start()
    copy.wait()


def outputs_kernel(got_ref, student_ref, weight_out, feature_out):
    chips, rows_each, columns = got_ref.shape
    rows, width = student_ref.shape
    pieces = rows // rows_each
    count = columns - pieces * width
    total = got_ref[0, :, count:].astype(jnp.float32)
    for chip in range(1, chips):
        total = total + got_ref[chip, :, count:].astype(jnp.float32)
    total = jnp.concatenate([total[:, piece * width : (piece + 1) * width] for piece in range(pieces)], axis=0)
    hat, length = unit_rows(student_ref[...])
    feature_out[...] = (total - hat * jnp.sum(hat * total, axis=1, keepdims=True)) / length
    for chip in range(chips):
        weight_out[:, chip * count : (chip + 1) * count] = got_ref[chip, :, :count].astype(jnp.float32)


def kernel_body(teacher_feat, student_feat, crop_weight, teacher_v, student_v):
    f32, bf16 = jnp.float32, jnp.bfloat16
    shape = jax.ShapeDtypeStruct
    blocks, fsdp = lax.axis_size("block"), lax.axis_size("fsdp")
    chips = blocks * GROUPS
    members, devices = blocks * fsdp, chips * fsdp
    rows, width = teacher_feat.shape
    crops = rows * devices
    lines = crops // LANES
    kept = teacher_v.shape[1]
    prototypes = kept * fsdp
    count = kept // blocks
    group, block = lax.axis_index("group")[None], lax.axis_index("block")[None]
    core = lax.axis_index("fsdp")[None]
    place = jnp.concatenate([group, block, core])
    elements = count * crops
    smem, vmem = pl.BlockSpec(memory_space=pltpu.SMEM), pl.BlockSpec(memory_space=pltpu.VMEM)

    def swap(values):
        return lax.ppermute(values, "fsdp", [(0, 1), (1, 0)])

    def share(values):
        return lax.all_to_all(values, GROUP, 0, 0)

    dma = pltpu.SemaphoreType.DMA
    hbm = functools.partial(pltpu.with_memory_space_constraint, memory_space=pltpu.HBM)
    sent = call(
        units_kernel,
        shape((chips, rows, 2 * width), bf16),
        in_specs=[pl.BlockSpec(memory_space=pl.ANY)] * 2,
        scratch_shapes=[pltpu.VMEM((rows, width), bf16), pltpu.VMEM((rows, width), bf16), dma((2,))],
    )(hbm(teacher_feat), hbm(student_feat))
    own = lax.all_to_all(sent, CHIPS, 0, 0)

    device = (core[0] * chips + group[0] * blocks + block[0]) * rows
    weights = lax.dynamic_update_slice(jnp.zeros((crops,), f32), crop_weight.astype(f32), (device,)).reshape(lines, LANES)
    placed = weights
    for move in range(1, GROUPS):
        placed = placed + lax.ppermute(weights, "group", [(at, (at + move) % GROUPS) for at in range(GROUPS)])

    span = 2 * TILE
    spans = count // span
    column = pl.BlockSpec((width, span), lambda step, at: (0, at[0] * spans + step))
    turned = pl.BlockSpec((span, width), lambda step, at: (step, 0))
    line = pl.BlockSpec((1, span), lambda step, at: (0, step))
    teacher_w, student_w, inverse = call(
        directions_kernel,
        (
            pltpu.HBM((count, width), bf16),
            pltpu.HBM((count, width), bf16),
            shape((1, count), f32),
        ),
        flops=12 * count * width,
        moved=8 * count * width,
        grid_spec=pltpu.PrefetchScalarGridSpec(
            num_scalar_prefetch=1,
            grid=(spans,),
            in_specs=[column, column],
            out_specs=[turned, turned, line],
        ),
    )(
        block,
        hbm(teacher_v),
        hbm(student_v),
    )

    own, teacher_w, placed = lax.optimization_barrier((own, teacher_w, placed))
    other = swap(own)
    half = crops // 2
    anyspace = pl.BlockSpec(memory_space=pl.ANY)
    pieces = count // (FETCH * TILE)
    halved = dict(flops=2 * elements * width, exps=elements)
    own_mass, own_student, teacher_w, student_w, own_part, own_turned = call(
        own_kernel,
        (
            shape((count, half), f32),
            shape((count, half), f32),
            shape((count, width), bf16),
            shape((count, width), bf16),
            shape((8, half), f32),
            shape((width, half), bf16),
        ),
        in_specs=[anyspace] * 2 + [vmem],
        scratch_shapes=[dma((2, pieces))],
        **halved,
    )(hbm(teacher_w), hbm(student_w), own)
    other_mass, other_student, sent, student_part, other_turned = call(
        functools.partial(other_kernel, prototypes),
        (
            shape((count, half), f32),
            shape((count, half), f32),
            shape((members, 2 * lines, LANES), bf16),
            shape((lines, LANES), f32),
            shape((width, half), bf16),
        ),
        in_specs=[smem] + [vmem] * 6,
        **halved,
    )(place, teacher_w, student_w, other, own_mass, own_part, placed)
    first = share(sent)
    sent = call(
        functools.partial(sweep_kernel, prototypes, crops),
        shape((members, 2 * lines, LANES), bf16),
        flops=4 * elements,
        in_specs=[smem] + [vmem] * 4,
    )(place, own_mass, other_mass, first, student_part)
    second = share(sent)
    sent, scale, student_copy = call(
        functools.partial(last_sweep_kernel, prototypes, crops),
        (
            shape((members, lines, LANES), bf16),
            shape((count, LANES), f32),
            shape((pieces, width, count // pieces), bf16),
        ),
        flops=4 * elements,
        in_specs=[smem] + [vmem] * 3 + [anyspace],
        scratch_shapes=[dma((pieces,))],
    )(place, own_mass, other_mass, second, hbm(student_v))
    third = share(sent)

    gradient, keep, give = call(
        gradient_kernel,
        (shape((2, count, half), bf16), shape((half // GROUPS, width), f32), shape((half // GROUPS, width), bf16)),
        flops=2 * elements * width // GROUPS,
        in_specs=[smem] + [vmem] * 10,
        scratch_shapes=[pltpu.VMEM((width, count), bf16)],
    )(place, own_mass, other_mass, own_student, other_student, scale, first, second, third, inverse, student_copy)
    other = swap(give)
    out_rows = width // chips
    per_chip = rows * width // out_rows
    sent = call(
        weight_kernel,
        shape((blocks, out_rows, count + per_chip), bf16),
        flops=2 * elements * width,
        in_specs=[smem] + [vmem] * 5,
        scratch_shapes=[pltpu.VMEM((count // TILE, width, TILE), f32)],
    )(place, gradient, own_turned, other_turned, inverse, student_copy)
    sent = call(
        pack_kernel,
        shape((blocks, out_rows, count + per_chip), bf16),
        in_specs=[vmem] * 2 + [anyspace],
        out_specs=anyspace,
        input_output_aliases={2: 0},
        scratch_shapes=[pltpu.VMEM((blocks, out_rows, per_chip), bf16), dma],
    )(keep, other, sent)
    got = lax.all_to_all(sent, "block", 0, 0)
    return call(
        outputs_kernel, (shape((out_rows, kept), f32), shape((rows, width), f32))
    )(got, student_feat)


def solution(mesh):
    dp, fsdp = mesh.shape["dp"], mesh.shape["fsdp"]
    blocks = dp // GROUPS

    def run(teacher_feat, student_feat, crop_weight, teacher_v, student_v):
        crops = teacher_feat.shape[0]
        count = teacher_v.shape[1] // (blocks * fsdp)
        fits = fsdp == 2 and dp == 16 and count % (2 * TILE) == 0 and crops == 1024
        if fits and 8 * count * crops <= KEPT_BYTES:
            grid = Mesh(mesh.devices.reshape(GROUPS, blocks, fsdp), (*CHIPS, "fsdp"))
            body, chips = kernel_body, CHIPS
        else:
            grid, body, chips = mesh, plain_body, ("dp",)
        every = P((*chips, "fsdp"))
        return jax.shard_map(
            body,
            mesh=grid,
            in_specs=(every, every, every, P(None, "fsdp"), P(None, "fsdp")),
            out_specs=(P(chips, "fsdp"), every),
            check_vma=False,
        )(teacher_feat, student_feat, crop_weight, teacher_v, student_v)

    return run
```

```python
import functools
import math

import jax
import jax.numpy as jnp
from jax import lax
from jax.experimental import pallas as pl
from jax.experimental.pallas import tpu as pltpu
from jax.sharding import Mesh
from jax.sharding import PartitionSpec as P

ITERS = 3

teacher_temp = 0.04
student_temp = 0.1
epsilon = 1e-06

GROUPS = 2
TILE = 256
HALF_TILE = 512
FETCH = 2
LANES = 128
VMEM_BYTES = 12 << 20
KEPT_BYTES = 18 << 20

EVERY = ("dp", "fsdp")
CHIPS = ("group", "block")
GROUP = ("block", "fsdp")


def unit_rows(values):
    floats = values.astype(jnp.float32)
    length = jnp.sqrt(jnp.sum(floats * floats, axis=1, keepdims=True) + epsilon)
    return (floats / length, length)


def unit_columns(values):
    floats = values.astype(jnp.float32)
    length = jnp.sqrt(jnp.sum(floats * floats, axis=0, keepdims=True) + epsilon)
    return (floats / length, length)


COPY_BYTES = 1 << 22


def share(values, axes):
    count = lax.axis_size(axes)
    if count * values.size * values.dtype.itemsize > COPY_BYTES:
        return lax.all_gather(values, axes)
    return lax.all_to_all(jnp.broadcast_to(values, (count, *values.shape)), axes, 0, 0)


def add_up(values):
    if lax.axis_size(EVERY) * values.size * values.dtype.itemsize > COPY_BYTES:
        return lax.psum(values, EVERY)
    return jnp.sum(share(values, EVERY), axis=0)


def plain_body(teacher_feat, student_feat, crop_weight, teacher_v, student_v):
    fsdp = lax.axis_size("fsdp")
    devices = lax.axis_size("dp") * fsdp
    own_rows, width = teacher_feat.shape
    crops = own_rows * devices
    block = teacher_v.shape[1] // lax.axis_size("dp")
    prototypes = block * devices
    first = lax.axis_index("dp") * block

    teacher_hat, _ = unit_rows(teacher_feat)
    student_hat, student_len = unit_rows(student_feat)
    units = jnp.concatenate(
        [teacher_hat.astype(jnp.bfloat16), student_hat.astype(jnp.bfloat16)], axis=1
    )
    units = share(share(units, "dp"), "fsdp").reshape(crops, 2 * width)
    teacher_unit, student_unit = units[:, :width], units[:, width:]

    teacher_w, _ = unit_columns(lax.dynamic_slice_in_dim(teacher_v, first, block, 1))
    student_w, student_wlen = unit_columns(lax.dynamic_slice_in_dim(student_v, first, block, 1))
    student_wunit = student_w.astype(jnp.bfloat16)

    mass = jnp.exp(
        jnp.dot(teacher_unit, teacher_w.astype(jnp.bfloat16), preferred_element_type=jnp.float32)
        / teacher_temp
    )
    student_mass = jnp.exp(
        jnp.dot(student_unit, student_wunit, preferred_element_type=jnp.float32) / student_temp
    )
    student_part = jnp.sum(student_mass, axis=1)

    crop_scale = None
    for sweep in range(ITERS):
        scaled = mass if sweep == 0 else mass * crop_scale[:, None]
        proto_scale = 1.0 / (prototypes * jnp.sum(scaled, axis=0))
        crop_part = jnp.sum(mass * proto_scale[None, :], axis=1)
        if sweep == 0:
            placed = jnp.zeros((fsdp, crops // (fsdp * own_rows), own_rows), jnp.float32)
            own = crop_weight.astype(jnp.float32)[None, None]
            spot = (lax.axis_index("fsdp"), lax.axis_index("dp"), 0)
            placed = lax.dynamic_update_slice(placed, own, spot).reshape(crops)
            sums = add_up(jnp.stack([crop_part, student_part, placed]))
            crop_mass, student_total, weights = sums[0], sums[1], sums[2]
        else:
            crop_mass = add_up(crop_part)
        crop_scale = 1.0 / (crops * crop_mass)

    target = crops * (mass * crop_scale[:, None] * proto_scale[None, :])
    student_prob = student_mass / student_total[:, None]
    gradient = ((student_prob - target) * weights[:, None] / student_temp).astype(jnp.bfloat16)
    feature_part = lax.dot_general(
        gradient, student_wunit, (((1,), (1,)), ((), ())), preferred_element_type=jnp.float32
    )
    weight_grad = lax.dot_general(
        student_unit, gradient, (((0,), (0,)), ((), ())), preferred_element_type=jnp.float32
    )
    weight_dot = jnp.sum(student_w * weight_grad, axis=0, keepdims=True)
    grad_block = (weight_grad - student_w * weight_dot) / student_wlen

    feature_sent = feature_part.astype(jnp.bfloat16).reshape(fsdp, -1, own_rows, width)
    feature_sent = jnp.swapaxes(feature_sent, 0, 1).reshape(devices, own_rows, width)
    feature_all = lax.all_to_all(feature_sent, EVERY, 0, 0)
    feature_grad = jnp.sum(feature_all.astype(jnp.float32), axis=0)
    grad_feat = (
        feature_grad - student_hat * jnp.sum(student_hat * feature_grad, axis=1, keepdims=True)
    ) / student_len
    grad_v = lax.all_to_all(grad_block.astype(jnp.bfloat16), "dp", 0, 1, tiled=True)
    return (grad_v.astype(jnp.float32), grad_feat)


def call(kernel, out_shape, flops=0, moved=0, exps=0, **more):
    return pl.pallas_call(
        kernel,
        out_shape=out_shape,
        compiler_params=pltpu.CompilerParams(vmem_limit_bytes=VMEM_BYTES),
        cost_estimate=pl.CostEstimate(flops=flops, bytes_accessed=moved, transcendentals=exps),
        **more,
    )


def units_kernel(teacher_ref, student_ref, sent_ref, teacher_vmem, student_vmem, sems):
    copies = [
        pltpu.make_async_copy(teacher_ref, teacher_vmem, sems.at[0]),
        pltpu.make_async_copy(student_ref, student_vmem, sems.at[1]),
    ]
    for copy in copies:
        copy.start()
    for copy in copies:
        copy.wait()
    width = teacher_vmem.shape[1]
    teacher = unit_rows(teacher_vmem[...])[0].astype(jnp.bfloat16)
    student = unit_rows(student_vmem[...])[0].astype(jnp.bfloat16)
    for chip in range(sent_ref.shape[0]):
        sent_ref[chip, :, :width] = teacher
        sent_ref[chip, :, width:] = student


def directions_kernel(block_ref, teacher_ref, student_ref, teacher_out, student_out, inverse_out):
    teacher, _ = unit_columns(teacher_ref[...])
    teacher_out[...] = jnp.transpose(teacher).astype(jnp.bfloat16)
    student, length = unit_columns(student_ref[...])
    student_out[...] = jnp.transpose(student).astype(jnp.bfloat16)
    inverse_out[...] = 1.0 / length


def exponentials(directions, units, temperature):
    logits = lax.dot_general(
        directions, units, (((1,), (1,)), ((), ())), preferred_element_type=jnp.float32
    )
    return jnp.exp2(logits * (math.log2(math.e) / temperature))


def fold(values):
    rows, lanes = values.shape
    return jnp.sum(values.reshape(rows // 8, 8, lanes), axis=0)


def as_rows(line):
    return jnp.concatenate([line[:, at : at + LANES] for at in range(0, line.shape[1], LANES)], axis=0)


def as_line(rows):
    return jnp.concatenate([rows[at : at + 1, :] for at in range(rows.shape[0])], axis=1)


def in_core_order(core, own, other, body):
    @pl.when(core == 0)
    def _():
        body(own, other)

    @pl.when(core == 1)
    def _():
        body(other, own)


def sums(first, second):
    lines = [as_rows(jnp.sum(total, axis=0, keepdims=True)) for total in (first, second)]
    return jnp.concatenate(lines, axis=0)


def send(sent_ref, *rows):
    values = jnp.concatenate(rows, axis=0).astype(jnp.bfloat16)
    for device in range(sent_ref.shape[0]):
        sent_ref[device] = values


def halves(rows):
    line = as_line(rows)
    half = line.shape[1] // 2
    return line[:, :half], line[:, half:]


def received(got_ref):
    total = got_ref[0].astype(jnp.float32)
    for device in range(1, got_ref.shape[0]):
        total = total + got_ref[device].astype(jnp.float32)
    return total


def units_of(got_ref, width, side):
    chips, rows, _ = got_ref.shape
    return got_ref[:, :, side * width : (side + 1) * width].reshape(chips * rows, width)


def turn(units):
    return jnp.transpose(units.astype(jnp.float32)).astype(jnp.bfloat16)


def own_kernel(
    teacher_hbm, student_hbm, got_ref, teacher_ref, student_ref, teacher_w_ref, student_w_ref, part_ref, turned_ref, sems
):
    count, width = teacher_w_ref.shape
    span = FETCH * TILE
    copies = []
    for piece in range(count // span):
        rows = pl.ds(piece * span, span)
        copies.append((
            pltpu.make_async_copy(teacher_hbm.at[rows], teacher_w_ref.at[rows], sems.at[0, piece]),
            pltpu.make_async_copy(student_hbm.at[rows], student_w_ref.at[rows], sems.at[1, piece]),
        ))
        copies[-1][0].start()
        copies[-1][1].start()
    teacher, student = units_of(got_ref, width, 0), units_of(got_ref, width, 1)
    turned_ref[...] = turn(student)
    part = 0.0
    for start in range(0, count, HALF_TILE):
        here = slice(start, start + HALF_TILE)
        if start % span == 0:
            copies[start // span][0].wait()
            copies[start // span][1].wait()
        teacher_ref[here, :] = exponentials(teacher_w_ref[here, :], teacher, teacher_temp)
        mass = exponentials(student_w_ref[here, :], student, student_temp)
        student_ref[here, :] = mass
        part = part + fold(mass)
    part_ref[...] = part


def other_kernel(
    prototypes, teacher_w_ref, student_w_ref, got_ref, own_ref, own_part_ref, weight_ref,
    teacher_ref, student_ref, sent_ref, part_ref, turned_ref,
):
    count, width = teacher_w_ref.shape
    core = lax.axis_index("fsdp")
    teacher, student = units_of(got_ref, width, 0), units_of(got_ref, width, 1)
    turned_ref[...] = turn(student)
    own_total = total = part = 0.0
    for start in range(0, count, HALF_TILE):
        here = slice(start, start + HALF_TILE)
        mass = exponentials(teacher_w_ref[here, :], teacher, teacher_temp)
        teacher_ref[here, :] = mass
        own = own_ref[here, :]
        proto = jnp.sum(own + mass, axis=1, keepdims=True)
        scale = 1.0 / (prototypes * proto)
        own_total = own_total + fold(own * scale)
        total = total + fold(mass * scale)
        mass = exponentials(student_w_ref[here, :], student, student_temp)
        student_ref[here, :] = mass
        part = part + fold(mass)

    def finish(first, second):
        send(sent_ref, sums(first[0], second[0]), weight_ref[...])
        part_ref[...] = sums(first[1], second[1])

    in_core_order(core, (own_total, own_part_ref[...]), (total, part), finish)


def sweep(prototypes, crops, first_ref, second_ref, got_ref):
    first_crop, second_crop = halves(1.0 / (crops * received(got_ref)[: crops // LANES]))
    first_total = second_total = 0.0
    scales = []
    for start in range(0, first_ref.shape[0], TILE):
        first, second = first_ref[start : start + TILE, :], second_ref[start : start + TILE, :]
        proto = jnp.sum(first * first_crop + second * second_crop, axis=1, keepdims=True)
        scales.append(1.0 / (prototypes * proto))
        first_total = first_total + fold(first * scales[-1])
        second_total = second_total + fold(second * scales[-1])
    return sums(first_total, second_total), scales


def sweep_kernel(prototypes, crops, own_ref, other_ref, got_ref, part_ref, sent_ref):
    def body(first_ref, second_ref):
        send(sent_ref, sweep(prototypes, crops, first_ref, second_ref, got_ref)[0], part_ref[...])

    in_core_order(lax.axis_index("fsdp"), own_ref, other_ref, body)


def last_sweep_kernel(
    prototypes, crops, own_ref, other_ref, got_ref, directions_ref, sent_ref, scale_ref, copy_ref, sems
):
    pieces, _, span = copy_ref.shape
    copies = []
    for piece in range(pieces):
        columns = pl.ds(pl.multiple_of((lax.axis_index("block") * pieces + piece) * span, span), span)
        copies.append(pltpu.make_async_copy(directions_ref.at[:, columns], copy_ref.at[piece], sems.at[piece]))
        copies[-1].start()

    def body(first_ref, second_ref):
        total, scales = sweep(prototypes, crops, first_ref, second_ref, got_ref)
        for index, scale in enumerate(scales):
            scale_ref[index * TILE : (index + 1) * TILE, :] = scale
        send(sent_ref, total)

    in_core_order(lax.axis_index("fsdp"), own_ref, other_ref, body)
    for copy in copies:
        copy.wait()


def units_tile(copy_ref, inverse_ref, start):
    span = copy_ref.shape[2]
    at = start % span
    return copy_ref[start // span, :, at : at + TILE].astype(jnp.float32) * inverse_ref[:, start : start + TILE]


def gradient_kernel(
    own_mass_ref, other_mass_ref, own_student_ref, other_student_ref, scale_ref, first_ref, second_ref, third_ref,
    inverse_ref, copy_ref, gradient_ref, keep_ref, give_ref, unit_ref,
):
    group, core = lax.axis_index("group"), lax.axis_index("fsdp")
    count, half = own_mass_ref.shape
    lines = 2 * half // LANES
    weights = received(first_ref)[lines:] / student_temp
    teacher_scales = halves(weights / received(third_ref))
    student_scales = halves(weights / received(second_ref)[lines:])

    def body(first_refs, second_refs):
        for start in range(0, count, TILE):
            here = slice(start, start + TILE)
            for (side, mass_ref, student_ref), teacher_scale, student_scale in zip(
                (first_refs, second_refs), teacher_scales, student_scales
            ):
                teacher = mass_ref[here, :] * scale_ref[here, :] * teacher_scale
                gradient = student_ref[here, :] * student_scale - teacher
                gradient_ref[side, start : start + TILE, :] = gradient.astype(jnp.bfloat16)

    in_core_order(core, (0, own_mass_ref, own_student_ref), (1, other_mass_ref, other_student_ref), body)
    for start in range(0, count, TILE):
        unit_ref[:, start : start + TILE] = units_tile(copy_ref, inverse_ref, start).astype(jnp.bfloat16)
    kept = half // GROUPS
    lanes = pl.ds(pl.multiple_of(group * kept, kept), kept)
    for side, out_ref in enumerate((keep_ref, give_ref)):
        feature = jnp.dot(unit_ref[...], gradient_ref[side, :, lanes], preferred_element_type=jnp.float32)
        out_ref[...] = jnp.transpose(feature).astype(out_ref.dtype)


def weight_kernel(gradient_ref, own_turned_ref, other_turned_ref, inverse_ref, copy_ref, sent_ref, grad_ref):
    chips, rows_each, _ = sent_ref.shape
    count = gradient_ref.shape[1]
    width = own_turned_ref.shape[0]
    kept = width // GROUPS
    own_rows = pl.ds(pl.multiple_of(lax.axis_index("group") * kept, kept), kept)
    for start in range(0, count, TILE):
        here, slot = slice(start, start + TILE), start // TILE
        weight_grad = 0.0
        for side, turned_ref in enumerate((own_turned_ref, other_turned_ref)):
            weight_grad = weight_grad + lax.dot_general(
                turned_ref[...], gradient_ref[side, here, :], (((1,), (1,)), ((), ())), preferred_element_type=jnp.float32
            )
        unit = units_tile(copy_ref, inverse_ref, start)
        dot = jnp.sum(unit * weight_grad, axis=0, keepdims=True)
        grad_ref[slot] = (weight_grad - unit * dot) * inverse_ref[:, here]
        own = grad_ref[slot, own_rows, :].astype(jnp.bfloat16)
        sent_ref[:, :, here] = own.reshape(chips, rows_each, TILE)


def pack_kernel(keep_ref, other_ref, _, sent_ref, packed_ref, sem):
    chips, rows_each, lanes = packed_ref.shape
    width = keep_ref.shape[1]
    total = (keep_ref[...] + other_ref[...].astype(jnp.float32)).astype(jnp.bfloat16)
    total = total.reshape(chips, -1, width)
    for piece in range(lanes // width):
        packed_ref[:, :, piece * width : (piece + 1) * width] = total[:, piece * rows_each : (piece + 1) * rows_each, :]
    copy = pltpu.make_async_copy(packed_ref, sent_ref.at[:, :, pl.ds(sent_ref.shape[2] - lanes, lanes)], sem)
    copy.start()
    copy.wait()


def outputs_kernel(got_ref, student_ref, weight_out, feature_out):
    chips, rows_each, columns = got_ref.shape
    rows, width = student_ref.shape
    pieces = rows // rows_each
    count = columns - pieces * width
    total = got_ref[0, :, count:].astype(jnp.float32)
    for chip in range(1, chips):
        total = total + got_ref[chip, :, count:].astype(jnp.float32)
    total = jnp.concatenate([total[:, piece * width : (piece + 1) * width] for piece in range(pieces)], axis=0)
    hat, length = unit_rows(student_ref[...])
    feature_out[...] = (total - hat * jnp.sum(hat * total, axis=1, keepdims=True)) / length
    for chip in range(chips):
        weight_out[:, chip * count : (chip + 1) * count] = got_ref[chip, :, :count].astype(jnp.float32)


def kernel_body(teacher_feat, student_feat, crop_weight, teacher_v, student_v):
    f32, bf16 = jnp.float32, jnp.bfloat16
    shape = jax.ShapeDtypeStruct
    blocks, fsdp = lax.axis_size("block"), lax.axis_size("fsdp")
    chips = blocks * GROUPS
    members, devices = blocks * fsdp, chips * fsdp
    rows, width = teacher_feat.shape
    crops = rows * devices
    lines = crops // LANES
    kept = teacher_v.shape[1]
    prototypes = kept * fsdp
    count = kept // blocks
    group, block = lax.axis_index("group")[None], lax.axis_index("block")[None]
    core = lax.axis_index("fsdp")[None]
    elements = count * crops
    vmem = pl.BlockSpec(memory_space=pltpu.VMEM)

    def swap(values):
        return lax.ppermute(values, "fsdp", [(0, 1), (1, 0)])

    def share(values):
        return lax.all_to_all(values, GROUP, 0, 0)

    dma = pltpu.SemaphoreType.DMA
    hbm = functools.partial(pltpu.with_memory_space_constraint, memory_space=pltpu.HBM)
    sent = call(
        units_kernel,
        shape((chips, rows, 2 * width), bf16),
        in_specs=[pl.BlockSpec(memory_space=pl.ANY)] * 2,
        scratch_shapes=[pltpu.VMEM((rows, width), bf16), pltpu.VMEM((rows, width), bf16), dma((2,))],
    )(hbm(teacher_feat), hbm(student_feat))
    own = lax.all_to_all(sent, CHIPS, 0, 0)

    device = (core[0] * chips + group[0] * blocks + block[0]) * rows
    weights = lax.dynamic_update_slice(jnp.zeros((crops,), f32), crop_weight.astype(f32), (device,)).reshape(lines, LANES)
    placed = weights
    for move in range(1, GROUPS):
        placed = placed + lax.ppermute(weights, "group", [(at, (at + move) % GROUPS) for at in range(GROUPS)])

    span = 2 * TILE
    spans = count // span
    column = pl.BlockSpec((width, span), lambda step, at: (0, at[0] * spans + step))
    turned = pl.BlockSpec((span, width), lambda step, at: (step, 0))
    line = pl.BlockSpec((1, span), lambda step, at: (0, step))
    teacher_w, student_w, inverse = call(
        directions_kernel,
        (
            pltpu.HBM((count, width), bf16),
            pltpu.HBM((count, width), bf16),
            shape((1, count), f32),
        ),
        flops=12 * count * width,
        moved=8 * count * width,
        grid_spec=pltpu.PrefetchScalarGridSpec(
            num_scalar_prefetch=1,
            grid=(spans,),
            in_specs=[column, column],
            out_specs=[turned, turned, line],
        ),
    )(
        block,
        hbm(teacher_v),
        hbm(student_v),
    )

    own, teacher_w, placed = lax.optimization_barrier((own, teacher_w, placed))
    other = swap(own)
    half = crops // 2
    anyspace = pl.BlockSpec(memory_space=pl.ANY)
    pieces = count // (FETCH * TILE)
    halved = dict(flops=2 * elements * width, exps=elements)
    own_mass, own_student, teacher_w, student_w, own_part, own_turned = call(
        own_kernel,
        (
            shape((count, half), f32),
            shape((count, half), f32),
            shape((count, width), bf16),
            shape((count, width), bf16),
            shape((8, half), f32),
            shape((width, half), bf16),
        ),
        in_specs=[anyspace] * 2 + [vmem],
        scratch_shapes=[dma((2, pieces))],
        **halved,
    )(hbm(teacher_w), hbm(student_w), own)
    other_mass, other_student, sent, student_part, other_turned = call(
        functools.partial(other_kernel, prototypes),
        (
            shape((count, half), f32),
            shape((count, half), f32),
            shape((members, 2 * lines, LANES), bf16),
            shape((lines, LANES), f32),
            shape((width, half), bf16),
        ),
        in_specs=[vmem] * 6,
        **halved,
    )(teacher_w, student_w, other, own_mass, own_part, placed)
    first = share(sent)
    sent = call(
        functools.partial(sweep_kernel, prototypes, crops),
        shape((members, 2 * lines, LANES), bf16),
        flops=4 * elements,
        in_specs=[vmem] * 4,
    )(own_mass, other_mass, first, student_part)
    second = share(sent)
    sent, scale, student_copy = call(
        functools.partial(last_sweep_kernel, prototypes, crops),
        (
            shape((members, lines, LANES), bf16),
            shape((count, 1), f32),
            shape((pieces, width, count // pieces), bf16),
        ),
        flops=4 * elements,
        in_specs=[vmem] * 3 + [anyspace],
        scratch_shapes=[dma((pieces,))],
    )(own_mass, other_mass, second, hbm(student_v))
    third = share(sent)

    gradient, keep, give = call(
        gradient_kernel,
        (shape((2, count, half), bf16), shape((half // GROUPS, width), f32), shape((half // GROUPS, width), bf16)),
        flops=2 * elements * width // GROUPS,
        in_specs=[vmem] * 10,
        scratch_shapes=[pltpu.VMEM((width, count), bf16)],
    )(own_mass, other_mass, own_student, other_student, scale, first, second, third, inverse, student_copy)
    other = swap(give)
    out_rows = width // chips
    per_chip = rows * width // out_rows
    sent = call(
        weight_kernel,
        shape((blocks, out_rows, count + per_chip), bf16),
        flops=2 * elements * width,
        in_specs=[vmem] * 5,
        scratch_shapes=[pltpu.VMEM((count // TILE, width, TILE), f32)],
    )(gradient, own_turned, other_turned, inverse, student_copy)
    sent = call(
        pack_kernel,
        shape((blocks, out_rows, count + per_chip), bf16),
        in_specs=[vmem] * 2 + [anyspace],
        out_specs=anyspace,
        input_output_aliases={2: 0},
        scratch_shapes=[pltpu.VMEM((blocks, out_rows, per_chip), bf16), dma],
    )(keep, other, sent)
    got = lax.all_to_all(sent, "block", 0, 0)
    return call(
        outputs_kernel, (shape((out_rows, kept), f32), shape((rows, width), f32))
    )(got, student_feat)


def solution(mesh):
    dp, fsdp = mesh.shape["dp"], mesh.shape["fsdp"]
    blocks = dp // GROUPS

    def run(teacher_feat, student_feat, crop_weight, teacher_v, student_v):
        crops = teacher_feat.shape[0]
        count = teacher_v.shape[1] // (blocks * fsdp)
        fits = fsdp == 2 and dp == 16 and count % (2 * TILE) == 0 and crops == 1024
        if fits and 8 * count * crops <= KEPT_BYTES:
            grid = Mesh(mesh.devices.reshape(GROUPS, blocks, fsdp), (*CHIPS, "fsdp"))
            body, chips = kernel_body, CHIPS
        else:
            grid, body, chips = mesh, plain_body, ("dp",)
        every = P((*chips, "fsdp"))
        return jax.shard_map(
            body,
            mesh=grid,
            in_specs=(every, every, every, P(None, "fsdp"), P(None, "fsdp")),
            out_specs=(P(chips, "fsdp"), every),
            check_vma=False,
        )(teacher_feat, student_feat, crop_weight, teacher_v, student_v)

    return run
```

```python
import functools
import math

import jax
import jax.numpy as jnp
from jax import lax
from jax.experimental import pallas as pl
from jax.experimental.pallas import tpu as pltpu
from jax.sharding import Mesh
from jax.sharding import PartitionSpec as P

ITERS = 3

teacher_temp = 0.04
student_temp = 0.1
epsilon = 1e-06

GROUPS = 2
TILE = 256
HALF_TILE = 512
FETCH = 2
LANES = 128
VMEM_BYTES = 12 << 20
KEPT_BYTES = 18 << 20

EVERY = ("dp", "fsdp")
CHIPS = ("group", "block")
GROUP = ("block", "fsdp")


def unit_rows(values):
    floats = values.astype(jnp.float32)
    length = jnp.sqrt(jnp.sum(floats * floats, axis=1, keepdims=True) + epsilon)
    return (floats / length, length)


def unit_columns(values):
    floats = values.astype(jnp.float32)
    length = jnp.sqrt(jnp.sum(floats * floats, axis=0, keepdims=True) + epsilon)
    return (floats / length, length)


COPY_BYTES = 1 << 22


def share(values, axes):
    count = lax.axis_size(axes)
    if count * values.size * values.dtype.itemsize > COPY_BYTES:
        return lax.all_gather(values, axes)
    return lax.all_to_all(jnp.broadcast_to(values, (count, *values.shape)), axes, 0, 0)


def add_up(values):
    if lax.axis_size(EVERY) * values.size * values.dtype.itemsize > COPY_BYTES:
        return lax.psum(values, EVERY)
    return jnp.sum(share(values, EVERY), axis=0)


def plain_body(teacher_feat, student_feat, crop_weight, teacher_v, student_v):
    fsdp = lax.axis_size("fsdp")
    devices = lax.axis_size("dp") * fsdp
    own_rows, width = teacher_feat.shape
    crops = own_rows * devices
    block = teacher_v.shape[1] // lax.axis_size("dp")
    prototypes = block * devices
    first = lax.axis_index("dp") * block

    teacher_hat, _ = unit_rows(teacher_feat)
    student_hat, student_len = unit_rows(student_feat)
    units = jnp.concatenate(
        [teacher_hat.astype(jnp.bfloat16), student_hat.astype(jnp.bfloat16)], axis=1
    )
    units = share(share(units, "dp"), "fsdp").reshape(crops, 2 * width)
    teacher_unit, student_unit = units[:, :width], units[:, width:]

    teacher_w, _ = unit_columns(lax.dynamic_slice_in_dim(teacher_v, first, block, 1))
    student_w, student_wlen = unit_columns(lax.dynamic_slice_in_dim(student_v, first, block, 1))
    student_wunit = student_w.astype(jnp.bfloat16)

    mass = jnp.exp(
        jnp.dot(teacher_unit, teacher_w.astype(jnp.bfloat16), preferred_element_type=jnp.float32)
        / teacher_temp
    )
    student_mass = jnp.exp(
        jnp.dot(student_unit, student_wunit, preferred_element_type=jnp.float32) / student_temp
    )
    student_part = jnp.sum(student_mass, axis=1)

    crop_scale = None
    for sweep in range(ITERS):
        scaled = mass if sweep == 0 else mass * crop_scale[:, None]
        proto_scale = 1.0 / (prototypes * jnp.sum(scaled, axis=0))
        crop_part = jnp.sum(mass * proto_scale[None, :], axis=1)
        if sweep == 0:
            placed = jnp.zeros((fsdp, crops // (fsdp * own_rows), own_rows), jnp.float32)
            own = crop_weight.astype(jnp.float32)[None, None]
            spot = (lax.axis_index("fsdp"), lax.axis_index("dp"), 0)
            placed = lax.dynamic_update_slice(placed, own, spot).reshape(crops)
            sums = add_up(jnp.stack([crop_part, student_part, placed]))
            crop_mass, student_total, weights = sums[0], sums[1], sums[2]
        else:
            crop_mass = add_up(crop_part)
        crop_scale = 1.0 / (crops * crop_mass)

    target = crops * (mass * crop_scale[:, None] * proto_scale[None, :])
    student_prob = student_mass / student_total[:, None]
    gradient = ((student_prob - target) * weights[:, None] / student_temp).astype(jnp.bfloat16)
    feature_part = lax.dot_general(
        gradient, student_wunit, (((1,), (1,)), ((), ())), preferred_element_type=jnp.float32
    )
    weight_grad = lax.dot_general(
        student_unit, gradient, (((0,), (0,)), ((), ())), preferred_element_type=jnp.float32
    )
    weight_dot = jnp.sum(student_w * weight_grad, axis=0, keepdims=True)
    grad_block = (weight_grad - student_w * weight_dot) / student_wlen

    feature_sent = feature_part.astype(jnp.bfloat16).reshape(fsdp, -1, own_rows, width)
    feature_sent = jnp.swapaxes(feature_sent, 0, 1).reshape(devices, own_rows, width)
    feature_all = lax.all_to_all(feature_sent, EVERY, 0, 0)
    feature_grad = jnp.sum(feature_all.astype(jnp.float32), axis=0)
    grad_feat = (
        feature_grad - student_hat * jnp.sum(student_hat * feature_grad, axis=1, keepdims=True)
    ) / student_len
    grad_v = lax.all_to_all(grad_block.astype(jnp.bfloat16), "dp", 0, 1, tiled=True)
    return (grad_v.astype(jnp.float32), grad_feat)


def call(kernel, out_shape, flops=0, moved=0, exps=0, **more):
    return pl.pallas_call(
        kernel,
        out_shape=out_shape,
        compiler_params=pltpu.CompilerParams(vmem_limit_bytes=VMEM_BYTES),
        cost_estimate=pl.CostEstimate(flops=flops, bytes_accessed=moved, transcendentals=exps),
        **more,
    )


def units_kernel(teacher_ref, student_ref, sent_ref, teacher_vmem, student_vmem, sems):
    copies = [
        pltpu.make_async_copy(teacher_ref, teacher_vmem, sems.at[0]),
        pltpu.make_async_copy(student_ref, student_vmem, sems.at[1]),
    ]
    for copy in copies:
        copy.start()
    for copy in copies:
        copy.wait()
    width = teacher_vmem.shape[1]
    teacher = unit_rows(teacher_vmem[...])[0].astype(jnp.bfloat16)
    student = unit_rows(student_vmem[...])[0].astype(jnp.bfloat16)
    for chip in range(sent_ref.shape[0]):
        sent_ref[chip, :, :width] = teacher
        sent_ref[chip, :, width:] = student


def directions_kernel(block_ref, teacher_ref, student_ref, teacher_out, student_out, inverse_out):
    teacher, _ = unit_columns(teacher_ref[...])
    teacher_out[...] = jnp.transpose(teacher).astype(jnp.bfloat16)
    student, length = unit_columns(student_ref[...])
    student_out[...] = jnp.transpose(student).astype(jnp.bfloat16)
    inverse_out[...] = 1.0 / length


def exponentials(directions, units, temperature):
    logits = lax.dot_general(
        directions, units, (((1,), (1,)), ((), ())), preferred_element_type=jnp.float32
    )
    return jnp.exp2(logits * (math.log2(math.e) / temperature))


def fold(values):
    rows, lanes = values.shape
    return jnp.sum(values.reshape(rows // 8, 8, lanes), axis=0)


def as_rows(line):
    return jnp.concatenate([line[:, at : at + LANES] for at in range(0, line.shape[1], LANES)], axis=0)


def as_line(rows):
    return jnp.concatenate([rows[at : at + 1, :] for at in range(rows.shape[0])], axis=1)


def in_core_order(core, own, other, body):
    @pl.when(core == 0)
    def _():
        body(own, other)

    @pl.when(core == 1)
    def _():
        body(other, own)


def sums(first, second):
    lines = [as_rows(jnp.sum(total, axis=0, keepdims=True)) for total in (first, second)]
    return jnp.concatenate(lines, axis=0)


def send(sent_ref, *rows):
    values = jnp.concatenate(rows, axis=0).astype(jnp.bfloat16)
    for device in range(sent_ref.shape[0]):
        sent_ref[device] = values


def halves(rows):
    line = as_line(rows)
    half = line.shape[1] // 2
    return line[:, :half], line[:, half:]


def received(got_ref):
    total = got_ref[0].astype(jnp.float32)
    for device in range(1, got_ref.shape[0]):
        total = total + got_ref[device].astype(jnp.float32)
    return total


def units_of(got_ref, width, side):
    chips, rows, _ = got_ref.shape
    return got_ref[:, :, side * width : (side + 1) * width].reshape(chips * rows, width)


def turn(units):
    return jnp.transpose(units.astype(jnp.float32)).astype(jnp.bfloat16)


def own_kernel(teacher_w_ref, student_hbm, got_ref, teacher_ref, student_ref, student_w_ref, part_ref, turned_ref, sems):
    count, width = teacher_w_ref.shape
    span = FETCH * TILE
    copies = []
    for piece in range(count // span):
        rows = pl.ds(piece * span, span)
        copies.append(pltpu.make_async_copy(student_hbm.at[rows], student_w_ref.at[rows], sems.at[piece]))
        copies[-1].start()
    teacher, student = units_of(got_ref, width, 0), units_of(got_ref, width, 1)
    turned_ref[...] = turn(student)
    part = 0.0
    for start in range(0, count, HALF_TILE):
        here = slice(start, start + HALF_TILE)
        teacher_ref[here, :] = exponentials(teacher_w_ref[here, :], teacher, teacher_temp)
        if start % span == 0:
            copies[start // span].wait()
        mass = exponentials(student_w_ref[here, :], student, student_temp)
        student_ref[here, :] = mass
        part = part + fold(mass)
    part_ref[...] = part


def other_kernel(
    prototypes, teacher_w_ref, student_w_ref, got_ref, own_ref, own_part_ref, weight_ref,
    teacher_ref, student_ref, sent_ref, part_ref, turned_ref,
):
    count, width = teacher_w_ref.shape
    core = lax.axis_index("fsdp")
    teacher, student = units_of(got_ref, width, 0), units_of(got_ref, width, 1)
    turned_ref[...] = turn(student)
    own_total = total = part = 0.0
    for start in range(0, count, HALF_TILE):
        here = slice(start, start + HALF_TILE)
        mass = exponentials(teacher_w_ref[here, :], teacher, teacher_temp)
        teacher_ref[here, :] = mass
        own = own_ref[here, :]
        proto = jnp.sum(own + mass, axis=1, keepdims=True)
        scale = 1.0 / (prototypes * proto)
        own_total = own_total + fold(own * scale)
        total = total + fold(mass * scale)
        mass = exponentials(student_w_ref[here, :], student, student_temp)
        student_ref[here, :] = mass
        part = part + fold(mass)

    def finish(first, second):
        send(sent_ref, sums(first[0], second[0]), weight_ref[...])
        part_ref[...] = sums(first[1], second[1])

    in_core_order(core, (own_total, own_part_ref[...]), (total, part), finish)


def sweep(prototypes, crops, first_ref, second_ref, got_ref, scaled_refs=None):
    first_crop, second_crop = halves(1.0 / (crops * received(got_ref)[: crops // LANES]))
    first_total = second_total = 0.0
    for start in range(0, first_ref.shape[0], TILE):
        here = slice(start, start + TILE)
        first, second = first_ref[here, :], second_ref[here, :]
        proto = jnp.sum(first * first_crop + second * second_crop, axis=1, keepdims=True)
        scale = 1.0 / (prototypes * proto)
        first, second = first * scale, second * scale
        if scaled_refs is not None:
            scaled_refs[0][here, :], scaled_refs[1][here, :] = first, second
        first_total = first_total + fold(first)
        second_total = second_total + fold(second)
    return sums(first_total, second_total)


def sweep_kernel(prototypes, crops, own_ref, other_ref, got_ref, part_ref, sent_ref):
    def body(first_ref, second_ref):
        send(sent_ref, sweep(prototypes, crops, first_ref, second_ref, got_ref), part_ref[...])

    in_core_order(lax.axis_index("fsdp"), own_ref, other_ref, body)


def last_sweep_kernel(
    prototypes, crops, own_ref, other_ref, got_ref, directions_ref,
    sent_ref, own_scaled_ref, other_scaled_ref, copy_ref, sems,
):
    pieces, _, span = copy_ref.shape
    copies = []
    for piece in range(pieces):
        columns = pl.ds(pl.multiple_of((lax.axis_index("block") * pieces + piece) * span, span), span)
        copies.append(pltpu.make_async_copy(directions_ref.at[:, columns], copy_ref.at[piece], sems.at[piece]))
        copies[-1].start()

    def body(first_refs, second_refs):
        (first_ref, *scaled_refs), (second_ref, second_scaled_ref) = first_refs, second_refs
        send(sent_ref, sweep(prototypes, crops, first_ref, second_ref, got_ref, (*scaled_refs, second_scaled_ref)))

    in_core_order(lax.axis_index("fsdp"), (own_ref, own_scaled_ref), (other_ref, other_scaled_ref), body)
    for copy in copies:
        copy.wait()


def units_tile(copy_ref, inverse_ref, start):
    span = copy_ref.shape[2]
    at = start % span
    return copy_ref[start // span, :, at : at + TILE].astype(jnp.float32) * inverse_ref[:, start : start + TILE]


def gradient_kernel(
    own_mass_ref, other_mass_ref, own_student_ref, other_student_ref, first_ref, second_ref, third_ref,
    inverse_ref, copy_ref, gradient_ref, keep_ref, give_ref, unit_ref,
):
    group, core = lax.axis_index("group"), lax.axis_index("fsdp")
    count, half = own_mass_ref.shape
    lines = 2 * half // LANES
    weights = received(first_ref)[lines:] / student_temp
    teacher_scales = halves(weights / received(third_ref))
    student_scales = halves(weights / received(second_ref)[lines:])

    def body(first_refs, second_refs):
        for start in range(0, count, TILE):
            here = slice(start, start + TILE)
            for (side, mass_ref, student_ref), teacher_scale, student_scale in zip(
                (first_refs, second_refs), teacher_scales, student_scales
            ):
                gradient = student_ref[here, :] * student_scale - mass_ref[here, :] * teacher_scale
                gradient_ref[side, start : start + TILE, :] = gradient.astype(jnp.bfloat16)

    in_core_order(core, (0, own_mass_ref, own_student_ref), (1, other_mass_ref, other_student_ref), body)
    for start in range(0, count, TILE):
        unit_ref[:, start : start + TILE] = units_tile(copy_ref, inverse_ref, start).astype(jnp.bfloat16)
    kept = half // GROUPS
    lanes = pl.ds(pl.multiple_of(group * kept, kept), kept)
    for side, out_ref in enumerate((keep_ref, give_ref)):
        feature = jnp.dot(unit_ref[...], gradient_ref[side, :, lanes], preferred_element_type=jnp.float32)
        out_ref[...] = jnp.transpose(feature).astype(out_ref.dtype)


def weight_kernel(gradient_ref, own_turned_ref, other_turned_ref, inverse_ref, copy_ref, sent_ref, grad_ref):
    chips, rows_each, _ = sent_ref.shape
    count = gradient_ref.shape[1]
    width = own_turned_ref.shape[0]
    kept = width // GROUPS
    own_rows = pl.ds(pl.multiple_of(lax.axis_index("group") * kept, kept), kept)
    for start in range(0, count, TILE):
        here, slot = slice(start, start + TILE), start // TILE
        weight_grad = 0.0
        for side, turned_ref in enumerate((own_turned_ref, other_turned_ref)):
            weight_grad = weight_grad + lax.dot_general(
                turned_ref[...], gradient_ref[side, here, :], (((1,), (1,)), ((), ())), preferred_element_type=jnp.float32
            )
        unit = units_tile(copy_ref, inverse_ref, start)
        dot = jnp.sum(unit * weight_grad, axis=0, keepdims=True)
        grad_ref[slot] = (weight_grad - unit * dot) * inverse_ref[:, here]
        own = grad_ref[slot, own_rows, :].astype(jnp.bfloat16)
        sent_ref[:, :, here] = own.reshape(chips, rows_each, TILE)


def pack_kernel(keep_ref, other_ref, _, sent_ref, packed_ref, sem):
    chips, rows_each, lanes = packed_ref.shape
    width = keep_ref.shape[1]
    total = (keep_ref[...] + other_ref[...].astype(jnp.float32)).astype(jnp.bfloat16)
    total = total.reshape(chips, -1, width)
    for piece in range(lanes // width):
        packed_ref[:, :, piece * width : (piece + 1) * width] = total[:, piece * rows_each : (piece + 1) * rows_each, :]
    copy = pltpu.make_async_copy(packed_ref, sent_ref.at[:, :, pl.ds(sent_ref.shape[2] - lanes, lanes)], sem)
    copy.start()
    copy.wait()


def outputs_kernel(got_ref, student_ref, weight_out, feature_out, wide_ref, sems):
    chips, rows_each, columns = got_ref.shape
    rows, width = student_ref.shape
    pieces = rows // rows_each
    count = columns - pieces * width
    copies = []
    for chip in range(chips):
        here = slice(chip * count, (chip + 1) * count)
        wide_ref[:, here] = got_ref[chip, :, :count].astype(jnp.float32)
        here = pl.ds(chip * count, count)
        copies.append(pltpu.make_async_copy(wide_ref.at[:, here], weight_out.at[:, here], sems.at[chip]))
        copies[-1].start()
    total = got_ref[0, :, count:].astype(jnp.float32)
    for chip in range(1, chips):
        total = total + got_ref[chip, :, count:].astype(jnp.float32)
    total = jnp.concatenate([total[:, piece * width : (piece + 1) * width] for piece in range(pieces)], axis=0)
    hat, length = unit_rows(student_ref[...])
    feature_out[...] = (total - hat * jnp.sum(hat * total, axis=1, keepdims=True)) / length
    for copy in copies:
        copy.wait()


def kernel_body(teacher_feat, student_feat, crop_weight, teacher_v, student_v):
    f32, bf16 = jnp.float32, jnp.bfloat16
    shape = jax.ShapeDtypeStruct
    blocks, fsdp = lax.axis_size("block"), lax.axis_size("fsdp")
    chips = blocks * GROUPS
    members, devices = blocks * fsdp, chips * fsdp
    rows, width = teacher_feat.shape
    crops = rows * devices
    lines = crops // LANES
    kept = teacher_v.shape[1]
    prototypes = kept * fsdp
    count = kept // blocks
    group, block = lax.axis_index("group")[None], lax.axis_index("block")[None]
    core = lax.axis_index("fsdp")[None]
    elements = count * crops
    vmem = pl.BlockSpec(memory_space=pltpu.VMEM)

    def swap(values):
        return lax.ppermute(values, "fsdp", [(0, 1), (1, 0)])

    def share(values):
        return lax.all_to_all(values, GROUP, 0, 0)

    dma = pltpu.SemaphoreType.DMA
    hbm = functools.partial(pltpu.with_memory_space_constraint, memory_space=pltpu.HBM)
    sent = call(
        units_kernel,
        shape((chips, rows, 2 * width), bf16),
        in_specs=[pl.BlockSpec(memory_space=pl.ANY)] * 2,
        scratch_shapes=[pltpu.VMEM((rows, width), bf16), pltpu.VMEM((rows, width), bf16), dma((2,))],
    )(hbm(teacher_feat), hbm(student_feat))
    own = lax.all_to_all(sent, CHIPS, 0, 0)

    device = (core[0] * chips + group[0] * blocks + block[0]) * rows
    weights = lax.dynamic_update_slice(jnp.zeros((crops,), f32), crop_weight.astype(f32), (device,)).reshape(lines, LANES)
    placed = weights
    for move in range(1, GROUPS):
        placed = placed + lax.ppermute(weights, "group", [(at, (at + move) % GROUPS) for at in range(GROUPS)])

    span = 2 * TILE
    spans = count // span
    column = pl.BlockSpec((width, span), lambda step, at: (0, at[0] * spans + step))
    turned = pl.BlockSpec((span, width), lambda step, at: (step, 0))
    line = pl.BlockSpec((1, span), lambda step, at: (0, step))
    teacher_w, student_w, inverse = call(
        directions_kernel,
        (
            shape((count, width), bf16),
            pltpu.HBM((count, width), bf16),
            shape((1, count), f32),
        ),
        flops=12 * count * width,
        moved=8 * count * width,
        grid_spec=pltpu.PrefetchScalarGridSpec(
            num_scalar_prefetch=1,
            grid=(spans,),
            in_specs=[column, column],
            out_specs=[turned, turned, line],
        ),
    )(
        block,
        hbm(teacher_v),
        hbm(student_v),
    )

    own, teacher_w, placed = lax.optimization_barrier((own, teacher_w, placed))
    other = swap(own)
    half = crops // 2
    anyspace = pl.BlockSpec(memory_space=pl.ANY)
    pieces = count // (FETCH * TILE)
    halved = dict(flops=2 * elements * width, exps=elements)
    own_mass, own_student, student_w, own_part, own_turned = call(
        own_kernel,
        (
            shape((count, half), f32),
            shape((count, half), f32),
            shape((count, width), bf16),
            shape((8, half), f32),
            shape((width, half), bf16),
        ),
        in_specs=[vmem, anyspace, vmem],
        scratch_shapes=[dma((pieces,))],
        **halved,
    )(teacher_w, hbm(student_w), own)
    other_mass, other_student, sent, student_part, other_turned = call(
        functools.partial(other_kernel, prototypes),
        (
            shape((count, half), f32),
            shape((count, half), f32),
            shape((members, 2 * lines, LANES), bf16),
            shape((lines, LANES), f32),
            shape((width, half), bf16),
        ),
        in_specs=[vmem] * 6,
        **halved,
    )(teacher_w, student_w, other, own_mass, own_part, placed)
    first = share(sent)
    sent = call(
        functools.partial(sweep_kernel, prototypes, crops),
        shape((members, 2 * lines, LANES), bf16),
        flops=4 * elements,
        in_specs=[vmem] * 4,
    )(own_mass, other_mass, first, student_part)
    second = share(sent)
    sent, own_scaled, other_scaled, student_copy = call(
        functools.partial(last_sweep_kernel, prototypes, crops),
        (
            shape((members, lines, LANES), bf16),
            shape((count, half), f32),
            shape((count, half), f32),
            shape((pieces, width, count // pieces), bf16),
        ),
        flops=4 * elements,
        in_specs=[vmem] * 3 + [anyspace],
        scratch_shapes=[dma((pieces,))],
    )(own_mass, other_mass, second, hbm(student_v))
    third = share(sent)

    gradient, keep, give = call(
        gradient_kernel,
        (shape((2, count, half), bf16), shape((half // GROUPS, width), f32), shape((half // GROUPS, width), bf16)),
        flops=2 * elements * width // GROUPS,
        in_specs=[vmem] * 9,
        scratch_shapes=[pltpu.VMEM((width, count), bf16)],
    )(own_scaled, other_scaled, own_student, other_student, first, second, third, inverse, student_copy)
    other = swap(give)
    out_rows = width // chips
    per_chip = rows * width // out_rows
    sent = call(
        weight_kernel,
        shape((blocks, out_rows, count + per_chip), bf16),
        flops=2 * elements * width,
        in_specs=[vmem] * 5,
        scratch_shapes=[pltpu.VMEM((count // TILE, width, TILE), f32)],
    )(gradient, own_turned, other_turned, inverse, student_copy)
    sent = call(
        pack_kernel,
        shape((blocks, out_rows, count + per_chip), bf16),
        in_specs=[vmem] * 2 + [anyspace],
        out_specs=anyspace,
        input_output_aliases={2: 0},
        scratch_shapes=[pltpu.VMEM((blocks, out_rows, per_chip), bf16), dma],
    )(keep, other, sent)
    got = lax.all_to_all(sent, "block", 0, 0)
    return call(
        outputs_kernel,
        (shape((out_rows, kept), f32), shape((rows, width), f32)),
        out_specs=[anyspace, vmem],
        scratch_shapes=[pltpu.VMEM((out_rows, kept), f32), dma((blocks,))],
    )(got, student_feat)


def solution(mesh):
    dp, fsdp = mesh.shape["dp"], mesh.shape["fsdp"]
    blocks = dp // GROUPS

    def run(teacher_feat, student_feat, crop_weight, teacher_v, student_v):
        crops = teacher_feat.shape[0]
        count = teacher_v.shape[1] // (blocks * fsdp)
        fits = fsdp == 2 and dp == 16 and count % (2 * TILE) == 0 and crops == 1024
        if fits and 8 * count * crops <= KEPT_BYTES:
            grid = Mesh(mesh.devices.reshape(GROUPS, blocks, fsdp), (*CHIPS, "fsdp"))
            body, chips = kernel_body, CHIPS
        else:
            grid, body, chips = mesh, plain_body, ("dp",)
        every = P((*chips, "fsdp"))
        return jax.shard_map(
            body,
            mesh=grid,
            in_specs=(every, every, every, P(None, "fsdp"), P(None, "fsdp")),
            out_specs=(P(chips, "fsdp"), every),
            check_vma=False,
        )(teacher_feat, student_feat, crop_weight, teacher_v, student_v)

    return run
```

```python
import functools
import math

import jax
import jax.numpy as jnp
from jax import lax
from jax.experimental import pallas as pl
from jax.experimental.pallas import tpu as pltpu
from jax.sharding import Mesh
from jax.sharding import PartitionSpec as P

ITERS = 3

teacher_temp = 0.04
student_temp = 0.1
epsilon = 1e-06

GROUPS = 2
TILE = 256
HALF_TILE = 512
FETCH = 2
LANES = 128
VMEM_BYTES = 12 << 20
KEPT_BYTES = 18 << 20

EVERY = ("dp", "fsdp")
CHIPS = ("group", "block")
GROUP = ("block", "fsdp")


def unit_rows(values):
    floats = values.astype(jnp.float32)
    length = jnp.sqrt(jnp.sum(floats * floats, axis=1, keepdims=True) + epsilon)
    return (floats / length, length)


def unit_columns(values):
    floats = values.astype(jnp.float32)
    length = jnp.sqrt(jnp.sum(floats * floats, axis=0, keepdims=True) + epsilon)
    return (floats / length, length)


COPY_BYTES = 1 << 22


def share(values, axes):
    count = lax.axis_size(axes)
    if count * values.size * values.dtype.itemsize > COPY_BYTES:
        return lax.all_gather(values, axes)
    return lax.all_to_all(jnp.broadcast_to(values, (count, *values.shape)), axes, 0, 0)


def add_up(values):
    if lax.axis_size(EVERY) * values.size * values.dtype.itemsize > COPY_BYTES:
        return lax.psum(values, EVERY)
    return jnp.sum(share(values, EVERY), axis=0)


def plain_body(teacher_feat, student_feat, crop_weight, teacher_v, student_v):
    fsdp = lax.axis_size("fsdp")
    devices = lax.axis_size("dp") * fsdp
    own_rows, width = teacher_feat.shape
    crops = own_rows * devices
    block = teacher_v.shape[1] // lax.axis_size("dp")
    prototypes = block * devices
    first = lax.axis_index("dp") * block

    teacher_hat, _ = unit_rows(teacher_feat)
    student_hat, student_len = unit_rows(student_feat)
    units = jnp.concatenate(
        [teacher_hat.astype(jnp.bfloat16), student_hat.astype(jnp.bfloat16)], axis=1
    )
    units = share(share(units, "dp"), "fsdp").reshape(crops, 2 * width)
    teacher_unit, student_unit = units[:, :width], units[:, width:]

    teacher_w, _ = unit_columns(lax.dynamic_slice_in_dim(teacher_v, first, block, 1))
    student_w, student_wlen = unit_columns(lax.dynamic_slice_in_dim(student_v, first, block, 1))
    student_wunit = student_w.astype(jnp.bfloat16)

    mass = jnp.exp(
        jnp.dot(teacher_unit, teacher_w.astype(jnp.bfloat16), preferred_element_type=jnp.float32)
        / teacher_temp
    )
    student_mass = jnp.exp(
        jnp.dot(student_unit, student_wunit, preferred_element_type=jnp.float32) / student_temp
    )
    student_part = jnp.sum(student_mass, axis=1)

    crop_scale = None
    for sweep in range(ITERS):
        scaled = mass if sweep == 0 else mass * crop_scale[:, None]
        proto_scale = 1.0 / (prototypes * jnp.sum(scaled, axis=0))
        crop_part = jnp.sum(mass * proto_scale[None, :], axis=1)
        if sweep == 0:
            placed = jnp.zeros((fsdp, crops // (fsdp * own_rows), own_rows), jnp.float32)
            own = crop_weight.astype(jnp.float32)[None, None]
            spot = (lax.axis_index("fsdp"), lax.axis_index("dp"), 0)
            placed = lax.dynamic_update_slice(placed, own, spot).reshape(crops)
            sums = add_up(jnp.stack([crop_part, student_part, placed]))
            crop_mass, student_total, weights = sums[0], sums[1], sums[2]
        else:
            crop_mass = add_up(crop_part)
        crop_scale = 1.0 / (crops * crop_mass)

    target = crops * (mass * crop_scale[:, None] * proto_scale[None, :])
    student_prob = student_mass / student_total[:, None]
    gradient = ((student_prob - target) * weights[:, None] / student_temp).astype(jnp.bfloat16)
    feature_part = lax.dot_general(
        gradient, student_wunit, (((1,), (1,)), ((), ())), preferred_element_type=jnp.float32
    )
    weight_grad = lax.dot_general(
        student_unit, gradient, (((0,), (0,)), ((), ())), preferred_element_type=jnp.float32
    )
    weight_dot = jnp.sum(student_w * weight_grad, axis=0, keepdims=True)
    grad_block = (weight_grad - student_w * weight_dot) / student_wlen

    feature_sent = feature_part.astype(jnp.bfloat16).reshape(fsdp, -1, own_rows, width)
    feature_sent = jnp.swapaxes(feature_sent, 0, 1).reshape(devices, own_rows, width)
    feature_all = lax.all_to_all(feature_sent, EVERY, 0, 0)
    feature_grad = jnp.sum(feature_all.astype(jnp.float32), axis=0)
    grad_feat = (
        feature_grad - student_hat * jnp.sum(student_hat * feature_grad, axis=1, keepdims=True)
    ) / student_len
    grad_v = lax.all_to_all(grad_block.astype(jnp.bfloat16), "dp", 0, 1, tiled=True)
    return (grad_v.astype(jnp.float32), grad_feat)


def call(kernel, out_shape, flops=0, moved=0, exps=0, **more):
    return pl.pallas_call(
        kernel,
        out_shape=out_shape,
        compiler_params=pltpu.CompilerParams(vmem_limit_bytes=VMEM_BYTES),
        cost_estimate=pl.CostEstimate(flops=flops, bytes_accessed=moved, transcendentals=exps),
        **more,
    )


def units_kernel(teacher_ref, student_ref, teacher_out, student_out, teacher_vmem, student_vmem, sems):
    copies = [
        pltpu.make_async_copy(teacher_ref, teacher_vmem, sems.at[0]),
        pltpu.make_async_copy(student_ref, student_vmem, sems.at[1]),
    ]
    for copy in copies:
        copy.start()
    for copy in copies:
        copy.wait()
    teacher = unit_rows(teacher_vmem[...])[0].astype(jnp.bfloat16)
    student_out[...] = unit_rows(student_vmem[...])[0].astype(jnp.bfloat16)
    for chip in range(teacher_out.shape[0]):
        teacher_out[chip] = teacher


def directions_kernel(block_ref, teacher_ref, student_ref, teacher_out, student_out, inverse_out):
    teacher, _ = unit_columns(teacher_ref[...])
    teacher_out[...] = jnp.transpose(teacher).astype(jnp.bfloat16)
    student, length = unit_columns(student_ref[...])
    student_out[...] = jnp.transpose(student).astype(jnp.bfloat16)
    inverse_out[...] = 1.0 / length


def exponentials(directions, units, temperature):
    logits = lax.dot_general(
        directions, units, (((1,), (1,)), ((), ())), preferred_element_type=jnp.float32
    )
    return jnp.exp2(logits * (math.log2(math.e) / temperature))


def fold(values):
    rows, lanes = values.shape
    return jnp.sum(values.reshape(rows // 8, 8, lanes), axis=0)


def as_rows(line):
    return jnp.concatenate([line[:, at : at + LANES] for at in range(0, line.shape[1], LANES)], axis=0)


def as_line(rows):
    return jnp.concatenate([rows[at : at + 1, :] for at in range(rows.shape[0])], axis=1)


def in_core_order(core, own, other, body):
    @pl.when(core == 0)
    def _():
        body(own, other)

    @pl.when(core == 1)
    def _():
        body(other, own)


def sums(first, second):
    lines = [as_rows(jnp.sum(total, axis=0, keepdims=True)) for total in (first, second)]
    return jnp.concatenate(lines, axis=0)


def send(sent_ref, *rows):
    values = jnp.concatenate(rows, axis=0).astype(jnp.bfloat16)
    for device in range(sent_ref.shape[0]):
        sent_ref[device] = values


def halves(rows):
    line = as_line(rows)
    half = line.shape[1] // 2
    return line[:, :half], line[:, half:]


def received(got_ref, at=0):
    total = got_ref[0, at:, :].astype(jnp.float32)
    for device in range(1, got_ref.shape[0]):
        total = total + got_ref[device, at:, :].astype(jnp.float32)
    return total


def units_of(got_ref):
    chips, rows, width = got_ref.shape
    return got_ref[...].reshape(chips * rows, width)


def in_chip_order(got_ref, units_ref):
    chips = got_ref.shape[0]
    rows = units_ref.shape[0] // (GROUPS * chips)
    group = lax.axis_index("group")
    for back in range(GROUPS):
        for chip in range(chips):
            at = (((group + GROUPS - back) % GROUPS) * chips + chip) * rows
            here = pl.ds(pl.multiple_of(at, rows), rows)
            units_ref[here, :] = got_ref[chip, back * rows : (back + 1) * rows, :]


def turn(units):
    return jnp.transpose(units.astype(jnp.float32)).astype(jnp.bfloat16)


def own_teacher_kernel(teacher_w_ref, got_ref, mass_ref):
    units = units_of(got_ref)
    for start in range(0, mass_ref.shape[0], HALF_TILE):
        here = slice(start, start + HALF_TILE)
        mass_ref[here, :] = exponentials(teacher_w_ref[here, :], units, teacher_temp)


def other_teacher_kernel(prototypes, teacher_w_ref, got_ref, own_ref, weight_ref, *refs):
    *student_refs, mass_ref, sent_ref = refs
    units = units_of(got_ref)
    own_total = total = 0.0
    for start in range(0, mass_ref.shape[0], HALF_TILE):
        here = slice(start, start + HALF_TILE)
        mass = exponentials(teacher_w_ref[here, :], units, teacher_temp)
        mass_ref[here, :] = mass
        own = own_ref[here, :]
        scale = 1.0 / (prototypes * jnp.sum(own + mass, axis=1, keepdims=True))
        own_total = own_total + fold(own * scale)
        total = total + fold(mass * scale)

    def finish(first, second):
        extra = jnp.concatenate([sums(first, second), weight_ref[...]], axis=1)
        extra = jnp.concatenate([extra, jnp.zeros_like(extra)], axis=0)
        values = jnp.concatenate([ref[...] for ref in student_refs] + [extra.astype(jnp.bfloat16)], axis=0)
        for chip in range(sent_ref.shape[0]):
            sent_ref[chip] = values

    in_core_order(lax.axis_index("fsdp"), own_total, total, finish)


def own_student_kernel(student_hbm, got_ref, mass_ref, student_w_ref, part_ref, turned_ref, units_ref, sems):
    count = student_w_ref.shape[0]
    span = FETCH * TILE
    copies = []
    for piece in range(count // span):
        rows = pl.ds(piece * span, span)
        copies.append(pltpu.make_async_copy(student_hbm.at[rows], student_w_ref.at[rows], sems.at[piece]))
        copies[-1].start()
    in_chip_order(got_ref, units_ref)
    turned_ref[...] = turn(units_ref[...])
    part = 0.0
    for start in range(0, count, HALF_TILE):
        here = slice(start, start + HALF_TILE)
        if start % span == 0:
            copies[start // span].wait()
        mass = exponentials(student_w_ref[here, :], units_ref[...], student_temp)
        mass_ref[here, :] = mass
        part = part + fold(mass)
    part_ref[...] = part


def other_student_kernel(student_w_ref, got_ref, own_part_ref, mass_ref, part_ref, turned_ref, units_ref):
    in_chip_order(got_ref, units_ref)
    turned_ref[...] = turn(units_ref[...])
    part = 0.0
    for start in range(0, student_w_ref.shape[0], HALF_TILE):
        here = slice(start, start + HALF_TILE)
        mass = exponentials(student_w_ref[here, :], units_ref[...], student_temp)
        mass_ref[here, :] = mass
        part = part + fold(mass)

    def finish(first, second):
        part_ref[...] = sums(first, second)

    in_core_order(lax.axis_index("fsdp"), own_part_ref[...], part, finish)


def sweep(prototypes, crops, first_ref, second_ref, received_sums, scaled_refs=None):
    first_crop, second_crop = halves(1.0 / (crops * received_sums))
    first_total = second_total = 0.0
    for start in range(0, first_ref.shape[0], TILE):
        here = slice(start, start + TILE)
        first, second = first_ref[here, :], second_ref[here, :]
        proto = jnp.sum(first * first_crop + second * second_crop, axis=1, keepdims=True)
        scale = 1.0 / (prototypes * proto)
        first, second = first * scale, second * scale
        if scaled_refs is not None:
            scaled_refs[0][here, :], scaled_refs[1][here, :] = first, second
        first_total = first_total + fold(first)
        second_total = second_total + fold(second)
    return sums(first_total, second_total)


def sweep_kernel(prototypes, crops, own_ref, other_ref, got_ref, other_got_ref, part_ref, sent_ref, weight_ref):
    lines = crops // LANES
    at = got_ref.shape[1] - 2 * lines
    extra = received(got_ref, at) + received(other_got_ref, at)
    weight_ref[...] = extra[:lines, LANES:]

    def body(first_ref, second_ref):
        send(sent_ref, sweep(prototypes, crops, first_ref, second_ref, extra[:lines, :LANES]), part_ref[...])

    in_core_order(lax.axis_index("fsdp"), own_ref, other_ref, body)


def last_sweep_kernel(
    prototypes, crops, own_ref, other_ref, got_ref, directions_ref,
    sent_ref, own_scaled_ref, other_scaled_ref, copy_ref, sems,
):
    pieces, _, span = copy_ref.shape
    copies = []
    for piece in range(pieces):
        columns = pl.ds(pl.multiple_of((lax.axis_index("block") * pieces + piece) * span, span), span)
        copies.append(pltpu.make_async_copy(directions_ref.at[:, columns], copy_ref.at[piece], sems.at[piece]))
        copies[-1].start()

    total = received(got_ref)[: crops // LANES]

    def body(first_refs, second_refs):
        (first_ref, *scaled_refs), (second_ref, second_scaled_ref) = first_refs, second_refs
        send(sent_ref, sweep(prototypes, crops, first_ref, second_ref, total, (*scaled_refs, second_scaled_ref)))

    in_core_order(lax.axis_index("fsdp"), (own_ref, own_scaled_ref), (other_ref, other_scaled_ref), body)
    for copy in copies:
        copy.wait()


def units_tile(copy_ref, inverse_ref, start):
    span = copy_ref.shape[2]
    at = start % span
    return copy_ref[start // span, :, at : at + TILE].astype(jnp.float32) * inverse_ref[:, start : start + TILE]


def gradient_kernel(
    own_mass_ref, other_mass_ref, own_student_ref, other_student_ref, weight_ref, second_ref, third_ref,
    inverse_ref, copy_ref, gradient_ref, keep_ref, give_ref, unit_ref,
):
    group, core = lax.axis_index("group"), lax.axis_index("fsdp")
    count, half = own_mass_ref.shape
    lines = 2 * half // LANES
    weights = weight_ref[...] / student_temp
    teacher_scales = halves(weights / received(third_ref))
    student_scales = halves(weights / received(second_ref)[lines:])

    def body(first_refs, second_refs):
        for start in range(0, count, TILE):
            here = slice(start, start + TILE)
            for (side, mass_ref, student_ref), teacher_scale, student_scale in zip(
                (first_refs, second_refs), teacher_scales, student_scales
            ):
                gradient = student_ref[here, :] * student_scale - mass_ref[here, :] * teacher_scale
                gradient_ref[side, start : start + TILE, :] = gradient.astype(jnp.bfloat16)

    in_core_order(core, (0, own_mass_ref, own_student_ref), (1, other_mass_ref, other_student_ref), body)
    for start in range(0, count, TILE):
        unit_ref[:, start : start + TILE] = units_tile(copy_ref, inverse_ref, start).astype(jnp.bfloat16)
    kept = half // GROUPS
    lanes = pl.ds(pl.multiple_of(group * kept, kept), kept)
    for side, out_ref in enumerate((keep_ref, give_ref)):
        feature = jnp.dot(unit_ref[...], gradient_ref[side, :, lanes], preferred_element_type=jnp.float32)
        out_ref[...] = jnp.transpose(feature).astype(out_ref.dtype)


def weight_kernel(gradient_ref, own_turned_ref, other_turned_ref, inverse_ref, copy_ref, sent_ref, grad_ref):
    chips, rows_each, _ = sent_ref.shape
    count = gradient_ref.shape[1]
    width = own_turned_ref.shape[0]
    kept = width // GROUPS
    own_rows = pl.ds(pl.multiple_of(lax.axis_index("group") * kept, kept), kept)
    for start in range(0, count, TILE):
        here, slot = slice(start, start + TILE), start // TILE
        weight_grad = 0.0
        for side, turned_ref in enumerate((own_turned_ref, other_turned_ref)):
            weight_grad = weight_grad + lax.dot_general(
                turned_ref[...], gradient_ref[side, here, :], (((1,), (1,)), ((), ())), preferred_element_type=jnp.float32
            )
        unit = units_tile(copy_ref, inverse_ref, start)
        dot = jnp.sum(unit * weight_grad, axis=0, keepdims=True)
        grad_ref[slot] = (weight_grad - unit * dot) * inverse_ref[:, here]
        own = grad_ref[slot, own_rows, :].astype(jnp.bfloat16)
        sent_ref[:, :, here] = own.reshape(chips, rows_each, TILE)


def pack_kernel(keep_ref, other_ref, _, sent_ref, packed_ref, sem):
    chips, rows_each, lanes = packed_ref.shape
    width = keep_ref.shape[1]
    total = (keep_ref[...] + other_ref[...].astype(jnp.float32)).astype(jnp.bfloat16)
    total = total.reshape(chips, -1, width)
    for piece in range(lanes // width):
        packed_ref[:, :, piece * width : (piece + 1) * width] = total[:, piece * rows_each : (piece + 1) * rows_each, :]
    copy = pltpu.make_async_copy(packed_ref, sent_ref.at[:, :, pl.ds(sent_ref.shape[2] - lanes, lanes)], sem)
    copy.start()
    copy.wait()


def outputs_kernel(got_ref, student_ref, weight_out, feature_out):
    chips, rows_each, columns = got_ref.shape
    rows, width = student_ref.shape
    pieces = rows // rows_each
    count = columns - pieces * width
    total = got_ref[0, :, count:].astype(jnp.float32)
    for chip in range(1, chips):
        total = total + got_ref[chip, :, count:].astype(jnp.float32)
    total = jnp.concatenate([total[:, piece * width : (piece + 1) * width] for piece in range(pieces)], axis=0)
    hat, length = unit_rows(student_ref[...])
    feature_out[...] = (total - hat * jnp.sum(hat * total, axis=1, keepdims=True)) / length
    for chip in range(chips):
        weight_out[:, chip * count : (chip + 1) * count] = got_ref[chip, :, :count].astype(jnp.float32)


def kernel_body(teacher_feat, student_feat, crop_weight, teacher_v, student_v):
    f32, bf16 = jnp.float32, jnp.bfloat16
    shape = jax.ShapeDtypeStruct
    blocks, fsdp = lax.axis_size("block"), lax.axis_size("fsdp")
    chips = blocks * GROUPS
    members, devices = blocks * fsdp, chips * fsdp
    rows, width = teacher_feat.shape
    crops = rows * devices
    lines = crops // LANES
    kept = teacher_v.shape[1]
    prototypes = kept * fsdp
    count = kept // blocks
    group, block = lax.axis_index("group")[None], lax.axis_index("block")[None]
    core = lax.axis_index("fsdp")[None]
    elements = count * crops
    vmem = pl.BlockSpec(memory_space=pltpu.VMEM)

    def swap(values):
        return lax.ppermute(values, "fsdp", [(0, 1), (1, 0)])

    def share(values):
        return lax.all_to_all(values, GROUP, 0, 0)

    dma = pltpu.SemaphoreType.DMA
    hbm = functools.partial(pltpu.with_memory_space_constraint, memory_space=pltpu.HBM)
    teacher_sent, student_unit = call(
        units_kernel,
        (shape((chips, rows, width), bf16), shape((rows, width), bf16)),
        in_specs=[pl.BlockSpec(memory_space=pl.ANY)] * 2,
        scratch_shapes=[pltpu.VMEM((rows, width), bf16), pltpu.VMEM((rows, width), bf16), dma((2,))],
    )(hbm(teacher_feat), hbm(student_feat))
    teacher_own = lax.all_to_all(teacher_sent, CHIPS, 0, 0)

    def groups_back(values, back):
        return lax.ppermute(values, "group", [(at, (at + back) % GROUPS) for at in range(GROUPS)])

    device = (core[0] * chips + group[0] * blocks + block[0]) * rows
    weights = lax.dynamic_update_slice(jnp.zeros((crops,), f32), crop_weight.astype(f32), (device,)).reshape(lines, LANES)
    placed = weights
    for move in range(1, GROUPS):
        placed = placed + groups_back(weights, move)
    student_units = [student_unit] + [groups_back(student_unit, back) for back in range(1, GROUPS)]

    span = 2 * TILE
    spans = count // span
    column = pl.BlockSpec((width, span), lambda step, at: (0, at[0] * spans + step))
    turned = pl.BlockSpec((span, width), lambda step, at: (step, 0))
    line = pl.BlockSpec((1, span), lambda step, at: (0, step))
    teacher_w, student_w, inverse = call(
        directions_kernel,
        (
            shape((count, width), bf16),
            pltpu.HBM((count, width), bf16),
            shape((1, count), f32),
        ),
        flops=12 * count * width,
        moved=8 * count * width,
        grid_spec=pltpu.PrefetchScalarGridSpec(
            num_scalar_prefetch=1,
            grid=(spans,),
            in_specs=[column, column],
            out_specs=[turned, turned, line],
        ),
    )(
        block,
        hbm(teacher_v),
        hbm(student_v),
    )

    teacher_own, teacher_w, placed, student_units = lax.optimization_barrier(
        (teacher_own, teacher_w, placed, student_units)
    )
    teacher_other = swap(teacher_own)
    half = crops // 2
    anyspace = pl.BlockSpec(memory_space=pl.ANY)
    pieces = count // (FETCH * TILE)
    quarter = dict(flops=elements * width, exps=elements // 2)
    own_mass = call(own_teacher_kernel, shape((count, half), f32), **quarter)(teacher_w, teacher_own)
    other_mass, sent = call(
        functools.partial(other_teacher_kernel, prototypes),
        (shape((count, half), f32), shape((blocks, GROUPS * rows + 2 * lines, width), bf16)),
        **quarter,
    )(teacher_w, teacher_other, own_mass, placed, *student_units)
    first = lax.all_to_all(sent, "block", 0, 0)
    first_other = swap(first)
    units = pltpu.VMEM((half, width), bf16)
    own_student, student_w, own_part, own_turned = call(
        own_student_kernel,
        (shape((count, half), f32), shape((count, width), bf16), shape((8, half), f32), shape((width, half), bf16)),
        in_specs=[anyspace, vmem],
        scratch_shapes=[units, dma((pieces,))],
        **quarter,
    )(hbm(student_w), first)
    other_student, student_part, other_turned = call(
        other_student_kernel,
        (shape((count, half), f32), shape((lines, LANES), f32), shape((width, half), bf16)),
        scratch_shapes=[units],
        **quarter,
    )(student_w, first_other, own_part)
    sent, weights = call(
        functools.partial(sweep_kernel, prototypes, crops),
        (shape((members, 2 * lines, LANES), bf16), shape((lines, LANES), f32)),
        flops=4 * elements,
    )(own_mass, other_mass, first, first_other, student_part)
    second = share(sent)
    sent, own_scaled, other_scaled, student_copy = call(
        functools.partial(last_sweep_kernel, prototypes, crops),
        (
            shape((members, lines, LANES), bf16),
            shape((count, half), f32),
            shape((count, half), f32),
            shape((pieces, width, count // pieces), bf16),
        ),
        flops=4 * elements,
        in_specs=[vmem] * 3 + [anyspace],
        scratch_shapes=[dma((pieces,))],
    )(own_mass, other_mass, second, hbm(student_v))
    third = share(sent)

    gradient, keep, give = call(
        gradient_kernel,
        (shape((2, count, half), bf16), shape((half // GROUPS, width), f32), shape((half // GROUPS, width), bf16)),
        flops=2 * elements * width // GROUPS,
        in_specs=[vmem] * 9,
        scratch_shapes=[pltpu.VMEM((width, count), bf16)],
    )(own_scaled, other_scaled, own_student, other_student, weights, second, third, inverse, student_copy)
    other = swap(give)
    out_rows = width // chips
    per_chip = rows * width // out_rows
    sent = call(
        weight_kernel,
        shape((blocks, out_rows, count + per_chip), bf16),
        flops=2 * elements * width,
        in_specs=[vmem] * 5,
        scratch_shapes=[pltpu.VMEM((count // TILE, width, TILE), f32)],
    )(gradient, own_turned, other_turned, inverse, student_copy)
    sent = call(
        pack_kernel,
        shape((blocks, out_rows, count + per_chip), bf16),
        in_specs=[vmem] * 2 + [anyspace],
        out_specs=anyspace,
        input_output_aliases={2: 0},
        scratch_shapes=[pltpu.VMEM((blocks, out_rows, per_chip), bf16), dma],
    )(keep, other, sent)
    got = lax.all_to_all(sent, "block", 0, 0)
    return call(
        outputs_kernel, (shape((out_rows, kept), f32), shape((rows, width), f32))
    )(got, student_feat)


def solution(mesh):
    dp, fsdp = mesh.shape["dp"], mesh.shape["fsdp"]
    blocks = dp // GROUPS

    def run(teacher_feat, student_feat, crop_weight, teacher_v, student_v):
        crops = teacher_feat.shape[0]
        count = teacher_v.shape[1] // (blocks * fsdp)
        fits = fsdp == 2 and dp == 16 and count % (2 * TILE) == 0 and crops == 1024
        if fits and 8 * count * crops <= KEPT_BYTES:
            grid = Mesh(mesh.devices.reshape(GROUPS, blocks, fsdp), (*CHIPS, "fsdp"))
            body, chips = kernel_body, CHIPS
        else:
            grid, body, chips = mesh, plain_body, ("dp",)
        every = P((*chips, "fsdp"))
        return jax.shard_map(
            body,
            mesh=grid,
            in_specs=(every, every, every, P(None, "fsdp"), P(None, "fsdp")),
            out_specs=(P(chips, "fsdp"), every),
            check_vma=False,
        )(teacher_feat, student_feat, crop_weight, teacher_v, student_v)

    return run
```

```python
import functools
import math

import jax
import jax.numpy as jnp
from jax import lax
from jax.experimental import pallas as pl
from jax.experimental.pallas import tpu as pltpu
from jax.sharding import Mesh
from jax.sharding import PartitionSpec as P

ITERS = 3

teacher_temp = 0.04
student_temp = 0.1
epsilon = 1e-06

GROUPS = 2
TILE = 256
HALF_TILE = 512
FETCH = 2
LANES = 128
VMEM_BYTES = 12 << 20
KEPT_BYTES = 18 << 20

EVERY = ("dp", "fsdp")
CHIPS = ("group", "block")
GROUP = ("block", "fsdp")


def unit_rows(values):
    floats = values.astype(jnp.float32)
    length = jnp.sqrt(jnp.sum(floats * floats, axis=1, keepdims=True) + epsilon)
    return (floats / length, length)


def unit_columns(values):
    floats = values.astype(jnp.float32)
    length = jnp.sqrt(jnp.sum(floats * floats, axis=0, keepdims=True) + epsilon)
    return (floats / length, length)


COPY_BYTES = 1 << 22


def share(values, axes):
    count = lax.axis_size(axes)
    if count * values.size * values.dtype.itemsize > COPY_BYTES:
        return lax.all_gather(values, axes)
    return lax.all_to_all(jnp.broadcast_to(values, (count, *values.shape)), axes, 0, 0)


def add_up(values):
    if lax.axis_size(EVERY) * values.size * values.dtype.itemsize > COPY_BYTES:
        return lax.psum(values, EVERY)
    return jnp.sum(share(values, EVERY), axis=0)


def plain_body(teacher_feat, student_feat, crop_weight, teacher_v, student_v):
    fsdp = lax.axis_size("fsdp")
    devices = lax.axis_size("dp") * fsdp
    own_rows, width = teacher_feat.shape
    crops = own_rows * devices
    block = teacher_v.shape[1] // lax.axis_size("dp")
    prototypes = block * devices
    first = lax.axis_index("dp") * block

    teacher_hat, _ = unit_rows(teacher_feat)
    student_hat, student_len = unit_rows(student_feat)
    units = jnp.concatenate(
        [teacher_hat.astype(jnp.bfloat16), student_hat.astype(jnp.bfloat16)], axis=1
    )
    units = share(share(units, "dp"), "fsdp").reshape(crops, 2 * width)
    teacher_unit, student_unit = units[:, :width], units[:, width:]

    teacher_w, _ = unit_columns(lax.dynamic_slice_in_dim(teacher_v, first, block, 1))
    student_w, student_wlen = unit_columns(lax.dynamic_slice_in_dim(student_v, first, block, 1))
    student_wunit = student_w.astype(jnp.bfloat16)

    mass = jnp.exp(
        jnp.dot(teacher_unit, teacher_w.astype(jnp.bfloat16), preferred_element_type=jnp.float32)
        / teacher_temp
    )
    student_mass = jnp.exp(
        jnp.dot(student_unit, student_wunit, preferred_element_type=jnp.float32) / student_temp
    )
    student_part = jnp.sum(student_mass, axis=1)

    crop_scale = None
    for sweep in range(ITERS):
        scaled = mass if sweep == 0 else mass * crop_scale[:, None]
        proto_scale = 1.0 / (prototypes * jnp.sum(scaled, axis=0))
        crop_part = jnp.sum(mass * proto_scale[None, :], axis=1)
        if sweep == 0:
            placed = jnp.zeros((fsdp, crops // (fsdp * own_rows), own_rows), jnp.float32)
            own = crop_weight.astype(jnp.float32)[None, None]
            spot = (lax.axis_index("fsdp"), lax.axis_index("dp"), 0)
            placed = lax.dynamic_update_slice(placed, own, spot).reshape(crops)
            sums = add_up(jnp.stack([crop_part, student_part, placed]))
            crop_mass, student_total, weights = sums[0], sums[1], sums[2]
        else:
            crop_mass = add_up(crop_part)
        crop_scale = 1.0 / (crops * crop_mass)

    target = crops * (mass * crop_scale[:, None] * proto_scale[None, :])
    student_prob = student_mass / student_total[:, None]
    gradient = ((student_prob - target) * weights[:, None] / student_temp).astype(jnp.bfloat16)
    feature_part = lax.dot_general(
        gradient, student_wunit, (((1,), (1,)), ((), ())), preferred_element_type=jnp.float32
    )
    weight_grad = lax.dot_general(
        student_unit, gradient, (((0,), (0,)), ((), ())), preferred_element_type=jnp.float32
    )
    weight_dot = jnp.sum(student_w * weight_grad, axis=0, keepdims=True)
    grad_block = (weight_grad - student_w * weight_dot) / student_wlen

    feature_sent = feature_part.astype(jnp.bfloat16).reshape(fsdp, -1, own_rows, width)
    feature_sent = jnp.swapaxes(feature_sent, 0, 1).reshape(devices, own_rows, width)
    feature_all = lax.all_to_all(feature_sent, EVERY, 0, 0)
    feature_grad = jnp.sum(feature_all.astype(jnp.float32), axis=0)
    grad_feat = (
        feature_grad - student_hat * jnp.sum(student_hat * feature_grad, axis=1, keepdims=True)
    ) / student_len
    grad_v = lax.all_to_all(grad_block.astype(jnp.bfloat16), "dp", 0, 1, tiled=True)
    return (grad_v.astype(jnp.float32), grad_feat)


def call(kernel, out_shape, flops=0, moved=0, exps=0, **more):
    return pl.pallas_call(
        kernel,
        out_shape=out_shape,
        compiler_params=pltpu.CompilerParams(vmem_limit_bytes=VMEM_BYTES),
        cost_estimate=pl.CostEstimate(flops=flops, bytes_accessed=moved, transcendentals=exps),
        **more,
    )


def units_kernel(teacher_ref, student_ref, teacher_out, student_out, teacher_vmem, student_vmem, sems):
    copies = [
        pltpu.make_async_copy(teacher_ref, teacher_vmem, sems.at[0]),
        pltpu.make_async_copy(student_ref, student_vmem, sems.at[1]),
    ]
    for copy in copies:
        copy.start()
    for copy in copies:
        copy.wait()
    teacher = unit_rows(teacher_vmem[...])[0].astype(jnp.bfloat16)
    student_out[...] = unit_rows(student_vmem[...])[0].astype(jnp.bfloat16)
    for chip in range(teacher_out.shape[0]):
        teacher_out[chip] = teacher


def placed_weights(student_refs, lines, rows, chips):
    group, block = lax.axis_index("group"), lax.axis_index("block")
    line = lax.broadcasted_iota(jnp.int32, (lines, LANES), 0)
    part = lax.broadcasted_iota(jnp.int32, (lines, LANES), 1) // rows
    each = LANES // rows
    placed = jnp.zeros((lines, LANES), jnp.float32)
    for back, ref in enumerate(student_refs):
        at = lax.axis_index("fsdp") * chips * GROUPS + ((group + GROUPS - back) % GROUPS) * chips + block
        weights = ref[rows:, :rows].astype(jnp.float32)[0:1, :]
        weights = jnp.concatenate([weights] * each, axis=1)
        here = (line == at // each) & (part == at % each)
        placed = placed + jnp.where(here, jnp.broadcast_to(weights, (lines, LANES)), 0.0)
    return placed


def directions_kernel(block_ref, teacher_ref, student_ref, teacher_out, student_out, inverse_out):
    teacher, _ = unit_columns(teacher_ref[...])
    teacher_out[...] = jnp.transpose(teacher).astype(jnp.bfloat16)
    student, length = unit_columns(student_ref[...])
    student_out[...] = jnp.transpose(student).astype(jnp.bfloat16)
    inverse_out[...] = 1.0 / length


def exponentials(directions, units, temperature):
    logits = lax.dot_general(
        directions, units, (((1,), (1,)), ((), ())), preferred_element_type=jnp.float32
    )
    return jnp.exp2(logits * (math.log2(math.e) / temperature))


def fold(values):
    rows, lanes = values.shape
    return jnp.sum(values.reshape(rows // 8, 8, lanes), axis=0)


def as_rows(line):
    return jnp.concatenate([line[:, at : at + LANES] for at in range(0, line.shape[1], LANES)], axis=0)


def as_line(rows):
    return jnp.concatenate([rows[at : at + 1, :] for at in range(rows.shape[0])], axis=1)


def in_core_order(core, own, other, body):
    @pl.when(core == 0)
    def _():
        body(own, other)

    @pl.when(core == 1)
    def _():
        body(other, own)


def sums(first, second):
    lines = [as_rows(jnp.sum(total, axis=0, keepdims=True)) for total in (first, second)]
    return jnp.concatenate(lines, axis=0)


def send(sent_ref, *rows):
    values = jnp.concatenate(rows, axis=0).astype(jnp.bfloat16)
    for device in range(sent_ref.shape[0]):
        sent_ref[device] = values


def halves(rows):
    line = as_line(rows)
    half = line.shape[1] // 2
    return line[:, :half], line[:, half:]


def received(got_ref, at=0):
    total = got_ref[0, at:, :].astype(jnp.float32)
    for device in range(1, got_ref.shape[0]):
        total = total + got_ref[device, at:, :].astype(jnp.float32)
    return total


def units_of(got_ref):
    chips, rows, width = got_ref.shape
    return got_ref[...].reshape(chips * rows, width)


def in_chip_order(got_ref, units_ref):
    chips = got_ref.shape[0]
    rows = units_ref.shape[0] // (GROUPS * chips)
    group = lax.axis_index("group")
    for back in range(GROUPS):
        for chip in range(chips):
            at = (((group + GROUPS - back) % GROUPS) * chips + chip) * rows
            here = pl.ds(pl.multiple_of(at, rows), rows)
            units_ref[here, :] = got_ref[chip, back * rows : (back + 1) * rows, :]


def turn(units):
    return jnp.transpose(units.astype(jnp.float32)).astype(jnp.bfloat16)


def own_teacher_kernel(teacher_w_ref, got_ref, mass_ref):
    units = units_of(got_ref)
    for start in range(0, mass_ref.shape[0], HALF_TILE):
        here = slice(start, start + HALF_TILE)
        mass_ref[here, :] = exponentials(teacher_w_ref[here, :], units, teacher_temp)


def other_teacher_kernel(prototypes, teacher_w_ref, got_ref, own_ref, student_hbm, *refs):
    *student_refs, mass_ref, sent_ref, student_w_ref, sem = refs
    copy = pltpu.make_async_copy(student_hbm, student_w_ref, sem)
    copy.start()
    chips, rows = sent_ref.shape[0], got_ref.shape[1]
    placed = placed_weights(student_refs, 2 * own_ref.shape[1] // LANES, rows, chips)
    units = units_of(got_ref)
    own_total = total = 0.0
    for start in range(0, mass_ref.shape[0], HALF_TILE):
        here = slice(start, start + HALF_TILE)
        mass = exponentials(teacher_w_ref[here, :], units, teacher_temp)
        mass_ref[here, :] = mass
        own = own_ref[here, :]
        scale = 1.0 / (prototypes * jnp.sum(own + mass, axis=1, keepdims=True))
        own_total = own_total + fold(own * scale)
        total = total + fold(mass * scale)

    def finish(first, second):
        extra = jnp.concatenate([sums(first, second), placed], axis=1)
        extra = jnp.concatenate([extra, jnp.zeros_like(extra)], axis=0)
        values = jnp.concatenate([ref[:rows, :] for ref in student_refs] + [extra.astype(jnp.bfloat16)], axis=0)
        for chip in range(sent_ref.shape[0]):
            sent_ref[chip] = values

    in_core_order(lax.axis_index("fsdp"), own_total, total, finish)
    copy.wait()


def own_student_kernel(student_w_ref, got_ref, mass_ref, part_ref, turned_ref, units_ref):
    count = student_w_ref.shape[0]
    in_chip_order(got_ref, units_ref)
    turned_ref[...] = turn(units_ref[...])
    part = 0.0
    for start in range(0, count, HALF_TILE):
        here = slice(start, start + HALF_TILE)
        mass = exponentials(student_w_ref[here, :], units_ref[...], student_temp)
        mass_ref[here, :] = mass
        part = part + fold(mass)
    part_ref[...] = part


def other_student_kernel(student_w_ref, got_ref, own_part_ref, mass_ref, part_ref, turned_ref, units_ref):
    in_chip_order(got_ref, units_ref)
    turned_ref[...] = turn(units_ref[...])
    part = 0.0
    for start in range(0, student_w_ref.shape[0], HALF_TILE):
        here = slice(start, start + HALF_TILE)
        mass = exponentials(student_w_ref[here, :], units_ref[...], student_temp)
        mass_ref[here, :] = mass
        part = part + fold(mass)

    def finish(first, second):
        part_ref[...] = sums(first, second)

    in_core_order(lax.axis_index("fsdp"), own_part_ref[...], part, finish)


def sweep(prototypes, crops, first_ref, second_ref, received_sums, scaled_refs=None):
    first_crop, second_crop = halves(1.0 / (crops * received_sums))
    first_total = second_total = 0.0
    for start in range(0, first_ref.shape[0], TILE):
        here = slice(start, start + TILE)
        first, second = first_ref[here, :], second_ref[here, :]
        proto = jnp.sum(first * first_crop + second * second_crop, axis=1, keepdims=True)
        scale = 1.0 / (prototypes * proto)
        first, second = first * scale, second * scale
        if scaled_refs is not None:
            scaled_refs[0][here, :], scaled_refs[1][here, :] = first, second
        first_total = first_total + fold(first)
        second_total = second_total + fold(second)
    return sums(first_total, second_total)


def sweep_kernel(prototypes, crops, own_ref, other_ref, got_ref, other_got_ref, part_ref, sent_ref, weight_ref):
    lines = crops // LANES
    at = got_ref.shape[1] - 2 * lines
    extra = received(got_ref, at) + received(other_got_ref, at)
    weight_ref[...] = extra[:lines, LANES:]

    def body(first_ref, second_ref):
        send(sent_ref, sweep(prototypes, crops, first_ref, second_ref, extra[:lines, :LANES]), part_ref[...])

    in_core_order(lax.axis_index("fsdp"), own_ref, other_ref, body)


def last_sweep_kernel(
    prototypes, crops, own_ref, other_ref, got_ref, directions_ref,
    sent_ref, own_scaled_ref, other_scaled_ref, copy_ref, sems,
):
    pieces, _, span = copy_ref.shape
    copies = []
    for piece in range(pieces):
        columns = pl.ds(pl.multiple_of((lax.axis_index("block") * pieces + piece) * span, span), span)
        copies.append(pltpu.make_async_copy(directions_ref.at[:, columns], copy_ref.at[piece], sems.at[piece]))
        copies[-1].start()

    total = received(got_ref)[: crops // LANES]

    def body(first_refs, second_refs):
        (first_ref, *scaled_refs), (second_ref, second_scaled_ref) = first_refs, second_refs
        sent = sweep(prototypes, crops, first_ref, second_ref, total, (*scaled_refs, second_scaled_ref))
        send(sent_ref, sent, jnp.zeros_like(sent))

    in_core_order(lax.axis_index("fsdp"), (own_ref, own_scaled_ref), (other_ref, other_scaled_ref), body)
    for copy in copies:
        copy.wait()


def units_tile(copy_ref, inverse_ref, start):
    span = copy_ref.shape[2]
    at = start % span
    return copy_ref[start // span, :, at : at + TILE].astype(jnp.float32) * inverse_ref[:, start : start + TILE]


def gradient_kernel(
    own_mass_ref, other_mass_ref, own_student_ref, other_student_ref, weight_ref, second_ref, third_ref,
    inverse_ref, copy_ref, gradient_ref, keep_ref, give_ref, unit_ref,
):
    group, core = lax.axis_index("group"), lax.axis_index("fsdp")
    count, half = own_mass_ref.shape
    lines = 2 * half // LANES
    weights = weight_ref[...] / student_temp
    teacher_scales = halves(weights / received(third_ref)[:lines])
    student_scales = halves(weights / received(second_ref)[lines:])

    def body(first_refs, second_refs):
        for start in range(0, count, TILE):
            here = slice(start, start + TILE)
            for (side, mass_ref, student_ref), teacher_scale, student_scale in zip(
                (first_refs, second_refs), teacher_scales, student_scales
            ):
                gradient = student_ref[here, :] * student_scale - mass_ref[here, :] * teacher_scale
                gradient_ref[side, start : start + TILE, :] = gradient.astype(jnp.bfloat16)

    in_core_order(core, (0, own_mass_ref, own_student_ref), (1, other_mass_ref, other_student_ref), body)
    for start in range(0, count, TILE):
        unit_ref[:, start : start + TILE] = units_tile(copy_ref, inverse_ref, start).astype(jnp.bfloat16)
    kept = half // GROUPS
    lanes = pl.ds(pl.multiple_of(group * kept, kept), kept)
    for side, out_ref in enumerate((keep_ref, give_ref)):
        feature = jnp.dot(unit_ref[...], gradient_ref[side, :, lanes], preferred_element_type=jnp.float32)
        out_ref[...] = jnp.transpose(feature).astype(out_ref.dtype)


def weight_kernel(gradient_ref, own_turned_ref, other_turned_ref, inverse_ref, copy_ref, sent_ref, grad_ref):
    chips, rows_each, _ = sent_ref.shape
    count = gradient_ref.shape[1]
    width = own_turned_ref.shape[0]
    kept = width // GROUPS
    own_rows = pl.ds(pl.multiple_of(lax.axis_index("group") * kept, kept), kept)
    for start in range(0, count, TILE):
        here, slot = slice(start, start + TILE), start // TILE
        weight_grad = 0.0
        for side, turned_ref in enumerate((own_turned_ref, other_turned_ref)):
            weight_grad = weight_grad + lax.dot_general(
                turned_ref[...], gradient_ref[side, here, :], (((1,), (1,)), ((), ())), preferred_element_type=jnp.float32
            )
        unit = units_tile(copy_ref, inverse_ref, start)
        dot = jnp.sum(unit * weight_grad, axis=0, keepdims=True)
        grad_ref[slot] = (weight_grad - unit * dot) * inverse_ref[:, here]
        own = grad_ref[slot, own_rows, :].astype(jnp.bfloat16)
        sent_ref[:, :, here] = own.reshape(chips, rows_each, TILE)


def pack_kernel(keep_ref, other_ref, _, sent_ref, packed_ref, sem):
    chips, rows_each, lanes = packed_ref.shape
    width = keep_ref.shape[1]
    total = (keep_ref[...] + other_ref[...].astype(jnp.float32)).astype(jnp.bfloat16)
    total = total.reshape(chips, -1, width)
    for piece in range(lanes // width):
        packed_ref[:, :, piece * width : (piece + 1) * width] = total[:, piece * rows_each : (piece + 1) * rows_each, :]
    copy = pltpu.make_async_copy(packed_ref, sent_ref.at[:, :, pl.ds(sent_ref.shape[2] - lanes, lanes)], sem)
    copy.start()
    copy.wait()


def outputs_kernel(got_ref, student_ref, weight_out, feature_out):
    chips, rows_each, columns = got_ref.shape
    rows, width = student_ref.shape
    pieces = rows // rows_each
    count = columns - pieces * width
    total = got_ref[0, :, count:].astype(jnp.float32)
    for chip in range(1, chips):
        total = total + got_ref[chip, :, count:].astype(jnp.float32)
    total = jnp.concatenate([total[:, piece * width : (piece + 1) * width] for piece in range(pieces)], axis=0)
    hat, length = unit_rows(student_ref[...])
    feature_out[...] = (total - hat * jnp.sum(hat * total, axis=1, keepdims=True)) / length
    for chip in range(chips):
        weight_out[:, chip * count : (chip + 1) * count] = got_ref[chip, :, :count].astype(jnp.float32)


def kernel_body(teacher_feat, student_feat, crop_weight, teacher_v, student_v):
    f32, bf16 = jnp.float32, jnp.bfloat16
    shape = jax.ShapeDtypeStruct
    blocks, fsdp = lax.axis_size("block"), lax.axis_size("fsdp")
    chips = blocks * GROUPS
    members, devices = blocks * fsdp, chips * fsdp
    rows, width = teacher_feat.shape
    crops = rows * devices
    lines = crops // LANES
    kept = teacher_v.shape[1]
    prototypes = kept * fsdp
    count = kept // blocks
    group, block = lax.axis_index("group")[None], lax.axis_index("block")[None]
    core = lax.axis_index("fsdp")[None]
    elements = count * crops
    vmem = pl.BlockSpec(memory_space=pltpu.VMEM)

    def swap(values):
        return lax.ppermute(values, "fsdp", [(0, 1), (1, 0)])

    def share(values):
        return lax.all_to_all(values, GROUP, 0, 0)

    dma = pltpu.SemaphoreType.DMA
    hbm = functools.partial(pltpu.with_memory_space_constraint, memory_space=pltpu.HBM)
    teacher_sent, student_unit = call(
        units_kernel,
        (shape((chips, rows, width), bf16), shape((rows, width), bf16)),
        in_specs=[pl.BlockSpec(memory_space=pl.ANY)] * 2,
        scratch_shapes=[pltpu.VMEM((rows, width), bf16), pltpu.VMEM((rows, width), bf16), dma((2,))],
    )(hbm(teacher_feat), hbm(student_feat))
    teacher_own = lax.all_to_all(teacher_sent, CHIPS, 0, 0)

    def groups_back(values, back):
        return lax.ppermute(values, "group", [(at, (at + back) % GROUPS) for at in range(GROUPS)])

    weights = jnp.pad(crop_weight[None, :], ((0, 15), (0, width - rows)))
    student_unit = jnp.concatenate([student_unit, weights], axis=0)
    student_units = [student_unit] + [groups_back(student_unit, back) for back in range(1, GROUPS)]

    span = 2 * TILE
    spans = count // span
    column = pl.BlockSpec((width, span), lambda step, at: (0, at[0] * spans + step))
    turned = pl.BlockSpec((span, width), lambda step, at: (step, 0))
    line = pl.BlockSpec((1, span), lambda step, at: (0, step))
    teacher_w, student_w, inverse = call(
        directions_kernel,
        (
            shape((count, width), bf16),
            pltpu.HBM((count, width), bf16),
            shape((1, count), f32),
        ),
        flops=12 * count * width,
        moved=8 * count * width,
        grid_spec=pltpu.PrefetchScalarGridSpec(
            num_scalar_prefetch=1,
            grid=(spans,),
            in_specs=[column, column],
            out_specs=[turned, turned, line],
        ),
    )(
        block,
        hbm(teacher_v),
        hbm(student_v),
    )

    teacher_own, teacher_w, student_units = lax.optimization_barrier((teacher_own, teacher_w, student_units))
    teacher_other = swap(teacher_own)
    half = crops // 2
    anyspace = pl.BlockSpec(memory_space=pl.ANY)
    pieces = count // (FETCH * TILE)
    quarter = dict(flops=elements * width, exps=elements // 2)
    own_mass = call(own_teacher_kernel, shape((count, half), f32), **quarter)(teacher_w, teacher_own)
    other_mass, sent, student_w = call(
        functools.partial(other_teacher_kernel, prototypes),
        (
            shape((count, half), f32),
            shape((blocks, GROUPS * rows + 2 * lines, width), bf16),
            shape((count, width), bf16),
        ),
        in_specs=[vmem] * 3 + [anyspace] + [vmem] * GROUPS,
        scratch_shapes=[dma],
        **quarter,
    )(teacher_w, teacher_other, own_mass, hbm(student_w), *student_units)
    first = lax.all_to_all(sent, "block", 0, 0)
    first_other = swap(first)
    units = pltpu.VMEM((half, width), bf16)
    own_student, own_part, own_turned = call(
        own_student_kernel,
        (shape((count, half), f32), shape((8, half), f32), shape((width, half), bf16)),
        scratch_shapes=[units],
        **quarter,
    )(student_w, first)
    other_student, student_part, other_turned = call(
        other_student_kernel,
        (shape((count, half), f32), shape((lines, LANES), f32), shape((width, half), bf16)),
        scratch_shapes=[units],
        **quarter,
    )(student_w, first_other, own_part)
    sent, weights = call(
        functools.partial(sweep_kernel, prototypes, crops),
        (shape((members, 2 * lines, LANES), bf16), shape((lines, LANES), f32)),
        flops=4 * elements,
    )(own_mass, other_mass, first, first_other, student_part)
    second = share(sent)
    sent, own_scaled, other_scaled, student_copy = call(
        functools.partial(last_sweep_kernel, prototypes, crops),
        (
            shape((members, 2 * lines, LANES), bf16),
            shape((count, half), f32),
            shape((count, half), f32),
            shape((pieces, width, count // pieces), bf16),
        ),
        flops=4 * elements,
        in_specs=[vmem] * 3 + [anyspace],
        scratch_shapes=[dma((pieces,))],
    )(own_mass, other_mass, second, hbm(student_v))
    third = share(sent)

    gradient, keep, give = call(
        gradient_kernel,
        (shape((2, count, half), bf16), shape((half // GROUPS, width), f32), shape((half // GROUPS, width), bf16)),
        flops=2 * elements * width // GROUPS,
        in_specs=[vmem] * 9,
        scratch_shapes=[pltpu.VMEM((width, count), bf16)],
    )(own_scaled, other_scaled, own_student, other_student, weights, second, third, inverse, student_copy)
    other = swap(give)
    out_rows = width // chips
    per_chip = rows * width // out_rows
    sent = call(
        weight_kernel,
        shape((blocks, out_rows, count + per_chip), bf16),
        flops=2 * elements * width,
        in_specs=[vmem] * 5,
        scratch_shapes=[pltpu.VMEM((count // TILE, width, TILE), f32)],
    )(gradient, own_turned, other_turned, inverse, student_copy)
    sent = call(
        pack_kernel,
        shape((blocks, out_rows, count + per_chip), bf16),
        in_specs=[vmem] * 2 + [anyspace],
        out_specs=anyspace,
        input_output_aliases={2: 0},
        scratch_shapes=[pltpu.VMEM((blocks, out_rows, per_chip), bf16), dma],
    )(keep, other, sent)
    got = lax.all_to_all(sent, "block", 0, 0)
    return call(
        outputs_kernel, (shape((out_rows, kept), f32), shape((rows, width), f32))
    )(got, student_feat)


def solution(mesh):
    dp, fsdp = mesh.shape["dp"], mesh.shape["fsdp"]
    blocks = dp // GROUPS

    def run(teacher_feat, student_feat, crop_weight, teacher_v, student_v):
        crops = teacher_feat.shape[0]
        count = teacher_v.shape[1] // (blocks * fsdp)
        fits = fsdp == 2 and dp == 16 and count % (2 * TILE) == 0 and crops == 1024
        if fits and 8 * count * crops <= KEPT_BYTES:
            grid = Mesh(mesh.devices.reshape(GROUPS, blocks, fsdp), (*CHIPS, "fsdp"))
            body, chips = kernel_body, CHIPS
        else:
            grid, body, chips = mesh, plain_body, ("dp",)
        every = P((*chips, "fsdp"))
        return jax.shard_map(
            body,
            mesh=grid,
            in_specs=(every, every, every, P(None, "fsdp"), P(None, "fsdp")),
            out_specs=(P(chips, "fsdp"), every),
            check_vma=False,
        )(teacher_feat, student_feat, crop_weight, teacher_v, student_v)

    return run
```

```python
import functools
import math

import jax
import jax.numpy as jnp
from jax import lax
from jax.experimental import pallas as pl
from jax.experimental.pallas import tpu as pltpu
from jax.sharding import Mesh
from jax.sharding import PartitionSpec as P

ITERS = 3

teacher_temp = 0.04
student_temp = 0.1
epsilon = 1e-06

GROUPS = 2
TILE = 256
HALF_TILE = 512
FETCH = 2
LANES = 128
VMEM_BYTES = 12 << 20
KEPT_BYTES = 18 << 20

EVERY = ("dp", "fsdp")
CHIPS = ("group", "block")
GROUP = ("block", "fsdp")


def unit_rows(values):
    floats = values.astype(jnp.float32)
    length = jnp.sqrt(jnp.sum(floats * floats, axis=1, keepdims=True) + epsilon)
    return (floats / length, length)


def unit_columns(values):
    floats = values.astype(jnp.float32)
    length = jnp.sqrt(jnp.sum(floats * floats, axis=0, keepdims=True) + epsilon)
    return (floats / length, length)


COPY_BYTES = 1 << 22


def share(values, axes):
    count = lax.axis_size(axes)
    if count * values.size * values.dtype.itemsize > COPY_BYTES:
        return lax.all_gather(values, axes)
    return lax.all_to_all(jnp.broadcast_to(values, (count, *values.shape)), axes, 0, 0)


def add_up(values):
    if lax.axis_size(EVERY) * values.size * values.dtype.itemsize > COPY_BYTES:
        return lax.psum(values, EVERY)
    return jnp.sum(share(values, EVERY), axis=0)


def plain_body(teacher_feat, student_feat, crop_weight, teacher_v, student_v):
    fsdp = lax.axis_size("fsdp")
    devices = lax.axis_size("dp") * fsdp
    own_rows, width = teacher_feat.shape
    crops = own_rows * devices
    block = teacher_v.shape[1] // lax.axis_size("dp")
    prototypes = block * devices
    first = lax.axis_index("dp") * block

    teacher_hat, _ = unit_rows(teacher_feat)
    student_hat, student_len = unit_rows(student_feat)
    units = jnp.concatenate(
        [teacher_hat.astype(jnp.bfloat16), student_hat.astype(jnp.bfloat16)], axis=1
    )
    units = share(share(units, "dp"), "fsdp").reshape(crops, 2 * width)
    teacher_unit, student_unit = units[:, :width], units[:, width:]

    teacher_w, _ = unit_columns(lax.dynamic_slice_in_dim(teacher_v, first, block, 1))
    student_w, student_wlen = unit_columns(lax.dynamic_slice_in_dim(student_v, first, block, 1))
    student_wunit = student_w.astype(jnp.bfloat16)

    mass = jnp.exp(
        jnp.dot(teacher_unit, teacher_w.astype(jnp.bfloat16), preferred_element_type=jnp.float32)
        / teacher_temp
    )
    student_mass = jnp.exp(
        jnp.dot(student_unit, student_wunit, preferred_element_type=jnp.float32) / student_temp
    )
    student_part = jnp.sum(student_mass, axis=1)

    crop_scale = None
    for sweep in range(ITERS):
        scaled = mass if sweep == 0 else mass * crop_scale[:, None]
        proto_scale = 1.0 / (prototypes * jnp.sum(scaled, axis=0))
        crop_part = jnp.sum(mass * proto_scale[None, :], axis=1)
        if sweep == 0:
            placed = jnp.zeros((fsdp, crops // (fsdp * own_rows), own_rows), jnp.float32)
            own = crop_weight.astype(jnp.float32)[None, None]
            spot = (lax.axis_index("fsdp"), lax.axis_index("dp"), 0)
            placed = lax.dynamic_update_slice(placed, own, spot).reshape(crops)
            sums = add_up(jnp.stack([crop_part, student_part, placed]))
            crop_mass, student_total, weights = sums[0], sums[1], sums[2]
        else:
            crop_mass = add_up(crop_part)
        crop_scale = 1.0 / (crops * crop_mass)

    target = crops * (mass * crop_scale[:, None] * proto_scale[None, :])
    student_prob = student_mass / student_total[:, None]
    gradient = ((student_prob - target) * weights[:, None] / student_temp).astype(jnp.bfloat16)
    feature_part = lax.dot_general(
        gradient, student_wunit, (((1,), (1,)), ((), ())), preferred_element_type=jnp.float32
    )
    weight_grad = lax.dot_general(
        student_unit, gradient, (((0,), (0,)), ((), ())), preferred_element_type=jnp.float32
    )
    weight_dot = jnp.sum(student_w * weight_grad, axis=0, keepdims=True)
    grad_block = (weight_grad - student_w * weight_dot) / student_wlen

    feature_sent = feature_part.astype(jnp.bfloat16).reshape(fsdp, -1, own_rows, width)
    feature_sent = jnp.swapaxes(feature_sent, 0, 1).reshape(devices, own_rows, width)
    feature_all = lax.all_to_all(feature_sent, EVERY, 0, 0)
    feature_grad = jnp.sum(feature_all.astype(jnp.float32), axis=0)
    grad_feat = (
        feature_grad - student_hat * jnp.sum(student_hat * feature_grad, axis=1, keepdims=True)
    ) / student_len
    grad_v = lax.all_to_all(grad_block.astype(jnp.bfloat16), "dp", 0, 1, tiled=True)
    return (grad_v.astype(jnp.float32), grad_feat)


def call(kernel, out_shape, flops=0, moved=0, exps=0, **more):
    return pl.pallas_call(
        kernel,
        out_shape=out_shape,
        compiler_params=pltpu.CompilerParams(vmem_limit_bytes=VMEM_BYTES),
        cost_estimate=pl.CostEstimate(flops=flops, bytes_accessed=moved, transcendentals=exps),
        **more,
    )


def units_kernel(teacher_ref, student_ref, teacher_out, student_out, teacher_vmem, student_vmem, sems):
    copies = [
        pltpu.make_async_copy(teacher_ref, teacher_vmem, sems.at[0]),
        pltpu.make_async_copy(student_ref, student_vmem, sems.at[1]),
    ]
    for copy in copies:
        copy.start()
    for copy in copies:
        copy.wait()
    teacher = unit_rows(teacher_vmem[...])[0].astype(jnp.bfloat16)
    student_out[...] = unit_rows(student_vmem[...])[0].astype(jnp.bfloat16)
    for chip in range(teacher_out.shape[0]):
        teacher_out[chip] = teacher


def placed_weights(student_refs, lines, rows, chips):
    group, block = lax.axis_index("group"), lax.axis_index("block")
    line = lax.broadcasted_iota(jnp.int32, (lines, LANES), 0)
    part = lax.broadcasted_iota(jnp.int32, (lines, LANES), 1) // rows
    each = LANES // rows
    placed = jnp.zeros((lines, LANES), jnp.float32)
    for back, ref in enumerate(student_refs):
        at = lax.axis_index("fsdp") * chips * GROUPS + ((group + GROUPS - back) % GROUPS) * chips + block
        weights = ref[rows:, :rows].astype(jnp.float32)[0:1, :]
        weights = jnp.concatenate([weights] * each, axis=1)
        here = (line == at // each) & (part == at % each)
        placed = placed + jnp.where(here, jnp.broadcast_to(weights, (lines, LANES)), 0.0)
    return placed


def directions_kernel(block_ref, teacher_ref, student_ref, teacher_out, student_out, inverse_out):
    teacher, _ = unit_columns(teacher_ref[...])
    teacher_out[...] = jnp.transpose(teacher).astype(jnp.bfloat16)
    student, length = unit_columns(student_ref[...])
    student_out[...] = jnp.transpose(student).astype(jnp.bfloat16)
    inverse_out[...] = 1.0 / length


def exponentials(directions, units, temperature):
    logits = lax.dot_general(
        directions, units, (((1,), (1,)), ((), ())), preferred_element_type=jnp.float32
    )
    return jnp.exp2(logits * (math.log2(math.e) / temperature))


def fold(values):
    rows, lanes = values.shape
    return jnp.sum(values.reshape(rows // 8, 8, lanes), axis=0)


def as_rows(line):
    return jnp.concatenate([line[:, at : at + LANES] for at in range(0, line.shape[1], LANES)], axis=0)


def as_line(rows):
    return jnp.concatenate([rows[at : at + 1, :] for at in range(rows.shape[0])], axis=1)


def in_core_order(core, own, other, body):
    @pl.when(core == 0)
    def _():
        body(own, other)

    @pl.when(core == 1)
    def _():
        body(other, own)


def sums(first, second):
    lines = [as_rows(jnp.sum(total, axis=0, keepdims=True)) for total in (first, second)]
    return jnp.concatenate(lines, axis=0)


def send(sent_ref, *rows):
    values = jnp.concatenate(rows, axis=0).astype(jnp.bfloat16)
    for device in range(sent_ref.shape[0]):
        sent_ref[device] = values


def halves(rows):
    line = as_line(rows)
    half = line.shape[1] // 2
    return line[:, :half], line[:, half:]


def received(got_ref, at=0):
    total = got_ref[0, at:, :].astype(jnp.float32)
    for device in range(1, got_ref.shape[0]):
        total = total + got_ref[device, at:, :].astype(jnp.float32)
    return total


def units_of(got_ref):
    chips, rows, width = got_ref.shape
    return got_ref[...].reshape(chips * rows, width)


def in_chip_order(got_ref, units_ref):
    chips = got_ref.shape[0]
    rows = units_ref.shape[0] // (GROUPS * chips)
    group = lax.axis_index("group")
    for back in range(GROUPS):
        for chip in range(chips):
            at = (((group + GROUPS - back) % GROUPS) * chips + chip) * rows
            here = pl.ds(pl.multiple_of(at, rows), rows)
            units_ref[here, :] = got_ref[chip, back * rows : (back + 1) * rows, :]


def turn(units):
    return jnp.transpose(units.astype(jnp.float32)).astype(jnp.bfloat16)


def own_teacher_kernel(teacher_w_ref, got_ref, mass_ref):
    units = units_of(got_ref)
    for start in range(0, mass_ref.shape[0], HALF_TILE):
        here = slice(start, start + HALF_TILE)
        mass_ref[here, :] = exponentials(teacher_w_ref[here, :], units, teacher_temp)


def other_teacher_kernel(prototypes, teacher_w_ref, got_ref, own_ref, *refs):
    *student_refs, mass_ref, sent_ref = refs
    chips, rows = sent_ref.shape[0], got_ref.shape[1]
    placed = placed_weights(student_refs, 2 * own_ref.shape[1] // LANES, rows, chips)
    units = units_of(got_ref)
    own_total = total = 0.0
    for start in range(0, mass_ref.shape[0], HALF_TILE):
        here = slice(start, start + HALF_TILE)
        mass = exponentials(teacher_w_ref[here, :], units, teacher_temp)
        mass_ref[here, :] = mass
        own = own_ref[here, :]
        scale = 1.0 / (prototypes * jnp.sum(own + mass, axis=1, keepdims=True))
        own_total = own_total + fold(own * scale)
        total = total + fold(mass * scale)

    def finish(first, second):
        extra = jnp.concatenate([sums(first, second), placed], axis=1)
        extra = jnp.concatenate([extra, jnp.zeros_like(extra)], axis=0)
        values = jnp.concatenate([ref[:rows, :] for ref in student_refs] + [extra.astype(jnp.bfloat16)], axis=0)
        for chip in range(sent_ref.shape[0]):
            sent_ref[chip] = values

    in_core_order(lax.axis_index("fsdp"), own_total, total, finish)


def own_student_kernel(student_w_ref, got_ref, mass_ref, part_ref, turned_ref, units_ref):
    count = student_w_ref.shape[0]
    in_chip_order(got_ref, units_ref)
    turned_ref[...] = turn(units_ref[...])
    part = 0.0
    for start in range(0, count, HALF_TILE):
        here = slice(start, start + HALF_TILE)
        mass = exponentials(student_w_ref[here, :], units_ref[...], student_temp)
        mass_ref[here, :] = mass
        part = part + fold(mass)
    part_ref[...] = part


def other_student_kernel(student_w_ref, got_ref, own_part_ref, mass_ref, part_ref, turned_ref, units_ref):
    in_chip_order(got_ref, units_ref)
    turned_ref[...] = turn(units_ref[...])
    part = 0.0
    for start in range(0, student_w_ref.shape[0], HALF_TILE):
        here = slice(start, start + HALF_TILE)
        mass = exponentials(student_w_ref[here, :], units_ref[...], student_temp)
        mass_ref[here, :] = mass
        part = part + fold(mass)

    def finish(first, second):
        part_ref[...] = sums(first, second)

    in_core_order(lax.axis_index("fsdp"), own_part_ref[...], part, finish)


def sweep(prototypes, crops, first_ref, second_ref, received_sums, scaled_refs=None):
    first_crop, second_crop = halves(1.0 / (crops * received_sums))
    first_total = second_total = 0.0
    for start in range(0, first_ref.shape[0], TILE):
        here = slice(start, start + TILE)
        first, second = first_ref[here, :], second_ref[here, :]
        proto = jnp.sum(first * first_crop + second * second_crop, axis=1, keepdims=True)
        scale = 1.0 / (prototypes * proto)
        first, second = first * scale, second * scale
        if scaled_refs is not None:
            scaled_refs[0][here, :], scaled_refs[1][here, :] = first, second
        first_total = first_total + fold(first)
        second_total = second_total + fold(second)
    return sums(first_total, second_total)


def sweep_kernel(prototypes, crops, own_ref, other_ref, got_ref, other_got_ref, part_ref, sent_ref, weight_ref):
    lines = crops // LANES
    at = got_ref.shape[1] - 2 * lines
    extra = received(got_ref, at) + received(other_got_ref, at)
    weight_ref[...] = extra[:lines, LANES:]

    def body(first_ref, second_ref):
        send(sent_ref, sweep(prototypes, crops, first_ref, second_ref, extra[:lines, :LANES]), part_ref[...])

    in_core_order(lax.axis_index("fsdp"), own_ref, other_ref, body)


def last_sweep_kernel(
    prototypes, crops, own_ref, other_ref, got_ref, directions_ref,
    sent_ref, own_scaled_ref, other_scaled_ref, copy_ref, sems,
):
    pieces, _, span = copy_ref.shape
    copies = []
    for piece in range(pieces):
        columns = pl.ds(pl.multiple_of((lax.axis_index("block") * pieces + piece) * span, span), span)
        copies.append(pltpu.make_async_copy(directions_ref.at[:, columns], copy_ref.at[piece], sems.at[piece]))
        copies[-1].start()

    total = received(got_ref)[: crops // LANES]

    def body(first_refs, second_refs):
        (first_ref, *scaled_refs), (second_ref, second_scaled_ref) = first_refs, second_refs
        sent = sweep(prototypes, crops, first_ref, second_ref, total, (*scaled_refs, second_scaled_ref))
        send(sent_ref, sent, jnp.zeros_like(sent))

    in_core_order(lax.axis_index("fsdp"), (own_ref, own_scaled_ref), (other_ref, other_scaled_ref), body)
    for copy in copies:
        copy.wait()


def units_tile(copy_ref, inverse_ref, start):
    span = copy_ref.shape[2]
    at = start % span
    return copy_ref[start // span, :, at : at + TILE].astype(jnp.float32) * inverse_ref[:, start : start + TILE]


def gradient_kernel(
    own_mass_ref, other_mass_ref, own_student_ref, other_student_ref, weight_ref, second_ref, third_ref,
    inverse_ref, copy_ref, gradient_ref, keep_ref, give_ref, unit_ref,
):
    group, core = lax.axis_index("group"), lax.axis_index("fsdp")
    count, half = own_mass_ref.shape
    lines = 2 * half // LANES
    weights = weight_ref[...] / student_temp
    teacher_scales = halves(weights / received(third_ref)[:lines])
    student_scales = halves(weights / received(second_ref)[lines:])

    def body(first_refs, second_refs):
        for start in range(0, count, TILE):
            here = slice(start, start + TILE)
            for (side, mass_ref, student_ref), teacher_scale, student_scale in zip(
                (first_refs, second_refs), teacher_scales, student_scales
            ):
                gradient = student_ref[here, :] * student_scale - mass_ref[here, :] * teacher_scale
                gradient_ref[side, start : start + TILE, :] = gradient.astype(jnp.bfloat16)

    in_core_order(core, (0, own_mass_ref, own_student_ref), (1, other_mass_ref, other_student_ref), body)
    for start in range(0, count, TILE):
        unit_ref[:, start : start + TILE] = units_tile(copy_ref, inverse_ref, start).astype(jnp.bfloat16)
    kept = half // GROUPS
    lanes = pl.ds(pl.multiple_of(group * kept, kept), kept)
    for side, out_ref in enumerate((keep_ref, give_ref)):
        feature = jnp.dot(unit_ref[...], gradient_ref[side, :, lanes], preferred_element_type=jnp.float32)
        out_ref[...] = jnp.transpose(feature).astype(out_ref.dtype)


def weight_kernel(gradient_ref, own_turned_ref, other_turned_ref, inverse_ref, copy_ref, sent_ref, grad_ref):
    chips, rows_each, _ = sent_ref.shape
    count = gradient_ref.shape[1]
    width = own_turned_ref.shape[0]
    kept = width // GROUPS
    own_rows = pl.ds(pl.multiple_of(lax.axis_index("group") * kept, kept), kept)
    for start in range(0, count, TILE):
        here, slot = slice(start, start + TILE), start // TILE
        weight_grad = 0.0
        for side, turned_ref in enumerate((own_turned_ref, other_turned_ref)):
            weight_grad = weight_grad + lax.dot_general(
                turned_ref[...], gradient_ref[side, here, :], (((1,), (1,)), ((), ())), preferred_element_type=jnp.float32
            )
        unit = units_tile(copy_ref, inverse_ref, start)
        dot = jnp.sum(unit * weight_grad, axis=0, keepdims=True)
        grad_ref[slot] = (weight_grad - unit * dot) * inverse_ref[:, here]
        own = grad_ref[slot, own_rows, :].astype(jnp.bfloat16)
        sent_ref[:, :, here] = own.reshape(chips, rows_each, TILE)


def pack_kernel(keep_ref, other_ref, _, sent_ref, packed_ref, sem):
    chips, rows_each, lanes = packed_ref.shape
    width = keep_ref.shape[1]
    total = (keep_ref[...] + other_ref[...].astype(jnp.float32)).astype(jnp.bfloat16)
    total = total.reshape(chips, -1, width)
    for piece in range(lanes // width):
        packed_ref[:, :, piece * width : (piece + 1) * width] = total[:, piece * rows_each : (piece + 1) * rows_each, :]
    copy = pltpu.make_async_copy(packed_ref, sent_ref.at[:, :, pl.ds(sent_ref.shape[2] - lanes, lanes)], sem)
    copy.start()
    copy.wait()


def outputs_kernel(got_ref, student_ref, weight_out, feature_out):
    chips, rows_each, columns = got_ref.shape
    rows, width = student_ref.shape
    pieces = rows // rows_each
    count = columns - pieces * width
    total = got_ref[0, :, count:].astype(jnp.float32)
    for chip in range(1, chips):
        total = total + got_ref[chip, :, count:].astype(jnp.float32)
    total = jnp.concatenate([total[:, piece * width : (piece + 1) * width] for piece in range(pieces)], axis=0)
    hat, length = unit_rows(student_ref[...])
    feature_out[...] = (total - hat * jnp.sum(hat * total, axis=1, keepdims=True)) / length
    for chip in range(chips):
        weight_out[:, chip * count : (chip + 1) * count] = got_ref[chip, :, :count].astype(jnp.float32)


def kernel_body(teacher_feat, student_feat, crop_weight, teacher_v, student_v):
    f32, bf16 = jnp.float32, jnp.bfloat16
    shape = jax.ShapeDtypeStruct
    blocks, fsdp = lax.axis_size("block"), lax.axis_size("fsdp")
    chips = blocks * GROUPS
    members, devices = blocks * fsdp, chips * fsdp
    rows, width = teacher_feat.shape
    crops = rows * devices
    lines = crops // LANES
    kept = teacher_v.shape[1]
    prototypes = kept * fsdp
    count = kept // blocks
    group, block = lax.axis_index("group")[None], lax.axis_index("block")[None]
    core = lax.axis_index("fsdp")[None]
    elements = count * crops
    vmem = pl.BlockSpec(memory_space=pltpu.VMEM)

    def swap(values):
        return lax.ppermute(values, "fsdp", [(0, 1), (1, 0)])

    def share(values):
        return lax.all_to_all(values, GROUP, 0, 0)

    dma = pltpu.SemaphoreType.DMA
    hbm = functools.partial(pltpu.with_memory_space_constraint, memory_space=pltpu.HBM)
    teacher_sent, student_unit = call(
        units_kernel,
        (shape((chips, rows, width), bf16), shape((rows, width), bf16)),
        in_specs=[pl.BlockSpec(memory_space=pl.ANY)] * 2,
        scratch_shapes=[pltpu.VMEM((rows, width), bf16), pltpu.VMEM((rows, width), bf16), dma((2,))],
    )(hbm(teacher_feat), hbm(student_feat))
    teacher_own = lax.all_to_all(teacher_sent, CHIPS, 0, 0)

    def groups_back(values, back):
        return lax.ppermute(values, "group", [(at, (at + back) % GROUPS) for at in range(GROUPS)])

    weights = jnp.pad(crop_weight[None, :], ((0, 15), (0, width - rows)))
    student_unit = jnp.concatenate([student_unit, weights], axis=0)
    student_units = [student_unit] + [groups_back(student_unit, back) for back in range(1, GROUPS)]

    span = 2 * TILE
    spans = count // span
    column = pl.BlockSpec((width, span), lambda step, at: (0, at[0] * spans + step))
    turned = pl.BlockSpec((span, width), lambda step, at: (step, 0))
    line = pl.BlockSpec((1, span), lambda step, at: (0, step))
    teacher_w, student_w, inverse = call(
        directions_kernel,
        (
            shape((count, width), bf16),
            shape((count, width), bf16),
            shape((1, count), f32),
        ),
        flops=12 * count * width,
        moved=8 * count * width,
        grid_spec=pltpu.PrefetchScalarGridSpec(
            num_scalar_prefetch=1,
            grid=(spans,),
            in_specs=[column, column],
            out_specs=[turned, turned, line],
        ),
    )(
        block,
        hbm(teacher_v),
        hbm(student_v),
    )

    teacher_own, teacher_w, student_units = lax.optimization_barrier((teacher_own, teacher_w, student_units))
    teacher_other = swap(teacher_own)
    half = crops // 2
    anyspace = pl.BlockSpec(memory_space=pl.ANY)
    pieces = count // (FETCH * TILE)
    quarter = dict(flops=elements * width, exps=elements // 2)
    own_mass = call(own_teacher_kernel, shape((count, half), f32), **quarter)(teacher_w, teacher_own)
    other_mass, sent = call(
        functools.partial(other_teacher_kernel, prototypes),
        (
            shape((count, half), f32),
            shape((blocks, GROUPS * rows + 2 * lines, width), bf16),
        ),
        **quarter,
    )(teacher_w, teacher_other, own_mass, *student_units)
    first = lax.all_to_all(sent, "block", 0, 0)
    first_other = swap(first)
    units = pltpu.VMEM((half, width), bf16)
    own_student, own_part, own_turned = call(
        own_student_kernel,
        (shape((count, half), f32), shape((8, half), f32), shape((width, half), bf16)),
        scratch_shapes=[units],
        **quarter,
    )(student_w, first)
    other_student, student_part, other_turned = call(
        other_student_kernel,
        (shape((count, half), f32), shape((lines, LANES), f32), shape((width, half), bf16)),
        scratch_shapes=[units],
        **quarter,
    )(student_w, first_other, own_part)
    sent, weights = call(
        functools.partial(sweep_kernel, prototypes, crops),
        (shape((members, 2 * lines, LANES), bf16), shape((lines, LANES), f32)),
        flops=4 * elements,
    )(own_mass, other_mass, first, first_other, student_part)
    second = share(sent)
    sent, own_scaled, other_scaled, student_copy = call(
        functools.partial(last_sweep_kernel, prototypes, crops),
        (
            shape((members, 2 * lines, LANES), bf16),
            shape((count, half), f32),
            shape((count, half), f32),
            shape((pieces, width, count // pieces), bf16),
        ),
        flops=4 * elements,
        in_specs=[vmem] * 3 + [anyspace],
        scratch_shapes=[dma((pieces,))],
    )(own_mass, other_mass, second, hbm(student_v))
    third = share(sent)

    gradient, keep, give = call(
        gradient_kernel,
        (shape((2, count, half), bf16), shape((half // GROUPS, width), f32), shape((half // GROUPS, width), bf16)),
        flops=2 * elements * width // GROUPS,
        in_specs=[vmem] * 9,
        scratch_shapes=[pltpu.VMEM((width, count), bf16)],
    )(own_scaled, other_scaled, own_student, other_student, weights, second, third, inverse, student_copy)
    other = swap(give)
    out_rows = width // chips
    per_chip = rows * width // out_rows
    sent = call(
        weight_kernel,
        shape((blocks, out_rows, count + per_chip), bf16),
        flops=2 * elements * width,
        in_specs=[vmem] * 5,
        scratch_shapes=[pltpu.VMEM((count // TILE, width, TILE), f32)],
    )(gradient, own_turned, other_turned, inverse, student_copy)
    sent = call(
        pack_kernel,
        shape((blocks, out_rows, count + per_chip), bf16),
        in_specs=[vmem] * 2 + [anyspace],
        out_specs=anyspace,
        input_output_aliases={2: 0},
        scratch_shapes=[pltpu.VMEM((blocks, out_rows, per_chip), bf16), dma],
    )(keep, other, sent)
    got = lax.all_to_all(sent, "block", 0, 0)
    return call(
        outputs_kernel, (shape((out_rows, kept), f32), shape((rows, width), f32))
    )(got, student_feat)


def solution(mesh):
    dp, fsdp = mesh.shape["dp"], mesh.shape["fsdp"]
    blocks = dp // GROUPS

    def run(teacher_feat, student_feat, crop_weight, teacher_v, student_v):
        crops = teacher_feat.shape[0]
        count = teacher_v.shape[1] // (blocks * fsdp)
        fits = fsdp == 2 and dp == 16 and count % (2 * TILE) == 0 and crops == 1024
        if fits and 8 * count * crops <= KEPT_BYTES:
            grid = Mesh(mesh.devices.reshape(GROUPS, blocks, fsdp), (*CHIPS, "fsdp"))
            body, chips = kernel_body, CHIPS
        else:
            grid, body, chips = mesh, plain_body, ("dp",)
        every = P((*chips, "fsdp"))
        return jax.shard_map(
            body,
            mesh=grid,
            in_specs=(every, every, every, P(None, "fsdp"), P(None, "fsdp")),
            out_specs=(P(chips, "fsdp"), every),
            check_vma=False,
        )(teacher_feat, student_feat, crop_weight, teacher_v, student_v)

    return run
```

```python
import functools
import math

import jax
import jax.numpy as jnp
from jax import lax
from jax.experimental import pallas as pl
from jax.experimental.pallas import tpu as pltpu
from jax.sharding import Mesh
from jax.sharding import PartitionSpec as P

ITERS = 3

teacher_temp = 0.04
student_temp = 0.1
epsilon = 1e-06

GROUPS = 2
TILE = 256
HALF_TILE = 512
FETCH = 2
LANES = 128
VMEM_BYTES = 12 << 20
KEPT_BYTES = 18 << 20

EVERY = ("dp", "fsdp")
CHIPS = ("group", "block")
GROUP = ("block", "fsdp")


def unit_rows(values):
    floats = values.astype(jnp.float32)
    length = jnp.sqrt(jnp.sum(floats * floats, axis=1, keepdims=True) + epsilon)
    return (floats / length, length)


def unit_columns(values):
    floats = values.astype(jnp.float32)
    length = jnp.sqrt(jnp.sum(floats * floats, axis=0, keepdims=True) + epsilon)
    return (floats / length, length)


COPY_BYTES = 1 << 22


def share(values, axes):
    count = lax.axis_size(axes)
    if count * values.size * values.dtype.itemsize > COPY_BYTES:
        return lax.all_gather(values, axes)
    return lax.all_to_all(jnp.broadcast_to(values, (count, *values.shape)), axes, 0, 0)


def add_up(values):
    if lax.axis_size(EVERY) * values.size * values.dtype.itemsize > COPY_BYTES:
        return lax.psum(values, EVERY)
    return jnp.sum(share(values, EVERY), axis=0)


def plain_body(teacher_feat, student_feat, crop_weight, teacher_v, student_v):
    fsdp = lax.axis_size("fsdp")
    devices = lax.axis_size("dp") * fsdp
    own_rows, width = teacher_feat.shape
    crops = own_rows * devices
    block = teacher_v.shape[1] // lax.axis_size("dp")
    prototypes = block * devices
    first = lax.axis_index("dp") * block

    teacher_hat, _ = unit_rows(teacher_feat)
    student_hat, student_len = unit_rows(student_feat)
    units = jnp.concatenate(
        [teacher_hat.astype(jnp.bfloat16), student_hat.astype(jnp.bfloat16)], axis=1
    )
    units = share(share(units, "dp"), "fsdp").reshape(crops, 2 * width)
    teacher_unit, student_unit = units[:, :width], units[:, width:]

    teacher_w, _ = unit_columns(lax.dynamic_slice_in_dim(teacher_v, first, block, 1))
    student_w, student_wlen = unit_columns(lax.dynamic_slice_in_dim(student_v, first, block, 1))
    student_wunit = student_w.astype(jnp.bfloat16)

    mass = jnp.exp(
        jnp.dot(teacher_unit, teacher_w.astype(jnp.bfloat16), preferred_element_type=jnp.float32)
        / teacher_temp
    )
    student_mass = jnp.exp(
        jnp.dot(student_unit, student_wunit, preferred_element_type=jnp.float32) / student_temp
    )
    student_part = jnp.sum(student_mass, axis=1)

    crop_scale = None
    for sweep in range(ITERS):
        scaled = mass if sweep == 0 else mass * crop_scale[:, None]
        proto_scale = 1.0 / (prototypes * jnp.sum(scaled, axis=0))
        crop_part = jnp.sum(mass * proto_scale[None, :], axis=1)
        if sweep == 0:
            placed = jnp.zeros((fsdp, crops // (fsdp * own_rows), own_rows), jnp.float32)
            own = crop_weight.astype(jnp.float32)[None, None]
            spot = (lax.axis_index("fsdp"), lax.axis_index("dp"), 0)
            placed = lax.dynamic_update_slice(placed, own, spot).reshape(crops)
            sums = add_up(jnp.stack([crop_part, student_part, placed]))
            crop_mass, student_total, weights = sums[0], sums[1], sums[2]
        else:
            crop_mass = add_up(crop_part)
        crop_scale = 1.0 / (crops * crop_mass)

    target = crops * (mass * crop_scale[:, None] * proto_scale[None, :])
    student_prob = student_mass / student_total[:, None]
    gradient = ((student_prob - target) * weights[:, None] / student_temp).astype(jnp.bfloat16)
    feature_part = lax.dot_general(
        gradient, student_wunit, (((1,), (1,)), ((), ())), preferred_element_type=jnp.float32
    )
    weight_grad = lax.dot_general(
        student_unit, gradient, (((0,), (0,)), ((), ())), preferred_element_type=jnp.float32
    )
    weight_dot = jnp.sum(student_w * weight_grad, axis=0, keepdims=True)
    grad_block = (weight_grad - student_w * weight_dot) / student_wlen

    feature_sent = feature_part.astype(jnp.bfloat16).reshape(fsdp, -1, own_rows, width)
    feature_sent = jnp.swapaxes(feature_sent, 0, 1).reshape(devices, own_rows, width)
    feature_all = lax.all_to_all(feature_sent, EVERY, 0, 0)
    feature_grad = jnp.sum(feature_all.astype(jnp.float32), axis=0)
    grad_feat = (
        feature_grad - student_hat * jnp.sum(student_hat * feature_grad, axis=1, keepdims=True)
    ) / student_len
    grad_v = lax.all_to_all(grad_block.astype(jnp.bfloat16), "dp", 0, 1, tiled=True)
    return (grad_v.astype(jnp.float32), grad_feat)


def call(kernel, out_shape, flops=0, moved=0, exps=0, **more):
    return pl.pallas_call(
        kernel,
        out_shape=out_shape,
        compiler_params=pltpu.CompilerParams(vmem_limit_bytes=VMEM_BYTES),
        cost_estimate=pl.CostEstimate(flops=flops, bytes_accessed=moved, transcendentals=exps),
        **more,
    )


def units_kernel(teacher_ref, student_ref, units_out, teacher_vmem, student_vmem, sems):
    copies = [
        pltpu.make_async_copy(teacher_ref, teacher_vmem, sems.at[0]),
        pltpu.make_async_copy(student_ref, student_vmem, sems.at[1]),
    ]
    for copy in copies:
        copy.start()
    for copy in copies:
        copy.wait()
    width = teacher_vmem.shape[1]
    units_out[:, :width] = unit_rows(teacher_vmem[...])[0].astype(jnp.bfloat16)
    units_out[:, width:] = unit_rows(student_vmem[...])[0].astype(jnp.bfloat16)


def spread_kernel(*refs):
    *unit_refs, sent_ref = refs
    values = jnp.concatenate([ref[...] for ref in unit_refs], axis=0)
    for chip in range(sent_ref.shape[0]):
        sent_ref[chip] = values


def placed_weights(weight_refs, lines, rows, chips):
    group, block = lax.axis_index("group"), lax.axis_index("block")
    line = lax.broadcasted_iota(jnp.int32, (lines, LANES), 0)
    part = lax.broadcasted_iota(jnp.int32, (lines, LANES), 1) // rows
    each = LANES // rows
    placed = jnp.zeros((lines, LANES), jnp.float32)
    for back, ref in enumerate(weight_refs):
        at = lax.axis_index("fsdp") * chips * GROUPS + ((group + GROUPS - back) % GROUPS) * chips + block
        weights = ref[:, :rows].astype(jnp.float32)[0:1, :]
        weights = jnp.concatenate([weights] * each, axis=1)
        here = (line == at // each) & (part == at % each)
        placed = placed + jnp.where(here, jnp.broadcast_to(weights, (lines, LANES)), 0.0)
    return placed


def directions_kernel(block_ref, teacher_ref, student_ref, teacher_out, student_out, inverse_out):
    teacher, _ = unit_columns(teacher_ref[...])
    teacher_out[...] = jnp.transpose(teacher).astype(jnp.bfloat16)
    student, length = unit_columns(student_ref[...])
    student_out[...] = jnp.transpose(student).astype(jnp.bfloat16)
    inverse_out[...] = 1.0 / length


def exponentials(directions, units, temperature):
    logits = lax.dot_general(
        directions, units, (((1,), (1,)), ((), ())), preferred_element_type=jnp.float32
    )
    return jnp.exp2(logits * (math.log2(math.e) / temperature))


def fold(values):
    rows, lanes = values.shape
    return jnp.sum(values.reshape(rows // 8, 8, lanes), axis=0)


def as_rows(line):
    return jnp.concatenate([line[:, at : at + LANES] for at in range(0, line.shape[1], LANES)], axis=0)


def as_line(rows):
    return jnp.concatenate([rows[at : at + 1, :] for at in range(rows.shape[0])], axis=1)


def in_core_order(core, own, other, body):
    @pl.when(core == 0)
    def _():
        body(own, other)

    @pl.when(core == 1)
    def _():
        body(other, own)


def sums(first, second):
    lines = [as_rows(jnp.sum(total, axis=0, keepdims=True)) for total in (first, second)]
    return jnp.concatenate(lines, axis=0)


def send(sent_ref, *rows):
    values = jnp.concatenate(rows, axis=0).astype(jnp.bfloat16)
    for device in range(sent_ref.shape[0]):
        sent_ref[device] = values


def halves(rows):
    line = as_line(rows)
    half = line.shape[1] // 2
    return line[:, :half], line[:, half:]


def received(got_ref, at=0):
    total = got_ref[0, at:, :].astype(jnp.float32)
    for device in range(1, got_ref.shape[0]):
        total = total + got_ref[device, at:, :].astype(jnp.float32)
    return total


def in_chip_order(got_ref, teacher_ref, student_ref):
    chips = got_ref.shape[0]
    width = teacher_ref.shape[1]
    rows = teacher_ref.shape[0] // (GROUPS * chips)
    group = lax.axis_index("group")
    for back in range(GROUPS):
        for chip in range(chips):
            at = (((group + GROUPS - back) % GROUPS) * chips + chip) * rows
            here = pl.ds(pl.multiple_of(at, rows), rows)
            teacher_ref[here, :] = got_ref[chip, back * rows : (back + 1) * rows, :width]
            student_ref[here, :] = got_ref[chip, back * rows : (back + 1) * rows, width:]


def turn(units):
    return jnp.transpose(units.astype(jnp.float32)).astype(jnp.bfloat16)


def own_kernel(
    teacher_w_ref, student_w_ref, got_ref, teacher_ref, student_ref, part_ref, turned_ref, teacher_units, student_units
):
    in_chip_order(got_ref, teacher_units, student_units)
    turned_ref[...] = turn(student_units[...])
    part = 0.0
    for start in range(0, teacher_ref.shape[0], HALF_TILE):
        here = slice(start, start + HALF_TILE)
        teacher_ref[here, :] = exponentials(teacher_w_ref[here, :], teacher_units[...], teacher_temp)
        mass = exponentials(student_w_ref[here, :], student_units[...], student_temp)
        student_ref[here, :] = mass
        part = part + fold(mass)
    part_ref[...] = part


def other_kernel(prototypes, teacher_w_ref, student_w_ref, got_ref, own_ref, own_part_ref, *refs):
    weight_refs = refs[:GROUPS]
    teacher_ref, student_ref, sent_ref, part_ref, turned_ref, teacher_units, student_units = refs[GROUPS:]
    chips = got_ref.shape[0]
    in_chip_order(got_ref, teacher_units, student_units)
    turned_ref[...] = turn(student_units[...])
    half = own_ref.shape[1]
    placed = placed_weights(weight_refs, 2 * half // LANES, half // (GROUPS * chips), chips)
    own_total = total = part = 0.0
    for start in range(0, teacher_ref.shape[0], HALF_TILE):
        here = slice(start, start + HALF_TILE)
        mass = exponentials(teacher_w_ref[here, :], teacher_units[...], teacher_temp)
        teacher_ref[here, :] = mass
        own = own_ref[here, :]
        scale = 1.0 / (prototypes * jnp.sum(own + mass, axis=1, keepdims=True))
        own_total = own_total + fold(own * scale)
        total = total + fold(mass * scale)
        mass = exponentials(student_w_ref[here, :], student_units[...], student_temp)
        student_ref[here, :] = mass
        part = part + fold(mass)

    def finish(first, second):
        send(sent_ref, sums(first[0], second[0]), placed)
        part_ref[...] = sums(first[1], second[1])

    in_core_order(lax.axis_index("fsdp"), (own_total, own_part_ref[...]), (total, part), finish)


def sweep(prototypes, crops, first_ref, second_ref, received_sums, scaled_refs=None):
    first_crop, second_crop = halves(1.0 / (crops * received_sums))
    first_total = second_total = 0.0
    for start in range(0, first_ref.shape[0], TILE):
        here = slice(start, start + TILE)
        first, second = first_ref[here, :], second_ref[here, :]
        proto = jnp.sum(first * first_crop + second * second_crop, axis=1, keepdims=True)
        scale = 1.0 / (prototypes * proto)
        first, second = first * scale, second * scale
        if scaled_refs is not None:
            scaled_refs[0][here, :], scaled_refs[1][here, :] = first, second
        first_total = first_total + fold(first)
        second_total = second_total + fold(second)
    return sums(first_total, second_total)


def sweep_kernel(prototypes, crops, own_ref, other_ref, got_ref, part_ref, sent_ref, weight_ref):
    lines = crops // LANES
    extra = received(got_ref)
    weight_ref[...] = extra[lines:]

    def body(first_ref, second_ref):
        send(sent_ref, sweep(prototypes, crops, first_ref, second_ref, extra[:lines]), part_ref[...])

    in_core_order(lax.axis_index("fsdp"), own_ref, other_ref, body)


def last_sweep_kernel(
    prototypes, crops, own_ref, other_ref, got_ref, directions_ref,
    sent_ref, own_scaled_ref, other_scaled_ref, copy_ref, sems,
):
    pieces, _, span = copy_ref.shape
    copies = []
    for piece in range(pieces):
        columns = pl.ds(pl.multiple_of((lax.axis_index("block") * pieces + piece) * span, span), span)
        copies.append(pltpu.make_async_copy(directions_ref.at[:, columns], copy_ref.at[piece], sems.at[piece]))
        copies[-1].start()

    total = received(got_ref)[: crops // LANES]

    def body(first_refs, second_refs):
        (first_ref, *scaled_refs), (second_ref, second_scaled_ref) = first_refs, second_refs
        sent = sweep(prototypes, crops, first_ref, second_ref, total, (*scaled_refs, second_scaled_ref))
        send(sent_ref, sent)

    in_core_order(lax.axis_index("fsdp"), (own_ref, own_scaled_ref), (other_ref, other_scaled_ref), body)
    for copy in copies:
        copy.wait()


def units_tile(copy_ref, inverse_ref, start):
    span = copy_ref.shape[2]
    at = start % span
    return copy_ref[start // span, :, at : at + TILE].astype(jnp.float32) * inverse_ref[:, start : start + TILE]


def gradient_kernel(
    own_mass_ref, other_mass_ref, own_student_ref, other_student_ref, weight_ref, second_ref, third_ref,
    inverse_ref, copy_ref, gradient_ref, keep_ref, give_ref, unit_ref,
):
    group, core = lax.axis_index("group"), lax.axis_index("fsdp")
    count, half = own_mass_ref.shape
    lines = 2 * half // LANES
    weights = weight_ref[...] / student_temp
    teacher_scales = halves(weights / received(third_ref)[:lines])
    student_scales = halves(weights / received(second_ref)[lines:])

    def body(first_refs, second_refs):
        for start in range(0, count, TILE):
            here = slice(start, start + TILE)
            for (side, mass_ref, student_ref), teacher_scale, student_scale in zip(
                (first_refs, second_refs), teacher_scales, student_scales
            ):
                gradient = student_ref[here, :] * student_scale - mass_ref[here, :] * teacher_scale
                gradient_ref[side, start : start + TILE, :] = gradient.astype(jnp.bfloat16)

    in_core_order(core, (0, own_mass_ref, own_student_ref), (1, other_mass_ref, other_student_ref), body)
    for start in range(0, count, TILE):
        unit_ref[:, start : start + TILE] = units_tile(copy_ref, inverse_ref, start).astype(jnp.bfloat16)
    kept = half // GROUPS
    lanes = pl.ds(pl.multiple_of(group * kept, kept), kept)
    for side, out_ref in enumerate((keep_ref, give_ref)):
        feature = jnp.dot(unit_ref[...], gradient_ref[side, :, lanes], preferred_element_type=jnp.float32)
        out_ref[...] = jnp.transpose(feature).astype(out_ref.dtype)


def weight_kernel(gradient_ref, own_turned_ref, other_turned_ref, inverse_ref, copy_ref, sent_ref, grad_ref):
    chips, rows_each, _ = sent_ref.shape
    count = gradient_ref.shape[1]
    width = own_turned_ref.shape[0]
    kept = width // GROUPS
    own_rows = pl.ds(pl.multiple_of(lax.axis_index("group") * kept, kept), kept)
    for start in range(0, count, TILE):
        here, slot = slice(start, start + TILE), start // TILE
        weight_grad = 0.0
        for side, turned_ref in enumerate((own_turned_ref, other_turned_ref)):
            weight_grad = weight_grad + lax.dot_general(
                turned_ref[...], gradient_ref[side, here, :], (((1,), (1,)), ((), ())), preferred_element_type=jnp.float32
            )
        unit = units_tile(copy_ref, inverse_ref, start)
        dot = jnp.sum(unit * weight_grad, axis=0, keepdims=True)
        grad_ref[slot] = (weight_grad - unit * dot) * inverse_ref[:, here]
        own = grad_ref[slot, own_rows, :].astype(jnp.bfloat16)
        sent_ref[:, :, here] = own.reshape(chips, rows_each, TILE)


def pack_kernel(keep_ref, other_ref, _, sent_ref, packed_ref, sem):
    chips, rows_each, lanes = packed_ref.shape
    width = keep_ref.shape[1]
    total = (keep_ref[...] + other_ref[...].astype(jnp.float32)).astype(jnp.bfloat16)
    total = total.reshape(chips, -1, width)
    for piece in range(lanes // width):
        packed_ref[:, :, piece * width : (piece + 1) * width] = total[:, piece * rows_each : (piece + 1) * rows_each, :]
    copy = pltpu.make_async_copy(packed_ref, sent_ref.at[:, :, pl.ds(sent_ref.shape[2] - lanes, lanes)], sem)
    copy.start()
    copy.wait()


def outputs_kernel(got_ref, student_ref, weight_out, feature_out):
    chips, rows_each, columns = got_ref.shape
    rows, width = student_ref.shape
    pieces = rows // rows_each
    count = columns - pieces * width
    total = got_ref[0, :, count:].astype(jnp.float32)
    for chip in range(1, chips):
        total = total + got_ref[chip, :, count:].astype(jnp.float32)
    total = jnp.concatenate([total[:, piece * width : (piece + 1) * width] for piece in range(pieces)], axis=0)
    hat, length = unit_rows(student_ref[...])
    feature_out[...] = (total - hat * jnp.sum(hat * total, axis=1, keepdims=True)) / length
    for chip in range(chips):
        weight_out[:, chip * count : (chip + 1) * count] = got_ref[chip, :, :count].astype(jnp.float32)


def kernel_body(teacher_feat, student_feat, crop_weight, teacher_v, student_v):
    f32, bf16 = jnp.float32, jnp.bfloat16
    shape = jax.ShapeDtypeStruct
    blocks, fsdp = lax.axis_size("block"), lax.axis_size("fsdp")
    chips = blocks * GROUPS
    members, devices = blocks * fsdp, chips * fsdp
    rows, width = teacher_feat.shape
    crops = rows * devices
    lines = crops // LANES
    kept = teacher_v.shape[1]
    prototypes = kept * fsdp
    count = kept // blocks
    group, block = lax.axis_index("group")[None], lax.axis_index("block")[None]
    core = lax.axis_index("fsdp")[None]
    elements = count * crops
    vmem = pl.BlockSpec(memory_space=pltpu.VMEM)

    def swap(values):
        return lax.ppermute(values, "fsdp", [(0, 1), (1, 0)])

    def share(values):
        return lax.all_to_all(values, GROUP, 0, 0)

    dma = pltpu.SemaphoreType.DMA
    hbm = functools.partial(pltpu.with_memory_space_constraint, memory_space=pltpu.HBM)
    units = call(
        units_kernel,
        shape((rows, 2 * width), bf16),
        in_specs=[pl.BlockSpec(memory_space=pl.ANY)] * 2,
        scratch_shapes=[pltpu.VMEM((rows, width), bf16), pltpu.VMEM((rows, width), bf16), dma((2,))],
    )(hbm(teacher_feat), hbm(student_feat))

    def of_groups(values):
        return [values] + [
            lax.ppermute(values, "group", [(at, (at + back) % GROUPS) for at in range(GROUPS)]) for back in range(1, GROUPS)
        ]

    units = of_groups(units)
    weights = of_groups(jnp.pad(crop_weight[None, :], ((0, 15), (0, width - rows))))

    span = 2 * TILE
    spans = count // span
    column = pl.BlockSpec((width, span), lambda step, at: (0, at[0] * spans + step))
    turned = pl.BlockSpec((span, width), lambda step, at: (step, 0))
    line = pl.BlockSpec((1, span), lambda step, at: (0, step))
    teacher_w, student_w, inverse = call(
        directions_kernel,
        (
            shape((count, width), bf16),
            shape((count, width), bf16),
            shape((1, count), f32),
        ),
        flops=12 * count * width,
        moved=8 * count * width,
        grid_spec=pltpu.PrefetchScalarGridSpec(
            num_scalar_prefetch=1,
            grid=(spans,),
            in_specs=[column, column],
            out_specs=[turned, turned, line],
        ),
    )(
        block,
        hbm(teacher_v),
        hbm(student_v),
    )

    units, weights, teacher_w = lax.optimization_barrier((units, weights, teacher_w))
    sent = call(spread_kernel, shape((blocks, GROUPS * rows, 2 * width), bf16))(*units)
    own = lax.all_to_all(sent, "block", 0, 0)
    other = swap(own)
    half = crops // 2
    anyspace = pl.BlockSpec(memory_space=pl.ANY)
    pieces = count // (FETCH * TILE)
    halved = dict(flops=2 * elements * width, exps=elements)
    units = pltpu.VMEM((half, width), bf16)
    own_mass, own_student, own_part, own_turned = call(
        own_kernel,
        (
            shape((count, half), f32),
            shape((count, half), f32),
            shape((8, half), f32),
            shape((width, half), bf16),
        ),
        scratch_shapes=[units, units],
        **halved,
    )(teacher_w, student_w, own)
    other_mass, other_student, sent, student_part, other_turned = call(
        functools.partial(other_kernel, prototypes),
        (
            shape((count, half), f32),
            shape((count, half), f32),
            shape((members, 2 * lines, LANES), bf16),
            shape((lines, LANES), f32),
            shape((width, half), bf16),
        ),
        scratch_shapes=[units, units],
        **halved,
    )(teacher_w, student_w, other, own_mass, own_part, *weights)
    first = share(sent)
    sent, weights = call(
        functools.partial(sweep_kernel, prototypes, crops),
        (shape((members, 2 * lines, LANES), bf16), shape((lines, LANES), f32)),
        flops=4 * elements,
    )(own_mass, other_mass, first, student_part)
    second = share(sent)
    sent, own_scaled, other_scaled, student_copy = call(
        functools.partial(last_sweep_kernel, prototypes, crops),
        (
            shape((members, lines, LANES), bf16),
            shape((count, half), f32),
            shape((count, half), f32),
            shape((pieces, width, count // pieces), bf16),
        ),
        flops=4 * elements,
        in_specs=[vmem] * 3 + [anyspace],
        scratch_shapes=[dma((pieces,))],
    )(own_mass, other_mass, second, hbm(student_v))
    third = share(sent)

    gradient, keep, give = call(
        gradient_kernel,
        (shape((2, count, half), bf16), shape((half // GROUPS, width), f32), shape((half // GROUPS, width), bf16)),
        flops=2 * elements * width // GROUPS,
        in_specs=[vmem] * 9,
        scratch_shapes=[pltpu.VMEM((width, count), bf16)],
    )(own_scaled, other_scaled, own_student, other_student, weights, second, third, inverse, student_copy)
    other = swap(give)
    out_rows = width // chips
    per_chip = rows * width // out_rows
    sent = call(
        weight_kernel,
        shape((blocks, out_rows, count + per_chip), bf16),
        flops=2 * elements * width,
        in_specs=[vmem] * 5,
        scratch_shapes=[pltpu.VMEM((count // TILE, width, TILE), f32)],
    )(gradient, own_turned, other_turned, inverse, student_copy)
    sent = call(
        pack_kernel,
        shape((blocks, out_rows, count + per_chip), bf16),
        in_specs=[vmem] * 2 + [anyspace],
        out_specs=anyspace,
        input_output_aliases={2: 0},
        scratch_shapes=[pltpu.VMEM((blocks, out_rows, per_chip), bf16), dma],
    )(keep, other, sent)
    got = lax.all_to_all(sent, "block", 0, 0)
    return call(
        outputs_kernel, (shape((out_rows, kept), f32), shape((rows, width), f32))
    )(got, student_feat)


def solution(mesh):
    dp, fsdp = mesh.shape["dp"], mesh.shape["fsdp"]
    blocks = dp // GROUPS

    def run(teacher_feat, student_feat, crop_weight, teacher_v, student_v):
        crops = teacher_feat.shape[0]
        count = teacher_v.shape[1] // (blocks * fsdp)
        fits = fsdp == 2 and dp == 16 and count % (2 * TILE) == 0 and crops == 1024
        if fits and 8 * count * crops <= KEPT_BYTES:
            grid = Mesh(mesh.devices.reshape(GROUPS, blocks, fsdp), (*CHIPS, "fsdp"))
            body, chips = kernel_body, CHIPS
        else:
            grid, body, chips = mesh, plain_body, ("dp",)
        every = P((*chips, "fsdp"))
        return jax.shard_map(
            body,
            mesh=grid,
            in_specs=(every, every, every, P(None, "fsdp"), P(None, "fsdp")),
            out_specs=(P(chips, "fsdp"), every),
            check_vma=False,
        )(teacher_feat, student_feat, crop_weight, teacher_v, student_v)

    return run
```

```python
import functools
import math

import jax
import jax.numpy as jnp
from jax import lax
from jax.experimental import pallas as pl
from jax.experimental.pallas import tpu as pltpu
from jax.sharding import Mesh
from jax.sharding import PartitionSpec as P

ITERS = 3

teacher_temp = 0.04
student_temp = 0.1
epsilon = 1e-06

GROUPS = 2
TILE = 256
HALF_TILE = 512
FETCH = 2
LANES = 128
VMEM_BYTES = 12 << 20
KEPT_BYTES = 18 << 20

EVERY = ("dp", "fsdp")
CHIPS = ("group", "block")
GROUP = ("block", "fsdp")


def unit_rows(values):
    floats = values.astype(jnp.float32)
    length = jnp.sqrt(jnp.sum(floats * floats, axis=1, keepdims=True) + epsilon)
    return (floats / length, length)


def unit_columns(values):
    floats = values.astype(jnp.float32)
    length = jnp.sqrt(jnp.sum(floats * floats, axis=0, keepdims=True) + epsilon)
    return (floats / length, length)


COPY_BYTES = 1 << 22


def share(values, axes):
    count = lax.axis_size(axes)
    if count * values.size * values.dtype.itemsize > COPY_BYTES:
        return lax.all_gather(values, axes)
    return lax.all_to_all(jnp.broadcast_to(values, (count, *values.shape)), axes, 0, 0)


def add_up(values):
    if lax.axis_size(EVERY) * values.size * values.dtype.itemsize > COPY_BYTES:
        return lax.psum(values, EVERY)
    return jnp.sum(share(values, EVERY), axis=0)


def plain_body(teacher_feat, student_feat, crop_weight, teacher_v, student_v):
    fsdp = lax.axis_size("fsdp")
    devices = lax.axis_size("dp") * fsdp
    own_rows, width = teacher_feat.shape
    crops = own_rows * devices
    block = teacher_v.shape[1] // lax.axis_size("dp")
    prototypes = block * devices
    first = lax.axis_index("dp") * block

    teacher_hat, _ = unit_rows(teacher_feat)
    student_hat, student_len = unit_rows(student_feat)
    units = jnp.concatenate(
        [teacher_hat.astype(jnp.bfloat16), student_hat.astype(jnp.bfloat16)], axis=1
    )
    units = share(share(units, "dp"), "fsdp").reshape(crops, 2 * width)
    teacher_unit, student_unit = units[:, :width], units[:, width:]

    teacher_w, _ = unit_columns(lax.dynamic_slice_in_dim(teacher_v, first, block, 1))
    student_w, student_wlen = unit_columns(lax.dynamic_slice_in_dim(student_v, first, block, 1))
    student_wunit = student_w.astype(jnp.bfloat16)

    mass = jnp.exp(
        jnp.dot(teacher_unit, teacher_w.astype(jnp.bfloat16), preferred_element_type=jnp.float32)
        / teacher_temp
    )
    student_mass = jnp.exp(
        jnp.dot(student_unit, student_wunit, preferred_element_type=jnp.float32) / student_temp
    )
    student_part = jnp.sum(student_mass, axis=1)

    crop_scale = None
    for sweep in range(ITERS):
        scaled = mass if sweep == 0 else mass * crop_scale[:, None]
        proto_scale = 1.0 / (prototypes * jnp.sum(scaled, axis=0))
        crop_part = jnp.sum(mass * proto_scale[None, :], axis=1)
        if sweep == 0:
            placed = jnp.zeros((fsdp, crops // (fsdp * own_rows), own_rows), jnp.float32)
            own = crop_weight.astype(jnp.float32)[None, None]
            spot = (lax.axis_index("fsdp"), lax.axis_index("dp"), 0)
            placed = lax.dynamic_update_slice(placed, own, spot).reshape(crops)
            sums = add_up(jnp.stack([crop_part, student_part, placed]))
            crop_mass, student_total, weights = sums[0], sums[1], sums[2]
        else:
            crop_mass = add_up(crop_part)
        crop_scale = 1.0 / (crops * crop_mass)

    target = crops * (mass * crop_scale[:, None] * proto_scale[None, :])
    student_prob = student_mass / student_total[:, None]
    gradient = ((student_prob - target) * weights[:, None] / student_temp).astype(jnp.bfloat16)
    feature_part = lax.dot_general(
        gradient, student_wunit, (((1,), (1,)), ((), ())), preferred_element_type=jnp.float32
    )
    weight_grad = lax.dot_general(
        student_unit, gradient, (((0,), (0,)), ((), ())), preferred_element_type=jnp.float32
    )
    weight_dot = jnp.sum(student_w * weight_grad, axis=0, keepdims=True)
    grad_block = (weight_grad - student_w * weight_dot) / student_wlen

    feature_sent = feature_part.astype(jnp.bfloat16).reshape(fsdp, -1, own_rows, width)
    feature_sent = jnp.swapaxes(feature_sent, 0, 1).reshape(devices, own_rows, width)
    feature_all = lax.all_to_all(feature_sent, EVERY, 0, 0)
    feature_grad = jnp.sum(feature_all.astype(jnp.float32), axis=0)
    grad_feat = (
        feature_grad - student_hat * jnp.sum(student_hat * feature_grad, axis=1, keepdims=True)
    ) / student_len
    grad_v = lax.all_to_all(grad_block.astype(jnp.bfloat16), "dp", 0, 1, tiled=True)
    return (grad_v.astype(jnp.float32), grad_feat)


def call(kernel, out_shape, flops=0, moved=0, exps=0, **more):
    return pl.pallas_call(
        kernel,
        out_shape=out_shape,
        compiler_params=pltpu.CompilerParams(vmem_limit_bytes=VMEM_BYTES),
        cost_estimate=pl.CostEstimate(flops=flops, bytes_accessed=moved, transcendentals=exps),
        **more,
    )


def units_kernel(teacher_ref, student_ref, weight_ref, units_out, teacher_vmem, student_vmem, weight_vmem, sems):
    copies = [
        pltpu.make_async_copy(teacher_ref, teacher_vmem, sems.at[0]),
        pltpu.make_async_copy(student_ref, student_vmem, sems.at[1]),
        pltpu.make_async_copy(weight_ref, weight_vmem, sems.at[2]),
    ]
    for copy in copies:
        copy.start()
    for copy in copies:
        copy.wait()
    rows, width = teacher_vmem.shape
    units_out[:rows, :width] = unit_rows(teacher_vmem[...])[0].astype(jnp.bfloat16)
    units_out[:rows, width:] = unit_rows(student_vmem[...])[0].astype(jnp.bfloat16)
    weights = weight_vmem[...].astype(jnp.float32)
    weights = jnp.concatenate([weights, jnp.zeros((1, 2 * width - rows), jnp.float32)], axis=1)
    units_out[rows:, :] = jnp.broadcast_to(weights, (units_out.shape[0] - rows, 2 * width)).astype(jnp.bfloat16)


def spread_kernel(*refs):
    *unit_refs, sent_ref = refs
    rows = sent_ref.shape[1] // GROUPS
    values = jnp.concatenate([ref[:rows, :] for ref in unit_refs], axis=0)
    for chip in range(sent_ref.shape[0]):
        sent_ref[chip] = values


def placed_weights(unit_refs, lines, rows, chips):
    group, block = lax.axis_index("group"), lax.axis_index("block")
    line = lax.broadcasted_iota(jnp.int32, (lines, LANES), 0)
    part = lax.broadcasted_iota(jnp.int32, (lines, LANES), 1) // rows
    each = LANES // rows
    placed = jnp.zeros((lines, LANES), jnp.float32)
    for back, ref in enumerate(unit_refs):
        at = lax.axis_index("fsdp") * chips * GROUPS + ((group + GROUPS - back) % GROUPS) * chips + block
        weights = ref[rows:, :LANES].astype(jnp.float32)[0:1, :rows]
        weights = jnp.concatenate([weights] * each, axis=1)
        here = (line == at // each) & (part == at % each)
        placed = placed + jnp.where(here, jnp.broadcast_to(weights, (lines, LANES)), 0.0)
    return placed


def directions_kernel(block_ref, teacher_ref, student_ref, teacher_out, student_out, inverse_out):
    teacher, _ = unit_columns(teacher_ref[...])
    teacher_out[...] = jnp.transpose(teacher).astype(jnp.bfloat16)
    student, length = unit_columns(student_ref[...])
    student_out[...] = jnp.transpose(student).astype(jnp.bfloat16)
    inverse_out[...] = 1.0 / length


def exponentials(directions, units, temperature):
    logits = lax.dot_general(
        directions, units, (((1,), (1,)), ((), ())), preferred_element_type=jnp.float32
    )
    return jnp.exp2(logits * (math.log2(math.e) / temperature))


def fold(values):
    rows, lanes = values.shape
    return jnp.sum(values.reshape(rows // 8, 8, lanes), axis=0)


def as_rows(line):
    return jnp.concatenate([line[:, at : at + LANES] for at in range(0, line.shape[1], LANES)], axis=0)


def as_line(rows):
    return jnp.concatenate([rows[at : at + 1, :] for at in range(rows.shape[0])], axis=1)


def in_core_order(core, own, other, body):
    @pl.when(core == 0)
    def _():
        body(own, other)

    @pl.when(core == 1)
    def _():
        body(other, own)


def sums(first, second):
    lines = [as_rows(jnp.sum(total, axis=0, keepdims=True)) for total in (first, second)]
    return jnp.concatenate(lines, axis=0)


def send(sent_ref, *rows):
    values = jnp.concatenate(rows, axis=0).astype(jnp.bfloat16)
    for device in range(sent_ref.shape[0]):
        sent_ref[device] = values


def halves(rows):
    line = as_line(rows)
    half = line.shape[1] // 2
    return line[:, :half], line[:, half:]


def received(got_ref, at=0):
    total = got_ref[0, at:, :].astype(jnp.float32)
    for device in range(1, got_ref.shape[0]):
        total = total + got_ref[device, at:, :].astype(jnp.float32)
    return total


def in_chip_order(got_ref, teacher_ref, student_ref):
    chips = got_ref.shape[0]
    width = teacher_ref.shape[1]
    rows = teacher_ref.shape[0] // (GROUPS * chips)
    group = lax.axis_index("group")
    for back in range(GROUPS):
        for chip in range(chips):
            at = (((group + GROUPS - back) % GROUPS) * chips + chip) * rows
            here = pl.ds(pl.multiple_of(at, rows), rows)
            teacher_ref[here, :] = got_ref[chip, back * rows : (back + 1) * rows, :width]
            student_ref[here, :] = got_ref[chip, back * rows : (back + 1) * rows, width:]


def turn(units):
    return jnp.transpose(units.astype(jnp.float32)).astype(jnp.bfloat16)


def own_kernel(
    teacher_w_ref, student_w_ref, got_ref, teacher_ref, student_ref, part_ref, turned_ref, teacher_units, student_units
):
    in_chip_order(got_ref, teacher_units, student_units)
    turned_ref[...] = turn(student_units[...])
    part = 0.0
    for start in range(0, teacher_ref.shape[0], HALF_TILE):
        here = slice(start, start + HALF_TILE)
        teacher_ref[here, :] = exponentials(teacher_w_ref[here, :], teacher_units[...], teacher_temp)
        mass = exponentials(student_w_ref[here, :], student_units[...], student_temp)
        student_ref[here, :] = mass
        part = part + fold(mass)
    part_ref[...] = part


def other_kernel(prototypes, teacher_w_ref, student_w_ref, got_ref, own_ref, own_part_ref, *refs):
    unit_refs = refs[:GROUPS]
    teacher_ref, student_ref, sent_ref, part_ref, turned_ref, teacher_units, student_units = refs[GROUPS:]
    chips = got_ref.shape[0]
    in_chip_order(got_ref, teacher_units, student_units)
    turned_ref[...] = turn(student_units[...])
    half = own_ref.shape[1]
    placed = placed_weights(unit_refs, 2 * half // LANES, half // (GROUPS * chips), chips)
    own_total = total = part = 0.0
    for start in range(0, teacher_ref.shape[0], HALF_TILE):
        here = slice(start, start + HALF_TILE)
        mass = exponentials(teacher_w_ref[here, :], teacher_units[...], teacher_temp)
        teacher_ref[here, :] = mass
        own = own_ref[here, :]
        scale = 1.0 / (prototypes * jnp.sum(own + mass, axis=1, keepdims=True))
        own_total = own_total + fold(own * scale)
        total = total + fold(mass * scale)
        mass = exponentials(student_w_ref[here, :], student_units[...], student_temp)
        student_ref[here, :] = mass
        part = part + fold(mass)

    def finish(first, second):
        send(sent_ref, sums(first[0], second[0]), placed)
        part_ref[...] = sums(first[1], second[1])

    in_core_order(lax.axis_index("fsdp"), (own_total, own_part_ref[...]), (total, part), finish)


def sweep(prototypes, crops, first_ref, second_ref, received_sums, scaled_refs=None):
    first_crop, second_crop = halves(1.0 / (crops * received_sums))
    first_total = second_total = 0.0
    for start in range(0, first_ref.shape[0], TILE):
        here = slice(start, start + TILE)
        first, second = first_ref[here, :], second_ref[here, :]
        proto = jnp.sum(first * first_crop + second * second_crop, axis=1, keepdims=True)
        scale = 1.0 / (prototypes * proto)
        first, second = first * scale, second * scale
        if scaled_refs is not None:
            scaled_refs[0][here, :], scaled_refs[1][here, :] = first, second
        first_total = first_total + fold(first)
        second_total = second_total + fold(second)
    return sums(first_total, second_total)


def sweep_kernel(prototypes, crops, own_ref, other_ref, got_ref, part_ref, sent_ref, weight_ref):
    lines = crops // LANES
    extra = received(got_ref)
    weight_ref[...] = extra[lines:]

    def body(first_ref, second_ref):
        send(sent_ref, sweep(prototypes, crops, first_ref, second_ref, extra[:lines]), part_ref[...])

    in_core_order(lax.axis_index("fsdp"), own_ref, other_ref, body)


def last_sweep_kernel(
    prototypes, crops, own_ref, other_ref, got_ref, directions_ref,
    sent_ref, own_scaled_ref, other_scaled_ref, copy_ref, sems,
):
    pieces, _, span = copy_ref.shape
    copies = []
    for piece in range(pieces):
        columns = pl.ds(pl.multiple_of((lax.axis_index("block") * pieces + piece) * span, span), span)
        copies.append(pltpu.make_async_copy(directions_ref.at[:, columns], copy_ref.at[piece], sems.at[piece]))
        copies[-1].start()

    total = received(got_ref)[: crops // LANES]

    def body(first_refs, second_refs):
        (first_ref, *scaled_refs), (second_ref, second_scaled_ref) = first_refs, second_refs
        sent = sweep(prototypes, crops, first_ref, second_ref, total, (*scaled_refs, second_scaled_ref))
        send(sent_ref, sent)

    in_core_order(lax.axis_index("fsdp"), (own_ref, own_scaled_ref), (other_ref, other_scaled_ref), body)
    for copy in copies:
        copy.wait()


def units_tile(copy_ref, inverse_ref, start):
    span = copy_ref.shape[2]
    at = start % span
    return copy_ref[start // span, :, at : at + TILE].astype(jnp.float32) * inverse_ref[:, start : start + TILE]


def gradient_kernel(
    own_mass_ref, other_mass_ref, own_student_ref, other_student_ref, weight_ref, second_ref, third_ref,
    inverse_ref, copy_ref, gradient_ref, keep_ref, give_ref, unit_ref,
):
    group, core = lax.axis_index("group"), lax.axis_index("fsdp")
    count, half = own_mass_ref.shape
    lines = 2 * half // LANES
    weights = weight_ref[...] / student_temp
    teacher_scales = halves(weights / received(third_ref)[:lines])
    student_scales = halves(weights / received(second_ref)[lines:])

    def body(first_refs, second_refs):
        for start in range(0, count, TILE):
            here = slice(start, start + TILE)
            for (side, mass_ref, student_ref), teacher_scale, student_scale in zip(
                (first_refs, second_refs), teacher_scales, student_scales
            ):
                gradient = student_ref[here, :] * student_scale - mass_ref[here, :] * teacher_scale
                gradient_ref[side, start : start + TILE, :] = gradient.astype(jnp.bfloat16)

    in_core_order(core, (0, own_mass_ref, own_student_ref), (1, other_mass_ref, other_student_ref), body)
    for start in range(0, count, TILE):
        unit_ref[:, start : start + TILE] = units_tile(copy_ref, inverse_ref, start).astype(jnp.bfloat16)
    kept = half // GROUPS
    lanes = pl.ds(pl.multiple_of(group * kept, kept), kept)
    for side, out_ref in enumerate((keep_ref, give_ref)):
        feature = jnp.dot(unit_ref[...], gradient_ref[side, :, lanes], preferred_element_type=jnp.float32)
        out_ref[...] = jnp.transpose(feature).astype(out_ref.dtype)


def weight_kernel(gradient_ref, own_turned_ref, other_turned_ref, inverse_ref, copy_ref, sent_ref, grad_ref):
    chips, rows_each, _ = sent_ref.shape
    count = gradient_ref.shape[1]
    width = own_turned_ref.shape[0]
    kept = width // GROUPS
    own_rows = pl.ds(pl.multiple_of(lax.axis_index("group") * kept, kept), kept)
    for start in range(0, count, TILE):
        here, slot = slice(start, start + TILE), start // TILE
        weight_grad = 0.0
        for side, turned_ref in enumerate((own_turned_ref, other_turned_ref)):
            weight_grad = weight_grad + lax.dot_general(
                turned_ref[...], gradient_ref[side, here, :], (((1,), (1,)), ((), ())), preferred_element_type=jnp.float32
            )
        unit = units_tile(copy_ref, inverse_ref, start)
        dot = jnp.sum(unit * weight_grad, axis=0, keepdims=True)
        grad_ref[slot] = (weight_grad - unit * dot) * inverse_ref[:, here]
        own = grad_ref[slot, own_rows, :].astype(jnp.bfloat16)
        sent_ref[:, :, here] = own.reshape(chips, rows_each, TILE)


def pack_kernel(keep_ref, other_ref, _, sent_ref, packed_ref, sem):
    chips, rows_each, lanes = packed_ref.shape
    width = keep_ref.shape[1]
    total = (keep_ref[...] + other_ref[...].astype(jnp.float32)).astype(jnp.bfloat16)
    total = total.reshape(chips, -1, width)
    for piece in range(lanes // width):
        packed_ref[:, :, piece * width : (piece + 1) * width] = total[:, piece * rows_each : (piece + 1) * rows_each, :]
    copy = pltpu.make_async_copy(packed_ref, sent_ref.at[:, :, pl.ds(sent_ref.shape[2] - lanes, lanes)], sem)
    copy.start()
    copy.wait()


def outputs_kernel(got_ref, student_ref, weight_out, feature_out):
    chips, rows_each, columns = got_ref.shape
    rows, width = student_ref.shape
    pieces = rows // rows_each
    count = columns - pieces * width
    total = got_ref[0, :, count:].astype(jnp.float32)
    for chip in range(1, chips):
        total = total + got_ref[chip, :, count:].astype(jnp.float32)
    total = jnp.concatenate([total[:, piece * width : (piece + 1) * width] for piece in range(pieces)], axis=0)
    hat, length = unit_rows(student_ref[...])
    feature_out[...] = (total - hat * jnp.sum(hat * total, axis=1, keepdims=True)) / length
    for chip in range(chips):
        weight_out[:, chip * count : (chip + 1) * count] = got_ref[chip, :, :count].astype(jnp.float32)


def kernel_body(teacher_feat, student_feat, crop_weight, teacher_v, student_v):
    f32, bf16 = jnp.float32, jnp.bfloat16
    shape = jax.ShapeDtypeStruct
    blocks, fsdp = lax.axis_size("block"), lax.axis_size("fsdp")
    chips = blocks * GROUPS
    members, devices = blocks * fsdp, chips * fsdp
    rows, width = teacher_feat.shape
    crops = rows * devices
    lines = crops // LANES
    kept = teacher_v.shape[1]
    prototypes = kept * fsdp
    count = kept // blocks
    group, block = lax.axis_index("group")[None], lax.axis_index("block")[None]
    core = lax.axis_index("fsdp")[None]
    elements = count * crops
    vmem = pl.BlockSpec(memory_space=pltpu.VMEM)

    def swap(values):
        return lax.ppermute(values, "fsdp", [(0, 1), (1, 0)])

    def share(values):
        return lax.all_to_all(values, GROUP, 0, 0)

    dma = pltpu.SemaphoreType.DMA
    hbm = functools.partial(pltpu.with_memory_space_constraint, memory_space=pltpu.HBM)
    units = call(
        units_kernel,
        shape((rows + 16, 2 * width), bf16),
        in_specs=[pl.BlockSpec(memory_space=pl.ANY)] * 3,
        scratch_shapes=[pltpu.VMEM((rows, width), bf16)] * 2 + [pltpu.VMEM((1, rows), bf16), dma((3,))],
    )(hbm(teacher_feat), hbm(student_feat), hbm(crop_weight[None, :]))

    def of_groups(values):
        return [values] + [
            lax.ppermute(values, "group", [(at, (at + back) % GROUPS) for at in range(GROUPS)]) for back in range(1, GROUPS)
        ]

    units = of_groups(units)

    span = 2 * TILE
    spans = count // span
    column = pl.BlockSpec((width, span), lambda step, at: (0, at[0] * spans + step))
    turned = pl.BlockSpec((span, width), lambda step, at: (step, 0))
    line = pl.BlockSpec((1, span), lambda step, at: (0, step))
    teacher_w, student_w, inverse = call(
        directions_kernel,
        (
            shape((count, width), bf16),
            shape((count, width), bf16),
            shape((1, count), f32),
        ),
        flops=12 * count * width,
        moved=8 * count * width,
        grid_spec=pltpu.PrefetchScalarGridSpec(
            num_scalar_prefetch=1,
            grid=(spans,),
            in_specs=[column, column],
            out_specs=[turned, turned, line],
        ),
    )(
        block,
        hbm(teacher_v),
        hbm(student_v),
    )

    units, teacher_w = lax.optimization_barrier((units, teacher_w))
    sent = call(spread_kernel, shape((blocks, GROUPS * rows, 2 * width), bf16))(*units)
    own = lax.all_to_all(sent, "block", 0, 0)
    other = swap(own)
    half = crops // 2
    anyspace = pl.BlockSpec(memory_space=pl.ANY)
    pieces = count // (FETCH * TILE)
    halved = dict(flops=2 * elements * width, exps=elements)
    scratch = [pltpu.VMEM((half, width), bf16)] * 2
    own_mass, own_student, own_part, own_turned = call(
        own_kernel,
        (
            shape((count, half), f32),
            shape((count, half), f32),
            shape((8, half), f32),
            shape((width, half), bf16),
        ),
        scratch_shapes=scratch,
        **halved,
    )(teacher_w, student_w, own)
    other_mass, other_student, sent, student_part, other_turned = call(
        functools.partial(other_kernel, prototypes),
        (
            shape((count, half), f32),
            shape((count, half), f32),
            shape((members, 2 * lines, LANES), bf16),
            shape((lines, LANES), f32),
            shape((width, half), bf16),
        ),
        scratch_shapes=scratch,
        **halved,
    )(teacher_w, student_w, other, own_mass, own_part, *units)
    first = share(sent)
    sent, weights = call(
        functools.partial(sweep_kernel, prototypes, crops),
        (shape((members, 2 * lines, LANES), bf16), shape((lines, LANES), f32)),
        flops=4 * elements,
    )(own_mass, other_mass, first, student_part)
    second = share(sent)
    sent, own_scaled, other_scaled, student_copy = call(
        functools.partial(last_sweep_kernel, prototypes, crops),
        (
            shape((members, lines, LANES), bf16),
            shape((count, half), f32),
            shape((count, half), f32),
            shape((pieces, width, count // pieces), bf16),
        ),
        flops=4 * elements,
        in_specs=[vmem] * 3 + [anyspace],
        scratch_shapes=[dma((pieces,))],
    )(own_mass, other_mass, second, hbm(student_v))
    third = share(sent)

    gradient, keep, give = call(
        gradient_kernel,
        (shape((2, count, half), bf16), shape((half // GROUPS, width), f32), shape((half // GROUPS, width), bf16)),
        flops=2 * elements * width // GROUPS,
        in_specs=[vmem] * 9,
        scratch_shapes=[pltpu.VMEM((width, count), bf16)],
    )(own_scaled, other_scaled, own_student, other_student, weights, second, third, inverse, student_copy)
    other = swap(give)
    out_rows = width // chips
    per_chip = rows * width // out_rows
    sent = call(
        weight_kernel,
        shape((blocks, out_rows, count + per_chip), bf16),
        flops=2 * elements * width,
        in_specs=[vmem] * 5,
        scratch_shapes=[pltpu.VMEM((count // TILE, width, TILE), f32)],
    )(gradient, own_turned, other_turned, inverse, student_copy)
    sent = call(
        pack_kernel,
        shape((blocks, out_rows, count + per_chip), bf16),
        in_specs=[vmem] * 2 + [anyspace],
        out_specs=anyspace,
        input_output_aliases={2: 0},
        scratch_shapes=[pltpu.VMEM((blocks, out_rows, per_chip), bf16), dma],
    )(keep, other, sent)
    got = lax.all_to_all(sent, "block", 0, 0)
    return call(
        outputs_kernel, (shape((out_rows, kept), f32), shape((rows, width), f32))
    )(got, student_feat)


def solution(mesh):
    dp, fsdp = mesh.shape["dp"], mesh.shape["fsdp"]
    blocks = dp // GROUPS

    def run(teacher_feat, student_feat, crop_weight, teacher_v, student_v):
        crops = teacher_feat.shape[0]
        count = teacher_v.shape[1] // (blocks * fsdp)
        fits = fsdp == 2 and dp == 16 and count % (2 * TILE) == 0 and crops == 1024
        if fits and 8 * count * crops <= KEPT_BYTES:
            grid = Mesh(mesh.devices.reshape(GROUPS, blocks, fsdp), (*CHIPS, "fsdp"))
            body, chips = kernel_body, CHIPS
        else:
            grid, body, chips = mesh, plain_body, ("dp",)
        every = P((*chips, "fsdp"))
        return jax.shard_map(
            body,
            mesh=grid,
            in_specs=(every, every, every, P(None, "fsdp"), P(None, "fsdp")),
            out_specs=(P(chips, "fsdp"), every),
            check_vma=False,
        )(teacher_feat, student_feat, crop_weight, teacher_v, student_v)

    return run
```

```python
import functools
import math

import jax
import jax.numpy as jnp
from jax import lax
from jax.experimental import pallas as pl
from jax.experimental.pallas import tpu as pltpu
from jax.sharding import Mesh
from jax.sharding import PartitionSpec as P

ITERS = 3

teacher_temp = 0.04
student_temp = 0.1
epsilon = 1e-06

GROUPS = 2
TILE = 256
HALF_TILE = 512
LANES = 128
VMEM_BYTES = 12 << 20
KEPT_BYTES = 18 << 20

EVERY = ("dp", "fsdp")
CHIPS = ("group", "block")
GROUP = ("block", "fsdp")


def unit_rows(values):
    floats = values.astype(jnp.float32)
    length = jnp.sqrt(jnp.sum(floats * floats, axis=1, keepdims=True) + epsilon)
    return (floats / length, length)


def unit_columns(values):
    floats = values.astype(jnp.float32)
    length = jnp.sqrt(jnp.sum(floats * floats, axis=0, keepdims=True) + epsilon)
    return (floats / length, length)


COPY_BYTES = 1 << 22


def share(values, axes):
    count = lax.axis_size(axes)
    if count * values.size * values.dtype.itemsize > COPY_BYTES:
        return lax.all_gather(values, axes)
    return lax.all_to_all(jnp.broadcast_to(values, (count, *values.shape)), axes, 0, 0)


def add_up(values):
    if lax.axis_size(EVERY) * values.size * values.dtype.itemsize > COPY_BYTES:
        return lax.psum(values, EVERY)
    return jnp.sum(share(values, EVERY), axis=0)


def plain_body(teacher_feat, student_feat, crop_weight, teacher_v, student_v):
    fsdp = lax.axis_size("fsdp")
    devices = lax.axis_size("dp") * fsdp
    own_rows, width = teacher_feat.shape
    crops = own_rows * devices
    block = teacher_v.shape[1] // lax.axis_size("dp")
    prototypes = block * devices
    first = lax.axis_index("dp") * block

    teacher_hat, _ = unit_rows(teacher_feat)
    student_hat, student_len = unit_rows(student_feat)
    units = jnp.concatenate(
        [teacher_hat.astype(jnp.bfloat16), student_hat.astype(jnp.bfloat16)], axis=1
    )
    units = share(share(units, "dp"), "fsdp").reshape(crops, 2 * width)
    teacher_unit, student_unit = units[:, :width], units[:, width:]

    teacher_w, _ = unit_columns(lax.dynamic_slice_in_dim(teacher_v, first, block, 1))
    student_w, student_wlen = unit_columns(lax.dynamic_slice_in_dim(student_v, first, block, 1))
    student_wunit = student_w.astype(jnp.bfloat16)

    mass = jnp.exp(
        jnp.dot(teacher_unit, teacher_w.astype(jnp.bfloat16), preferred_element_type=jnp.float32)
        / teacher_temp
    )
    student_mass = jnp.exp(
        jnp.dot(student_unit, student_wunit, preferred_element_type=jnp.float32) / student_temp
    )
    student_part = jnp.sum(student_mass, axis=1)

    crop_scale = None
    for sweep in range(ITERS):
        scaled = mass if sweep == 0 else mass * crop_scale[:, None]
        proto_scale = 1.0 / (prototypes * jnp.sum(scaled, axis=0))
        crop_part = jnp.sum(mass * proto_scale[None, :], axis=1)
        if sweep == 0:
            placed = jnp.zeros((fsdp, crops // (fsdp * own_rows), own_rows), jnp.float32)
            own = crop_weight.astype(jnp.float32)[None, None]
            spot = (lax.axis_index("fsdp"), lax.axis_index("dp"), 0)
            placed = lax.dynamic_update_slice(placed, own, spot).reshape(crops)
            sums = add_up(jnp.stack([crop_part, student_part, placed]))
            crop_mass, student_total, weights = sums[0], sums[1], sums[2]
        else:
            crop_mass = add_up(crop_part)
        crop_scale = 1.0 / (crops * crop_mass)

    target = crops * (mass * crop_scale[:, None] * proto_scale[None, :])
    student_prob = student_mass / student_total[:, None]
    gradient = ((student_prob - target) * weights[:, None] / student_temp).astype(jnp.bfloat16)
    feature_part = lax.dot_general(
        gradient, student_wunit, (((1,), (1,)), ((), ())), preferred_element_type=jnp.float32
    )
    weight_grad = lax.dot_general(
        student_unit, gradient, (((0,), (0,)), ((), ())), preferred_element_type=jnp.float32
    )
    weight_dot = jnp.sum(student_w * weight_grad, axis=0, keepdims=True)
    grad_block = (weight_grad - student_w * weight_dot) / student_wlen

    feature_sent = feature_part.astype(jnp.bfloat16).reshape(fsdp, -1, own_rows, width)
    feature_sent = jnp.swapaxes(feature_sent, 0, 1).reshape(devices, own_rows, width)
    feature_all = lax.all_to_all(feature_sent, EVERY, 0, 0)
    feature_grad = jnp.sum(feature_all.astype(jnp.float32), axis=0)
    grad_feat = (
        feature_grad - student_hat * jnp.sum(student_hat * feature_grad, axis=1, keepdims=True)
    ) / student_len
    grad_v = lax.all_to_all(grad_block.astype(jnp.bfloat16), "dp", 0, 1, tiled=True)
    return (grad_v.astype(jnp.float32), grad_feat)


def call(kernel, out_shape, flops=0, moved=0, exps=0, **more):
    return pl.pallas_call(
        kernel,
        out_shape=out_shape,
        compiler_params=pltpu.CompilerParams(vmem_limit_bytes=VMEM_BYTES),
        cost_estimate=pl.CostEstimate(flops=flops, bytes_accessed=moved, transcendentals=exps),
        **more,
    )


def units_kernel(teacher_ref, student_ref, weight_ref, units_out, teacher_vmem, student_vmem, weight_vmem, sems):
    copies = [
        pltpu.make_async_copy(teacher_ref, teacher_vmem, sems.at[0]),
        pltpu.make_async_copy(student_ref, student_vmem, sems.at[1]),
        pltpu.make_async_copy(weight_ref, weight_vmem, sems.at[2]),
    ]
    for copy in copies:
        copy.start()
    for copy in copies:
        copy.wait()
    rows, width = teacher_vmem.shape
    units_out[:rows, :width] = unit_rows(teacher_vmem[...])[0].astype(jnp.bfloat16)
    units_out[:rows, width:] = unit_rows(student_vmem[...])[0].astype(jnp.bfloat16)
    weights = weight_vmem[...].astype(jnp.float32)
    weights = jnp.concatenate([weights, jnp.zeros((1, 2 * width - rows), jnp.float32)], axis=1)
    units_out[rows:, :] = jnp.broadcast_to(weights, (units_out.shape[0] - rows, 2 * width)).astype(jnp.bfloat16)


def spread_kernel(*refs):
    *unit_refs, sent_ref = refs
    rows = sent_ref.shape[1] // GROUPS
    values = jnp.concatenate([ref[:rows, :] for ref in unit_refs], axis=0)
    for chip in range(sent_ref.shape[0]):
        sent_ref[chip] = values


def placed_weights(unit_refs, lines, rows, chips):
    group, block = lax.axis_index("group"), lax.axis_index("block")
    line = lax.broadcasted_iota(jnp.int32, (lines, LANES), 0)
    part = lax.broadcasted_iota(jnp.int32, (lines, LANES), 1) // rows
    each = LANES // rows
    placed = jnp.zeros((lines, LANES), jnp.float32)
    for back, ref in enumerate(unit_refs):
        at = lax.axis_index("fsdp") * chips * GROUPS + ((group + GROUPS - back) % GROUPS) * chips + block
        weights = ref[rows:, :LANES].astype(jnp.float32)[0:1, :rows]
        weights = jnp.concatenate([weights] * each, axis=1)
        here = (line == at // each) & (part == at % each)
        placed = placed + jnp.where(here, jnp.broadcast_to(weights, (lines, LANES)), 0.0)
    return placed


def directions_kernel(block_ref, teacher_ref, student_ref, teacher_out, student_out, unit_out, inverse_out):
    teacher, _ = unit_columns(teacher_ref[...])
    teacher_out[...] = jnp.transpose(teacher).astype(jnp.bfloat16)
    student, length = unit_columns(student_ref[...])
    student_out[...] = jnp.transpose(student).astype(jnp.bfloat16)
    unit_out[...] = student
    inverse_out[...] = 1.0 / length


def exponentials(directions, units, temperature):
    logits = lax.dot_general(
        directions, units, (((1,), (1,)), ((), ())), preferred_element_type=jnp.float32
    )
    return jnp.exp2(logits * (math.log2(math.e) / temperature))


def fold(values):
    rows, lanes = values.shape
    return jnp.sum(values.reshape(rows // 8, 8, lanes), axis=0)


def as_rows(line):
    return jnp.concatenate([line[:, at : at + LANES] for at in range(0, line.shape[1], LANES)], axis=0)


def as_line(rows):
    return jnp.concatenate([rows[at : at + 1, :] for at in range(rows.shape[0])], axis=1)


def in_core_order(core, own, other, body):
    @pl.when(core == 0)
    def _():
        body(own, other)

    @pl.when(core == 1)
    def _():
        body(other, own)


def sums(first, second):
    lines = [as_rows(jnp.sum(total, axis=0, keepdims=True)) for total in (first, second)]
    return jnp.concatenate(lines, axis=0)


def send(sent_ref, *rows):
    values = jnp.concatenate(rows, axis=0).astype(jnp.bfloat16)
    for device in range(sent_ref.shape[0]):
        sent_ref[device] = values


def halves(rows):
    line = as_line(rows)
    half = line.shape[1] // 2
    return line[:, :half], line[:, half:]


def received(got_ref, at=0):
    total = got_ref[0, at:, :].astype(jnp.float32)
    for device in range(1, got_ref.shape[0]):
        total = total + got_ref[device, at:, :].astype(jnp.float32)
    return total


def in_chip_order(got_ref, teacher_ref, student_ref):
    chips = got_ref.shape[0]
    width = teacher_ref.shape[1]
    rows = teacher_ref.shape[0] // (GROUPS * chips)
    group = lax.axis_index("group")
    for back in range(GROUPS):
        for chip in range(chips):
            at = (((group + GROUPS - back) % GROUPS) * chips + chip) * rows
            here = pl.ds(pl.multiple_of(at, rows), rows)
            teacher_ref[here, :] = got_ref[chip, back * rows : (back + 1) * rows, :width]
            student_ref[here, :] = got_ref[chip, back * rows : (back + 1) * rows, width:]


def turn(units):
    return jnp.transpose(units.astype(jnp.float32)).astype(jnp.bfloat16)


def own_kernel(
    teacher_w_ref, student_w_ref, got_ref, teacher_ref, student_ref, part_ref, turned_ref, teacher_units, student_units
):
    in_chip_order(got_ref, teacher_units, student_units)
    turned_ref[...] = turn(student_units[...])
    part = 0.0
    for start in range(0, teacher_ref.shape[0], HALF_TILE):
        here = slice(start, start + HALF_TILE)
        teacher_ref[here, :] = exponentials(teacher_w_ref[here, :], teacher_units[...], teacher_temp)
        mass = exponentials(student_w_ref[here, :], student_units[...], student_temp)
        student_ref[here, :] = mass
        part = part + fold(mass)
    part_ref[...] = part


def other_kernel(prototypes, teacher_w_ref, student_w_ref, got_ref, own_ref, own_part_ref, *refs):
    unit_refs = refs[:GROUPS]
    teacher_ref, student_ref, sent_ref, part_ref, turned_ref, teacher_units, student_units = refs[GROUPS:]
    chips = got_ref.shape[0]
    in_chip_order(got_ref, teacher_units, student_units)
    turned_ref[...] = turn(student_units[...])
    half = own_ref.shape[1]
    placed = placed_weights(unit_refs, 2 * half // LANES, half // (GROUPS * chips), chips)
    own_total = total = part = 0.0
    for start in range(0, teacher_ref.shape[0], HALF_TILE):
        here = slice(start, start + HALF_TILE)
        mass = exponentials(teacher_w_ref[here, :], teacher_units[...], teacher_temp)
        teacher_ref[here, :] = mass
        own = own_ref[here, :]
        scale = 1.0 / (prototypes * jnp.sum(own + mass, axis=1, keepdims=True))
        own_total = own_total + fold(own * scale)
        total = total + fold(mass * scale)
        mass = exponentials(student_w_ref[here, :], student_units[...], student_temp)
        student_ref[here, :] = mass
        part = part + fold(mass)

    def finish(first, second):
        send(sent_ref, sums(first[0], second[0]), placed)
        part_ref[...] = sums(first[1], second[1])

    in_core_order(lax.axis_index("fsdp"), (own_total, own_part_ref[...]), (total, part), finish)


def sweep(prototypes, crops, first_ref, second_ref, received_sums, scaled_refs=None):
    first_crop, second_crop = halves(1.0 / (crops * received_sums))
    first_total = second_total = 0.0
    for start in range(0, first_ref.shape[0], TILE):
        here = slice(start, start + TILE)
        first, second = first_ref[here, :], second_ref[here, :]
        proto = jnp.sum(first * first_crop + second * second_crop, axis=1, keepdims=True)
        scale = 1.0 / (prototypes * proto)
        first, second = first * scale, second * scale
        if scaled_refs is not None:
            scaled_refs[0][here, :], scaled_refs[1][here, :] = first, second
        first_total = first_total + fold(first)
        second_total = second_total + fold(second)
    return sums(first_total, second_total)


def sweep_kernel(prototypes, crops, own_ref, other_ref, got_ref, part_ref, sent_ref, weight_ref):
    lines = crops // LANES
    extra = received(got_ref)
    weight_ref[...] = extra[lines:]

    def body(first_ref, second_ref):
        send(sent_ref, sweep(prototypes, crops, first_ref, second_ref, extra[:lines]), part_ref[...])

    in_core_order(lax.axis_index("fsdp"), own_ref, other_ref, body)


def last_sweep_kernel(prototypes, crops, own_ref, other_ref, got_ref, sent_ref, own_scaled_ref, other_scaled_ref):
    total = received(got_ref)[: crops // LANES]

    def body(first_refs, second_refs):
        (first_ref, *scaled_refs), (second_ref, second_scaled_ref) = first_refs, second_refs
        sent = sweep(prototypes, crops, first_ref, second_ref, total, (*scaled_refs, second_scaled_ref))
        send(sent_ref, sent)

    in_core_order(lax.axis_index("fsdp"), (own_ref, own_scaled_ref), (other_ref, other_scaled_ref), body)


def gradient_kernel(
    own_mass_ref, other_mass_ref, own_student_ref, other_student_ref, weight_ref, second_ref, third_ref,
    unit_ref, gradient_ref, keep_ref, give_ref,
):
    group, core = lax.axis_index("group"), lax.axis_index("fsdp")
    count, half = own_mass_ref.shape
    lines = 2 * half // LANES
    weights = weight_ref[...] / student_temp
    teacher_scales = halves(weights / received(third_ref)[:lines])
    student_scales = halves(weights / received(second_ref)[lines:])

    def body(first_refs, second_refs):
        for start in range(0, count, TILE):
            here = slice(start, start + TILE)
            for (side, mass_ref, student_ref), teacher_scale, student_scale in zip(
                (first_refs, second_refs), teacher_scales, student_scales
            ):
                gradient = student_ref[here, :] * student_scale - mass_ref[here, :] * teacher_scale
                gradient_ref[side, start : start + TILE, :] = gradient.astype(jnp.bfloat16)

    in_core_order(core, (0, own_mass_ref, own_student_ref), (1, other_mass_ref, other_student_ref), body)
    unit = unit_ref[...].astype(jnp.bfloat16)
    kept = half // GROUPS
    lanes = pl.ds(pl.multiple_of(group * kept, kept), kept)
    for side, out_ref in enumerate((keep_ref, give_ref)):
        feature = jnp.dot(unit, gradient_ref[side, :, lanes], preferred_element_type=jnp.float32)
        out_ref[...] = jnp.transpose(feature).astype(out_ref.dtype)


def weight_kernel(gradient_ref, own_turned_ref, other_turned_ref, inverse_ref, unit_ref, sent_ref, grad_ref):
    chips, rows_each, _ = sent_ref.shape
    count = gradient_ref.shape[1]
    width = own_turned_ref.shape[0]
    kept = width // GROUPS
    own_rows = pl.ds(pl.multiple_of(lax.axis_index("group") * kept, kept), kept)
    for start in range(0, count, TILE):
        here, slot = slice(start, start + TILE), start // TILE
        weight_grad = 0.0
        for side, turned_ref in enumerate((own_turned_ref, other_turned_ref)):
            weight_grad = weight_grad + lax.dot_general(
                turned_ref[...], gradient_ref[side, here, :], (((1,), (1,)), ((), ())), preferred_element_type=jnp.float32
            )
        unit = unit_ref[:, here]
        dot = jnp.sum(unit * weight_grad, axis=0, keepdims=True)
        grad_ref[slot] = (weight_grad - unit * dot) * inverse_ref[:, here]
        own = grad_ref[slot, own_rows, :].astype(jnp.bfloat16)
        sent_ref[:, :, here] = own.reshape(chips, rows_each, TILE)


def pack_kernel(keep_ref, other_ref, _, sent_ref, packed_ref, sem):
    chips, rows_each, lanes = packed_ref.shape
    width = keep_ref.shape[1]
    total = (keep_ref[...] + other_ref[...].astype(jnp.float32)).astype(jnp.bfloat16)
    total = total.reshape(chips, -1, width)
    for piece in range(lanes // width):
        packed_ref[:, :, piece * width : (piece + 1) * width] = total[:, piece * rows_each : (piece + 1) * rows_each, :]
    copy = pltpu.make_async_copy(packed_ref, sent_ref.at[:, :, pl.ds(sent_ref.shape[2] - lanes, lanes)], sem)
    copy.start()
    copy.wait()


def outputs_kernel(got_ref, student_ref, weight_out, feature_out):
    chips, rows_each, columns = got_ref.shape
    rows, width = student_ref.shape
    pieces = rows // rows_each
    count = columns - pieces * width
    total = got_ref[0, :, count:].astype(jnp.float32)
    for chip in range(1, chips):
        total = total + got_ref[chip, :, count:].astype(jnp.float32)
    total = jnp.concatenate([total[:, piece * width : (piece + 1) * width] for piece in range(pieces)], axis=0)
    hat, length = unit_rows(student_ref[...])
    feature_out[...] = (total - hat * jnp.sum(hat * total, axis=1, keepdims=True)) / length
    for chip in range(chips):
        weight_out[:, chip * count : (chip + 1) * count] = got_ref[chip, :, :count].astype(jnp.float32)


def kernel_body(teacher_feat, student_feat, crop_weight, teacher_v, student_v):
    f32, bf16 = jnp.float32, jnp.bfloat16
    shape = jax.ShapeDtypeStruct
    blocks, fsdp = lax.axis_size("block"), lax.axis_size("fsdp")
    chips = blocks * GROUPS
    members, devices = blocks * fsdp, chips * fsdp
    rows, width = teacher_feat.shape
    crops = rows * devices
    lines = crops // LANES
    kept = teacher_v.shape[1]
    prototypes = kept * fsdp
    count = kept // blocks
    group, block = lax.axis_index("group")[None], lax.axis_index("block")[None]
    core = lax.axis_index("fsdp")[None]
    elements = count * crops
    vmem = pl.BlockSpec(memory_space=pltpu.VMEM)

    def swap(values):
        return lax.ppermute(values, "fsdp", [(0, 1), (1, 0)])

    def share(values):
        return lax.all_to_all(values, GROUP, 0, 0)

    dma = pltpu.SemaphoreType.DMA
    hbm = functools.partial(pltpu.with_memory_space_constraint, memory_space=pltpu.HBM)
    units = call(
        units_kernel,
        shape((rows + 16, 2 * width), bf16),
        in_specs=[pl.BlockSpec(memory_space=pl.ANY)] * 3,
        scratch_shapes=[pltpu.VMEM((rows, width), bf16)] * 2 + [pltpu.VMEM((1, rows), bf16), dma((3,))],
    )(hbm(teacher_feat), hbm(student_feat), hbm(crop_weight[None, :]))

    def of_groups(values):
        return [values] + [
            lax.ppermute(values, "group", [(at, (at + back) % GROUPS) for at in range(GROUPS)]) for back in range(1, GROUPS)
        ]

    units = of_groups(units)

    span = 2 * TILE
    spans = count // span
    column = pl.BlockSpec((width, span), lambda step, at: (0, at[0] * spans + step))
    turned = pl.BlockSpec((span, width), lambda step, at: (step, 0))
    straight = pl.BlockSpec((width, span), lambda step, at: (0, step))
    line = pl.BlockSpec((1, span), lambda step, at: (0, step))
    teacher_w, student_w, student_unit, inverse = call(
        directions_kernel,
        (
            shape((count, width), bf16),
            shape((count, width), bf16),
            shape((width, count), f32),
            shape((1, count), f32),
        ),
        flops=12 * count * width,
        moved=8 * count * width,
        grid_spec=pltpu.PrefetchScalarGridSpec(
            num_scalar_prefetch=1,
            grid=(spans,),
            in_specs=[column, column],
            out_specs=[turned, turned, straight, line],
        ),
    )(
        block,
        hbm(teacher_v),
        hbm(student_v),
    )

    units, teacher_w = lax.optimization_barrier((units, teacher_w))
    sent = call(spread_kernel, shape((blocks, GROUPS * rows, 2 * width), bf16))(*units)
    own = lax.all_to_all(sent, "block", 0, 0)
    other = swap(own)
    half = crops // 2
    anyspace = pl.BlockSpec(memory_space=pl.ANY)
    halved = dict(flops=2 * elements * width, exps=elements)
    scratch = [pltpu.VMEM((half, width), bf16)] * 2
    own_mass, own_student, own_part, own_turned = call(
        own_kernel,
        (
            shape((count, half), f32),
            shape((count, half), f32),
            shape((8, half), f32),
            shape((width, half), bf16),
        ),
        scratch_shapes=scratch,
        **halved,
    )(teacher_w, student_w, own)
    other_mass, other_student, sent, student_part, other_turned = call(
        functools.partial(other_kernel, prototypes),
        (
            shape((count, half), f32),
            shape((count, half), f32),
            shape((members, 2 * lines, LANES), bf16),
            shape((lines, LANES), f32),
            shape((width, half), bf16),
        ),
        scratch_shapes=scratch,
        **halved,
    )(teacher_w, student_w, other, own_mass, own_part, *units)
    first = share(sent)
    sent, weights = call(
        functools.partial(sweep_kernel, prototypes, crops),
        (shape((members, 2 * lines, LANES), bf16), shape((lines, LANES), f32)),
        flops=4 * elements,
    )(own_mass, other_mass, first, student_part)
    second = share(sent)
    sent, own_scaled, other_scaled = call(
        functools.partial(last_sweep_kernel, prototypes, crops),
        (
            shape((members, lines, LANES), bf16),
            shape((count, half), f32),
            shape((count, half), f32),
        ),
        flops=4 * elements,
    )(own_mass, other_mass, second)
    third = share(sent)

    gradient, keep, give = call(
        gradient_kernel,
        (shape((2, count, half), bf16), shape((half // GROUPS, width), f32), shape((half // GROUPS, width), bf16)),
        flops=2 * elements * width // GROUPS,
    )(own_scaled, other_scaled, own_student, other_student, weights, second, third, student_unit)
    other = swap(give)
    out_rows = width // chips
    per_chip = rows * width // out_rows
    sent = call(
        weight_kernel,
        shape((blocks, out_rows, count + per_chip), bf16),
        flops=2 * elements * width,
        in_specs=[vmem] * 5,
        scratch_shapes=[pltpu.VMEM((count // TILE, width, TILE), f32)],
    )(gradient, own_turned, other_turned, inverse, student_unit)
    sent = call(
        pack_kernel,
        shape((blocks, out_rows, count + per_chip), bf16),
        in_specs=[vmem] * 2 + [anyspace],
        out_specs=anyspace,
        input_output_aliases={2: 0},
        scratch_shapes=[pltpu.VMEM((blocks, out_rows, per_chip), bf16), dma],
    )(keep, other, sent)
    got = lax.all_to_all(sent, "block", 0, 0)
    return call(
        outputs_kernel, (shape((out_rows, kept), f32), shape((rows, width), f32))
    )(got, student_feat)


def solution(mesh):
    dp, fsdp = mesh.shape["dp"], mesh.shape["fsdp"]
    blocks = dp // GROUPS

    def run(teacher_feat, student_feat, crop_weight, teacher_v, student_v):
        crops = teacher_feat.shape[0]
        count = teacher_v.shape[1] // (blocks * fsdp)
        fits = fsdp == 2 and dp == 16 and count % (2 * TILE) == 0 and crops == 1024
        if fits and 8 * count * crops <= KEPT_BYTES:
            grid = Mesh(mesh.devices.reshape(GROUPS, blocks, fsdp), (*CHIPS, "fsdp"))
            body, chips = kernel_body, CHIPS
        else:
            grid, body, chips = mesh, plain_body, ("dp",)
        every = P((*chips, "fsdp"))
        return jax.shard_map(
            body,
            mesh=grid,
            in_specs=(every, every, every, P(None, "fsdp"), P(None, "fsdp")),
            out_specs=(P(chips, "fsdp"), every),
            check_vma=False,
        )(teacher_feat, student_feat, crop_weight, teacher_v, student_v)

    return run
```

```python
import functools
import math

import jax
import jax.numpy as jnp
from jax import lax
from jax.experimental import pallas as pl
from jax.experimental.pallas import tpu as pltpu
from jax.sharding import Mesh
from jax.sharding import PartitionSpec as P

ITERS = 3

teacher_temp = 0.04
student_temp = 0.1
epsilon = 1e-06

GROUPS = 2
TILE = 256
HALF_TILE = 256
FETCH = 2
LANES = 128
VMEM_BYTES = 12 << 20
KEPT_BYTES = 18 << 20

EVERY = ("dp", "fsdp")
CHIPS = ("group", "block")
GROUP = ("block", "fsdp")


def unit_rows(values):
    floats = values.astype(jnp.float32)
    length = jnp.sqrt(jnp.sum(floats * floats, axis=1, keepdims=True) + epsilon)
    return (floats / length, length)


def unit_columns(values):
    floats = values.astype(jnp.float32)
    length = jnp.sqrt(jnp.sum(floats * floats, axis=0, keepdims=True) + epsilon)
    return (floats / length, length)


COPY_BYTES = 1 << 22


def share(values, axes):
    count = lax.axis_size(axes)
    if count * values.size * values.dtype.itemsize > COPY_BYTES:
        return lax.all_gather(values, axes)
    return lax.all_to_all(jnp.broadcast_to(values, (count, *values.shape)), axes, 0, 0)


def add_up(values):
    if lax.axis_size(EVERY) * values.size * values.dtype.itemsize > COPY_BYTES:
        return lax.psum(values, EVERY)
    return jnp.sum(share(values, EVERY), axis=0)


def plain_body(teacher_feat, student_feat, crop_weight, teacher_v, student_v):
    fsdp = lax.axis_size("fsdp")
    devices = lax.axis_size("dp") * fsdp
    own_rows, width = teacher_feat.shape
    crops = own_rows * devices
    block = teacher_v.shape[1] // lax.axis_size("dp")
    prototypes = block * devices
    first = lax.axis_index("dp") * block

    teacher_hat, _ = unit_rows(teacher_feat)
    student_hat, student_len = unit_rows(student_feat)
    units = jnp.concatenate(
        [teacher_hat.astype(jnp.bfloat16), student_hat.astype(jnp.bfloat16)], axis=1
    )
    units = share(share(units, "dp"), "fsdp").reshape(crops, 2 * width)
    teacher_unit, student_unit = units[:, :width], units[:, width:]

    teacher_w, _ = unit_columns(lax.dynamic_slice_in_dim(teacher_v, first, block, 1))
    student_w, student_wlen = unit_columns(lax.dynamic_slice_in_dim(student_v, first, block, 1))
    student_wunit = student_w.astype(jnp.bfloat16)

    mass = jnp.exp(
        jnp.dot(teacher_unit, teacher_w.astype(jnp.bfloat16), preferred_element_type=jnp.float32)
        / teacher_temp
    )
    student_mass = jnp.exp(
        jnp.dot(student_unit, student_wunit, preferred_element_type=jnp.float32) / student_temp
    )
    student_part = jnp.sum(student_mass, axis=1)

    crop_scale = None
    for sweep in range(ITERS):
        scaled = mass if sweep == 0 else mass * crop_scale[:, None]
        proto_scale = 1.0 / (prototypes * jnp.sum(scaled, axis=0))
        crop_part = jnp.sum(mass * proto_scale[None, :], axis=1)
        if sweep == 0:
            placed = jnp.zeros((fsdp, crops // (fsdp * own_rows), own_rows), jnp.float32)
            own = crop_weight.astype(jnp.float32)[None, None]
            spot = (lax.axis_index("fsdp"), lax.axis_index("dp"), 0)
            placed = lax.dynamic_update_slice(placed, own, spot).reshape(crops)
            sums = add_up(jnp.stack([crop_part, student_part, placed]))
            crop_mass, student_total, weights = sums[0], sums[1], sums[2]
        else:
            crop_mass = add_up(crop_part)
        crop_scale = 1.0 / (crops * crop_mass)

    target = crops * (mass * crop_scale[:, None] * proto_scale[None, :])
    student_prob = student_mass / student_total[:, None]
    gradient = ((student_prob - target) * weights[:, None] / student_temp).astype(jnp.bfloat16)
    feature_part = lax.dot_general(
        gradient, student_wunit, (((1,), (1,)), ((), ())), preferred_element_type=jnp.float32
    )
    weight_grad = lax.dot_general(
        student_unit, gradient, (((0,), (0,)), ((), ())), preferred_element_type=jnp.float32
    )
    weight_dot = jnp.sum(student_w * weight_grad, axis=0, keepdims=True)
    grad_block = (weight_grad - student_w * weight_dot) / student_wlen

    feature_sent = feature_part.astype(jnp.bfloat16).reshape(fsdp, -1, own_rows, width)
    feature_sent = jnp.swapaxes(feature_sent, 0, 1).reshape(devices, own_rows, width)
    feature_all = lax.all_to_all(feature_sent, EVERY, 0, 0)
    feature_grad = jnp.sum(feature_all.astype(jnp.float32), axis=0)
    grad_feat = (
        feature_grad - student_hat * jnp.sum(student_hat * feature_grad, axis=1, keepdims=True)
    ) / student_len
    grad_v = lax.all_to_all(grad_block.astype(jnp.bfloat16), "dp", 0, 1, tiled=True)
    return (grad_v.astype(jnp.float32), grad_feat)


def call(kernel, out_shape, flops=0, moved=0, exps=0, **more):
    return pl.pallas_call(
        kernel,
        out_shape=out_shape,
        compiler_params=pltpu.CompilerParams(vmem_limit_bytes=VMEM_BYTES),
        cost_estimate=pl.CostEstimate(flops=flops, bytes_accessed=moved, transcendentals=exps),
        **more,
    )


def units_kernel(teacher_ref, student_ref, weight_ref, units_out, teacher_vmem, student_vmem, weight_vmem, sems):
    copies = [
        pltpu.make_async_copy(teacher_ref, teacher_vmem, sems.at[0]),
        pltpu.make_async_copy(student_ref, student_vmem, sems.at[1]),
        pltpu.make_async_copy(weight_ref, weight_vmem, sems.at[2]),
    ]
    for copy in copies:
        copy.start()
    for copy in copies:
        copy.wait()
    rows, width = teacher_vmem.shape
    units_out[:rows, :width] = unit_rows(teacher_vmem[...])[0].astype(jnp.bfloat16)
    units_out[:rows, width:] = unit_rows(student_vmem[...])[0].astype(jnp.bfloat16)
    weights = weight_vmem[...].astype(jnp.float32)
    weights = jnp.concatenate([weights, jnp.zeros((1, 2 * width - rows), jnp.float32)], axis=1)
    units_out[rows:, :] = jnp.broadcast_to(weights, (units_out.shape[0] - rows, 2 * width)).astype(jnp.bfloat16)


def spread_kernel(*refs):
    *unit_refs, sent_ref = refs
    rows = sent_ref.shape[1] // GROUPS
    values = jnp.concatenate([ref[:rows, :] for ref in unit_refs], axis=0)
    for chip in range(sent_ref.shape[0]):
        sent_ref[chip] = values


def placed_weights(unit_refs, lines, rows, chips):
    group, block = lax.axis_index("group"), lax.axis_index("block")
    line = lax.broadcasted_iota(jnp.int32, (lines, LANES), 0)
    part = lax.broadcasted_iota(jnp.int32, (lines, LANES), 1) // rows
    each = LANES // rows
    placed = jnp.zeros((lines, LANES), jnp.float32)
    for back, ref in enumerate(unit_refs):
        at = lax.axis_index("fsdp") * chips * GROUPS + ((group + GROUPS - back) % GROUPS) * chips + block
        weights = ref[rows:, :LANES].astype(jnp.float32)[0:1, :rows]
        weights = jnp.concatenate([weights] * each, axis=1)
        here = (line == at // each) & (part == at % each)
        placed = placed + jnp.where(here, jnp.broadcast_to(weights, (lines, LANES)), 0.0)
    return placed


def directions_kernel(block_ref, teacher_ref, student_ref, teacher_out, student_out, inverse_out):
    teacher, _ = unit_columns(teacher_ref[...])
    teacher_out[...] = jnp.transpose(teacher).astype(jnp.bfloat16)
    student, length = unit_columns(student_ref[...])
    student_out[...] = jnp.transpose(student).astype(jnp.bfloat16)
    inverse_out[...] = 1.0 / length


def exponentials(directions, units, temperature):
    logits = lax.dot_general(
        directions, units, (((1,), (1,)), ((), ())), preferred_element_type=jnp.float32
    )
    return jnp.exp2(logits * (math.log2(math.e) / temperature))


def fold(values):
    rows, lanes = values.shape
    return jnp.sum(values.reshape(rows // 8, 8, lanes), axis=0)


def as_rows(line):
    return jnp.concatenate([line[:, at : at + LANES] for at in range(0, line.shape[1], LANES)], axis=0)


def as_line(rows):
    return jnp.concatenate([rows[at : at + 1, :] for at in range(rows.shape[0])], axis=1)


def in_core_order(core, own, other, body):
    @pl.when(core == 0)
    def _():
        body(own, other)

    @pl.when(core == 1)
    def _():
        body(other, own)


def sums(first, second):
    lines = [as_rows(jnp.sum(total, axis=0, keepdims=True)) for total in (first, second)]
    return jnp.concatenate(lines, axis=0)


def send(sent_ref, *rows):
    values = jnp.concatenate(rows, axis=0).astype(jnp.bfloat16)
    for device in range(sent_ref.shape[0]):
        sent_ref[device] = values


def halves(rows):
    line = as_line(rows)
    half = line.shape[1] // 2
    return line[:, :half], line[:, half:]


def received(got_ref, at=0):
    total = got_ref[0, at:, :].astype(jnp.float32)
    for device in range(1, got_ref.shape[0]):
        total = total + got_ref[device, at:, :].astype(jnp.float32)
    return total


def in_chip_order(got_ref, teacher_ref, student_ref):
    chips = got_ref.shape[0]
    width = teacher_ref.shape[1]
    rows = teacher_ref.shape[0] // (GROUPS * chips)
    group = lax.axis_index("group")
    for back in range(GROUPS):
        for chip in range(chips):
            at = (((group + GROUPS - back) % GROUPS) * chips + chip) * rows
            here = pl.ds(pl.multiple_of(at, rows), rows)
            teacher_ref[here, :] = got_ref[chip, back * rows : (back + 1) * rows, :width]
            student_ref[here, :] = got_ref[chip, back * rows : (back + 1) * rows, width:]


def turn(units):
    return jnp.transpose(units.astype(jnp.float32)).astype(jnp.bfloat16)


def own_kernel(
    teacher_w_ref, student_w_ref, got_ref, teacher_ref, student_ref, part_ref, turned_ref, teacher_units, student_units
):
    in_chip_order(got_ref, teacher_units, student_units)
    turned_ref[...] = turn(student_units[...])
    part = 0.0
    for start in range(0, teacher_ref.shape[0], HALF_TILE):
        here = slice(start, start + HALF_TILE)
        teacher_ref[here, :] = exponentials(teacher_w_ref[here, :], teacher_units[...], teacher_temp)
        mass = exponentials(student_w_ref[here, :], student_units[...], student_temp)
        student_ref[here, :] = mass
        part = part + fold(mass)
    part_ref[...] = part


def other_kernel(prototypes, teacher_w_ref, student_w_ref, got_ref, own_ref, own_part_ref, *refs):
    unit_refs = refs[:GROUPS]
    teacher_ref, student_ref, sent_ref, part_ref, turned_ref, teacher_units, student_units = refs[GROUPS:]
    chips = got_ref.shape[0]
    in_chip_order(got_ref, teacher_units, student_units)
    turned_ref[...] = turn(student_units[...])
    half = own_ref.shape[1]
    placed = placed_weights(unit_refs, 2 * half // LANES, half // (GROUPS * chips), chips)
    own_total = total = part = 0.0
    for start in range(0, teacher_ref.shape[0], HALF_TILE):
        here = slice(start, start + HALF_TILE)
        mass = exponentials(teacher_w_ref[here, :], teacher_units[...], teacher_temp)
        teacher_ref[here, :] = mass
        own = own_ref[here, :]
        scale = 1.0 / (prototypes * jnp.sum(own + mass, axis=1, keepdims=True))
        own_total = own_total + fold(own * scale)
        total = total + fold(mass * scale)
        mass = exponentials(student_w_ref[here, :], student_units[...], student_temp)
        student_ref[here, :] = mass
        part = part + fold(mass)

    def finish(first, second):
        send(sent_ref, sums(first[0], second[0]), placed)
        part_ref[...] = sums(first[1], second[1])

    in_core_order(lax.axis_index("fsdp"), (own_total, own_part_ref[...]), (total, part), finish)


def sweep(prototypes, crops, first_ref, second_ref, received_sums, scaled_refs=None):
    first_crop, second_crop = halves(1.0 / (crops * received_sums))
    first_total = second_total = 0.0
    for start in range(0, first_ref.shape[0], TILE):
        here = slice(start, start + TILE)
        first, second = first_ref[here, :], second_ref[here, :]
        proto = jnp.sum(first * first_crop + second * second_crop, axis=1, keepdims=True)
        scale = 1.0 / (prototypes * proto)
        first, second = first * scale, second * scale
        if scaled_refs is not None:
            scaled_refs[0][here, :], scaled_refs[1][here, :] = first, second
        first_total = first_total + fold(first)
        second_total = second_total + fold(second)
    return sums(first_total, second_total)


def sweep_kernel(prototypes, crops, own_ref, other_ref, got_ref, part_ref, sent_ref, weight_ref):
    lines = crops // LANES
    extra = received(got_ref)
    weight_ref[...] = extra[lines:]

    def body(first_ref, second_ref):
        send(sent_ref, sweep(prototypes, crops, first_ref, second_ref, extra[:lines]), part_ref[...])

    in_core_order(lax.axis_index("fsdp"), own_ref, other_ref, body)


def last_sweep_kernel(
    prototypes, crops, own_ref, other_ref, got_ref, directions_ref,
    sent_ref, own_scaled_ref, other_scaled_ref, copy_ref, sems,
):
    pieces, _, span = copy_ref.shape
    copies = []
    for piece in range(pieces):
        columns = pl.ds(pl.multiple_of((lax.axis_index("block") * pieces + piece) * span, span), span)
        copies.append(pltpu.make_async_copy(directions_ref.at[:, columns], copy_ref.at[piece], sems.at[piece]))
        copies[-1].start()

    total = received(got_ref)[: crops // LANES]

    def body(first_refs, second_refs):
        (first_ref, *scaled_refs), (second_ref, second_scaled_ref) = first_refs, second_refs
        sent = sweep(prototypes, crops, first_ref, second_ref, total, (*scaled_refs, second_scaled_ref))
        send(sent_ref, sent)

    in_core_order(lax.axis_index("fsdp"), (own_ref, own_scaled_ref), (other_ref, other_scaled_ref), body)
    for copy in copies:
        copy.wait()


def units_tile(copy_ref, inverse_ref, start):
    span = copy_ref.shape[2]
    at = start % span
    return copy_ref[start // span, :, at : at + TILE].astype(jnp.float32) * inverse_ref[:, start : start + TILE]


def gradient_kernel(
    own_mass_ref, other_mass_ref, own_student_ref, other_student_ref, weight_ref, second_ref, third_ref,
    inverse_ref, copy_ref, gradient_ref, keep_ref, give_ref, unit_ref,
):
    group, core = lax.axis_index("group"), lax.axis_index("fsdp")
    count, half = own_mass_ref.shape
    lines = 2 * half // LANES
    weights = weight_ref[...] / student_temp
    teacher_scales = halves(weights / received(third_ref)[:lines])
    student_scales = halves(weights / received(second_ref)[lines:])

    def body(first_refs, second_refs):
        for start in range(0, count, TILE):
            here = slice(start, start + TILE)
            for (side, mass_ref, student_ref), teacher_scale, student_scale in zip(
                (first_refs, second_refs), teacher_scales, student_scales
            ):
                gradient = student_ref[here, :] * student_scale - mass_ref[here, :] * teacher_scale
                gradient_ref[side, start : start + TILE, :] = gradient.astype(jnp.bfloat16)

    in_core_order(core, (0, own_mass_ref, own_student_ref), (1, other_mass_ref, other_student_ref), body)
    for start in range(0, count, TILE):
        unit_ref[:, start : start + TILE] = units_tile(copy_ref, inverse_ref, start).astype(jnp.bfloat16)
    kept = half // GROUPS
    lanes = pl.ds(pl.multiple_of(group * kept, kept), kept)
    for side, out_ref in enumerate((keep_ref, give_ref)):
        feature = jnp.dot(unit_ref[...], gradient_ref[side, :, lanes], preferred_element_type=jnp.float32)
        out_ref[...] = jnp.transpose(feature).astype(out_ref.dtype)


def weight_kernel(gradient_ref, own_turned_ref, other_turned_ref, inverse_ref, copy_ref, sent_ref, grad_ref):
    chips, rows_each, _ = sent_ref.shape
    count = gradient_ref.shape[1]
    width = own_turned_ref.shape[0]
    kept = width // GROUPS
    own_rows = pl.ds(pl.multiple_of(lax.axis_index("group") * kept, kept), kept)
    for start in range(0, count, TILE):
        here, slot = slice(start, start + TILE), start // TILE
        weight_grad = 0.0
        for side, turned_ref in enumerate((own_turned_ref, other_turned_ref)):
            weight_grad = weight_grad + lax.dot_general(
                turned_ref[...], gradient_ref[side, here, :], (((1,), (1,)), ((), ())), preferred_element_type=jnp.float32
            )
        unit = units_tile(copy_ref, inverse_ref, start)
        dot = jnp.sum(unit * weight_grad, axis=0, keepdims=True)
        grad_ref[slot] = (weight_grad - unit * dot) * inverse_ref[:, here]
        own = grad_ref[slot, own_rows, :].astype(jnp.bfloat16)
        sent_ref[:, :, here] = own.reshape(chips, rows_each, TILE)


def pack_kernel(keep_ref, other_ref, _, sent_ref, packed_ref, sem):
    chips, rows_each, lanes = packed_ref.shape
    width = keep_ref.shape[1]
    total = (keep_ref[...] + other_ref[...].astype(jnp.float32)).astype(jnp.bfloat16)
    total = total.reshape(chips, -1, width)
    for piece in range(lanes // width):
        packed_ref[:, :, piece * width : (piece + 1) * width] = total[:, piece * rows_each : (piece + 1) * rows_each, :]
    copy = pltpu.make_async_copy(packed_ref, sent_ref.at[:, :, pl.ds(sent_ref.shape[2] - lanes, lanes)], sem)
    copy.start()
    copy.wait()


def outputs_kernel(got_ref, student_ref, weight_out, feature_out):
    chips, rows_each, columns = got_ref.shape
    rows, width = student_ref.shape
    pieces = rows // rows_each
    count = columns - pieces * width
    step = pl.program_id(0)
    each = chips // pl.num_programs(0)
    for chip in range(each):
        weight_out[:, chip * count : (chip + 1) * count] = got_ref[step * each + chip, :, :count].astype(jnp.float32)

    @pl.when(step == 0)
    def _():
        total = got_ref[0, :, count:].astype(jnp.float32)
        for chip in range(1, chips):
            total = total + got_ref[chip, :, count:].astype(jnp.float32)
        total = jnp.concatenate([total[:, piece * width : (piece + 1) * width] for piece in range(pieces)], axis=0)
        hat, length = unit_rows(student_ref[...])
        feature_out[...] = (total - hat * jnp.sum(hat * total, axis=1, keepdims=True)) / length


def kernel_body(teacher_feat, student_feat, crop_weight, teacher_v, student_v):
    f32, bf16 = jnp.float32, jnp.bfloat16
    shape = jax.ShapeDtypeStruct
    blocks, fsdp = lax.axis_size("block"), lax.axis_size("fsdp")
    chips = blocks * GROUPS
    members, devices = blocks * fsdp, chips * fsdp
    rows, width = teacher_feat.shape
    crops = rows * devices
    lines = crops // LANES
    kept = teacher_v.shape[1]
    prototypes = kept * fsdp
    count = kept // blocks
    group, block = lax.axis_index("group")[None], lax.axis_index("block")[None]
    core = lax.axis_index("fsdp")[None]
    elements = count * crops
    vmem = pl.BlockSpec(memory_space=pltpu.VMEM)

    def swap(values):
        return lax.ppermute(values, "fsdp", [(0, 1), (1, 0)])

    def share(values):
        return lax.all_to_all(values, GROUP, 0, 0)

    dma = pltpu.SemaphoreType.DMA
    hbm = functools.partial(pltpu.with_memory_space_constraint, memory_space=pltpu.HBM)
    units = call(
        units_kernel,
        shape((rows + 16, 2 * width), bf16),
        in_specs=[pl.BlockSpec(memory_space=pl.ANY)] * 3,
        scratch_shapes=[pltpu.VMEM((rows, width), bf16)] * 2 + [pltpu.VMEM((1, rows), bf16), dma((3,))],
    )(hbm(teacher_feat), hbm(student_feat), hbm(crop_weight[None, :]))

    def of_groups(values):
        return [values] + [
            lax.ppermute(values, "group", [(at, (at + back) % GROUPS) for at in range(GROUPS)]) for back in range(1, GROUPS)
        ]

    units = of_groups(units)

    span = 2 * TILE
    spans = count // span
    column = pl.BlockSpec((width, span), lambda step, at: (0, at[0] * spans + step))
    turned = pl.BlockSpec((span, width), lambda step, at: (step, 0))
    line = pl.BlockSpec((1, span), lambda step, at: (0, step))
    teacher_w, student_w, inverse = call(
        directions_kernel,
        (
            shape((count, width), bf16),
            shape((count, width), bf16),
            shape((1, count), f32),
        ),
        flops=12 * count * width,
        moved=8 * count * width,
        grid_spec=pltpu.PrefetchScalarGridSpec(
            num_scalar_prefetch=1,
            grid=(spans,),
            in_specs=[column, column],
            out_specs=[turned, turned, line],
        ),
    )(
        block,
        hbm(teacher_v),
        hbm(student_v),
    )

    units, teacher_w = lax.optimization_barrier((units, teacher_w))
    sent = call(spread_kernel, shape((blocks, GROUPS * rows, 2 * width), bf16))(*units)
    own = lax.all_to_all(sent, "block", 0, 0)
    other = swap(own)
    half = crops // 2
    anyspace = pl.BlockSpec(memory_space=pl.ANY)
    pieces = count // (FETCH * TILE)
    halved = dict(flops=2 * elements * width, exps=elements)
    scratch = [pltpu.VMEM((half, width), bf16)] * 2
    own_mass, own_student, own_part, own_turned = call(
        own_kernel,
        (
            shape((count, half), f32),
            shape((count, half), f32),
            shape((8, half), f32),
            shape((width, half), bf16),
        ),
        scratch_shapes=scratch,
        **halved,
    )(teacher_w, student_w, own)
    other_mass, other_student, sent, student_part, other_turned = call(
        functools.partial(other_kernel, prototypes),
        (
            shape((count, half), f32),
            shape((count, half), f32),
            shape((members, 2 * lines, LANES), bf16),
            shape((lines, LANES), f32),
            shape((width, half), bf16),
        ),
        scratch_shapes=scratch,
        **halved,
    )(teacher_w, student_w, other, own_mass, own_part, *units)
    first = share(sent)
    sent, weights = call(
        functools.partial(sweep_kernel, prototypes, crops),
        (shape((members, 2 * lines, LANES), bf16), shape((lines, LANES), f32)),
        flops=4 * elements,
    )(own_mass, other_mass, first, student_part)
    second = share(sent)
    sent, own_scaled, other_scaled, student_copy = call(
        functools.partial(last_sweep_kernel, prototypes, crops),
        (
            shape((members, lines, LANES), bf16),
            shape((count, half), f32),
            shape((count, half), f32),
            shape((pieces, width, count // pieces), bf16),
        ),
        flops=4 * elements,
        in_specs=[vmem] * 3 + [anyspace],
        scratch_shapes=[dma((pieces,))],
    )(own_mass, other_mass, second, hbm(student_v))
    third = share(sent)

    gradient, keep, give = call(
        gradient_kernel,
        (shape((2, count, half), bf16), shape((half // GROUPS, width), f32), shape((half // GROUPS, width), bf16)),
        flops=2 * elements * width // GROUPS,
        in_specs=[vmem] * 9,
        scratch_shapes=[pltpu.VMEM((width, count), bf16)],
    )(own_scaled, other_scaled, own_student, other_student, weights, second, third, inverse, student_copy)
    other = swap(give)
    out_rows = width // chips
    per_chip = rows * width // out_rows
    sent = call(
        weight_kernel,
        shape((blocks, out_rows, count + per_chip), bf16),
        flops=2 * elements * width,
        in_specs=[vmem] * 5,
        scratch_shapes=[pltpu.VMEM((count // TILE, width, TILE), f32)],
    )(gradient, own_turned, other_turned, inverse, student_copy)
    sent = call(
        pack_kernel,
        shape((blocks, out_rows, count + per_chip), bf16),
        in_specs=[vmem] * 2 + [anyspace],
        out_specs=anyspace,
        input_output_aliases={2: 0},
        scratch_shapes=[pltpu.VMEM((blocks, out_rows, per_chip), bf16), dma],
    )(keep, other, sent)
    got = lax.all_to_all(sent, "block", 0, 0)
    return call(
        outputs_kernel,
        (shape((out_rows, kept), f32), shape((rows, width), f32)),
        grid=(2,),
        in_specs=[vmem, vmem],
        out_specs=[
            pl.BlockSpec((out_rows, kept // 2), lambda step: (0, step)),
            pl.BlockSpec((rows, width), lambda step: (0, 0)),
        ],
    )(got, student_feat)


def solution(mesh):
    dp, fsdp = mesh.shape["dp"], mesh.shape["fsdp"]
    blocks = dp // GROUPS

    def run(teacher_feat, student_feat, crop_weight, teacher_v, student_v):
        crops = teacher_feat.shape[0]
        count = teacher_v.shape[1] // (blocks * fsdp)
        fits = fsdp == 2 and dp == 16 and count % (2 * TILE) == 0 and crops == 1024
        if fits and 8 * count * crops <= KEPT_BYTES:
            grid = Mesh(mesh.devices.reshape(GROUPS, blocks, fsdp), (*CHIPS, "fsdp"))
            body, chips = kernel_body, CHIPS
        else:
            grid, body, chips = mesh, plain_body, ("dp",)
        every = P((*chips, "fsdp"))
        return jax.shard_map(
            body,
            mesh=grid,
            in_specs=(every, every, every, P(None, "fsdp"), P(None, "fsdp")),
            out_specs=(P(chips, "fsdp"), every),
            check_vma=False,
        )(teacher_feat, student_feat, crop_weight, teacher_v, student_v)

    return run
```

```python
import functools
import math

import jax
import jax.numpy as jnp
from jax import lax
from jax.experimental import pallas as pl
from jax.experimental.pallas import tpu as pltpu
from jax.sharding import Mesh
from jax.sharding import PartitionSpec as P

ITERS = 3

teacher_temp = 0.04
student_temp = 0.1
epsilon = 1e-06

GROUPS = 2
TILE = 256
HALF_TILE = 256
FETCH = 2
LANES = 128
VMEM_BYTES = 12 << 20
KEPT_BYTES = 18 << 20

EVERY = ("dp", "fsdp")
CHIPS = ("group", "block")
GROUP = ("block", "fsdp")


def unit_rows(values):
    floats = values.astype(jnp.float32)
    length = jnp.sqrt(jnp.sum(floats * floats, axis=1, keepdims=True) + epsilon)
    return (floats / length, length)


def unit_columns(values):
    floats = values.astype(jnp.float32)
    length = jnp.sqrt(jnp.sum(floats * floats, axis=0, keepdims=True) + epsilon)
    return (floats / length, length)


COPY_BYTES = 1 << 22


def share(values, axes):
    count = lax.axis_size(axes)
    if count * values.size * values.dtype.itemsize > COPY_BYTES:
        return lax.all_gather(values, axes)
    return lax.all_to_all(jnp.broadcast_to(values, (count, *values.shape)), axes, 0, 0)


def add_up(values):
    if lax.axis_size(EVERY) * values.size * values.dtype.itemsize > COPY_BYTES:
        return lax.psum(values, EVERY)
    return jnp.sum(share(values, EVERY), axis=0)


def plain_body(teacher_feat, student_feat, crop_weight, teacher_v, student_v):
    fsdp = lax.axis_size("fsdp")
    devices = lax.axis_size("dp") * fsdp
    own_rows, width = teacher_feat.shape
    crops = own_rows * devices
    block = teacher_v.shape[1] // lax.axis_size("dp")
    prototypes = block * devices
    first = lax.axis_index("dp") * block

    teacher_hat, _ = unit_rows(teacher_feat)
    student_hat, student_len = unit_rows(student_feat)
    units = jnp.concatenate(
        [teacher_hat.astype(jnp.bfloat16), student_hat.astype(jnp.bfloat16)], axis=1
    )
    units = share(share(units, "dp"), "fsdp").reshape(crops, 2 * width)
    teacher_unit, student_unit = units[:, :width], units[:, width:]

    teacher_w, _ = unit_columns(lax.dynamic_slice_in_dim(teacher_v, first, block, 1))
    student_w, student_wlen = unit_columns(lax.dynamic_slice_in_dim(student_v, first, block, 1))
    student_wunit = student_w.astype(jnp.bfloat16)

    mass = jnp.exp(
        jnp.dot(teacher_unit, teacher_w.astype(jnp.bfloat16), preferred_element_type=jnp.float32)
        / teacher_temp
    )
    student_mass = jnp.exp(
        jnp.dot(student_unit, student_wunit, preferred_element_type=jnp.float32) / student_temp
    )
    student_part = jnp.sum(student_mass, axis=1)

    crop_scale = None
    for sweep in range(ITERS):
        scaled = mass if sweep == 0 else mass * crop_scale[:, None]
        proto_scale = 1.0 / (prototypes * jnp.sum(scaled, axis=0))
        crop_part = jnp.sum(mass * proto_scale[None, :], axis=1)
        if sweep == 0:
            placed = jnp.zeros((fsdp, crops // (fsdp * own_rows), own_rows), jnp.float32)
            own = crop_weight.astype(jnp.float32)[None, None]
            spot = (lax.axis_index("fsdp"), lax.axis_index("dp"), 0)
            placed = lax.dynamic_update_slice(placed, own, spot).reshape(crops)
            sums = add_up(jnp.stack([crop_part, student_part, placed]))
            crop_mass, student_total, weights = sums[0], sums[1], sums[2]
        else:
            crop_mass = add_up(crop_part)
        crop_scale = 1.0 / (crops * crop_mass)

    target = crops * (mass * crop_scale[:, None] * proto_scale[None, :])
    student_prob = student_mass / student_total[:, None]
    gradient = ((student_prob - target) * weights[:, None] / student_temp).astype(jnp.bfloat16)
    feature_part = lax.dot_general(
        gradient, student_wunit, (((1,), (1,)), ((), ())), preferred_element_type=jnp.float32
    )
    weight_grad = lax.dot_general(
        student_unit, gradient, (((0,), (0,)), ((), ())), preferred_element_type=jnp.float32
    )
    weight_dot = jnp.sum(student_w * weight_grad, axis=0, keepdims=True)
    grad_block = (weight_grad - student_w * weight_dot) / student_wlen

    feature_sent = feature_part.astype(jnp.bfloat16).reshape(fsdp, -1, own_rows, width)
    feature_sent = jnp.swapaxes(feature_sent, 0, 1).reshape(devices, own_rows, width)
    feature_all = lax.all_to_all(feature_sent, EVERY, 0, 0)
    feature_grad = jnp.sum(feature_all.astype(jnp.float32), axis=0)
    grad_feat = (
        feature_grad - student_hat * jnp.sum(student_hat * feature_grad, axis=1, keepdims=True)
    ) / student_len
    grad_v = lax.all_to_all(grad_block.astype(jnp.bfloat16), "dp", 0, 1, tiled=True)
    return (grad_v.astype(jnp.float32), grad_feat)


def call(kernel, out_shape, flops=0, moved=0, exps=0, **more):
    return pl.pallas_call(
        kernel,
        out_shape=out_shape,
        compiler_params=pltpu.CompilerParams(vmem_limit_bytes=VMEM_BYTES),
        cost_estimate=pl.CostEstimate(flops=flops, bytes_accessed=moved, transcendentals=exps),
        **more,
    )


def units_kernel(teacher_ref, student_ref, weight_ref, units_out, teacher_vmem, student_vmem, weight_vmem, sems):
    copies = [
        pltpu.make_async_copy(teacher_ref, teacher_vmem, sems.at[0]),
        pltpu.make_async_copy(student_ref, student_vmem, sems.at[1]),
        pltpu.make_async_copy(weight_ref, weight_vmem, sems.at[2]),
    ]
    for copy in copies:
        copy.start()
    for copy in copies:
        copy.wait()
    rows, width = teacher_vmem.shape
    units_out[:rows, :width] = unit_rows(teacher_vmem[...])[0].astype(jnp.bfloat16)
    units_out[:rows, width:] = unit_rows(student_vmem[...])[0].astype(jnp.bfloat16)
    weights = weight_vmem[...].astype(jnp.float32)
    weights = jnp.concatenate([weights, jnp.zeros((1, 2 * width - rows), jnp.float32)], axis=1)
    units_out[rows:, :] = jnp.broadcast_to(weights, (units_out.shape[0] - rows, 2 * width)).astype(jnp.bfloat16)


def spread_kernel(*refs):
    *unit_refs, sent_ref = refs
    rows = sent_ref.shape[1] // GROUPS
    values = jnp.concatenate([ref[:rows, :] for ref in unit_refs], axis=0)
    for chip in range(sent_ref.shape[0]):
        sent_ref[chip] = values


def placed_weights(unit_refs, lines, rows, chips):
    group, block = lax.axis_index("group"), lax.axis_index("block")
    line = lax.broadcasted_iota(jnp.int32, (lines, LANES), 0)
    part = lax.broadcasted_iota(jnp.int32, (lines, LANES), 1) // rows
    each = LANES // rows
    placed = jnp.zeros((lines, LANES), jnp.float32)
    for back, ref in enumerate(unit_refs):
        at = lax.axis_index("fsdp") * chips * GROUPS + ((group + GROUPS - back) % GROUPS) * chips + block
        weights = ref[rows:, :LANES].astype(jnp.float32)[0:1, :rows]
        weights = jnp.concatenate([weights] * each, axis=1)
        here = (line == at // each) & (part == at % each)
        placed = placed + jnp.where(here, jnp.broadcast_to(weights, (lines, LANES)), 0.0)
    return placed


def directions_kernel(block_ref, teacher_ref, student_ref, teacher_out, student_out, inverse_out):
    teacher, _ = unit_columns(teacher_ref[...])
    teacher_out[...] = jnp.transpose(teacher).astype(jnp.bfloat16)
    student, length = unit_columns(student_ref[...])
    student_out[...] = jnp.transpose(student).astype(jnp.bfloat16)
    inverse_out[...] = 1.0 / length


def exponentials(directions, units, temperature):
    logits = lax.dot_general(
        directions, units, (((1,), (1,)), ((), ())), preferred_element_type=jnp.float32
    )
    return jnp.exp2(logits * (math.log2(math.e) / temperature))


def fold(values):
    rows, lanes = values.shape
    return jnp.sum(values.reshape(rows // 8, 8, lanes), axis=0)


def as_rows(line):
    return jnp.concatenate([line[:, at : at + LANES] for at in range(0, line.shape[1], LANES)], axis=0)


def as_line(rows):
    return jnp.concatenate([rows[at : at + 1, :] for at in range(rows.shape[0])], axis=1)


def in_core_order(core, own, other, body):
    @pl.when(core == 0)
    def _():
        body(own, other)

    @pl.when(core == 1)
    def _():
        body(other, own)


def sums(first, second):
    lines = [as_rows(jnp.sum(total, axis=0, keepdims=True)) for total in (first, second)]
    return jnp.concatenate(lines, axis=0)


def send(sent_ref, *rows):
    values = jnp.concatenate(rows, axis=0).astype(jnp.bfloat16)
    for device in range(sent_ref.shape[0]):
        sent_ref[device] = values


def halves(rows):
    line = as_line(rows)
    half = line.shape[1] // 2
    return line[:, :half], line[:, half:]


def received(got_ref, at=0):
    total = got_ref[0, at:, :].astype(jnp.float32)
    for device in range(1, got_ref.shape[0]):
        total = total + got_ref[device, at:, :].astype(jnp.float32)
    return total


def in_chip_order(got_ref, teacher_ref, student_ref):
    chips = got_ref.shape[0]
    width = teacher_ref.shape[1]
    rows = teacher_ref.shape[0] // (GROUPS * chips)
    group = lax.axis_index("group")
    for back in range(GROUPS):
        for chip in range(chips):
            at = (((group + GROUPS - back) % GROUPS) * chips + chip) * rows
            here = pl.ds(pl.multiple_of(at, rows), rows)
            teacher_ref[here, :] = got_ref[chip, back * rows : (back + 1) * rows, :width]
            student_ref[here, :] = got_ref[chip, back * rows : (back + 1) * rows, width:]


def turn(units):
    return jnp.transpose(units.astype(jnp.float32)).astype(jnp.bfloat16)


def own_kernel(
    teacher_w_ref, student_w_ref, got_ref, teacher_ref, student_ref, part_ref, turned_ref, teacher_units, student_units
):
    in_chip_order(got_ref, teacher_units, student_units)
    turned_ref[...] = turn(student_units[...])
    part = 0.0
    for start in range(0, teacher_ref.shape[0], HALF_TILE):
        here = slice(start, start + HALF_TILE)
        teacher_ref[here, :] = exponentials(teacher_w_ref[here, :], teacher_units[...], teacher_temp)
        mass = exponentials(student_w_ref[here, :], student_units[...], student_temp)
        student_ref[here, :] = mass
        part = part + fold(mass)
    part_ref[...] = part


def other_kernel(prototypes, teacher_w_ref, student_w_ref, got_ref, own_ref, own_part_ref, *refs):
    unit_refs = refs[:GROUPS]
    teacher_ref, student_ref, sent_ref, part_ref, turned_ref, teacher_units, student_units = refs[GROUPS:]
    chips = got_ref.shape[0]
    in_chip_order(got_ref, teacher_units, student_units)
    turned_ref[...] = turn(student_units[...])
    half = own_ref.shape[1]
    placed = placed_weights(unit_refs, 2 * half // LANES, half // (GROUPS * chips), chips)
    own_total = total = part = 0.0
    for start in range(0, teacher_ref.shape[0], HALF_TILE):
        here = slice(start, start + HALF_TILE)
        mass = exponentials(teacher_w_ref[here, :], teacher_units[...], teacher_temp)
        teacher_ref[here, :] = mass
        own = own_ref[here, :]
        scale = 1.0 / (prototypes * jnp.sum(own + mass, axis=1, keepdims=True))
        own_total = own_total + fold(own * scale)
        total = total + fold(mass * scale)
        mass = exponentials(student_w_ref[here, :], student_units[...], student_temp)
        student_ref[here, :] = mass
        part = part + fold(mass)

    def finish(first, second):
        send(sent_ref, sums(first[0], second[0]), placed)
        part_ref[...] = sums(first[1], second[1])

    in_core_order(lax.axis_index("fsdp"), (own_total, own_part_ref[...]), (total, part), finish)


def sweep(prototypes, crops, first_ref, second_ref, received_sums, scaled_refs=None):
    first_crop, second_crop = halves(1.0 / (crops * received_sums))
    first_total = second_total = 0.0
    for start in range(0, first_ref.shape[0], TILE):
        here = slice(start, start + TILE)
        first, second = first_ref[here, :], second_ref[here, :]
        proto = jnp.sum(first * first_crop + second * second_crop, axis=1, keepdims=True)
        scale = 1.0 / (prototypes * proto)
        first, second = first * scale, second * scale
        if scaled_refs is not None:
            scaled_refs[0][here, :], scaled_refs[1][here, :] = first, second
        first_total = first_total + fold(first)
        second_total = second_total + fold(second)
    return sums(first_total, second_total)


def sweep_kernel(prototypes, crops, own_ref, other_ref, got_ref, part_ref, sent_ref, weight_ref):
    lines = crops // LANES
    extra = received(got_ref)
    weight_ref[...] = extra[lines:]

    def body(first_ref, second_ref):
        send(sent_ref, sweep(prototypes, crops, first_ref, second_ref, extra[:lines]), part_ref[...])

    in_core_order(lax.axis_index("fsdp"), own_ref, other_ref, body)


def last_sweep_kernel(
    prototypes, crops, own_ref, other_ref, got_ref, directions_ref,
    sent_ref, own_scaled_ref, other_scaled_ref, copy_ref, sems,
):
    pieces, _, span = copy_ref.shape
    copies = []
    for piece in range(pieces):
        columns = pl.ds(pl.multiple_of((lax.axis_index("block") * pieces + piece) * span, span), span)
        copies.append(pltpu.make_async_copy(directions_ref.at[:, columns], copy_ref.at[piece], sems.at[piece]))
        copies[-1].start()

    total = received(got_ref)[: crops // LANES]

    def body(first_refs, second_refs):
        (first_ref, *scaled_refs), (second_ref, second_scaled_ref) = first_refs, second_refs
        sent = sweep(prototypes, crops, first_ref, second_ref, total, (*scaled_refs, second_scaled_ref))
        send(sent_ref, sent)

    in_core_order(lax.axis_index("fsdp"), (own_ref, own_scaled_ref), (other_ref, other_scaled_ref), body)
    for copy in copies:
        copy.wait()


def units_tile(copy_ref, inverse_ref, start):
    span = copy_ref.shape[2]
    at = start % span
    return copy_ref[start // span, :, at : at + TILE].astype(jnp.float32) * inverse_ref[:, start : start + TILE]


def gradient_kernel(
    own_mass_ref, other_mass_ref, own_student_ref, other_student_ref, weight_ref, second_ref, third_ref,
    inverse_ref, copy_ref, turned_ref, gradient_ref, weight_out, keep_ref, give_ref, unit_ref,
):
    group, core = lax.axis_index("group"), lax.axis_index("fsdp")
    count, half = own_mass_ref.shape
    lines = 2 * half // LANES
    weights = weight_ref[...] / student_temp
    teacher_scales = halves(weights / received(third_ref)[:lines])
    student_scales = halves(weights / received(second_ref)[lines:])

    def body(first_refs, second_refs):
        for start in range(0, count, TILE):
            here = slice(start, start + TILE)
            for (side, mass_ref, student_ref), teacher_scale, student_scale in zip(
                (first_refs, second_refs), teacher_scales, student_scales
            ):
                gradient = student_ref[here, :] * student_scale - mass_ref[here, :] * teacher_scale
                gradient_ref[side, start : start + TILE, :] = gradient.astype(jnp.bfloat16)
                if side == 0:
                    weight_out[:, here] = lax.dot_general(
                        turned_ref[...], gradient_ref[0, here, :], (((1,), (1,)), ((), ())), preferred_element_type=jnp.float32
                    )

    in_core_order(core, (0, own_mass_ref, own_student_ref), (1, other_mass_ref, other_student_ref), body)
    for start in range(0, count, TILE):
        unit_ref[:, start : start + TILE] = units_tile(copy_ref, inverse_ref, start).astype(jnp.bfloat16)
    kept = half // GROUPS
    lanes = pl.ds(pl.multiple_of(group * kept, kept), kept)
    for side, out_ref in enumerate((keep_ref, give_ref)):
        feature = jnp.dot(unit_ref[...], gradient_ref[side, :, lanes], preferred_element_type=jnp.float32)
        out_ref[...] = jnp.transpose(feature).astype(out_ref.dtype)


def weight_kernel(gradient_ref, own_weight_ref, turned_ref, inverse_ref, copy_ref, sent_ref, grad_ref):
    chips, rows_each, _ = sent_ref.shape
    count = gradient_ref.shape[1]
    width = turned_ref.shape[0]
    kept = width // GROUPS
    own_rows = pl.ds(pl.multiple_of(lax.axis_index("group") * kept, kept), kept)
    for start in range(0, count, TILE):
        here, slot = slice(start, start + TILE), start // TILE
        weight_grad = own_weight_ref[:, here] + lax.dot_general(
            turned_ref[...], gradient_ref[1, here, :], (((1,), (1,)), ((), ())), preferred_element_type=jnp.float32
        )
        unit = units_tile(copy_ref, inverse_ref, start)
        dot = jnp.sum(unit * weight_grad, axis=0, keepdims=True)
        grad_ref[slot] = (weight_grad - unit * dot) * inverse_ref[:, here]
        own = grad_ref[slot, own_rows, :].astype(jnp.bfloat16)
        sent_ref[:, :, here] = own.reshape(chips, rows_each, TILE)


def pack_kernel(keep_ref, other_ref, _, sent_ref, packed_ref, sem):
    chips, rows_each, lanes = packed_ref.shape
    width = keep_ref.shape[1]
    total = (keep_ref[...] + other_ref[...].astype(jnp.float32)).astype(jnp.bfloat16)
    total = total.reshape(chips, -1, width)
    for piece in range(lanes // width):
        packed_ref[:, :, piece * width : (piece + 1) * width] = total[:, piece * rows_each : (piece + 1) * rows_each, :]
    copy = pltpu.make_async_copy(packed_ref, sent_ref.at[:, :, pl.ds(sent_ref.shape[2] - lanes, lanes)], sem)
    copy.start()
    copy.wait()


def outputs_kernel(got_ref, student_ref, weight_out, feature_out):
    chips, rows_each, columns = got_ref.shape
    rows, width = student_ref.shape
    pieces = rows // rows_each
    count = columns - pieces * width
    step = pl.program_id(0)
    each = chips // pl.num_programs(0)
    for chip in range(each):
        weight_out[:, chip * count : (chip + 1) * count] = got_ref[step * each + chip, :, :count].astype(jnp.float32)

    @pl.when(step == 0)
    def _():
        total = got_ref[0, :, count:].astype(jnp.float32)
        for chip in range(1, chips):
            total = total + got_ref[chip, :, count:].astype(jnp.float32)
        total = jnp.concatenate([total[:, piece * width : (piece + 1) * width] for piece in range(pieces)], axis=0)
        hat, length = unit_rows(student_ref[...])
        feature_out[...] = (total - hat * jnp.sum(hat * total, axis=1, keepdims=True)) / length


def kernel_body(teacher_feat, student_feat, crop_weight, teacher_v, student_v):
    f32, bf16 = jnp.float32, jnp.bfloat16
    shape = jax.ShapeDtypeStruct
    blocks, fsdp = lax.axis_size("block"), lax.axis_size("fsdp")
    chips = blocks * GROUPS
    members, devices = blocks * fsdp, chips * fsdp
    rows, width = teacher_feat.shape
    crops = rows * devices
    lines = crops // LANES
    kept = teacher_v.shape[1]
    prototypes = kept * fsdp
    count = kept // blocks
    group, block = lax.axis_index("group")[None], lax.axis_index("block")[None]
    core = lax.axis_index("fsdp")[None]
    elements = count * crops
    vmem = pl.BlockSpec(memory_space=pltpu.VMEM)

    def swap(values):
        return lax.ppermute(values, "fsdp", [(0, 1), (1, 0)])

    def share(values):
        return lax.all_to_all(values, GROUP, 0, 0)

    dma = pltpu.SemaphoreType.DMA
    hbm = functools.partial(pltpu.with_memory_space_constraint, memory_space=pltpu.HBM)
    units = call(
        units_kernel,
        shape((rows + 16, 2 * width), bf16),
        in_specs=[pl.BlockSpec(memory_space=pl.ANY)] * 3,
        scratch_shapes=[pltpu.VMEM((rows, width), bf16)] * 2 + [pltpu.VMEM((1, rows), bf16), dma((3,))],
    )(hbm(teacher_feat), hbm(student_feat), hbm(crop_weight[None, :]))

    def of_groups(values):
        return [values] + [
            lax.ppermute(values, "group", [(at, (at + back) % GROUPS) for at in range(GROUPS)]) for back in range(1, GROUPS)
        ]

    units = of_groups(units)

    span = 2 * TILE
    spans = count // span
    column = pl.BlockSpec((width, span), lambda step, at: (0, at[0] * spans + step))
    turned = pl.BlockSpec((span, width), lambda step, at: (step, 0))
    line = pl.BlockSpec((1, span), lambda step, at: (0, step))
    teacher_w, student_w, inverse = call(
        directions_kernel,
        (
            shape((count, width), bf16),
            shape((count, width), bf16),
            shape((1, count), f32),
        ),
        flops=12 * count * width,
        moved=8 * count * width,
        grid_spec=pltpu.PrefetchScalarGridSpec(
            num_scalar_prefetch=1,
            grid=(spans,),
            in_specs=[column, column],
            out_specs=[turned, turned, line],
        ),
    )(
        block,
        hbm(teacher_v),
        hbm(student_v),
    )

    units, teacher_w = lax.optimization_barrier((units, teacher_w))
    sent = call(spread_kernel, shape((blocks, GROUPS * rows, 2 * width), bf16))(*units)
    own = lax.all_to_all(sent, "block", 0, 0)
    other = swap(own)
    half = crops // 2
    anyspace = pl.BlockSpec(memory_space=pl.ANY)
    pieces = count // (FETCH * TILE)
    halved = dict(flops=2 * elements * width, exps=elements)
    scratch = [pltpu.VMEM((half, width), bf16)] * 2
    own_mass, own_student, own_part, own_turned = call(
        own_kernel,
        (
            shape((count, half), f32),
            shape((count, half), f32),
            shape((8, half), f32),
            shape((width, half), bf16),
        ),
        scratch_shapes=scratch,
        **halved,
    )(teacher_w, student_w, own)
    other_mass, other_student, sent, student_part, other_turned = call(
        functools.partial(other_kernel, prototypes),
        (
            shape((count, half), f32),
            shape((count, half), f32),
            shape((members, 2 * lines, LANES), bf16),
            shape((lines, LANES), f32),
            shape((width, half), bf16),
        ),
        scratch_shapes=scratch,
        **halved,
    )(teacher_w, student_w, other, own_mass, own_part, *units)
    first = share(sent)
    sent, weights = call(
        functools.partial(sweep_kernel, prototypes, crops),
        (shape((members, 2 * lines, LANES), bf16), shape((lines, LANES), f32)),
        flops=4 * elements,
    )(own_mass, other_mass, first, student_part)
    second = share(sent)
    sent, own_scaled, other_scaled, student_copy = call(
        functools.partial(last_sweep_kernel, prototypes, crops),
        (
            shape((members, lines, LANES), bf16),
            shape((count, half), f32),
            shape((count, half), f32),
            shape((pieces, width, count // pieces), bf16),
        ),
        flops=4 * elements,
        in_specs=[vmem] * 3 + [anyspace],
        scratch_shapes=[dma((pieces,))],
    )(own_mass, other_mass, second, hbm(student_v))
    third = share(sent)

    gradient, own_weight, keep, give = call(
        gradient_kernel,
        (shape((2, count, half), bf16), shape((width, count), f32), shape((half // GROUPS, width), f32), shape((half // GROUPS, width), bf16)),
        flops=2 * elements * width // GROUPS,
        in_specs=[vmem] * 10,
        scratch_shapes=[pltpu.VMEM((width, count), bf16)],
    )(own_scaled, other_scaled, own_student, other_student, weights, second, third, inverse, student_copy, own_turned)
    other = swap(give)
    out_rows = width // chips
    per_chip = rows * width // out_rows
    sent = call(
        weight_kernel,
        shape((blocks, out_rows, count + per_chip), bf16),
        flops=2 * elements * width,
        in_specs=[vmem] * 5,
        scratch_shapes=[pltpu.VMEM((count // TILE, width, TILE), f32)],
    )(gradient, own_weight, other_turned, inverse, student_copy)
    sent = call(
        pack_kernel,
        shape((blocks, out_rows, count + per_chip), bf16),
        in_specs=[vmem] * 2 + [anyspace],
        out_specs=anyspace,
        input_output_aliases={2: 0},
        scratch_shapes=[pltpu.VMEM((blocks, out_rows, per_chip), bf16), dma],
    )(keep, other, sent)
    got = lax.all_to_all(sent, "block", 0, 0)
    return call(
        outputs_kernel,
        (shape((out_rows, kept), f32), shape((rows, width), f32)),
        grid=(2,),
        in_specs=[vmem, vmem],
        out_specs=[
            pl.BlockSpec((out_rows, kept // 2), lambda step: (0, step)),
            pl.BlockSpec((rows, width), lambda step: (0, 0)),
        ],
    )(got, student_feat)


def solution(mesh):
    dp, fsdp = mesh.shape["dp"], mesh.shape["fsdp"]
    blocks = dp // GROUPS

    def run(teacher_feat, student_feat, crop_weight, teacher_v, student_v):
        crops = teacher_feat.shape[0]
        count = teacher_v.shape[1] // (blocks * fsdp)
        fits = fsdp == 2 and dp == 16 and count % (2 * TILE) == 0 and crops == 1024
        if fits and 8 * count * crops <= KEPT_BYTES:
            grid = Mesh(mesh.devices.reshape(GROUPS, blocks, fsdp), (*CHIPS, "fsdp"))
            body, chips = kernel_body, CHIPS
        else:
            grid, body, chips = mesh, plain_body, ("dp",)
        every = P((*chips, "fsdp"))
        return jax.shard_map(
            body,
            mesh=grid,
            in_specs=(every, every, every, P(None, "fsdp"), P(None, "fsdp")),
            out_specs=(P(chips, "fsdp"), every),
            check_vma=False,
        )(teacher_feat, student_feat, crop_weight, teacher_v, student_v)

    return run
```

```python
import functools
import math

import jax
import jax.numpy as jnp
from jax import lax
from jax.experimental import pallas as pl
from jax.experimental.pallas import tpu as pltpu
from jax.sharding import Mesh
from jax.sharding import PartitionSpec as P

ITERS = 3

teacher_temp = 0.04
student_temp = 0.1
epsilon = 1e-06

GROUPS = 2
TILE = 256
HALF_TILE = 256
FETCH = 2
LANES = 128
VMEM_BYTES = 12 << 20
KEPT_BYTES = 18 << 20

EVERY = ("dp", "fsdp")
CHIPS = ("group", "block")
GROUP = ("fsdp", "block")


def unit_rows(values):
    floats = values.astype(jnp.float32)
    length = jnp.sqrt(jnp.sum(floats * floats, axis=1, keepdims=True) + epsilon)
    return (floats / length, length)


def unit_columns(values):
    floats = values.astype(jnp.float32)
    length = jnp.sqrt(jnp.sum(floats * floats, axis=0, keepdims=True) + epsilon)
    return (floats / length, length)


COPY_BYTES = 1 << 22


def share(values, axes):
    count = lax.axis_size(axes)
    if count * values.size * values.dtype.itemsize > COPY_BYTES:
        return lax.all_gather(values, axes)
    return lax.all_to_all(jnp.broadcast_to(values, (count, *values.shape)), axes, 0, 0)


def add_up(values):
    if lax.axis_size(EVERY) * values.size * values.dtype.itemsize > COPY_BYTES:
        return lax.psum(values, EVERY)
    return jnp.sum(share(values, EVERY), axis=0)


def plain_body(teacher_feat, student_feat, crop_weight, teacher_v, student_v):
    fsdp = lax.axis_size("fsdp")
    devices = lax.axis_size("dp") * fsdp
    own_rows, width = teacher_feat.shape
    crops = own_rows * devices
    block = teacher_v.shape[1] // lax.axis_size("dp")
    prototypes = block * devices
    first = lax.axis_index("dp") * block

    teacher_hat, _ = unit_rows(teacher_feat)
    student_hat, student_len = unit_rows(student_feat)
    units = jnp.concatenate(
        [teacher_hat.astype(jnp.bfloat16), student_hat.astype(jnp.bfloat16)], axis=1
    )
    units = share(share(units, "dp"), "fsdp").reshape(crops, 2 * width)
    teacher_unit, student_unit = units[:, :width], units[:, width:]

    teacher_w, _ = unit_columns(lax.dynamic_slice_in_dim(teacher_v, first, block, 1))
    student_w, student_wlen = unit_columns(lax.dynamic_slice_in_dim(student_v, first, block, 1))
    student_wunit = student_w.astype(jnp.bfloat16)

    mass = jnp.exp(
        jnp.dot(teacher_unit, teacher_w.astype(jnp.bfloat16), preferred_element_type=jnp.float32)
        / teacher_temp
    )
    student_mass = jnp.exp(
        jnp.dot(student_unit, student_wunit, preferred_element_type=jnp.float32) / student_temp
    )
    student_part = jnp.sum(student_mass, axis=1)

    crop_scale = None
    for sweep in range(ITERS):
        scaled = mass if sweep == 0 else mass * crop_scale[:, None]
        proto_scale = 1.0 / (prototypes * jnp.sum(scaled, axis=0))
        crop_part = jnp.sum(mass * proto_scale[None, :], axis=1)
        if sweep == 0:
            placed = jnp.zeros((fsdp, crops // (fsdp * own_rows), own_rows), jnp.float32)
            own = crop_weight.astype(jnp.float32)[None, None]
            spot = (lax.axis_index("fsdp"), lax.axis_index("dp"), 0)
            placed = lax.dynamic_update_slice(placed, own, spot).reshape(crops)
            sums = add_up(jnp.stack([crop_part, student_part, placed]))
            crop_mass, student_total, weights = sums[0], sums[1], sums[2]
        else:
            crop_mass = add_up(crop_part)
        crop_scale = 1.0 / (crops * crop_mass)

    target = crops * (mass * crop_scale[:, None] * proto_scale[None, :])
    student_prob = student_mass / student_total[:, None]
    gradient = ((student_prob - target) * weights[:, None] / student_temp).astype(jnp.bfloat16)
    feature_part = lax.dot_general(
        gradient, student_wunit, (((1,), (1,)), ((), ())), preferred_element_type=jnp.float32
    )
    weight_grad = lax.dot_general(
        student_unit, gradient, (((0,), (0,)), ((), ())), preferred_element_type=jnp.float32
    )
    weight_dot = jnp.sum(student_w * weight_grad, axis=0, keepdims=True)
    grad_block = (weight_grad - student_w * weight_dot) / student_wlen

    feature_sent = feature_part.astype(jnp.bfloat16).reshape(fsdp, -1, own_rows, width)
    feature_sent = jnp.swapaxes(feature_sent, 0, 1).reshape(devices, own_rows, width)
    feature_all = lax.all_to_all(feature_sent, EVERY, 0, 0)
    feature_grad = jnp.sum(feature_all.astype(jnp.float32), axis=0)
    grad_feat = (
        feature_grad - student_hat * jnp.sum(student_hat * feature_grad, axis=1, keepdims=True)
    ) / student_len
    grad_v = lax.all_to_all(grad_block.astype(jnp.bfloat16), "dp", 0, 1, tiled=True)
    return (grad_v.astype(jnp.float32), grad_feat)


def call(kernel, out_shape, flops=0, moved=0, exps=0, **more):
    return pl.pallas_call(
        kernel,
        out_shape=out_shape,
        compiler_params=pltpu.CompilerParams(vmem_limit_bytes=VMEM_BYTES),
        cost_estimate=pl.CostEstimate(flops=flops, bytes_accessed=moved, transcendentals=exps),
        **more,
    )


def units_kernel(teacher_ref, student_ref, weight_ref, units_out, teacher_vmem, student_vmem, weight_vmem, sems):
    copies = [
        pltpu.make_async_copy(teacher_ref, teacher_vmem, sems.at[0]),
        pltpu.make_async_copy(student_ref, student_vmem, sems.at[1]),
        pltpu.make_async_copy(weight_ref, weight_vmem, sems.at[2]),
    ]
    for copy in copies:
        copy.start()
    for copy in copies:
        copy.wait()
    rows, width = teacher_vmem.shape
    units_out[:rows, :width] = unit_rows(teacher_vmem[...])[0].astype(jnp.bfloat16)
    units_out[:rows, width:] = unit_rows(student_vmem[...])[0].astype(jnp.bfloat16)
    weights = weight_vmem[...].astype(jnp.float32)
    weights = jnp.concatenate([weights, jnp.zeros((1, 2 * width - rows), jnp.float32)], axis=1)
    units_out[rows:, :] = jnp.broadcast_to(weights, (units_out.shape[0] - rows, 2 * width)).astype(jnp.bfloat16)


def spread_kernel(*refs):
    *unit_refs, sent_ref = refs
    rows = sent_ref.shape[1] // GROUPS
    values = jnp.concatenate([ref[:rows, :] for ref in unit_refs], axis=0)
    for chip in range(sent_ref.shape[0]):
        sent_ref[chip] = values


def placed_weights(unit_refs, lines, rows, chips):
    group, block = lax.axis_index("group"), lax.axis_index("block")
    line = lax.broadcasted_iota(jnp.int32, (lines, LANES), 0)
    part = lax.broadcasted_iota(jnp.int32, (lines, LANES), 1) // rows
    each = LANES // rows
    placed = jnp.zeros((lines, LANES), jnp.float32)
    for back, ref in enumerate(unit_refs):
        at = lax.axis_index("fsdp") * chips * GROUPS + ((group + GROUPS - back) % GROUPS) * chips + block
        weights = ref[rows:, :LANES].astype(jnp.float32)[0:1, :rows]
        weights = jnp.concatenate([weights] * each, axis=1)
        here = (line == at // each) & (part == at % each)
        placed = placed + jnp.where(here, jnp.broadcast_to(weights, (lines, LANES)), 0.0)
    return placed


def directions_kernel(block_ref, teacher_ref, student_ref, teacher_out, student_out, inverse_out):
    teacher, _ = unit_columns(teacher_ref[...])
    teacher_out[...] = jnp.transpose(teacher).astype(jnp.bfloat16)
    student, length = unit_columns(student_ref[...])
    student_out[...] = jnp.transpose(student).astype(jnp.bfloat16)
    inverse_out[...] = 1.0 / length


def exponentials(directions, units, temperature):
    logits = lax.dot_general(
        directions, units, (((1,), (1,)), ((), ())), preferred_element_type=jnp.float32
    )
    return jnp.exp2(logits * (math.log2(math.e) / temperature))


def fold(values):
    rows, lanes = values.shape
    return jnp.sum(values.reshape(rows // 8, 8, lanes), axis=0)


def as_rows(line):
    return jnp.concatenate([line[:, at : at + LANES] for at in range(0, line.shape[1], LANES)], axis=0)


def as_line(rows):
    return jnp.concatenate([rows[at : at + 1, :] for at in range(rows.shape[0])], axis=1)


def in_core_order(core, own, other, body):
    @pl.when(core == 0)
    def _():
        body(own, other)

    @pl.when(core == 1)
    def _():
        body(other, own)


def sums(first, second):
    lines = [as_rows(jnp.sum(total, axis=0, keepdims=True)) for total in (first, second)]
    return jnp.concatenate(lines, axis=0)


def send(sent_ref, *rows):
    values = jnp.concatenate(rows, axis=0).astype(jnp.bfloat16)
    for device in range(sent_ref.shape[0]):
        sent_ref[device] = values


def halves(rows):
    line = as_line(rows)
    half = line.shape[1] // 2
    return line[:, :half], line[:, half:]


def received(got_ref, at=0):
    total = got_ref[0, at:, :].astype(jnp.float32)
    for device in range(1, got_ref.shape[0]):
        total = total + got_ref[device, at:, :].astype(jnp.float32)
    return total


def in_chip_order(got_ref, teacher_ref, student_ref):
    chips = got_ref.shape[0]
    width = teacher_ref.shape[1]
    rows = teacher_ref.shape[0] // (GROUPS * chips)
    group = lax.axis_index("group")
    for back in range(GROUPS):
        for chip in range(chips):
            at = (((group + GROUPS - back) % GROUPS) * chips + chip) * rows
            here = pl.ds(pl.multiple_of(at, rows), rows)
            teacher_ref[here, :] = got_ref[chip, back * rows : (back + 1) * rows, :width]
            student_ref[here, :] = got_ref[chip, back * rows : (back + 1) * rows, width:]


def turn(units):
    return jnp.transpose(units.astype(jnp.float32)).astype(jnp.bfloat16)


def own_kernel(
    teacher_w_ref, student_w_ref, got_ref, teacher_ref, student_ref, part_ref, turned_ref, teacher_units, student_units
):
    in_chip_order(got_ref, teacher_units, student_units)
    turned_ref[...] = turn(student_units[...])
    part = 0.0
    for start in range(0, teacher_ref.shape[0], HALF_TILE):
        here = slice(start, start + HALF_TILE)
        teacher_ref[here, :] = exponentials(teacher_w_ref[here, :], teacher_units[...], teacher_temp)
        mass = exponentials(student_w_ref[here, :], student_units[...], student_temp)
        student_ref[here, :] = mass
        part = part + fold(mass)
    part_ref[...] = part


def other_kernel(prototypes, teacher_w_ref, student_w_ref, got_ref, own_ref, own_part_ref, *refs):
    unit_refs = refs[:GROUPS]
    teacher_ref, student_ref, sent_ref, part_ref, turned_ref, teacher_units, student_units = refs[GROUPS:]
    chips = got_ref.shape[0]
    in_chip_order(got_ref, teacher_units, student_units)
    turned_ref[...] = turn(student_units[...])
    half = own_ref.shape[1]
    placed = placed_weights(unit_refs, 2 * half // LANES, half // (GROUPS * chips), chips)
    own_total = total = part = 0.0
    for start in range(0, teacher_ref.shape[0], HALF_TILE):
        here = slice(start, start + HALF_TILE)
        mass = exponentials(teacher_w_ref[here, :], teacher_units[...], teacher_temp)
        teacher_ref[here, :] = mass
        own = own_ref[here, :]
        scale = 1.0 / (prototypes * jnp.sum(own + mass, axis=1, keepdims=True))
        own_total = own_total + fold(own * scale)
        total = total + fold(mass * scale)
        mass = exponentials(student_w_ref[here, :], student_units[...], student_temp)
        student_ref[here, :] = mass
        part = part + fold(mass)

    def finish(first, second):
        send(sent_ref, sums(first[0], second[0]), placed)
        part_ref[...] = sums(first[1], second[1])

    in_core_order(lax.axis_index("fsdp"), (own_total, own_part_ref[...]), (total, part), finish)


def sweep(prototypes, crops, first_ref, second_ref, received_sums, scaled_refs=None):
    first_crop, second_crop = halves(1.0 / (crops * received_sums))
    first_total = second_total = 0.0
    for start in range(0, first_ref.shape[0], TILE):
        here = slice(start, start + TILE)
        first, second = first_ref[here, :], second_ref[here, :]
        proto = jnp.sum(first * first_crop + second * second_crop, axis=1, keepdims=True)
        scale = 1.0 / (prototypes * proto)
        first, second = first * scale, second * scale
        if scaled_refs is not None:
            scaled_refs[0][here, :], scaled_refs[1][here, :] = first, second
        first_total = first_total + fold(first)
        second_total = second_total + fold(second)
    return sums(first_total, second_total)


def sweep_kernel(prototypes, crops, own_ref, other_ref, got_ref, part_ref, sent_ref, weight_ref):
    lines = crops // LANES
    extra = received(got_ref)
    weight_ref[...] = extra[lines:]

    def body(first_ref, second_ref):
        send(sent_ref, sweep(prototypes, crops, first_ref, second_ref, extra[:lines]), part_ref[...])

    in_core_order(lax.axis_index("fsdp"), own_ref, other_ref, body)


def last_sweep_kernel(
    prototypes, crops, own_ref, other_ref, got_ref, directions_ref,
    sent_ref, own_scaled_ref, other_scaled_ref, copy_ref, sems,
):
    pieces, _, span = copy_ref.shape
    copies = []
    for piece in range(pieces):
        columns = pl.ds(pl.multiple_of((lax.axis_index("block") * pieces + piece) * span, span), span)
        copies.append(pltpu.make_async_copy(directions_ref.at[:, columns], copy_ref.at[piece], sems.at[piece]))
        copies[-1].start()

    total = received(got_ref)[: crops // LANES]

    def body(first_refs, second_refs):
        (first_ref, *scaled_refs), (second_ref, second_scaled_ref) = first_refs, second_refs
        sent = sweep(prototypes, crops, first_ref, second_ref, total, (*scaled_refs, second_scaled_ref))
        send(sent_ref, sent)

    in_core_order(lax.axis_index("fsdp"), (own_ref, own_scaled_ref), (other_ref, other_scaled_ref), body)
    for copy in copies:
        copy.wait()


def units_tile(copy_ref, inverse_ref, start):
    span = copy_ref.shape[2]
    at = start % span
    return copy_ref[start // span, :, at : at + TILE].astype(jnp.float32) * inverse_ref[:, start : start + TILE]


def gradient_kernel(
    own_mass_ref, other_mass_ref, own_student_ref, other_student_ref, weight_ref, second_ref, third_ref,
    inverse_ref, copy_ref, gradient_ref, keep_ref, give_ref, unit_ref,
):
    group, core = lax.axis_index("group"), lax.axis_index("fsdp")
    count, half = own_mass_ref.shape
    lines = 2 * half // LANES
    weights = weight_ref[...] / student_temp
    teacher_scales = halves(weights / received(third_ref)[:lines])
    student_scales = halves(weights / received(second_ref)[lines:])

    def body(first_refs, second_refs):
        for start in range(0, count, TILE):
            here = slice(start, start + TILE)
            for (side, mass_ref, student_ref), teacher_scale, student_scale in zip(
                (first_refs, second_refs), teacher_scales, student_scales
            ):
                gradient = student_ref[here, :] * student_scale - mass_ref[here, :] * teacher_scale
                gradient_ref[side, start : start + TILE, :] = gradient.astype(jnp.bfloat16)

    in_core_order(core, (0, own_mass_ref, own_student_ref), (1, other_mass_ref, other_student_ref), body)
    for start in range(0, count, TILE):
        unit_ref[:, start : start + TILE] = units_tile(copy_ref, inverse_ref, start).astype(jnp.bfloat16)
    kept = half // GROUPS
    lanes = pl.ds(pl.multiple_of(group * kept, kept), kept)
    for side, out_ref in enumerate((keep_ref, give_ref)):
        feature = jnp.dot(unit_ref[...], gradient_ref[side, :, lanes], preferred_element_type=jnp.float32)
        out_ref[...] = jnp.transpose(feature).astype(out_ref.dtype)


def weight_kernel(gradient_ref, own_turned_ref, other_turned_ref, inverse_ref, copy_ref, sent_ref, grad_ref):
    chips, rows_each, _ = sent_ref.shape
    count = gradient_ref.shape[1]
    width = own_turned_ref.shape[0]
    kept = width // GROUPS
    own_rows = pl.ds(pl.multiple_of(lax.axis_index("group") * kept, kept), kept)
    for start in range(0, count, TILE):
        here, slot = slice(start, start + TILE), start // TILE
        weight_grad = 0.0
        for side, turned_ref in enumerate((own_turned_ref, other_turned_ref)):
            weight_grad = weight_grad + lax.dot_general(
                turned_ref[...], gradient_ref[side, here, :], (((1,), (1,)), ((), ())), preferred_element_type=jnp.float32
            )
        unit = units_tile(copy_ref, inverse_ref, start)
        dot = jnp.sum(unit * weight_grad, axis=0, keepdims=True)
        grad_ref[slot] = (weight_grad - unit * dot) * inverse_ref[:, here]
        own = grad_ref[slot, own_rows, :].astype(jnp.bfloat16)
        sent_ref[:, :, here] = own.reshape(chips, rows_each, TILE)


def pack_kernel(keep_ref, other_ref, _, sent_ref, packed_ref, sem):
    chips, rows_each, lanes = packed_ref.shape
    width = keep_ref.shape[1]
    total = (keep_ref[...] + other_ref[...].astype(jnp.float32)).astype(jnp.bfloat16)
    total = total.reshape(chips, -1, width)
    for piece in range(lanes // width):
        packed_ref[:, :, piece * width : (piece + 1) * width] = total[:, piece * rows_each : (piece + 1) * rows_each, :]
    copy = pltpu.make_async_copy(packed_ref, sent_ref.at[:, :, pl.ds(sent_ref.shape[2] - lanes, lanes)], sem)
    copy.start()
    copy.wait()


def outputs_kernel(got_ref, student_ref, weight_out, feature_out):
    chips, rows_each, columns = got_ref.shape
    rows, width = student_ref.shape
    pieces = rows // rows_each
    count = columns - pieces * width
    step = pl.program_id(0)
    each = chips // pl.num_programs(0)
    for chip in range(each):
        weight_out[:, chip * count : (chip + 1) * count] = got_ref[step * each + chip, :, :count].astype(jnp.float32)

    @pl.when(step == 0)
    def _():
        total = got_ref[0, :, count:].astype(jnp.float32)
        for chip in range(1, chips):
            total = total + got_ref[chip, :, count:].astype(jnp.float32)
        total = jnp.concatenate([total[:, piece * width : (piece + 1) * width] for piece in range(pieces)], axis=0)
        hat, length = unit_rows(student_ref[...])
        feature_out[...] = (total - hat * jnp.sum(hat * total, axis=1, keepdims=True)) / length


def kernel_body(teacher_feat, student_feat, crop_weight, teacher_v, student_v):
    f32, bf16 = jnp.float32, jnp.bfloat16
    shape = jax.ShapeDtypeStruct
    blocks, fsdp = lax.axis_size("block"), lax.axis_size("fsdp")
    chips = blocks * GROUPS
    members, devices = blocks * fsdp, chips * fsdp
    rows, width = teacher_feat.shape
    crops = rows * devices
    lines = crops // LANES
    kept = teacher_v.shape[1]
    prototypes = kept * fsdp
    count = kept // blocks
    group, block = lax.axis_index("group")[None], lax.axis_index("block")[None]
    core = lax.axis_index("fsdp")[None]
    elements = count * crops
    vmem = pl.BlockSpec(memory_space=pltpu.VMEM)

    def swap(values):
        return lax.ppermute(values, "fsdp", [(0, 1), (1, 0)])

    def share(values):
        return lax.all_to_all(values, GROUP, 0, 0)

    dma = pltpu.SemaphoreType.DMA
    hbm = functools.partial(pltpu.with_memory_space_constraint, memory_space=pltpu.HBM)
    units = call(
        units_kernel,
        shape((rows + 16, 2 * width), bf16),
        in_specs=[pl.BlockSpec(memory_space=pl.ANY)] * 3,
        scratch_shapes=[pltpu.VMEM((rows, width), bf16)] * 2 + [pltpu.VMEM((1, rows), bf16), dma((3,))],
    )(hbm(teacher_feat), hbm(student_feat), hbm(crop_weight[None, :]))

    def of_groups(values):
        return [values] + [
            lax.ppermute(values, "group", [(at, (at + back) % GROUPS) for at in range(GROUPS)]) for back in range(1, GROUPS)
        ]

    units = of_groups(units)

    span = 2 * TILE
    spans = count // span
    column = pl.BlockSpec((width, span), lambda step, at: (0, at[0] * spans + step))
    turned = pl.BlockSpec((span, width), lambda step, at: (step, 0))
    line = pl.BlockSpec((1, span), lambda step, at: (0, step))
    teacher_w, student_w, inverse = call(
        directions_kernel,
        (
            shape((count, width), bf16),
            shape((count, width), bf16),
            shape((1, count), f32),
        ),
        flops=12 * count * width,
        moved=8 * count * width,
        grid_spec=pltpu.PrefetchScalarGridSpec(
            num_scalar_prefetch=1,
            grid=(spans,),
            in_specs=[column, column],
            out_specs=[turned, turned, line],
        ),
    )(
        block,
        hbm(teacher_v),
        hbm(student_v),
    )

    units, teacher_w = lax.optimization_barrier((units, teacher_w))
    sent = call(spread_kernel, shape((blocks, GROUPS * rows, 2 * width), bf16))(*units)
    own = lax.all_to_all(sent, "block", 0, 0)
    other = swap(own)
    half = crops // 2
    anyspace = pl.BlockSpec(memory_space=pl.ANY)
    pieces = count // (FETCH * TILE)
    halved = dict(flops=2 * elements * width, exps=elements)
    scratch = [pltpu.VMEM((half, width), bf16)] * 2
    own_mass, own_student, own_part, own_turned = call(
        own_kernel,
        (
            shape((count, half), f32),
            shape((count, half), f32),
            shape((8, half), f32),
            shape((width, half), bf16),
        ),
        scratch_shapes=scratch,
        **halved,
    )(teacher_w, student_w, own)
    other_mass, other_student, sent, student_part, other_turned = call(
        functools.partial(other_kernel, prototypes),
        (
            shape((count, half), f32),
            shape((count, half), f32),
            shape((members, 2 * lines, LANES), bf16),
            shape((lines, LANES), f32),
            shape((width, half), bf16),
        ),
        scratch_shapes=scratch,
        **halved,
    )(teacher_w, student_w, other, own_mass, own_part, *units)
    first = share(sent)
    sent, weights = call(
        functools.partial(sweep_kernel, prototypes, crops),
        (shape((members, 2 * lines, LANES), bf16), shape((lines, LANES), f32)),
        flops=4 * elements,
    )(own_mass, other_mass, first, student_part)
    second = share(sent)
    sent, own_scaled, other_scaled, student_copy = call(
        functools.partial(last_sweep_kernel, prototypes, crops),
        (
            shape((members, lines, LANES), bf16),
            shape((count, half), f32),
            shape((count, half), f32),
            shape((pieces, width, count // pieces), bf16),
        ),
        flops=4 * elements,
        in_specs=[vmem] * 3 + [anyspace],
        scratch_shapes=[dma((pieces,))],
    )(own_mass, other_mass, second, hbm(student_v))
    third = share(sent)

    gradient, keep, give = call(
        gradient_kernel,
        (shape((2, count, half), bf16), shape((half // GROUPS, width), f32), shape((half // GROUPS, width), bf16)),
        flops=2 * elements * width // GROUPS,
        in_specs=[vmem] * 9,
        scratch_shapes=[pltpu.VMEM((width, count), bf16)],
    )(own_scaled, other_scaled, own_student, other_student, weights, second, third, inverse, student_copy)
    other = swap(give)
    out_rows = width // chips
    per_chip = rows * width // out_rows
    sent = call(
        weight_kernel,
        shape((blocks, out_rows, count + per_chip), bf16),
        flops=2 * elements * width,
        in_specs=[vmem] * 5,
        scratch_shapes=[pltpu.VMEM((count // TILE, width, TILE), f32)],
    )(gradient, own_turned, other_turned, inverse, student_copy)
    sent = call(
        pack_kernel,
        shape((blocks, out_rows, count + per_chip), bf16),
        in_specs=[vmem] * 2 + [anyspace],
        out_specs=anyspace,
        input_output_aliases={2: 0},
        scratch_shapes=[pltpu.VMEM((blocks, out_rows, per_chip), bf16), dma],
    )(keep, other, sent)
    got = lax.all_to_all(sent, "block", 0, 0)
    return call(
        outputs_kernel,
        (shape((out_rows, kept), f32), shape((rows, width), f32)),
        grid=(2,),
        in_specs=[vmem, vmem],
        out_specs=[
            pl.BlockSpec((out_rows, kept // 2), lambda step: (0, step)),
            pl.BlockSpec((rows, width), lambda step: (0, 0)),
        ],
    )(got, student_feat)


def solution(mesh):
    dp, fsdp = mesh.shape["dp"], mesh.shape["fsdp"]
    blocks = dp // GROUPS

    def run(teacher_feat, student_feat, crop_weight, teacher_v, student_v):
        crops = teacher_feat.shape[0]
        count = teacher_v.shape[1] // (blocks * fsdp)
        fits = fsdp == 2 and dp == 16 and count % (2 * TILE) == 0 and crops == 1024
        if fits and 8 * count * crops <= KEPT_BYTES:
            grid = Mesh(mesh.devices.reshape(GROUPS, blocks, fsdp), (*CHIPS, "fsdp"))
            body, chips = kernel_body, CHIPS
        else:
            grid, body, chips = mesh, plain_body, ("dp",)
        every = P((*chips, "fsdp"))
        return jax.shard_map(
            body,
            mesh=grid,
            in_specs=(every, every, every, P(None, "fsdp"), P(None, "fsdp")),
            out_specs=(P(chips, "fsdp"), every),
            check_vma=False,
        )(teacher_feat, student_feat, crop_weight, teacher_v, student_v)

    return run
```

```python
import functools
import math

import jax
import jax.numpy as jnp
from jax import lax
from jax.experimental import pallas as pl
from jax.experimental.pallas import tpu as pltpu
from jax.sharding import Mesh
from jax.sharding import PartitionSpec as P

ITERS = 3

teacher_temp = 0.04
student_temp = 0.1
epsilon = 1e-06

GROUPS = 2
TILE = 512
HALF_TILE = 256
FETCH = 2
LANES = 128
VMEM_BYTES = 12 << 20
KEPT_BYTES = 18 << 20

EVERY = ("dp", "fsdp")
CHIPS = ("group", "block")
GROUP = ("fsdp", "block")


def unit_rows(values):
    floats = values.astype(jnp.float32)
    length = jnp.sqrt(jnp.sum(floats * floats, axis=1, keepdims=True) + epsilon)
    return (floats / length, length)


def unit_columns(values):
    floats = values.astype(jnp.float32)
    length = jnp.sqrt(jnp.sum(floats * floats, axis=0, keepdims=True) + epsilon)
    return (floats / length, length)


COPY_BYTES = 1 << 22


def share(values, axes):
    count = lax.axis_size(axes)
    if count * values.size * values.dtype.itemsize > COPY_BYTES:
        return lax.all_gather(values, axes)
    return lax.all_to_all(jnp.broadcast_to(values, (count, *values.shape)), axes, 0, 0)


def add_up(values):
    if lax.axis_size(EVERY) * values.size * values.dtype.itemsize > COPY_BYTES:
        return lax.psum(values, EVERY)
    return jnp.sum(share(values, EVERY), axis=0)


def plain_body(teacher_feat, student_feat, crop_weight, teacher_v, student_v):
    fsdp = lax.axis_size("fsdp")
    devices = lax.axis_size("dp") * fsdp
    own_rows, width = teacher_feat.shape
    crops = own_rows * devices
    block = teacher_v.shape[1] // lax.axis_size("dp")
    prototypes = block * devices
    first = lax.axis_index("dp") * block

    teacher_hat, _ = unit_rows(teacher_feat)
    student_hat, student_len = unit_rows(student_feat)
    units = jnp.concatenate(
        [teacher_hat.astype(jnp.bfloat16), student_hat.astype(jnp.bfloat16)], axis=1
    )
    units = share(share(units, "dp"), "fsdp").reshape(crops, 2 * width)
    teacher_unit, student_unit = units[:, :width], units[:, width:]

    teacher_w, _ = unit_columns(lax.dynamic_slice_in_dim(teacher_v, first, block, 1))
    student_w, student_wlen = unit_columns(lax.dynamic_slice_in_dim(student_v, first, block, 1))
    student_wunit = student_w.astype(jnp.bfloat16)

    mass = jnp.exp(
        jnp.dot(teacher_unit, teacher_w.astype(jnp.bfloat16), preferred_element_type=jnp.float32)
        / teacher_temp
    )
    student_mass = jnp.exp(
        jnp.dot(student_unit, student_wunit, preferred_element_type=jnp.float32) / student_temp
    )
    student_part = jnp.sum(student_mass, axis=1)

    crop_scale = None
    for sweep in range(ITERS):
        scaled = mass if sweep == 0 else mass * crop_scale[:, None]
        proto_scale = 1.0 / (prototypes * jnp.sum(scaled, axis=0))
        crop_part = jnp.sum(mass * proto_scale[None, :], axis=1)
        if sweep == 0:
            placed = jnp.zeros((fsdp, crops // (fsdp * own_rows), own_rows), jnp.float32)
            own = crop_weight.astype(jnp.float32)[None, None]
            spot = (lax.axis_index("fsdp"), lax.axis_index("dp"), 0)
            placed = lax.dynamic_update_slice(placed, own, spot).reshape(crops)
            sums = add_up(jnp.stack([crop_part, student_part, placed]))
            crop_mass, student_total, weights = sums[0], sums[1], sums[2]
        else:
            crop_mass = add_up(crop_part)
        crop_scale = 1.0 / (crops * crop_mass)

    target = crops * (mass * crop_scale[:, None] * proto_scale[None, :])
    student_prob = student_mass / student_total[:, None]
    gradient = ((student_prob - target) * weights[:, None] / student_temp).astype(jnp.bfloat16)
    feature_part = lax.dot_general(
        gradient, student_wunit, (((1,), (1,)), ((), ())), preferred_element_type=jnp.float32
    )
    weight_grad = lax.dot_general(
        student_unit, gradient, (((0,), (0,)), ((), ())), preferred_element_type=jnp.float32
    )
    weight_dot = jnp.sum(student_w * weight_grad, axis=0, keepdims=True)
    grad_block = (weight_grad - student_w * weight_dot) / student_wlen

    feature_sent = feature_part.astype(jnp.bfloat16).reshape(fsdp, -1, own_rows, width)
    feature_sent = jnp.swapaxes(feature_sent, 0, 1).reshape(devices, own_rows, width)
    feature_all = lax.all_to_all(feature_sent, EVERY, 0, 0)
    feature_grad = jnp.sum(feature_all.astype(jnp.float32), axis=0)
    grad_feat = (
        feature_grad - student_hat * jnp.sum(student_hat * feature_grad, axis=1, keepdims=True)
    ) / student_len
    grad_v = lax.all_to_all(grad_block.astype(jnp.bfloat16), "dp", 0, 1, tiled=True)
    return (grad_v.astype(jnp.float32), grad_feat)


def call(kernel, out_shape, flops=0, moved=0, exps=0, **more):
    return pl.pallas_call(
        kernel,
        out_shape=out_shape,
        compiler_params=pltpu.CompilerParams(vmem_limit_bytes=VMEM_BYTES),
        cost_estimate=pl.CostEstimate(flops=flops, bytes_accessed=moved, transcendentals=exps),
        **more,
    )


def units_kernel(teacher_ref, student_ref, weight_ref, units_out, teacher_vmem, student_vmem, weight_vmem, sems):
    copies = [
        pltpu.make_async_copy(teacher_ref, teacher_vmem, sems.at[0]),
        pltpu.make_async_copy(student_ref, student_vmem, sems.at[1]),
        pltpu.make_async_copy(weight_ref, weight_vmem, sems.at[2]),
    ]
    for copy in copies:
        copy.start()
    for copy in copies:
        copy.wait()
    rows, width = teacher_vmem.shape
    units_out[:rows, :width] = unit_rows(teacher_vmem[...])[0].astype(jnp.bfloat16)
    units_out[:rows, width:] = unit_rows(student_vmem[...])[0].astype(jnp.bfloat16)
    weights = weight_vmem[...].astype(jnp.float32)
    weights = jnp.concatenate([weights, jnp.zeros((1, 2 * width - rows), jnp.float32)], axis=1)
    units_out[rows:, :] = jnp.broadcast_to(weights, (units_out.shape[0] - rows, 2 * width)).astype(jnp.bfloat16)


def spread_kernel(*refs):
    *unit_refs, sent_ref = refs
    rows = sent_ref.shape[1] // GROUPS
    values = jnp.concatenate([ref[:rows, :] for ref in unit_refs], axis=0)
    for chip in range(sent_ref.shape[0]):
        sent_ref[chip] = values


def placed_weights(unit_refs, lines, rows, chips):
    group, block = lax.axis_index("group"), lax.axis_index("block")
    line = lax.broadcasted_iota(jnp.int32, (lines, LANES), 0)
    part = lax.broadcasted_iota(jnp.int32, (lines, LANES), 1) // rows
    each = LANES // rows
    placed = jnp.zeros((lines, LANES), jnp.float32)
    for back, ref in enumerate(unit_refs):
        at = lax.axis_index("fsdp") * chips * GROUPS + ((group + GROUPS - back) % GROUPS) * chips + block
        weights = ref[rows:, :LANES].astype(jnp.float32)[0:1, :rows]
        weights = jnp.concatenate([weights] * each, axis=1)
        here = (line == at // each) & (part == at % each)
        placed = placed + jnp.where(here, jnp.broadcast_to(weights, (lines, LANES)), 0.0)
    return placed


def directions_kernel(block_ref, teacher_ref, student_ref, teacher_out, student_out, inverse_out):
    teacher, _ = unit_columns(teacher_ref[...])
    teacher_out[...] = jnp.transpose(teacher).astype(jnp.bfloat16)
    student, length = unit_columns(student_ref[...])
    student_out[...] = jnp.transpose(student).astype(jnp.bfloat16)
    inverse_out[...] = 1.0 / length


def exponentials(directions, units, temperature):
    logits = lax.dot_general(
        directions, units, (((1,), (1,)), ((), ())), preferred_element_type=jnp.float32
    )
    return jnp.exp2(logits * (math.log2(math.e) / temperature))


def fold(values):
    rows, lanes = values.shape
    return jnp.sum(values.reshape(rows // 8, 8, lanes), axis=0)


def as_rows(line):
    return jnp.concatenate([line[:, at : at + LANES] for at in range(0, line.shape[1], LANES)], axis=0)


def as_line(rows):
    return jnp.concatenate([rows[at : at + 1, :] for at in range(rows.shape[0])], axis=1)


def in_core_order(core, own, other, body):
    @pl.when(core == 0)
    def _():
        body(own, other)

    @pl.when(core == 1)
    def _():
        body(other, own)


def sums(first, second):
    lines = [as_rows(jnp.sum(total, axis=0, keepdims=True)) for total in (first, second)]
    return jnp.concatenate(lines, axis=0)


def send(sent_ref, *rows):
    values = jnp.concatenate(rows, axis=0).astype(jnp.bfloat16)
    for device in range(sent_ref.shape[0]):
        sent_ref[device] = values


def halves(rows):
    line = as_line(rows)
    half = line.shape[1] // 2
    return line[:, :half], line[:, half:]


def received(got_ref, at=0):
    total = got_ref[0, at:, :].astype(jnp.float32)
    for device in range(1, got_ref.shape[0]):
        total = total + got_ref[device, at:, :].astype(jnp.float32)
    return total


def in_chip_order(got_ref, teacher_ref, student_ref):
    chips = got_ref.shape[0]
    width = teacher_ref.shape[1]
    rows = teacher_ref.shape[0] // (GROUPS * chips)
    group = lax.axis_index("group")
    for back in range(GROUPS):
        for chip in range(chips):
            at = (((group + GROUPS - back) % GROUPS) * chips + chip) * rows
            here = pl.ds(pl.multiple_of(at, rows), rows)
            teacher_ref[here, :] = got_ref[chip, back * rows : (back + 1) * rows, :width]
            student_ref[here, :] = got_ref[chip, back * rows : (back + 1) * rows, width:]


def turn(units):
    return jnp.transpose(units.astype(jnp.float32)).astype(jnp.bfloat16)


def own_kernel(
    teacher_w_ref, student_w_ref, got_ref, teacher_ref, student_ref, part_ref, turned_ref, teacher_units, student_units
):
    in_chip_order(got_ref, teacher_units, student_units)
    turned_ref[...] = turn(student_units[...])
    part = 0.0
    for start in range(0, teacher_ref.shape[0], HALF_TILE):
        here = slice(start, start + HALF_TILE)
        teacher_ref[here, :] = exponentials(teacher_w_ref[here, :], teacher_units[...], teacher_temp)
        mass = exponentials(student_w_ref[here, :], student_units[...], student_temp)
        student_ref[here, :] = mass
        part = part + fold(mass)
    part_ref[...] = part


def other_kernel(prototypes, teacher_w_ref, student_w_ref, got_ref, own_ref, own_part_ref, *refs):
    unit_refs = refs[:GROUPS]
    teacher_ref, student_ref, sent_ref, part_ref, turned_ref, teacher_units, student_units = refs[GROUPS:]
    chips = got_ref.shape[0]
    in_chip_order(got_ref, teacher_units, student_units)
    turned_ref[...] = turn(student_units[...])
    half = own_ref.shape[1]
    placed = placed_weights(unit_refs, 2 * half // LANES, half // (GROUPS * chips), chips)
    own_total = total = part = 0.0
    for start in range(0, teacher_ref.shape[0], HALF_TILE):
        here = slice(start, start + HALF_TILE)
        mass = exponentials(teacher_w_ref[here, :], teacher_units[...], teacher_temp)
        teacher_ref[here, :] = mass
        own = own_ref[here, :]
        scale = 1.0 / (prototypes * jnp.sum(own + mass, axis=1, keepdims=True))
        own_total = own_total + fold(own * scale)
        total = total + fold(mass * scale)
        mass = exponentials(student_w_ref[here, :], student_units[...], student_temp)
        student_ref[here, :] = mass
        part = part + fold(mass)

    def finish(first, second):
        send(sent_ref, sums(first[0], second[0]), placed)
        part_ref[...] = sums(first[1], second[1])

    in_core_order(lax.axis_index("fsdp"), (own_total, own_part_ref[...]), (total, part), finish)


def sweep(prototypes, crops, first_ref, second_ref, received_sums, scaled_refs=None):
    first_crop, second_crop = halves(1.0 / (crops * received_sums))
    first_total = second_total = 0.0
    for start in range(0, first_ref.shape[0], TILE):
        here = slice(start, start + TILE)
        first, second = first_ref[here, :], second_ref[here, :]
        proto = jnp.sum(first * first_crop + second * second_crop, axis=1, keepdims=True)
        scale = 1.0 / (prototypes * proto)
        first, second = first * scale, second * scale
        if scaled_refs is not None:
            scaled_refs[0][here, :], scaled_refs[1][here, :] = first, second
        first_total = first_total + fold(first)
        second_total = second_total + fold(second)
    return sums(first_total, second_total)


def sweep_kernel(prototypes, crops, own_ref, other_ref, got_ref, part_ref, sent_ref, weight_ref):
    lines = crops // LANES
    extra = received(got_ref)
    weight_ref[...] = extra[lines:]

    def body(first_ref, second_ref):
        send(sent_ref, sweep(prototypes, crops, first_ref, second_ref, extra[:lines]), part_ref[...])

    in_core_order(lax.axis_index("fsdp"), own_ref, other_ref, body)


def last_sweep_kernel(
    prototypes, crops, own_ref, other_ref, got_ref, directions_ref,
    sent_ref, own_scaled_ref, other_scaled_ref, copy_ref, sems,
):
    pieces, _, span = copy_ref.shape
    copies = []
    for piece in range(pieces):
        columns = pl.ds(pl.multiple_of((lax.axis_index("block") * pieces + piece) * span, span), span)
        copies.append(pltpu.make_async_copy(directions_ref.at[:, columns], copy_ref.at[piece], sems.at[piece]))
        copies[-1].start()

    total = received(got_ref)[: crops // LANES]

    def body(first_refs, second_refs):
        (first_ref, *scaled_refs), (second_ref, second_scaled_ref) = first_refs, second_refs
        sent = sweep(prototypes, crops, first_ref, second_ref, total, (*scaled_refs, second_scaled_ref))
        send(sent_ref, sent)

    in_core_order(lax.axis_index("fsdp"), (own_ref, own_scaled_ref), (other_ref, other_scaled_ref), body)
    for copy in copies:
        copy.wait()


def units_tile(copy_ref, inverse_ref, start):
    span = copy_ref.shape[2]
    at = start % span
    return copy_ref[start // span, :, at : at + TILE].astype(jnp.float32) * inverse_ref[:, start : start + TILE]


def gradient_kernel(
    own_mass_ref, other_mass_ref, own_student_ref, other_student_ref, weight_ref, second_ref, third_ref,
    inverse_ref, copy_ref, gradient_ref, keep_ref, give_ref, unit_ref,
):
    group, core = lax.axis_index("group"), lax.axis_index("fsdp")
    count, half = own_mass_ref.shape
    lines = 2 * half // LANES
    weights = weight_ref[...] / student_temp
    teacher_scales = halves(weights / received(third_ref)[:lines])
    student_scales = halves(weights / received(second_ref)[lines:])

    def body(first_refs, second_refs):
        for start in range(0, count, TILE):
            here = slice(start, start + TILE)
            for (side, mass_ref, student_ref), teacher_scale, student_scale in zip(
                (first_refs, second_refs), teacher_scales, student_scales
            ):
                gradient = student_ref[here, :] * student_scale - mass_ref[here, :] * teacher_scale
                gradient_ref[side, start : start + TILE, :] = gradient.astype(jnp.bfloat16)

    in_core_order(core, (0, own_mass_ref, own_student_ref), (1, other_mass_ref, other_student_ref), body)
    for start in range(0, count, TILE):
        unit_ref[:, start : start + TILE] = units_tile(copy_ref, inverse_ref, start).astype(jnp.bfloat16)
    kept = half // GROUPS
    lanes = pl.ds(pl.multiple_of(group * kept, kept), kept)
    for side, out_ref in enumerate((keep_ref, give_ref)):
        feature = jnp.dot(unit_ref[...], gradient_ref[side, :, lanes], preferred_element_type=jnp.float32)
        out_ref[...] = jnp.transpose(feature).astype(out_ref.dtype)


def weight_kernel(gradient_ref, own_turned_ref, other_turned_ref, inverse_ref, copy_ref, sent_ref, grad_ref):
    chips, rows_each, _ = sent_ref.shape
    count = gradient_ref.shape[1]
    width = own_turned_ref.shape[0]
    kept = width // GROUPS
    own_rows = pl.ds(pl.multiple_of(lax.axis_index("group") * kept, kept), kept)
    for start in range(0, count, TILE):
        here, slot = slice(start, start + TILE), start // TILE
        weight_grad = 0.0
        for side, turned_ref in enumerate((own_turned_ref, other_turned_ref)):
            weight_grad = weight_grad + lax.dot_general(
                turned_ref[...], gradient_ref[side, here, :], (((1,), (1,)), ((), ())), preferred_element_type=jnp.float32
            )
        unit = units_tile(copy_ref, inverse_ref, start)
        dot = jnp.sum(unit * weight_grad, axis=0, keepdims=True)
        grad_ref[slot] = (weight_grad - unit * dot) * inverse_ref[:, here]
        own = grad_ref[slot, own_rows, :].astype(jnp.bfloat16)
        sent_ref[:, :, here] = own.reshape(chips, rows_each, TILE)


def pack_kernel(keep_ref, other_ref, _, sent_ref, packed_ref, sem):
    chips, rows_each, lanes = packed_ref.shape
    width = keep_ref.shape[1]
    total = (keep_ref[...] + other_ref[...].astype(jnp.float32)).astype(jnp.bfloat16)
    total = total.reshape(chips, -1, width)
    for piece in range(lanes // width):
        packed_ref[:, :, piece * width : (piece + 1) * width] = total[:, piece * rows_each : (piece + 1) * rows_each, :]
    copy = pltpu.make_async_copy(packed_ref, sent_ref.at[:, :, pl.ds(sent_ref.shape[2] - lanes, lanes)], sem)
    copy.start()
    copy.wait()


def outputs_kernel(got_ref, student_ref, weight_out, feature_out):
    chips, rows_each, columns = got_ref.shape
    rows, width = student_ref.shape
    pieces = rows // rows_each
    count = columns - pieces * width
    step = pl.program_id(0)
    each = chips // pl.num_programs(0)
    for chip in range(each):
        weight_out[:, chip * count : (chip + 1) * count] = got_ref[step * each + chip, :, :count].astype(jnp.float32)

    @pl.when(step == 0)
    def _():
        total = got_ref[0, :, count:].astype(jnp.float32)
        for chip in range(1, chips):
            total = total + got_ref[chip, :, count:].astype(jnp.float32)
        total = jnp.concatenate([total[:, piece * width : (piece + 1) * width] for piece in range(pieces)], axis=0)
        hat, length = unit_rows(student_ref[...])
        feature_out[...] = (total - hat * jnp.sum(hat * total, axis=1, keepdims=True)) / length


def kernel_body(teacher_feat, student_feat, crop_weight, teacher_v, student_v):
    f32, bf16 = jnp.float32, jnp.bfloat16
    shape = jax.ShapeDtypeStruct
    blocks, fsdp = lax.axis_size("block"), lax.axis_size("fsdp")
    chips = blocks * GROUPS
    members, devices = blocks * fsdp, chips * fsdp
    rows, width = teacher_feat.shape
    crops = rows * devices
    lines = crops // LANES
    kept = teacher_v.shape[1]
    prototypes = kept * fsdp
    count = kept // blocks
    group, block = lax.axis_index("group")[None], lax.axis_index("block")[None]
    core = lax.axis_index("fsdp")[None]
    elements = count * crops
    vmem = pl.BlockSpec(memory_space=pltpu.VMEM)

    def swap(values):
        return lax.ppermute(values, "fsdp", [(0, 1), (1, 0)])

    def share(values):
        return lax.all_to_all(values, GROUP, 0, 0)

    dma = pltpu.SemaphoreType.DMA
    hbm = functools.partial(pltpu.with_memory_space_constraint, memory_space=pltpu.HBM)
    units = call(
        units_kernel,
        shape((rows + 16, 2 * width), bf16),
        in_specs=[pl.BlockSpec(memory_space=pl.ANY)] * 3,
        scratch_shapes=[pltpu.VMEM((rows, width), bf16)] * 2 + [pltpu.VMEM((1, rows), bf16), dma((3,))],
    )(hbm(teacher_feat), hbm(student_feat), hbm(crop_weight[None, :]))

    def of_groups(values):
        return [values] + [
            lax.ppermute(values, "group", [(at, (at + back) % GROUPS) for at in range(GROUPS)]) for back in range(1, GROUPS)
        ]

    units = of_groups(units)

    span = 2 * TILE
    spans = count // span
    column = pl.BlockSpec((width, span), lambda step, at: (0, at[0] * spans + step))
    turned = pl.BlockSpec((span, width), lambda step, at: (step, 0))
    line = pl.BlockSpec((1, span), lambda step, at: (0, step))
    teacher_w, student_w, inverse = call(
        directions_kernel,
        (
            shape((count, width), bf16),
            shape((count, width), bf16),
            shape((1, count), f32),
        ),
        flops=12 * count * width,
        moved=8 * count * width,
        grid_spec=pltpu.PrefetchScalarGridSpec(
            num_scalar_prefetch=1,
            grid=(spans,),
            in_specs=[column, column],
            out_specs=[turned, turned, line],
        ),
    )(
        block,
        hbm(teacher_v),
        hbm(student_v),
    )

    units, teacher_w = lax.optimization_barrier((units, teacher_w))
    sent = call(spread_kernel, shape((blocks, GROUPS * rows, 2 * width), bf16))(*units)
    own = lax.all_to_all(sent, "block", 0, 0)
    other = swap(own)
    half = crops // 2
    anyspace = pl.BlockSpec(memory_space=pl.ANY)
    pieces = count // (FETCH * TILE)
    halved = dict(flops=2 * elements * width, exps=elements)
    scratch = [pltpu.VMEM((half, width), bf16)] * 2
    own_mass, own_student, own_part, own_turned = call(
        own_kernel,
        (
            shape((count, half), f32),
            shape((count, half), f32),
            shape((8, half), f32),
            shape((width, half), bf16),
        ),
        scratch_shapes=scratch,
        **halved,
    )(teacher_w, student_w, own)
    other_mass, other_student, sent, student_part, other_turned = call(
        functools.partial(other_kernel, prototypes),
        (
            shape((count, half), f32),
            shape((count, half), f32),
            shape((members, 2 * lines, LANES), bf16),
            shape((lines, LANES), f32),
            shape((width, half), bf16),
        ),
        scratch_shapes=scratch,
        **halved,
    )(teacher_w, student_w, other, own_mass, own_part, *units)
    first = share(sent)
    sent, weights = call(
        functools.partial(sweep_kernel, prototypes, crops),
        (shape((members, 2 * lines, LANES), bf16), shape((lines, LANES), f32)),
        flops=4 * elements,
    )(own_mass, other_mass, first, student_part)
    second = share(sent)
    sent, own_scaled, other_scaled, student_copy = call(
        functools.partial(last_sweep_kernel, prototypes, crops),
        (
            shape((members, lines, LANES), bf16),
            shape((count, half), f32),
            shape((count, half), f32),
            shape((pieces, width, count // pieces), bf16),
        ),
        flops=4 * elements,
        in_specs=[vmem] * 3 + [anyspace],
        scratch_shapes=[dma((pieces,))],
    )(own_mass, other_mass, second, hbm(student_v))
    third = share(sent)

    gradient, keep, give = call(
        gradient_kernel,
        (shape((2, count, half), bf16), shape((half // GROUPS, width), f32), shape((half // GROUPS, width), bf16)),
        flops=2 * elements * width // GROUPS,
        in_specs=[vmem] * 9,
        scratch_shapes=[pltpu.VMEM((width, count), bf16)],
    )(own_scaled, other_scaled, own_student, other_student, weights, second, third, inverse, student_copy)
    other = swap(give)
    out_rows = width // chips
    per_chip = rows * width // out_rows
    sent = call(
        weight_kernel,
        shape((blocks, out_rows, count + per_chip), bf16),
        flops=2 * elements * width,
        in_specs=[vmem] * 5,
        scratch_shapes=[pltpu.VMEM((count // TILE, width, TILE), f32)],
    )(gradient, own_turned, other_turned, inverse, student_copy)
    sent = call(
        pack_kernel,
        shape((blocks, out_rows, count + per_chip), bf16),
        in_specs=[vmem] * 2 + [anyspace],
        out_specs=anyspace,
        input_output_aliases={2: 0},
        scratch_shapes=[pltpu.VMEM((blocks, out_rows, per_chip), bf16), dma],
    )(keep, other, sent)
    got = lax.all_to_all(sent, "block", 0, 0)
    return call(
        outputs_kernel,
        (shape((out_rows, kept), f32), shape((rows, width), f32)),
        grid=(2,),
        in_specs=[vmem, vmem],
        out_specs=[
            pl.BlockSpec((out_rows, kept // 2), lambda step: (0, step)),
            pl.BlockSpec((rows, width), lambda step: (0, 0)),
        ],
    )(got, student_feat)


def solution(mesh):
    dp, fsdp = mesh.shape["dp"], mesh.shape["fsdp"]
    blocks = dp // GROUPS

    def run(teacher_feat, student_feat, crop_weight, teacher_v, student_v):
        crops = teacher_feat.shape[0]
        count = teacher_v.shape[1] // (blocks * fsdp)
        fits = fsdp == 2 and dp == 16 and count % (2 * TILE) == 0 and crops == 1024
        if fits and 8 * count * crops <= KEPT_BYTES:
            grid = Mesh(mesh.devices.reshape(GROUPS, blocks, fsdp), (*CHIPS, "fsdp"))
            body, chips = kernel_body, CHIPS
        else:
            grid, body, chips = mesh, plain_body, ("dp",)
        every = P((*chips, "fsdp"))
        return jax.shard_map(
            body,
            mesh=grid,
            in_specs=(every, every, every, P(None, "fsdp"), P(None, "fsdp")),
            out_specs=(P(chips, "fsdp"), every),
            check_vma=False,
        )(teacher_feat, student_feat, crop_weight, teacher_v, student_v)

    return run
```
